32 devices in a mesh: tm: 4 (over y, x), agent: 8 (over z, core).
Axes of the slice: x: 2, y: 2, z: 4, core: 2. Of those that a mesh axis runs over, the one named last changes fastest.
Arguments:
- tokens: bfloat16 [16, 512, 1024], P('tm', 'agent'), may hold values from -6 to 6
- conv_taps: float32 [5, 1024], replicated, may hold values from -3 to 3
- norm_first: float32 [1024], replicated, may hold values from 0.1 to 1.9
- norm_second: float32 [1024], replicated, may hold values from 0.1 to 1.9
- norm_third: float32 [1024], replicated, may hold values from 0.1 to 1.9
- w_in: bfloat16 [1024, 3072], replicated, may hold values from -0.1875 to 0.1875
- w_out: bfloat16 [3072, 1024], replicated, may hold values from -0.109375 to 0.109375
- w_query: bfloat16 [1024, 1024], replicated, may hold values from -16 to 16
- w_key: bfloat16 [1024, 1024], replicated, may hold values from -16 to 16
- w_value: bfloat16 [1024, 1024], replicated, may hold values from -0.1875 to 0.1875
- w_output: bfloat16 [1024, 1024], replicated, may hold values from -0.1875 to 0.1875
- agent_order: int32 [512], P('agent'), may hold values from 0 to 511, each once
- present_steps: int32 [512], P('agent'), may hold values from 1 to 16
Outputs:
- result: bfloat16 [16, 512, 1024], P('tm', 'agent')
The draws below stay inside these ranges and needn't reach their ends.
Inputs may be any that keep to these rules, and one draw needn't show every extreme that they name: `agent_order`: each of 0 to 511 appears once.
All inputs are finite; a program needn't handle non-finite values.
Results may differ from the reference program's by a relative error of at most 0.012.
Values may be sent and summed in bfloat16 or wider, within the bound.
No kernel may reach another device: no remote copies, remote signals or barrier semaphores. Data moves between devices by JAX's collectives and lax.ppermute only.
A program may use at most 192 MiB of HBM per device.

```python
import jax
import jax.numpy as jnp
from jax import lax

D = 1024
HEADS = 16
FF = 3072
KERNEL = 5
HEAD = 64
STEPS = 16
AGENTS = 512


def shared_base(key):
    return jax.random.normal(jax.random.fold_in(key, 101), (D, D), jnp.float32) * D ** (-0.5)


def draw_w_query(key, part):
    extra = jax.random.normal(jax.random.fold_in(key, 102), (D, D), jnp.float32) * D ** (-0.5)
    return (shared_base(key) + 0.7 * extra).astype(jnp.bfloat16)


def draw_w_key(key, part):
    extra = jax.random.normal(jax.random.fold_in(key, 103), (D, D), jnp.float32) * D ** (-0.5)
    return (1.2 * extra).astype(jnp.bfloat16)


def set_ends(array, own_key, smallest, high):
    longest = array.shape.index(max(array.shape))
    spots = []
    for shift in (0, 1):
        where = [jax.random.randint(jax.random.fold_in(own_key, axis), (), 0, length) for axis, length in enumerate(array.shape)]
        where[longest] = (where[longest] + shift) % array.shape[longest]
        spots.append(tuple(where))
    return array.at[spots[0]].set(smallest).at[spots[1]].set(high)


def levels(stream_key, extent, pieces, least, high):
    level, own = 1.0, jax.random.fold_in(stream_key, 6)
    for position, blocks in pieces:
        draws = jnp.exp(jax.random.uniform(jax.random.fold_in(own, position), (blocks,), jnp.float32, least / len(pieces), high / len(pieces)))
        level = level * jnp.repeat(draws, extent[position] // blocks).reshape([-1 if axis == position else 1 for axis in range(len(extent))])
    return level


def centred(key, dims, spread, most, pieces=(), held_as=jnp.bfloat16):
    drawn = spread * jax.random.normal(key, dims, jnp.float32)
    if pieces:
        drawn = drawn * levels(key, dims, pieces, -0.22, 0.18)
    return jnp.clip(drawn, -most, most).astype(held_as)


def setup_inputs(seed: int = 0) -> dict:
    splits = jax.random.split(jax.random.key(seed), 14)
    return {
        "tokens": centred(splits[0], (STEPS, AGENTS, D), 1.0, 6.0, ((0, 4), (1, 8))),
        "conv_taps": centred(splits[1], (KERNEL, D), 0.5, 3.0, (), jnp.float32),
        "norm_first": jnp.clip(1.0 + 0.18 * jax.random.normal(splits[2], (D,), jnp.float32), 0.1, 1.9),
        "norm_second": jnp.clip(1.0 + 0.18 * jax.random.normal(splits[3], (D,), jnp.float32), 0.1, 1.9),
        "norm_third": jnp.clip(1.0 + 0.18 * jax.random.normal(splits[4], (D,), jnp.float32), 0.1, 1.9),
        "w_in": centred(splits[5], (D, FF), D ** -0.5, 0.1875),
        "w_out": centred(splits[6], (FF, D), FF ** -0.5, 0.109375),
        "w_query": draw_w_query(jax.random.fold_in(splits[13], 71), 0),
        "w_key": draw_w_key(jax.random.fold_in(splits[13], 71), 0),
        "w_value": centred(splits[9], (D, D), D ** -0.5, 0.1875),
        "w_output": centred(splits[10], (D, D), D ** -0.5, 0.1875),
        "agent_order": jax.random.permutation(splits[11], AGENTS).astype(jnp.int32),
        "present_steps": set_ends(jax.random.randint(splits[12], (AGENTS,), 1, STEPS + 1), jax.random.fold_in(splits[12], 1), 1, STEPS).astype(jnp.int32),
    }


EPS = 1e-05

def normed_rows(rows, gain):
    values = rows.astype(jnp.float32)
    scale = lax.rsqrt(lax.optimization_barrier(jnp.mean(values * values, axis=-1, keepdims=True)) + EPS)
    return values * scale * gain.astype(jnp.float32)

def reference(tokens, conv_taps, norm_first, norm_second, norm_third, w_in, w_out, w_query, w_key, w_value, w_output, agent_order, present_steps):
    reach = KERNEL - 1
    normed = normed_rows(tokens, norm_first)
    padded = jnp.pad(normed, ((reach, 0), (0, 0), (0, 0)))
    mixed = jnp.zeros(normed.shape, jnp.float32)
    for lag in range(KERNEL):
        mixed = mixed + conv_taps[lag].astype(jnp.float32) * padded[reach - lag:reach - lag + STEPS]
    first = (tokens.astype(jnp.float32) + mixed).astype(jnp.bfloat16)
    flat = first.reshape(STEPS * AGENTS, D)
    inner = normed_rows(flat, norm_second).astype(jnp.bfloat16)
    hidden = jax.nn.gelu(jnp.dot(inner, w_in, preferred_element_type=jnp.float32), approximate=False).astype(jnp.bfloat16)
    second = (flat.astype(jnp.float32) + jnp.dot(hidden, w_out, preferred_element_type=jnp.float32)).astype(jnp.bfloat16)
    attn_in = normed_rows(second, norm_third).astype(jnp.bfloat16)
    query = jnp.dot(attn_in, w_query, preferred_element_type=jnp.float32).astype(jnp.bfloat16).reshape(STEPS, AGENTS, HEADS, HEAD)
    keys = jnp.dot(attn_in, w_key, preferred_element_type=jnp.float32).astype(jnp.bfloat16).reshape(STEPS, AGENTS, HEADS, HEAD)
    values = jnp.dot(attn_in, w_value, preferred_element_type=jnp.float32).astype(jnp.bfloat16).reshape(STEPS, AGENTS, HEADS, HEAD)
    earlier = agent_order[None, :] < agent_order[:, None]
    itself = agent_order[None, :] == agent_order[:, None]
    scale = HEAD ** (-0.5)

    def one_step(item):
        step_query, step_keys, step_values, step = item
        scores = jnp.einsum('ahd,bhd->hab', step_query.astype(jnp.float32), step_keys.astype(jnp.float32)) * scale
        visible = earlier & (step < present_steps[None, :]) | itself
        masked = jnp.where(visible[None], scores, -1e+30)
        top = lax.optimization_barrier(jnp.max(masked, axis=-1, keepdims=True))
        weights = jnp.where(visible[None], jnp.exp(masked - top), 0.0).astype(jnp.bfloat16)
        total = lax.optimization_barrier(jnp.sum(weights.astype(jnp.float32), axis=-1))
        summed = jnp.einsum('hab,bhd->ahd', weights.astype(jnp.float32), step_values.astype(jnp.float32))
        return (summed / jnp.transpose(total)[:, :, None]).astype(jnp.bfloat16)
    attended = lax.map(one_step, (query, keys, values, jnp.arange(STEPS, dtype=jnp.int32)))
    attended = attended.reshape(STEPS * AGENTS, D)
    result = second.astype(jnp.float32) + jnp.dot(attended, w_output, preferred_element_type=jnp.float32)
    return result.astype(jnp.bfloat16).reshape(STEPS, AGENTS, D)
```

```python
import functools

import jax
import jax.numpy as jnp
from jax import lax
from jax.experimental import pallas as pl
from jax.experimental.pallas import tpu as pltpu
from jax.sharding import PartitionSpec as P

HEAD = 64
EPS = 1e-05
LOG2E = 1.4426950408889634
MIB = 1024 * 1024
VMEM = pl.BlockSpec(memory_space=pltpu.VMEM)
ANY = pl.BlockSpec(memory_space=pl.ANY)
SMEM = pl.BlockSpec(memory_space=pltpu.SMEM)


def pinned(x):
    return pltpu.with_memory_space_constraint(x, pltpu.VMEM)


def dot(a, b):
    return jnp.dot(a, b, preferred_element_type=jnp.float32)


def dot_t(a, b):
    return lax.dot_general(a, b, (((1,), (1,)), ((), ())), preferred_element_type=jnp.float32)


def norm_scale(values):
    return lax.rsqrt(jnp.mean(values * values, axis=-1, keepdims=True) + EPS)


def gelu(x):
    return 0.5 * x * (1.0 + lax.erf(x * 0.7071067811865476))


def conv_kernel(steps, place, halo, tokens, taps, gain, *rest):
    outs, normed = rest[:steps], rest[steps]
    reach = taps.shape[0] - 1
    gains = gain[...]
    for step in range(steps):
        for part, base in ((halo, 0), (tokens, steps)):
            values = part[step].astype(jnp.float32)
            normed[base + step] = values * norm_scale(values) * gains
    z = place[0]
    for k in range(steps):
        step = z ^ k
        mixed = tokens[step].astype(jnp.float32)
        total = taps[0:1, :] * normed[steps + step]
        for lag in range(1, reach + 1):
            total = total + taps[lag : lag + 1, :] * normed[steps + step - lag]
        outs[k][...] = (mixed + total).astype(jnp.bfloat16)


def conv(place, halo, tokens, taps, gain):
    steps, agents, width = tokens.shape
    piece = jax.ShapeDtypeStruct((agents, width), jnp.bfloat16)
    return pl.pallas_call(
        functools.partial(conv_kernel, steps),
        out_shape=[piece] * steps,
        in_specs=[SMEM] + [VMEM] * 4,
        out_specs=[VMEM] * steps,
        scratch_shapes=[pltpu.VMEM((2 * steps, agents, width), jnp.float32)],
        compiler_params=pltpu.CompilerParams(vmem_limit_bytes=16 * MIB),
        cost_estimate=pl.CostEstimate(flops=10**7, bytes_accessed=2 * 10**6, transcendentals=0),
        name="conv",
    )(place, halo, tokens, taps, gain)


def feed_kernel(count, *refs):
    pieces = refs[:count]
    gain_in, gain_attn, w_in, w_out, w_query, w_key, w_value = refs[count : count + 7]
    query, keyval, second, hidden = refs[count + 7 :]
    first = jnp.concatenate([piece[...].astype(jnp.float32) for piece in pieces], axis=0)
    inner = (first * norm_scale(first) * gain_in[...]).astype(jnp.bfloat16)
    tile = 512
    for start in range(0, w_in.shape[1], tile):
        hidden[:, start : start + tile] = gelu(dot(inner, w_in[:, start : start + tile])).astype(jnp.bfloat16)
    total = (first + dot(hidden[...], w_out[...])).astype(jnp.bfloat16)
    second[...] = total
    values = total.astype(jnp.float32)
    attn_in = (values * norm_scale(values) * gain_attn[...]).astype(jnp.bfloat16)
    width = total.shape[1]
    query[...] = dot(attn_in, w_query[...]).astype(jnp.bfloat16)
    keyval[:, :width] = dot(attn_in, w_key[...]).astype(jnp.bfloat16)
    keyval[:, width:] = dot(attn_in, w_value[...]).astype(jnp.bfloat16)


def feed(pieces, gain_in, gain_attn, w_in, w_out, w_query, w_key, w_value):
    rows = sum(piece.shape[0] for piece in pieces)
    width = pieces[0].shape[1]
    return pl.pallas_call(
        functools.partial(feed_kernel, len(pieces)),
        out_shape=[
            jax.ShapeDtypeStruct((rows, width), jnp.bfloat16),
            jax.ShapeDtypeStruct((rows, 2 * width), jnp.bfloat16),
            jax.ShapeDtypeStruct((rows, width), jnp.bfloat16),
        ],
        in_specs=[VMEM] * (len(pieces) + 7),
        out_specs=[VMEM] * 3,
        scratch_shapes=[pltpu.VMEM((rows, w_in.shape[1]), jnp.bfloat16)],
        compiler_params=pltpu.CompilerParams(vmem_limit_bytes=16 * MIB),
        cost_estimate=pl.CostEstimate(flops=5 * 10**9, bytes_accessed=20 * 10**6, transcendentals=0),
        name="feed",
    )(*pieces, gain_in, gain_attn, pinned(w_in), pinned(w_out), pinned(w_query), pinned(w_key), pinned(w_value))


def attend_kernel(steps, others, place, info, query, second, w_output, *rest):
    blocks, outs = rest[: 1 + others], rest[1 + others : 1 + others + steps]
    bias, attended = rest[1 + others + steps :]
    rows, width = query.shape
    agents = rows // steps
    z, member, group, now = place[0], place[1], place[2], place[3]
    lane = lax.broadcasted_iota(jnp.int32, (agents, 128), 1)
    diagonal = lane == lax.broadcasted_iota(jnp.int32, (agents, 128), 0)
    first_half = lane < agents
    own_columns = []
    for k in range(steps):
        row = info[pl.ds(pl.multiple_of(8 * ((z ^ k) * group + member), 8), 8), :][0:1]
        own_columns.append(jnp.sum(jnp.where(diagonal, row, 0.0), axis=1, keepdims=True))
    own = jnp.concatenate(own_columns, axis=0)
    present_now = now.astype(jnp.float32)
    lane_row = lax.broadcasted_iota(jnp.int32, (1, 128), 1) < agents
    for r in range(1 + others):
        for pair in range(steps // 2):
            tiles = [
                info[pl.ds(pl.multiple_of(8 * ((z ^ k) * group + (member ^ r)), 8), 8), :]
                for k in (2 * pair, 2 * pair + 1)
            ]
            order = jnp.where(lane_row, tiles[0][0:1], tiles[1][0:1])
            present = jnp.where(lane_row, tiles[0][1:2], tiles[1][1:2])
            alive_order = jnp.where(present_now < present, order, 1e9)
            visible = (alive_order < own) | (order == own)
            start = r * rows + pair * 128
            bias[:, start : start + 128] = jnp.where(visible, 0.0, -1e30)
    scale = LOG2E * HEAD ** (-0.5)
    low = lax.broadcasted_iota(jnp.int32, (rows, 128), 1) < HEAD
    ones = jnp.ones((rows, 128), jnp.bfloat16)
    for head_pair in range(width // 128):
        columns = slice(128 * head_pair, 128 * head_pair + 128)
        value_columns = slice(width + 128 * head_pair, width + 128 * head_pair + 128)
        queries = query[:, columns]
        results = []
        for half in (low, ~low):
            masked = jnp.where(half, queries, jnp.zeros_like(queries))
            scores = [
                dot_t(masked, block[:, columns]) * scale + bias[:, r * rows : (r + 1) * rows]
                for r, block in enumerate(blocks)
            ]
            top = functools.reduce(jnp.maximum, [jnp.max(s, axis=1, keepdims=True) for s in scores])
            total = None
            for s, block in zip(scores, blocks):
                weights = jnp.exp2(s - top).astype(jnp.bfloat16)
                part = dot(weights, jnp.concatenate([block[:, value_columns], ones], axis=1))
                total = part if total is None else total + part
            results.append(total[:, :128] / total[:, 128:])
        attended[:, columns] = jnp.where(low, results[0], results[1]).astype(jnp.bfloat16)
    result = second[...].astype(jnp.float32) + dot(attended[...], w_output[...])
    for k in range(steps):
        outs[k][...] = result[k * agents : (k + 1) * agents].astype(jnp.bfloat16)


def attend(place, info, query, second, w_output, blocks, steps):
    rows, width = query.shape
    piece = jax.ShapeDtypeStruct((rows // steps, width), jnp.bfloat16)
    return pl.pallas_call(
        functools.partial(attend_kernel, steps, len(blocks) - 1),
        out_shape=[piece] * steps,
        in_specs=[SMEM] + [VMEM] * (4 + len(blocks)),
        out_specs=[VMEM] * steps,
        scratch_shapes=[
            pltpu.VMEM((rows, rows * len(blocks)), jnp.float32),
            pltpu.VMEM((rows, width), jnp.bfloat16),
        ],
        compiler_params=pltpu.CompilerParams(vmem_limit_bytes=24 * MIB),
        cost_estimate=pl.CostEstimate(flops=4 * 10**9, bytes_accessed=6 * 10**6, transcendentals=2 * 10**6),
        name="attend",
    )(place, info, query, second, pinned(w_output), *blocks)


def place_kernel(steps, place, *refs):
    pieces, out = refs[:steps], refs[steps]
    for k in range(steps):
        out[place[0] ^ k] = pieces[k][...]


def put_back(place, pieces):
    steps = len(pieces)
    agents, width = pieces[0].shape
    return pl.pallas_call(
        functools.partial(place_kernel, steps),
        out_shape=jax.ShapeDtypeStruct((steps, agents, width), jnp.bfloat16),
        in_specs=[SMEM] + [VMEM] * steps,
        out_specs=VMEM,
        compiler_params=pltpu.CompilerParams(vmem_limit_bytes=8 * MIB),
        name="put_back",
    )(place, *pieces)


def per_device(
    tokens,
    conv_taps,
    norm_first,
    norm_second,
    norm_third,
    w_in,
    w_out,
    w_query,
    w_key,
    w_value,
    w_output,
    agent_order,
    present_steps,
):
    steps, agents, width = tokens.shape
    tm_count, count = lax.axis_size("tm"), lax.axis_size("agent")
    group = count // steps
    assert group * steps == count and steps == 4 and agents == 64
    spot = lax.axis_index("agent")
    z, member = spot // group, spot % group
    now = lax.axis_index("tm") * steps + z
    place = jnp.stack([z, member, jnp.int32(group), now]).astype(jnp.int32)

    def across(x, k):
        return lax.ppermute(x, "agent", [(i, ((i // group) ^ k) * group + i % group) for i in range(count)])

    def within(x, r):
        return lax.ppermute(x, "agent", [(i, (i // group) * group + ((i % group) ^ r)) for i in range(count)])

    halo = lax.ppermute(tokens, "tm", [(i, i + 1) for i in range(tm_count - 1)])
    rows = jnp.stack([agent_order, present_steps]).astype(jnp.float32)
    info = jnp.pad(jnp.concatenate([rows, rows], axis=1), ((0, 6), (0, 0)))
    info = lax.all_gather(info, "agent", axis=0, tiled=True)
    pieces = conv(place, halo, tokens, conv_taps, norm_first.reshape(1, width))
    pieces = [pieces[0]] + [across(pieces[k], k) for k in range(1, steps)]
    query, keyval, second = feed(
        pieces, norm_second.reshape(1, width), norm_third.reshape(1, width), w_in, w_out, w_query, w_key, w_value
    )
    blocks = [keyval] + [within(keyval, r) for r in range(1, group)]
    results = attend(place, info, query, second, w_output, blocks, steps)
    results = [results[0]] + [across(results[k], k) for k in range(1, steps)]
    return put_back(place, results)


def solution(mesh):
    in_specs = (P("tm", "agent", None),) + (P(),) * 10 + (P("agent"), P("agent"))
    return jax.shard_map(
        per_device, mesh=mesh, in_specs=in_specs, out_specs=P("tm", "agent", None), check_vma=False
    )
```

```python
import functools

import jax
import jax.numpy as jnp
from jax import lax
from jax.experimental import pallas as pl
from jax.experimental.pallas import tpu as pltpu
from jax.sharding import PartitionSpec as P

HEAD = 64
CHUNKS = 1
EPS = 1e-05
LOG2E = 1.4426950408889634
MIB = 1024 * 1024
VMEM = pl.BlockSpec(memory_space=pltpu.VMEM)
ANY = pl.BlockSpec(memory_space=pl.ANY)
SMEM = pl.BlockSpec(memory_space=pltpu.SMEM)


HBM = pl.BlockSpec(memory_space=pltpu.HBM)


def pinned(x):
    return pltpu.with_memory_space_constraint(x, pltpu.VMEM)


def far(x):
    return pltpu.with_memory_space_constraint(x, pltpu.HBM)


def dot(a, b):
    return jnp.dot(a, b, preferred_element_type=jnp.float32)


def dot_t(a, b):
    return lax.dot_general(a, b, (((1,), (1,)), ((), ())), preferred_element_type=jnp.float32)


def norm_scale(values):
    return lax.rsqrt(jnp.mean(values * values, axis=-1, keepdims=True) + EPS)


def gelu(x):
    return 0.5 * x * (1.0 + lax.erf(x * 0.7071067811865476))


def stage_kernel(count, tokens, taps, gain, *rest):
    sources, partial, targets = rest[:count], rest[count], rest[count + 1 : 2 * count + 1]
    tokens_here, taps_here, gain_here, normed, small_sem, sem = rest[2 * count + 1 :]
    small = [
        pltpu.make_async_copy(source, target, small_sem.at[i])
        for i, (source, target) in enumerate(((tokens, tokens_here), (taps, taps_here), (gain, gain_here)))
    ]
    copies = [pltpu.make_async_copy(sources[i], targets[i], sem.at[i]) for i in range(count)]
    for copy in small + copies:
        copy.start()
    for copy in small:
        copy.wait()
    steps, reach = tokens.shape[0], taps.shape[0] - 1
    gains = gain_here[...]
    for step in range(steps):
        values = tokens_here[step].astype(jnp.float32)
        normed[step] = values * norm_scale(values) * gains
        total = values
        for lag in range(min(step, reach) + 1):
            total = total + taps_here[lag : lag + 1, :] * normed[step - lag]
        partial[step] = total
    for copy in copies:
        copy.wait()


def stage(tokens, taps, gain, arrays):
    steps, agents, width = tokens.shape
    count = len(arrays)
    return pl.pallas_call(
        functools.partial(stage_kernel, count),
        out_shape=[pltpu.VMEM((steps, agents, width), jnp.float32)] + [pltpu.VMEM(x.shape, x.dtype) for x in arrays],
        in_specs=[HBM] * (3 + count),
        out_specs=[VMEM] * (1 + count),
        scratch_shapes=[
            pltpu.VMEM(tokens.shape, tokens.dtype),
            pltpu.VMEM(taps.shape, taps.dtype),
            pltpu.VMEM(gain.shape, gain.dtype),
            pltpu.VMEM((steps, agents, width), jnp.float32),
            pltpu.SemaphoreType.DMA((3,)),
            pltpu.SemaphoreType.DMA((count,)),
        ],
        compiler_params=pltpu.CompilerParams(vmem_limit_bytes=8 * MIB),
        cost_estimate=pl.CostEstimate(flops=10**7, bytes_accessed=22 * 10**6, transcendentals=0),
        name="stage",
    )(*[far(x) for x in (tokens, taps, gain, *arrays)])


def conv_kernel(steps, place, halo, partial, taps, gain, *rest):
    outs, normed = rest[:steps], rest[steps]
    reach = taps.shape[0] - 1
    gains = gain[...]
    for step in range(steps):
        values = halo[step].astype(jnp.float32)
        normed[step] = values * norm_scale(values) * gains
    z = place[0]
    for step in range(steps):
        total = partial[step]
        for lag in range(step + 1, reach + 1):
            total = total + taps[lag : lag + 1, :] * normed[steps + step - lag]
        normed[steps + step] = total
    for k in range(steps):
        outs[k][...] = normed[steps + (z ^ k)].astype(jnp.bfloat16)


def conv(place, halo, partial, taps, gain):
    steps, agents, width = halo.shape
    piece = jax.ShapeDtypeStruct((agents, width), jnp.bfloat16)
    return pl.pallas_call(
        functools.partial(conv_kernel, steps),
        out_shape=[piece] * steps,
        in_specs=[SMEM] + [VMEM] * 4,
        out_specs=[VMEM] * steps,
        scratch_shapes=[pltpu.VMEM((2 * steps, agents, width), jnp.float32)],
        compiler_params=pltpu.CompilerParams(vmem_limit_bytes=8 * MIB),
        cost_estimate=pl.CostEstimate(flops=10**7, bytes_accessed=2 * 10**6, transcendentals=0),
        name="conv",
    )(place, halo, pinned(partial), pinned(taps), pinned(gain))


def mask_kernel(steps, chunks, agents, group, place, info, bias):
    z, member, now = place[0], place[1], place[2].astype(jnp.float32)
    lane = lax.broadcasted_iota(jnp.int32, (agents, 128), 1)
    diagonal = lane == lax.broadcasted_iota(jnp.int32, (agents, 128), 0)

    def tile(k, r):
        return info[pl.ds(pl.multiple_of(8 * ((z ^ k) * group + (member ^ r)), 8), 8), :]

    tiles = {(k, r): tile(k, r) for k in range(steps) for r in range(group)}
    own = jnp.concatenate(
        [
            jnp.sum(jnp.where(diagonal, tiles[k, 0][2 * j : 2 * j + 1], 0.0), axis=1, keepdims=True)
            for j in range(chunks)
            for k in range(steps)
        ],
        axis=0,
    )
    row_lane = lax.broadcasted_iota(jnp.int32, (1, 128), 1)
    per_tile = 128 // agents
    start = 0
    for r in range(group):
        for j in range(chunks):
            for first in range(0, steps, per_tile):
                order = tiles[first, r][2 * j : 2 * j + 1]
                present = tiles[first, r][2 * j + 1 : 2 * j + 2]
                for i in range(1, per_tile):
                    later = row_lane >= i * agents
                    order = jnp.where(later, tiles[first + i, r][2 * j : 2 * j + 1], order)
                    present = jnp.where(later, tiles[first + i, r][2 * j + 1 : 2 * j + 2], present)
                alive = jnp.where(now < present, order, 1e9)
                visible = (alive < own) | (order == own)
                bias[:, start : start + 128] = jnp.where(visible, 0.0, -1e30)
                start += 128


def mask(place, info, steps, agents, group):
    rows = steps * agents * CHUNKS
    return pl.pallas_call(
        functools.partial(mask_kernel, steps, CHUNKS, agents, group),
        out_shape=pltpu.VMEM((rows, rows * group), jnp.float32),
        in_specs=[SMEM, VMEM],
        out_specs=VMEM,
        compiler_params=pltpu.CompilerParams(vmem_limit_bytes=8 * MIB),
        cost_estimate=pl.CostEstimate(flops=10**6, bytes_accessed=10**6, transcendentals=0),
        name="mask",
    )(place, info)


def feed_kernel(count, *refs):
    pieces = refs[:count]
    gain_in, gain_attn, w_in, w_out, w_query, w_key, w_value = refs[count : count + 7]
    query, keyval, second, hidden = refs[count + 7 :]
    first = jnp.concatenate([piece[...].astype(jnp.float32) for piece in pieces], axis=0)
    inner = (first * norm_scale(first) * gain_in[...]).astype(jnp.bfloat16)
    tile = 512
    for start in range(0, w_in.shape[1], tile):
        hidden[:, start : start + tile] = gelu(dot(inner, w_in[:, start : start + tile])).astype(jnp.bfloat16)
    total = (first + dot(hidden[...], w_out[...])).astype(jnp.bfloat16)
    second[...] = total
    values = total.astype(jnp.float32)
    attn_in = (values * norm_scale(values) * gain_attn[...]).astype(jnp.bfloat16)
    width = total.shape[1]
    query[...] = dot(attn_in, w_query[...]).astype(jnp.bfloat16)
    keyval[:, :width] = dot(attn_in, w_key[...]).astype(jnp.bfloat16)
    keyval[:, width:] = dot(attn_in, w_value[...]).astype(jnp.bfloat16)


def feed(pieces, arrays):
    rows = sum(piece.shape[0] for piece in pieces)
    width = pieces[0].shape[1]
    hidden = arrays[2].shape[1]
    return pl.pallas_call(
        functools.partial(feed_kernel, len(pieces)),
        out_shape=[
            jax.ShapeDtypeStruct((rows, width), jnp.bfloat16),
            jax.ShapeDtypeStruct((rows, 2 * width), jnp.bfloat16),
            jax.ShapeDtypeStruct((rows, width), jnp.bfloat16),
        ],
        in_specs=[VMEM] * (len(pieces) + 7),
        out_specs=[VMEM] * 3,
        scratch_shapes=[pltpu.VMEM((rows, hidden), jnp.bfloat16)],
        compiler_params=pltpu.CompilerParams(vmem_limit_bytes=16 * MIB),
        cost_estimate=pl.CostEstimate(flops=5 * 10**9, bytes_accessed=20 * 10**6, transcendentals=0),
        name="feed",
    )(*pieces, *[pinned(x) for x in arrays])


def attend_kernel(steps, count, chunk, query, second, w_output, bias, *rest):
    blocks, outs, attended = rest[:count], rest[count : count + steps], rest[count + steps]
    rows, width = query.shape
    agents = rows // steps
    scale = LOG2E * HEAD ** (-0.5)
    low = lax.broadcasted_iota(jnp.int32, (rows, 128), 1) < HEAD
    ones = jnp.ones((blocks[0].shape[0], 128), jnp.bfloat16)
    here = slice(chunk * rows, chunk * rows + rows)
    for head_pair in range(width // 128):
        columns = slice(128 * head_pair, 128 * head_pair + 128)
        value_columns = slice(width + 128 * head_pair, width + 128 * head_pair + 128)
        queries = query[:, columns]
        results = []
        for half in (low, ~low):
            masked = jnp.where(half, queries, jnp.zeros_like(queries))
            scores, start = [], 0
            for block in blocks:
                end = start + block.shape[0]
                scores.append(dot_t(masked, block[:, columns]) * scale + bias[here, start:end])
                start = end
            top = functools.reduce(jnp.maximum, [jnp.max(s, axis=1, keepdims=True) for s in scores])
            total = None
            for s, block in zip(scores, blocks):
                weights = jnp.exp2(s - top).astype(jnp.bfloat16)
                part = dot(weights, jnp.concatenate([block[:, value_columns], ones], axis=1))
                total = part if total is None else total + part
            results.append(total[:, :128] / total[:, 128:])
        attended[:, columns] = jnp.where(low, results[0], results[1]).astype(jnp.bfloat16)
    result = second[...].astype(jnp.float32) + dot(attended[...], w_output[...])
    for k in range(steps):
        outs[k][...] = result[k * agents : (k + 1) * agents].astype(jnp.bfloat16)


def attend(chunk, query, second, w_output, bias, blocks, steps):
    rows, width = query.shape
    piece = jax.ShapeDtypeStruct((rows // steps, width), jnp.bfloat16)
    return pl.pallas_call(
        functools.partial(attend_kernel, steps, len(blocks), chunk),
        out_shape=[piece] * steps,
        in_specs=[VMEM] * (4 + len(blocks)),
        out_specs=[VMEM] * steps,
        scratch_shapes=[pltpu.VMEM((rows, width), jnp.bfloat16)],
        compiler_params=pltpu.CompilerParams(vmem_limit_bytes=16 * MIB),
        cost_estimate=pl.CostEstimate(flops=4 * 10**9, bytes_accessed=6 * 10**6, transcendentals=2 * 10**6),
        name="attend",
    )(query, second, pinned(w_output), pinned(bias), *blocks)


def put_back_kernel(steps, place, *refs):
    count = len(refs) - 2
    pieces, out, sem = refs[:count], refs[count], refs[count + 1]
    agents = pieces[0].shape[0]
    copies = []
    for i, piece in enumerate(pieces):
        chunk, k = divmod(i, steps)
        target = out.at[place[0] ^ k, pl.ds(chunk * agents, agents)]
        copies.append(pltpu.make_async_copy(piece, target, sem.at[i]))
    for copy in copies:
        copy.start()
    for copy in copies:
        copy.wait()


def put_back(place, pieces, shape):
    return pl.pallas_call(
        functools.partial(put_back_kernel, shape[0]),
        out_shape=jax.ShapeDtypeStruct(shape, jnp.bfloat16),
        in_specs=[SMEM] + [VMEM] * len(pieces),
        out_specs=ANY,
        scratch_shapes=[pltpu.SemaphoreType.DMA((len(pieces),))],
        compiler_params=pltpu.CompilerParams(vmem_limit_bytes=8 * MIB),
        name="put_back",
    )(place, *pieces)


def per_device(
    tokens,
    conv_taps,
    norm_first,
    norm_second,
    norm_third,
    w_in,
    w_out,
    w_query,
    w_key,
    w_value,
    w_output,
    agent_order,
    present_steps,
):
    steps, agents, width = tokens.shape
    tm_count, count = lax.axis_size("tm"), lax.axis_size("agent")
    group = count // steps
    part = agents // CHUNKS
    assert group * steps == count and steps == 4 and 128 % part == 0 and 2 * CHUNKS <= 8
    spot = lax.axis_index("agent")
    z, member = spot // group, spot % group
    now = lax.axis_index("tm") * steps + z
    place = jnp.stack([z, member, now]).astype(jnp.int32)

    def across(x, k):
        return lax.ppermute(x, "agent", [(i, ((i // group) ^ k) * group + i % group) for i in range(count)])

    def within(x, r):
        return lax.ppermute(x, "agent", [(i, (i // group) * group + ((i % group) ^ r)) for i in range(count)])

    halo = lax.ppermute(tokens, "tm", [(i, i + 1) for i in range(tm_count - 1)])
    rows = jnp.stack([agent_order.reshape(CHUNKS, part), present_steps.reshape(CHUNKS, part)], axis=1)
    rows = jnp.tile(rows.astype(jnp.float32).reshape(2 * CHUNKS, part), (1, 128 // part))
    info = jnp.pad(rows, ((0, 8 - 2 * CHUNKS), (0, 0)))
    partial, taps, gain_first, gain_second, gain_third, *weights = stage(
        tokens,
        conv_taps,
        norm_first.reshape(1, width),
        [conv_taps]
        + [x.reshape(1, width) for x in (norm_first, norm_second, norm_third)]
        + [w_in, w_out, w_query, w_key, w_value, w_output],
    )
    info = lax.all_gather(info, "agent", axis=0, tiled=True)
    halo, info, partial = lax.optimization_barrier((halo, info, partial))
    first = conv(place, halo, partial, taps, gain_first)
    first = [first[0]] + [across(first[k], k) for k in range(1, steps)]
    bias = mask(place, info, steps, part, group)
    *first, bias = lax.optimization_barrier((*first, bias))
    query, keyval, second = feed(first, [gain_second, gain_third, *weights[:5]])
    blocks = [keyval] + [within(keyval, r) for r in range(1, group)]
    results = attend(0, query, second, weights[5], bias, blocks, steps)
    results = [results[0]] + [across(results[k], k) for k in range(1, steps)]
    return put_back(place, results, tokens.shape)


def solution(mesh):
    in_specs = (P("tm", "agent", None),) + (P(),) * 10 + (P("agent"), P("agent"))
    return jax.shard_map(
        per_device, mesh=mesh, in_specs=in_specs, out_specs=P("tm", "agent", None), check_vma=False
    )
```

```python
import functools

import jax
import jax.numpy as jnp
from jax import lax
from jax.experimental import pallas as pl
from jax.experimental.pallas import tpu as pltpu
from jax.sharding import PartitionSpec as P

HEAD = 64
CHUNKS = 2
EPS = 1e-05
LOG2E = 1.4426950408889634
MIB = 1024 * 1024
VMEM = pl.BlockSpec(memory_space=pltpu.VMEM)
ANY = pl.BlockSpec(memory_space=pl.ANY)
SMEM = pl.BlockSpec(memory_space=pltpu.SMEM)


HBM = pl.BlockSpec(memory_space=pltpu.HBM)


def pinned(x):
    return pltpu.with_memory_space_constraint(x, pltpu.VMEM)


def far(x):
    return pltpu.with_memory_space_constraint(x, pltpu.HBM)


def dot(a, b):
    return jnp.dot(a, b, preferred_element_type=jnp.float32)


def dot_t(a, b):
    return lax.dot_general(a, b, (((1,), (1,)), ((), ())), preferred_element_type=jnp.float32)


def norm_scale(values):
    return lax.rsqrt(jnp.mean(values * values, axis=-1, keepdims=True) + EPS)


def gelu(x):
    return 0.5 * x * (1.0 + lax.erf(x * 0.7071067811865476))


def stage_kernel(count, tokens, taps, gain, *rest):
    sources, partial, targets = rest[:count], rest[count], rest[count + 1 : 2 * count + 1]
    tokens_here, taps_here, gain_here, normed, small_sem, sem = rest[2 * count + 1 :]
    small = [
        pltpu.make_async_copy(source, target, small_sem.at[i])
        for i, (source, target) in enumerate(((tokens, tokens_here), (taps, taps_here), (gain, gain_here)))
    ]
    copies = [pltpu.make_async_copy(sources[i], targets[i], sem.at[i]) for i in range(count)]
    for copy in small + copies:
        copy.start()
    for copy in small:
        copy.wait()
    steps, reach = tokens.shape[0], taps.shape[0] - 1
    gains = gain_here[...]
    for step in range(steps):
        values = tokens_here[step].astype(jnp.float32)
        normed[step] = values * norm_scale(values) * gains
        total = values
        for lag in range(min(step, reach) + 1):
            total = total + taps_here[lag : lag + 1, :] * normed[step - lag]
        partial[step] = total
    for copy in copies:
        copy.wait()


def stage(tokens, taps, gain, arrays):
    steps, agents, width = tokens.shape
    count = len(arrays)
    return pl.pallas_call(
        functools.partial(stage_kernel, count),
        out_shape=[pltpu.VMEM((steps, agents, width), jnp.float32)] + [pltpu.VMEM(x.shape, x.dtype) for x in arrays],
        in_specs=[HBM] * (3 + count),
        out_specs=[VMEM] * (1 + count),
        scratch_shapes=[
            pltpu.VMEM(tokens.shape, tokens.dtype),
            pltpu.VMEM(taps.shape, taps.dtype),
            pltpu.VMEM(gain.shape, gain.dtype),
            pltpu.VMEM((steps, agents, width), jnp.float32),
            pltpu.SemaphoreType.DMA((3,)),
            pltpu.SemaphoreType.DMA((count,)),
        ],
        compiler_params=pltpu.CompilerParams(vmem_limit_bytes=8 * MIB),
        cost_estimate=pl.CostEstimate(flops=10**7, bytes_accessed=22 * 10**6, transcendentals=0),
        name="stage",
    )(*[far(x) for x in (tokens, taps, gain, *arrays)])


def conv_kernel(steps, chunk, place, halo, partial, taps, gain, *rest):
    outs, normed = rest[:steps], rest[steps]
    reach = taps.shape[0] - 1
    agents = halo.shape[1]
    gains = gain[...]
    for step in range(steps):
        values = halo[step].astype(jnp.float32)
        normed[step] = values * norm_scale(values) * gains
    z = place[0]
    for step in range(steps):
        total = partial[step, chunk * agents : (chunk + 1) * agents, :]
        for lag in range(step + 1, reach + 1):
            total = total + taps[lag : lag + 1, :] * normed[steps + step - lag]
        normed[steps + step] = total
    for k in range(steps):
        outs[k][...] = normed[steps + (z ^ k)].astype(jnp.bfloat16)


def conv(chunk, place, halo, partial, taps, gain):
    steps, agents, width = halo.shape
    piece = jax.ShapeDtypeStruct((agents, width), jnp.bfloat16)
    return pl.pallas_call(
        functools.partial(conv_kernel, steps, chunk),
        out_shape=[piece] * steps,
        in_specs=[SMEM] + [VMEM] * 4,
        out_specs=[VMEM] * steps,
        scratch_shapes=[pltpu.VMEM((2 * steps, agents, width), jnp.float32)],
        compiler_params=pltpu.CompilerParams(vmem_limit_bytes=8 * MIB),
        cost_estimate=pl.CostEstimate(flops=10**7, bytes_accessed=2 * 10**6, transcendentals=0),
        name="conv",
    )(place, halo, pinned(partial), pinned(taps), pinned(gain))


def mask_kernel(steps, chunks, agents, group, place, *rest):
    infos, bias = rest[:group], rest[group]
    now = place[1].astype(jnp.float32)
    lane = lax.broadcasted_iota(jnp.int32, (agents, 128), 1)
    sublane = lax.broadcasted_iota(jnp.int32, (agents, 128), 0)
    tiles = {(k, r): infos[r][8 * k : 8 * k + 8] for k in range(steps) for r in range(group)}
    own = jnp.concatenate(
        [
            jnp.sum(jnp.where(lane == sublane + j * agents, tiles[k, 0][0:1], 0.0), axis=1, keepdims=True)
            for j in range(chunks)
            for k in range(steps)
        ],
        axis=0,
    )
    lane_all = lax.broadcasted_iota(jnp.int32, (8, 128), 1)
    per_tile = 128 // agents
    start = 0
    for r in range(group):
        for j in range(chunks):
            for first in range(0, steps, per_tile):
                both = None
                for i in range(per_tile):
                    moved = pltpu.roll(tiles[first + i, r], ((i - j) * agents) % 128, 1)
                    both = moved if both is None else jnp.where(lane_all >= i * agents, moved, both)
                order, present = both[0:1], both[1:2]
                alive = jnp.where(now < present, order, 1e9)
                visible = (alive < own) | (order == own)
                bias[:, start : start + 128] = jnp.where(visible, 0.0, -1e30)
                start += 128


def mask(infos, place, steps, agents):
    rows, group = steps * agents * CHUNKS, len(infos)
    return pl.pallas_call(
        functools.partial(mask_kernel, steps, CHUNKS, agents, group),
        out_shape=pltpu.VMEM((rows, rows * group), jnp.float32),
        in_specs=[SMEM] + [VMEM] * group,
        out_specs=VMEM,
        compiler_params=pltpu.CompilerParams(vmem_limit_bytes=8 * MIB),
        cost_estimate=pl.CostEstimate(flops=10**6, bytes_accessed=10**6, transcendentals=0),
        name="mask",
    )(place, *infos)


def feed_kernel(count, held, loaded, spare, *refs):
    pieces = refs[:count]
    gain_in, gain_attn = refs[count : count + 2]
    sources = refs[count + 2 : count + 2 + held + loaded + spare]
    rest = refs[count + 2 + held + loaded + spare :]
    query, keyval, second = rest[:3]
    targets = rest[3 : 3 + loaded + spare]
    hidden, sem = rest[3 + loaded + spare :]
    copies = [
        pltpu.make_async_copy(source, target, sem.at[i])
        for i, (source, target) in enumerate(zip(sources[held:], targets))
    ]
    for copy in copies:
        copy.start()
    weights = list(sources[:held]) + list(targets[:loaded])
    waits = [None] * held + copies

    def weight(i):
        if waits[i] is not None:
            waits[i].wait()
        return weights[i]

    first = jnp.concatenate([piece[...].astype(jnp.float32) for piece in pieces], axis=0)
    inner = (first * norm_scale(first) * gain_in[...]).astype(jnp.bfloat16)
    tile = 512
    w_in = weight(0)
    for start in range(0, w_in.shape[1], tile):
        hidden[:, start : start + tile] = gelu(dot(inner, w_in[:, start : start + tile])).astype(jnp.bfloat16)
    total = (first + dot(hidden[...], weight(1)[...])).astype(jnp.bfloat16)
    second[...] = total
    values = total.astype(jnp.float32)
    attn_in = (values * norm_scale(values) * gain_attn[...]).astype(jnp.bfloat16)
    width = total.shape[1]
    keyval[:, :width] = dot(attn_in, weight(2)[...]).astype(jnp.bfloat16)
    keyval[:, width:] = dot(attn_in, weight(3)[...]).astype(jnp.bfloat16)
    query[...] = dot(attn_in, weight(4)[...]).astype(jnp.bfloat16)
    for copy in copies[loaded:]:
        copy.wait()


def feed(pieces, gains, held, loaded, spare, last):
    rows = sum(piece.shape[0] for piece in pieces)
    width = pieces[0].shape[1]
    hidden = held[0].shape[1]
    fetched = [*loaded, *spare]
    return pl.pallas_call(
        functools.partial(feed_kernel, len(pieces), len(held), len(loaded), len(spare)),
        out_shape=[
            jax.ShapeDtypeStruct((rows, width), jnp.bfloat16),
            jax.ShapeDtypeStruct((rows, 2 * width), jnp.bfloat16),
            jax.ShapeDtypeStruct((rows, width), jnp.bfloat16),
        ]
        + [pltpu.VMEM(x.shape, x.dtype) for x in fetched],
        in_specs=[VMEM] * (len(pieces) + 2 + len(held)) + [HBM] * len(fetched),
        out_specs=[VMEM] * (3 + len(fetched)),
        scratch_shapes=[
            pltpu.VMEM((rows, hidden), jnp.bfloat16),
            pltpu.SemaphoreType.DMA((max(len(fetched), 1),)),
        ],
        compiler_params=pltpu.CompilerParams(vmem_limit_bytes=16 * MIB),
        cost_estimate=pl.CostEstimate(
            flops=10**10 if last else 10**6, bytes_accessed=2 * 10**7 if last else 10**5, transcendentals=0
        ),
        name="feed",
    )(*pieces, *[pinned(x) for x in (*gains, *held)], *[far(x) for x in fetched])


def attend_kernel(steps, count, chunk, query, second, w_output, bias, *rest):
    blocks, outs, attended = rest[:count], rest[count : count + steps], rest[count + steps]
    rows, width = query.shape
    agents = rows // steps
    scale = LOG2E * HEAD ** (-0.5)
    low = lax.broadcasted_iota(jnp.int32, (rows, 128), 1) < HEAD
    ones = jnp.ones((blocks[0].shape[0], 128), jnp.bfloat16)
    here = slice(chunk * rows, chunk * rows + rows)
    for head_pair in range(width // 128):
        columns = slice(128 * head_pair, 128 * head_pair + 128)
        value_columns = slice(width + 128 * head_pair, width + 128 * head_pair + 128)
        queries = query[:, columns]
        results = []
        for half in (low, ~low):
            masked = jnp.where(half, queries, jnp.zeros_like(queries))
            scores, start = [], 0
            for block in blocks:
                end = start + block.shape[0]
                scores.append(dot_t(masked, block[:, columns]) * scale + bias[here, start:end])
                start = end
            top = functools.reduce(jnp.maximum, [jnp.max(s, axis=1, keepdims=True) for s in scores])
            total = None
            for s, block in zip(scores, blocks):
                weights = jnp.exp2(s - top).astype(jnp.bfloat16)
                part = dot(weights, jnp.concatenate([block[:, value_columns], ones], axis=1))
                total = part if total is None else total + part
            results.append(total[:, :128] / total[:, 128:])
        attended[:, columns] = jnp.where(low, results[0], results[1]).astype(jnp.bfloat16)
    result = second[...].astype(jnp.float32) + dot(attended[...], w_output[...])
    for k in range(steps):
        outs[k][...] = result[k * agents : (k + 1) * agents].astype(jnp.bfloat16)


def attend(chunk, query, second, w_output, bias, blocks, steps):
    rows, width = query.shape
    piece = jax.ShapeDtypeStruct((rows // steps, width), jnp.bfloat16)
    return pl.pallas_call(
        functools.partial(attend_kernel, steps, len(blocks), chunk),
        out_shape=[piece] * steps,
        in_specs=[VMEM] * (4 + len(blocks)),
        out_specs=[VMEM] * steps,
        scratch_shapes=[pltpu.VMEM((rows, width), jnp.bfloat16)],
        compiler_params=pltpu.CompilerParams(vmem_limit_bytes=16 * MIB),
        cost_estimate=pl.CostEstimate(flops=4 * 10**9, bytes_accessed=6 * 10**6, transcendentals=2 * 10**6),
        name="attend",
    )(query, second, pinned(w_output), pinned(bias), *blocks)


def put_back_kernel(steps, place, *refs):
    count = len(refs) - 2
    pieces, out, sem = refs[:count], refs[count], refs[count + 1]
    agents = pieces[0].shape[0]
    copies = []
    for i, piece in enumerate(pieces):
        chunk, k = divmod(i, steps)
        target = out.at[place[0] ^ k, pl.ds(chunk * agents, agents)]
        copies.append(pltpu.make_async_copy(piece, target, sem.at[i]))
    for copy in copies:
        copy.start()
    for copy in copies:
        copy.wait()


def put_back(place, pieces, shape):
    return pl.pallas_call(
        functools.partial(put_back_kernel, shape[0]),
        out_shape=jax.ShapeDtypeStruct(shape, jnp.bfloat16),
        in_specs=[SMEM] + [VMEM] * len(pieces),
        out_specs=ANY,
        scratch_shapes=[pltpu.SemaphoreType.DMA((len(pieces),))],
        compiler_params=pltpu.CompilerParams(vmem_limit_bytes=8 * MIB),
        name="put_back",
    )(place, *pieces)


def per_device(
    tokens,
    conv_taps,
    norm_first,
    norm_second,
    norm_third,
    w_in,
    w_out,
    w_query,
    w_key,
    w_value,
    w_output,
    agent_order,
    present_steps,
):
    steps, agents, width = tokens.shape
    tm_count, count = lax.axis_size("tm"), lax.axis_size("agent")
    group = count // steps
    part = agents // CHUNKS
    assert group * steps == count and steps == 4 and 128 % part == 0 and 2 * CHUNKS <= 8
    spot = lax.axis_index("agent")
    z = spot // group
    now = lax.axis_index("tm") * steps + z
    place = jnp.stack([z, now]).astype(jnp.int32)

    def across(x, k):
        return lax.ppermute(x, "agent", [(i, ((i // group) ^ k) * group + i % group) for i in range(count)])

    def within(x, r):
        return lax.ppermute(x, "agent", [(i, (i // group) * group + ((i % group) ^ r)) for i in range(count)])

    halos = [
        lax.ppermute(
            tokens[:, j * part : (j + 1) * part], "tm", [(i, i + 1) for i in range(tm_count - 1)]
        )
        for j in range(CHUNKS)
    ]
    info = jnp.pad(jnp.stack([agent_order, present_steps]).astype(jnp.float32), ((0, 6), (0, 128 - agents)))
    infos = [info] + [across(info, k) for k in range(1, steps)]
    partial, taps, gain_first, gain_second, gain_third, held = stage(
        tokens,
        conv_taps,
        norm_first.reshape(1, width),
        [conv_taps] + [x.reshape(1, width) for x in (norm_first, norm_second, norm_third)] + [w_in],
    )
    *infos, halos[0], partial = lax.optimization_barrier((*infos, halos[0], partial))
    firsts, own = [], []
    for j in range(CHUNKS):
        pieces = list(conv(j, place, halos[j], partial, taps, gain_first))
        if j + 1 < CHUNKS:
            _, halos[j + 1] = lax.optimization_barrier((pieces[0], halos[j + 1]))
        own.append(pieces[0])
        if j > 0:
            for k in range(1, steps):
                firsts[j - 1][k], pieces[k] = lax.optimization_barrier((firsts[j - 1][k], pieces[k]))
        firsts.append([pieces[0]] + [across(pieces[k], k) for k in range(1, steps)])
    info = jnp.concatenate(infos, axis=0)
    *firsts[0], _ = lax.optimization_barrier((*firsts[0], own[-1]))
    held, loaded, spare = [held], [w_out, w_key, w_value, w_query], []
    queries, seconds, blocks = [], [], []
    for j in range(CHUNKS):
        if j == CHUNKS - 1:
            spare = [w_output]
        query, keyval, second, *fetched = feed(
            firsts[j], (gain_second, gain_third), held, loaded, spare, j == CHUNKS - 1
        )
        if j == 0:
            keyval, info = lax.optimization_barrier((keyval, info))
            infos = [info] + [within(info, r) for r in range(1, group)]
        else:
            keyval, *blocks[j - 1] = lax.optimization_barrier((keyval, *blocks[j - 1]))
            keyval, *infos = lax.optimization_barrier((keyval, *infos))
        held, loaded = held + fetched[: len(loaded)], []
        queries.append(query)
        seconds.append(second)
        blocks.append([keyval] + [within(keyval, r) for r in range(1, group)])
    project = fetched[-1]
    bias = mask(infos, place, steps, part)
    blocks = [blocks[j][r] for r in range(group) for j in range(CHUNKS)]
    pieces = []
    for j in range(CHUNKS):
        results = attend(j, queries[j], seconds[j], project, bias, blocks, steps)
        pieces += [results[0]] + [across(results[k], k) for k in range(1, steps)]
    return put_back(place, pieces, tokens.shape)


def solution(mesh):
    in_specs = (P("tm", "agent", None),) + (P(),) * 10 + (P("agent"), P("agent"))
    return jax.shard_map(
        per_device, mesh=mesh, in_specs=in_specs, out_specs=P("tm", "agent", None), check_vma=False
    )
```

```python
import functools

import jax
import jax.numpy as jnp
from jax import lax
from jax.experimental import pallas as pl
from jax.experimental.pallas import tpu as pltpu
from jax.sharding import PartitionSpec as P

HEAD = 64
CHUNKS = 2
RADIX = 32
EPS = 1e-05
LOG2E = 1.4426950408889634
MIB = 1024 * 1024
VMEM = pl.BlockSpec(memory_space=pltpu.VMEM)
ANY = pl.BlockSpec(memory_space=pl.ANY)
SMEM = pl.BlockSpec(memory_space=pltpu.SMEM)
HBM = pl.BlockSpec(memory_space=pltpu.HBM)


def pinned(x):
    return pltpu.with_memory_space_constraint(x, pltpu.VMEM)


def far(x):
    return pltpu.with_memory_space_constraint(x, pltpu.HBM)


def cost(microseconds):
    return pl.CostEstimate(
        flops=int(1.1e9 * microseconds) + 10**6, bytes_accessed=int(3.5e6 * microseconds) + 10**4, transcendentals=0
    )


def dot(a, b):
    return jnp.dot(a, b, preferred_element_type=jnp.float32)


def dot_t(a, b):
    return lax.dot_general(a, b, (((1,), (1,)), ((), ())), preferred_element_type=jnp.float32)


def norm_scale(values):
    return lax.rsqrt(jnp.mean(values * values, axis=-1, keepdims=True) + EPS)


def gelu(x):
    return 0.5 * x * (1.0 + lax.erf(x * 0.7071067811865476))


def stage_kernel(count, tokens, taps, gain, order, present, *rest):
    sources, (partial, tail), targets = rest[:count], rest[count : count + 2], rest[count + 2 : 2 * count + 2]
    tokens_here, taps_here, gain_here, order_here, present_here, normed, facts, sem = rest[2 * count + 2 :]
    pairs = [
        (tokens, tokens_here),
        (taps, taps_here),
        (gain, gain_here),
        (order, order_here),
        (present, present_here),
        *zip(sources, targets),
    ]
    copies = [pltpu.make_async_copy(source, target, sem.at[i]) for i, (source, target) in enumerate(pairs)]
    for copy in copies:
        copy.start()
    for copy in copies:
        copy.wait()
    agents = order.shape[1]
    facts[...] = jnp.zeros(facts.shape, jnp.float32)
    facts[0:1, :agents] = (order_here[...] // RADIX).astype(jnp.float32)
    facts[1:2, :agents] = (order_here[...] % RADIX).astype(jnp.float32)
    facts[2:3, :agents] = present_here[...].astype(jnp.float32)
    tail[...] = facts[...].astype(jnp.bfloat16)
    steps, reach = tokens.shape[0], taps.shape[0] - 1
    gains = gain_here[...]
    for step in range(steps):
        values = tokens_here[step].astype(jnp.float32)
        normed[step] = values * norm_scale(values) * gains
        total = values
        for lag in range(min(step, reach) + 1):
            total = total + taps_here[lag : lag + 1, :] * normed[step - lag]
        partial[step] = total


def stage(tokens, taps, gain, order, present, arrays):
    steps, agents, width = tokens.shape
    part = agents // CHUNKS
    inputs = (tokens, taps, gain, order, present)
    return pl.pallas_call(
        functools.partial(stage_kernel, len(arrays)),
        out_shape=[
            pltpu.VMEM((steps, agents, width), jnp.float32),
            pltpu.VMEM((part, 128), jnp.bfloat16),
        ]
        + [pltpu.VMEM(x.shape, x.dtype) for x in arrays],
        in_specs=[HBM] * (len(inputs) + len(arrays)),
        out_specs=[VMEM] * (2 + len(arrays)),
        scratch_shapes=[pltpu.VMEM(x.shape, x.dtype) for x in inputs]
        + [
            pltpu.VMEM((steps, agents, width), jnp.float32),
            pltpu.VMEM((part, 128), jnp.float32),
            pltpu.SemaphoreType.DMA((len(inputs) + len(arrays),)),
        ],
        compiler_params=pltpu.CompilerParams(vmem_limit_bytes=8 * MIB),
        cost_estimate=cost(30),
        name="stage",
    )(*[far(x) for x in (*inputs, *arrays)])


def conv_kernel(steps, chunk, with_tail, place, halo, partial, taps, gain, *rest):
    tail = rest[0] if with_tail else None
    outs, normed = rest[with_tail : with_tail + steps], rest[with_tail + steps]
    reach = taps.shape[0] - 1
    agents, width = halo.shape[1:]
    gains = gain[...]
    for step in range(steps):
        values = halo[step].astype(jnp.float32)
        normed[step] = values * norm_scale(values) * gains
    z = place[0]
    for step in range(steps):
        total = partial[step, chunk * agents : (chunk + 1) * agents, :]
        for lag in range(step + 1, reach + 1):
            total = total + taps[lag : lag + 1, :] * normed[steps + step - lag]
        normed[steps + step] = total
    for k in range(steps):
        outs[k][:, :width] = normed[steps + (z ^ k)].astype(jnp.bfloat16)
        if with_tail:
            outs[k][:, width:] = tail[...]


def conv(chunk, place, halo, partial, taps, gain, *tails):
    steps, agents, width = halo.shape
    piece = jax.ShapeDtypeStruct((agents, width + 128 * len(tails)), jnp.bfloat16)
    return pl.pallas_call(
        functools.partial(conv_kernel, steps, chunk, len(tails)),
        out_shape=[piece] * steps,
        in_specs=[SMEM] + [VMEM] * (4 + len(tails)),
        out_specs=[VMEM] * steps,
        scratch_shapes=[pltpu.VMEM((2 * steps, agents, width), jnp.float32)],
        compiler_params=pltpu.CompilerParams(vmem_limit_bytes=8 * MIB),
        cost_estimate=cost(0),
        name="conv",
    )(place, halo, *[pinned(x) for x in (partial, taps, gain, *tails)])


def feed_kernel(count, with_tail, *refs):
    pieces = refs[:count]
    gain_in, gain_attn, w_in, w_out, w_key, w_value, w_query = refs[count : count + 7]
    query, keyval, second, hidden = refs[count + 7 :]
    width = gain_in.shape[1]
    if with_tail:
        agents = pieces[0].shape[0]
        for k in range(count):
            keyval[agents * k : agents * (k + 1), 2 * width :] = pieces[k][:, width:]
    first = jnp.concatenate([piece[:, :width].astype(jnp.float32) for piece in pieces], axis=0)
    inner = (first * norm_scale(first) * gain_in[...]).astype(jnp.bfloat16)
    tile = 512
    for start in range(0, w_in.shape[1], tile):
        hidden[:, start : start + tile] = gelu(dot(inner, w_in[:, start : start + tile])).astype(jnp.bfloat16)
    total = (first + dot(hidden[...], w_out[...])).astype(jnp.bfloat16)
    second[...] = total
    values = total.astype(jnp.float32)
    attn_in = (values * norm_scale(values) * gain_attn[...]).astype(jnp.bfloat16)
    keyval[:, :width] = dot(attn_in, w_key[...]).astype(jnp.bfloat16)
    keyval[:, width : 2 * width] = dot(attn_in, w_value[...]).astype(jnp.bfloat16)
    query[...] = dot(attn_in, w_query[...]).astype(jnp.bfloat16)


def feed(pieces, gains, weights, microseconds):
    rows = sum(piece.shape[0] for piece in pieces)
    width = gains[0].shape[1]
    extra = pieces[0].shape[1] - width
    return pl.pallas_call(
        functools.partial(feed_kernel, len(pieces), extra > 0),
        out_shape=[
            jax.ShapeDtypeStruct((rows, width), jnp.bfloat16),
            jax.ShapeDtypeStruct((rows, 2 * width + extra), jnp.bfloat16),
            jax.ShapeDtypeStruct((rows, width), jnp.bfloat16),
        ],
        in_specs=[VMEM] * (len(pieces) + 7),
        out_specs=[VMEM] * 3,
        scratch_shapes=[pltpu.VMEM((rows, weights[0].shape[1]), jnp.bfloat16)],
        compiler_params=pltpu.CompilerParams(vmem_limit_bytes=16 * MIB),
        cost_estimate=cost(microseconds),
        name="feed",
    )(*pieces, *[pinned(x) for x in (*gains, *weights)])


def mask_kernel(steps, chunks, agents, group, width, place, *rest):
    blocks, bias = rest[:group], rest[group]
    now = place[1].astype(jnp.float32)
    lane = lax.broadcasted_iota(jnp.int32, (agents, 128), 1)
    sublane = lax.broadcasted_iota(jnp.int32, (agents, 128), 0)
    tiles = {}
    for r in range(group):
        for k in range(steps):
            tile = blocks[r][agents * k : agents * (k + 1), 2 * width :].astype(jnp.float32)
            tiles[k, r] = (tile[0:1] * RADIX + tile[1:2], tile[2:3])
    own = jnp.concatenate(
        [
            jnp.sum(jnp.where(lane == sublane + j * agents, tiles[k, 0][0], 0.0), axis=1, keepdims=True)
            for k in range(steps)
            for j in range(chunks)
        ],
        axis=0,
    )
    row_lane = lax.broadcasted_iota(jnp.int32, (1, 128), 1)
    per_tile = 128 // agents
    start = 0
    for r in range(group):
        for j in range(chunks):
            for first in range(0, steps, per_tile):
                both = [None, None]
                for i in range(per_tile):
                    for f in (0, 1):
                        moved = pltpu.roll(tiles[first + i, r][f], ((i - j) * agents) % 128, 1)
                        both[f] = moved if i == 0 else jnp.where(row_lane >= i * agents, moved, both[f])
                order, present = both
                alive = jnp.where(now < present, order, 1e9)
                visible = (alive < own) | (order == own)
                bias[:, start : start + 128] = jnp.where(visible, 0.0, -1e30)
                start += 128


def mask(blocks, place, steps, agents, width):
    rows, group = steps * agents * CHUNKS, len(blocks)
    return pl.pallas_call(
        functools.partial(mask_kernel, steps, CHUNKS, agents, group, width),
        out_shape=pltpu.VMEM((rows, rows * group), jnp.float32),
        in_specs=[SMEM] + [VMEM] * group,
        out_specs=VMEM,
        compiler_params=pltpu.CompilerParams(vmem_limit_bytes=8 * MIB),
        cost_estimate=cost(0),
        name="mask",
    )(place, *blocks)


def attend_kernel(ks, chunks, count, *refs):
    queries, seconds, (w_output, bias) = refs[:chunks], refs[chunks : 2 * chunks], refs[2 * chunks : 2 * chunks + 2]
    rest = refs[2 * chunks + 2 :]
    blocks, outs, attended = rest[:count], rest[count : count + len(ks)], rest[count + len(ks)]
    width = queries[0].shape[1]
    rows = attended.shape[0]
    agents = rows // (len(ks) * chunks)
    keys = sum(block.shape[0] for block in blocks)
    scale = LOG2E * HEAD ** (-0.5)
    low = lax.broadcasted_iota(jnp.int32, (rows, 128), 1) < HEAD
    ones = jnp.ones((keys, 128), jnp.bfloat16)
    first_row = ks[0] * agents * chunks

    def gather(parts, columns):
        return jnp.concatenate(
            [parts[j][agents * k : agents * (k + 1), columns] for k in ks for j in range(chunks)], axis=0
        )

    for pair in range(width // 128):
        columns = slice(128 * pair, 128 * pair + 128)
        value_columns = slice(width + 128 * pair, width + 128 * pair + 128)
        here = gather(queries, columns)
        zeros = jnp.zeros_like(here)
        stacked = jnp.concatenate([jnp.where(low, here, zeros), jnp.where(low, zeros, here)], axis=0)
        key = jnp.concatenate([block[:, columns] for block in blocks], axis=0)
        value = jnp.concatenate([block[:, value_columns] for block in blocks], axis=0)
        products = dot_t(stacked, key)
        weights = []
        for half in range(2):
            scores = products[half * rows : (half + 1) * rows] * scale + bias[first_row : first_row + rows, :]
            top = jnp.max(scores, axis=1, keepdims=True)
            weights.append(jnp.exp2(scores - top).astype(jnp.bfloat16))
        total = dot(jnp.concatenate(weights, axis=0), jnp.concatenate([value, ones], axis=1))
        ratio = total[:, :128] / total[:, 128:]
        attended[:, columns] = jnp.where(low, ratio[:rows], ratio[rows:]).astype(jnp.bfloat16)
    second = gather(seconds, slice(None)).astype(jnp.float32)
    result = second + dot(attended[...], w_output[...])
    for i in range(len(ks)):
        outs[i][...] = result[i * agents * chunks : (i + 1) * agents * chunks].astype(jnp.bfloat16)


def attend(ks, queries, seconds, w_output, bias, blocks, agents, microseconds):
    width = queries[0].shape[1]
    piece = jax.ShapeDtypeStruct((agents, width), jnp.bfloat16)
    return pl.pallas_call(
        functools.partial(attend_kernel, ks, len(queries), len(blocks)),
        out_shape=[piece] * len(ks),
        in_specs=[VMEM] * (2 * len(queries) + 2 + len(blocks)),
        out_specs=[VMEM] * len(ks),
        scratch_shapes=[pltpu.VMEM((len(ks) * agents, width), jnp.bfloat16)],
        compiler_params=pltpu.CompilerParams(vmem_limit_bytes=16 * MIB),
        cost_estimate=cost(microseconds),
        name="attend",
    )(*queries, *seconds, pinned(w_output), pinned(bias), *blocks)


def put_back_kernel(steps, place, *refs):
    count = len(refs) - 2
    pieces, out, sem = refs[:count], refs[count], refs[count + 1]
    copies = [pltpu.make_async_copy(pieces[k], out.at[place[0] ^ k], sem.at[k]) for k in range(steps)]
    for copy in copies:
        copy.start()
    for copy in copies:
        copy.wait()


def put_back(place, pieces, shape):
    return pl.pallas_call(
        functools.partial(put_back_kernel, shape[0]),
        out_shape=jax.ShapeDtypeStruct(shape, jnp.bfloat16),
        in_specs=[SMEM] + [VMEM] * len(pieces),
        out_specs=ANY,
        scratch_shapes=[pltpu.SemaphoreType.DMA((len(pieces),))],
        compiler_params=pltpu.CompilerParams(vmem_limit_bytes=8 * MIB),
        cost_estimate=cost(0),
        name="put_back",
    )(place, *pieces)


def after(x, *others):
    return lax.optimization_barrier((x, *others))[0]


def per_device(
    tokens,
    conv_taps,
    norm_first,
    norm_second,
    norm_third,
    w_in,
    w_out,
    w_query,
    w_key,
    w_value,
    w_output,
    agent_order,
    present_steps,
):
    steps, agents, width = tokens.shape
    tm_count, count = lax.axis_size("tm"), lax.axis_size("agent")
    group = count // steps
    part = agents // CHUNKS
    assert group * steps == count and steps == 4 and 128 % part == 0
    z = lax.axis_index("agent") // group
    place = jnp.stack([z, lax.axis_index("tm") * steps + z]).astype(jnp.int32)

    def across(x, k):
        return lax.ppermute(x, "agent", [(i, ((i // group) ^ k) * group + i % group) for i in range(count)])

    def within(x, r):
        return lax.ppermute(x, "agent", [(i, (i // group) * group + ((i % group) ^ r)) for i in range(count)])

    halos, source = [], tokens
    for j in range(CHUNKS):
        sliced = source[:, j * part : (j + 1) * part]
        halos.append(lax.ppermute(sliced, "tm", [(i, i + 1) for i in range(tm_count - 1)]))
        source = after(source, sliced)
    partial, tail, taps, *gains = stage(
        tokens,
        conv_taps,
        norm_first.reshape(1, width),
        agent_order.reshape(1, agents),
        present_steps.reshape(1, agents),
        [conv_taps] + [x.reshape(1, width) for x in (norm_first, norm_second, norm_third)],
    )
    halos[0] = after(halos[0], partial)
    firsts, last = [], None
    for j in range(CHUNKS):
        pieces = list(conv(j, place, halos[j], partial, taps, gains[0], *([tail] if j == 0 else [])))
        last = pieces[0]
        if j + 1 < CHUNKS:
            halos[j + 1] = after(halos[j + 1], last)
        if j > 0:
            for k in range(1, steps):
                pieces[k] = after(pieces[k], firsts[j - 1][k])
        firsts.append([pieces[0]] + [across(pieces[k], k) for k in range(1, steps)])
    firsts[0][0] = after(firsts[0][0], last)
    queries, seconds, blocks = [], [], []
    for j in range(CHUNKS):
        query, keyval, second = feed(
            firsts[j], gains[1:], (w_in, w_out, w_key, w_value, w_query), 25 if j == CHUNKS - 1 else 0
        )
        if j > 0:
            keyval = after(keyval, *blocks[j - 1])
        queries.append(query)
        seconds.append(second)
        blocks.append([keyval] + [within(keyval, r) for r in range(1, group)])
    bias = mask(blocks[0], place, steps, part, width)
    blocks = [blocks[j][r] for r in range(group) for j in range(CHUNKS)]
    far_pieces = attend((2, 3), queries, seconds, w_output, bias, blocks, agents, 0)
    far_back = [across(far_pieces[1], 3), across(far_pieces[0], 2)]
    near_pieces = attend((0, 1), queries, seconds, w_output, bias, blocks, agents, 10)
    near_back = across(near_pieces[1], 1)
    return put_back(place, [near_pieces[0], near_back, far_back[1], far_back[0]], tokens.shape)


def solution(mesh):
    in_specs = (P("tm", "agent", None),) + (P(),) * 10 + (P("agent"), P("agent"))
    return jax.shard_map(
        per_device, mesh=mesh, in_specs=in_specs, out_specs=P("tm", "agent", None), check_vma=False
    )
```

```python
import functools

import jax
import jax.numpy as jnp
from jax import lax
from jax.experimental import pallas as pl
from jax.experimental.pallas import tpu as pltpu
from jax.sharding import PartitionSpec as P

HEAD = 64
CHUNKS = 2
RADIX = 32
EPS = 1e-05
LOG2E = 1.4426950408889634
MIB = 1024 * 1024
VMEM = pl.BlockSpec(memory_space=pltpu.VMEM)
ANY = pl.BlockSpec(memory_space=pl.ANY)
HBM = pl.BlockSpec(memory_space=pltpu.HBM)


def pinned(x):
    return pltpu.with_memory_space_constraint(x, pltpu.VMEM)


def far(x):
    return pltpu.with_memory_space_constraint(x, pltpu.HBM)


def cost(microseconds):
    return pl.CostEstimate(
        flops=int(1.1e9 * microseconds) + 10**6, bytes_accessed=int(3.5e6 * microseconds) + 10**4, transcendentals=0
    )


def dot(a, b):
    return jnp.dot(a, b, preferred_element_type=jnp.float32)


def dot_t(a, b):
    return lax.dot_general(a, b, (((1,), (1,)), ((), ())), preferred_element_type=jnp.float32)


def norm_scale(values):
    return lax.rsqrt(jnp.mean(values * values, axis=-1, keepdims=True) + EPS)


def gelu(x):
    return 0.5 * x * (1.0 + lax.erf(x * 0.7071067811865476))


def split_kernel(parts, tokens, *rest):
    outs, sem = rest[:parts], rest[parts]
    agents = outs[0].shape[1]
    copies = [
        pltpu.make_async_copy(tokens.at[:, pl.ds(j * agents, agents)], outs[j], sem.at[j]) for j in range(parts)
    ]
    for copy in copies:
        copy.start()
    for copy in copies:
        copy.wait()


def split(tokens):
    steps, agents, width = tokens.shape
    return pl.pallas_call(
        functools.partial(split_kernel, CHUNKS),
        out_shape=[pltpu.VMEM((steps, agents // CHUNKS, width), tokens.dtype)] * CHUNKS,
        in_specs=[HBM],
        out_specs=[VMEM] * CHUNKS,
        scratch_shapes=[pltpu.SemaphoreType.DMA((CHUNKS,))],
        compiler_params=pltpu.CompilerParams(vmem_limit_bytes=4 * MIB),
        cost_estimate=cost(30),
        name="split",
    )(far(tokens))


def stage_kernel(parts, count, taps, gain, order, present, *rest):
    tokens, sources = rest[:parts], rest[parts : parts + count]
    rest = rest[parts + count :]
    partials, tail, targets = rest[:parts], rest[parts], rest[parts + 1 : parts + 1 + count]
    taps_here, gain_here, order_here, present_here, normed, facts, sem = rest[parts + 1 + count :]
    pairs = [
        (taps, taps_here),
        (gain, gain_here),
        (order, order_here),
        (present, present_here),
        *zip(sources, targets),
    ]
    copies = [pltpu.make_async_copy(source, target, sem.at[i]) for i, (source, target) in enumerate(pairs)]
    for copy in copies:
        copy.start()
    for copy in copies:
        copy.wait()
    agents = order.shape[1]
    facts[...] = jnp.zeros(facts.shape, jnp.float32)
    facts[0:1, :agents] = (order_here[...] // RADIX).astype(jnp.float32)
    facts[1:2, :agents] = (order_here[...] % RADIX).astype(jnp.float32)
    facts[2:3, :agents] = present_here[...].astype(jnp.float32)
    tail[...] = facts[...].astype(jnp.bfloat16)
    steps, reach = tokens[0].shape[0], taps.shape[0] - 1
    gains = gain_here[...]
    for j in range(parts):
        for step in range(steps):
            values = tokens[j][step].astype(jnp.float32)
            normed[step] = values * norm_scale(values) * gains
            total = values
            for lag in range(min(step, reach) + 1):
                total = total + taps_here[lag : lag + 1, :] * normed[step - lag]
            partials[j][step] = total


def stage(tokens, taps, gain, order, present, arrays):
    steps, part, width = tokens[0].shape
    inputs = (taps, gain, order, present)
    return pl.pallas_call(
        functools.partial(stage_kernel, CHUNKS, len(arrays)),
        out_shape=[pltpu.VMEM((steps, part, width), jnp.float32)] * CHUNKS
        + [pltpu.VMEM((part, 128), jnp.bfloat16)]
        + [pltpu.VMEM(x.shape, x.dtype) for x in arrays],
        in_specs=[HBM] * len(inputs) + [VMEM] * CHUNKS + [HBM] * len(arrays),
        out_specs=[VMEM] * (CHUNKS + 1 + len(arrays)),
        scratch_shapes=[pltpu.VMEM(x.shape, x.dtype) for x in inputs]
        + [
            pltpu.VMEM((steps, part, width), jnp.float32),
            pltpu.VMEM((part, 128), jnp.float32),
            pltpu.SemaphoreType.DMA((len(inputs) + len(arrays),)),
        ],
        compiler_params=pltpu.CompilerParams(vmem_limit_bytes=8 * MIB),
        cost_estimate=cost(0),
        name="stage",
    )(*[far(x) for x in inputs], *[pinned(x) for x in tokens], *[far(x) for x in arrays])


def front_kernel(with_tail, group, halo, partial, taps, gain_first, gain_second, w_in, w_out, *rest):
    tail = rest[0] if with_tail else None
    steps, agents, width = halo.shape
    outs = rest[with_tail : with_tail + steps]
    normed, first, hidden, second = rest[with_tail + steps :]
    reach = taps.shape[0] - 1
    gains = gain_first[...]
    for step in range(steps):
        values = halo[step].astype(jnp.float32)
        normed[step] = values * norm_scale(values) * gains
    for step in range(steps):
        total = partial[step]
        for lag in range(step + 1, reach + 1):
            total = total + taps[lag : lag + 1, :] * normed[steps + step - lag]
        first[step * agents : (step + 1) * agents, :] = total.astype(jnp.bfloat16).astype(jnp.float32)
    rows = first[...]
    inner = (rows * norm_scale(rows) * gain_second[...]).astype(jnp.bfloat16)
    tile = 512
    for start in range(0, w_in.shape[1], tile):
        hidden[:, start : start + tile] = gelu(dot(inner, w_in[:, start : start + tile])).astype(jnp.bfloat16)
    result = (first[...] + dot(hidden[...], w_out[...])).astype(jnp.bfloat16)
    for step in range(steps):
        second[step] = result[step * agents : (step + 1) * agents]
    z = lax.axis_index("agent") // group
    for k in range(steps):
        outs[k][:, :width] = second[z ^ k]
        if with_tail:
            outs[k][:, width:] = tail[...]


def front(group, halo, partial, taps, gains, w_in, w_out, *tails):
    steps, agents, width = halo.shape
    rows = steps * agents
    piece = jax.ShapeDtypeStruct((agents, width + 128 * len(tails)), jnp.bfloat16)
    return pl.pallas_call(
        functools.partial(front_kernel, len(tails), group),
        out_shape=[piece] * steps,
        in_specs=[VMEM] * (7 + len(tails)),
        out_specs=[VMEM] * steps,
        scratch_shapes=[
            pltpu.VMEM((steps, agents, width), jnp.float32),
            pltpu.VMEM((rows, width), jnp.float32),
            pltpu.VMEM((rows, w_in.shape[1]), jnp.bfloat16),
            pltpu.VMEM((steps, agents, width), jnp.bfloat16),
        ],
        compiler_params=pltpu.CompilerParams(vmem_limit_bytes=12 * MIB),
        cost_estimate=cost(0),
        name="front",
    )(halo, *[pinned(x) for x in (partial, taps, *gains, w_in, w_out, *tails)])


def project_kernel(count, with_tail, *refs):
    pieces = refs[:count]
    gain, w_key, w_value, w_query, query, keyval = refs[count:]
    width = gain.shape[1]
    if with_tail:
        agents = pieces[0].shape[0]
        for k in range(count):
            keyval[agents * k : agents * (k + 1), 2 * width :] = pieces[k][:, width:]
    values = jnp.concatenate([piece[:, :width].astype(jnp.float32) for piece in pieces], axis=0)
    attn_in = (values * norm_scale(values) * gain[...]).astype(jnp.bfloat16)
    keyval[:, :width] = dot(attn_in, w_key[...]).astype(jnp.bfloat16)
    keyval[:, width : 2 * width] = dot(attn_in, w_value[...]).astype(jnp.bfloat16)
    query[...] = dot(attn_in, w_query[...]).astype(jnp.bfloat16)


def project(pieces, gain, weights, microseconds):
    rows = sum(piece.shape[0] for piece in pieces)
    width = gain.shape[1]
    extra = pieces[0].shape[1] - width
    return pl.pallas_call(
        functools.partial(project_kernel, len(pieces), extra > 0),
        out_shape=[
            jax.ShapeDtypeStruct((rows, width), jnp.bfloat16),
            jax.ShapeDtypeStruct((rows, 2 * width + extra), jnp.bfloat16),
        ],
        in_specs=[VMEM] * (len(pieces) + 4),
        out_specs=[VMEM] * 2,
        compiler_params=pltpu.CompilerParams(vmem_limit_bytes=8 * MIB),
        cost_estimate=cost(microseconds),
        name="project",
    )(*pieces, *[pinned(x) for x in (gain, *weights)])


def mask_kernel(steps, chunks, agents, group, width, *rest):
    blocks, bias = rest[:group], rest[group]
    now = (lax.axis_index("tm") * steps + lax.axis_index("agent") // group).astype(jnp.float32)
    lane = lax.broadcasted_iota(jnp.int32, (agents, 128), 1)
    sublane = lax.broadcasted_iota(jnp.int32, (agents, 128), 0)
    tiles = {}
    for r in range(group):
        for k in range(steps):
            tile = blocks[r][agents * k : agents * (k + 1), 2 * width :].astype(jnp.float32)
            tiles[k, r] = (tile[0:1] * RADIX + tile[1:2], tile[2:3])
    own = jnp.concatenate(
        [
            jnp.sum(jnp.where(lane == sublane + j * agents, tiles[k, 0][0], 0.0), axis=1, keepdims=True)
            for k in range(steps)
            for j in range(chunks)
        ],
        axis=0,
    )
    row_lane = lax.broadcasted_iota(jnp.int32, (1, 128), 1)
    per_tile = 128 // agents
    start = 0
    for r in range(group):
        for j in range(chunks):
            for first in range(0, steps, per_tile):
                both = [None, None]
                for i in range(per_tile):
                    for f in (0, 1):
                        moved = pltpu.roll(tiles[first + i, r][f], ((i - j) * agents) % 128, 1)
                        both[f] = moved if i == 0 else jnp.where(row_lane >= i * agents, moved, both[f])
                order, present = both
                alive = jnp.where(now < present, order, 1e9)
                visible = (alive < own) | (order == own)
                bias[:, start : start + 128] = jnp.where(visible, 0.0, -1e30)
                start += 128


def mask(blocks, steps, agents, width):
    rows, group = steps * agents * CHUNKS, len(blocks)
    return pl.pallas_call(
        functools.partial(mask_kernel, steps, CHUNKS, agents, group, width),
        out_shape=pltpu.VMEM((rows, rows * group), jnp.float32),
        in_specs=[VMEM] * group,
        out_specs=VMEM,
        compiler_params=pltpu.CompilerParams(vmem_limit_bytes=8 * MIB),
        cost_estimate=cost(0),
        name="mask",
    )(*blocks)


def attend_kernel(ks, chunks, count, *refs):
    mine = len(ks) * chunks
    queries, seconds, (w_output, bias) = refs[:chunks], refs[chunks : chunks + mine], refs[chunks + mine : chunks + mine + 2]
    rest = refs[chunks + mine + 2 :]
    blocks, outs, attended = rest[:count], rest[count : count + len(ks)], rest[count + len(ks)]
    width = queries[0].shape[1]
    rows = attended.shape[0]
    agents = rows // (len(ks) * chunks)
    keys = sum(block.shape[0] for block in blocks)
    scale = LOG2E * HEAD ** (-0.5)
    low = lax.broadcasted_iota(jnp.int32, (rows, 128), 1) < HEAD
    ones = jnp.ones((keys, 128), jnp.bfloat16)
    first_row = ks[0] * agents * chunks

    for pair in range(width // 128):
        columns = slice(128 * pair, 128 * pair + 128)
        value_columns = slice(width + 128 * pair, width + 128 * pair + 128)
        here = jnp.concatenate(
            [queries[j][agents * k : agents * (k + 1), columns] for k in ks for j in range(chunks)], axis=0
        )
        zeros = jnp.zeros_like(here)
        stacked = jnp.concatenate([jnp.where(low, here, zeros), jnp.where(low, zeros, here)], axis=0)
        key = jnp.concatenate([block[:, columns] for block in blocks], axis=0)
        value = jnp.concatenate([block[:, value_columns] for block in blocks], axis=0)
        products = dot_t(stacked, key)
        weights = []
        for half in range(2):
            scores = products[half * rows : (half + 1) * rows] * scale + bias[first_row : first_row + rows, :]
            top = jnp.max(scores, axis=1, keepdims=True)
            weights.append(jnp.exp2(scores - top).astype(jnp.bfloat16))
        total = dot(jnp.concatenate(weights, axis=0), jnp.concatenate([value, ones], axis=1))
        ratio = total[:, :128] / total[:, 128:]
        attended[:, columns] = jnp.where(low, ratio[:rows], ratio[rows:]).astype(jnp.bfloat16)
    second = jnp.concatenate([piece[:, :width] for piece in seconds], axis=0).astype(jnp.float32)
    result = second + dot(attended[...], w_output[...])
    for i in range(len(ks)):
        outs[i][...] = result[i * agents * chunks : (i + 1) * agents * chunks].astype(jnp.bfloat16)


def attend(ks, queries, seconds, w_output, bias, blocks, agents, microseconds):
    width = queries[0].shape[1]
    piece = jax.ShapeDtypeStruct((agents, width), jnp.bfloat16)
    return pl.pallas_call(
        functools.partial(attend_kernel, ks, len(queries), len(blocks)),
        out_shape=[piece] * len(ks),
        in_specs=[VMEM] * (len(queries) + len(seconds) + 2 + len(blocks)),
        out_specs=[VMEM] * len(ks),
        scratch_shapes=[pltpu.VMEM((len(ks) * agents, width), jnp.bfloat16)],
        compiler_params=pltpu.CompilerParams(vmem_limit_bytes=16 * MIB),
        cost_estimate=cost(microseconds),
        name="attend",
    )(*queries, *seconds, pinned(w_output), pinned(bias), *blocks)


def put_back_kernel(steps, group, *refs):
    pieces, out, sem = refs[:steps], refs[steps], refs[steps + 1]
    z = lax.axis_index("agent") // group
    copies = [pltpu.make_async_copy(pieces[k], out.at[z ^ k], sem.at[k]) for k in range(steps)]
    for copy in copies:
        copy.start()
    for copy in copies:
        copy.wait()


def put_back(group, pieces, shape):
    return pl.pallas_call(
        functools.partial(put_back_kernel, shape[0], group),
        out_shape=jax.ShapeDtypeStruct(shape, jnp.bfloat16),
        in_specs=[VMEM] * len(pieces),
        out_specs=ANY,
        scratch_shapes=[pltpu.SemaphoreType.DMA((len(pieces),))],
        compiler_params=pltpu.CompilerParams(vmem_limit_bytes=4 * MIB),
        cost_estimate=cost(0),
        name="put_back",
    )(*pieces)


def after(x, *others):
    return lax.optimization_barrier((x, *others))[0]


def per_device(
    tokens,
    conv_taps,
    norm_first,
    norm_second,
    norm_third,
    w_in,
    w_out,
    w_query,
    w_key,
    w_value,
    w_output,
    agent_order,
    present_steps,
):
    steps, agents, width = tokens.shape
    tm_count, count = lax.axis_size("tm"), lax.axis_size("agent")
    group = count // steps
    part = agents // CHUNKS
    assert group * steps == count and steps == 4 and 128 % part == 0

    def across(x, k):
        return lax.ppermute(x, "agent", [(i, ((i // group) ^ k) * group + i % group) for i in range(count)])

    def within(x, r):
        return lax.ppermute(x, "agent", [(i, (i // group) * group + ((i % group) ^ r)) for i in range(count)])

    parts = split(tokens)
    halos = [lax.ppermute(x, "tm", [(i, i + 1) for i in range(tm_count - 1)]) for x in parts]
    *partials, tail, taps, gain_first, gain_second, gain_third = stage(
        parts,
        conv_taps,
        norm_first.reshape(1, width),
        agent_order.reshape(1, agents),
        present_steps.reshape(1, agents),
        [conv_taps] + [x.reshape(1, width) for x in (norm_first, norm_second, norm_third)],
    )
    halos[0] = after(halos[0], tail)
    pieces = []
    for j in range(CHUNKS):
        tails = [tail] if j == 0 else []
        made = list(front(group, halos[j], partials[j], taps, (gain_first, gain_second), w_in, w_out, *tails))
        last = made[0]
        if j + 1 < CHUNKS:
            halos[j + 1] = after(halos[j + 1], last)
        if j > 0:
            for k in range(1, steps):
                made[k] = after(made[k], pieces[j - 1][k])
        pieces.append([made[0]] + [across(made[k], k) for k in range(1, steps)])
    queries, blocks = [], []
    for j in range(CHUNKS):
        here = pieces[j] if j == CHUNKS - 1 else [after(pieces[j][0], last)] + pieces[j][1:]
        query, keyval = project(here, gain_third, (w_key, w_value, w_query), 25 if j == CHUNKS - 1 else 0)
        if j > 0:
            keyval = after(keyval, *blocks[j - 1])
        queries.append(query)
        blocks.append([keyval] + [within(keyval, r) for r in range(1, group)])
    bias = mask(blocks[0], steps, part, width)
    blocks = [blocks[j][r] for r in range(group) for j in range(CHUNKS)]

    def rows_of(ks, microseconds):
        seconds = [pieces[j][k] for k in ks for j in range(CHUNKS)]
        return attend(ks, queries, seconds, w_output, bias, blocks, agents, microseconds)

    far_pieces = rows_of((2, 3), 0)
    far_back = [across(far_pieces[1], 3), across(far_pieces[0], 2)]
    near_pieces = rows_of((0, 1), 10)
    near_back = across(near_pieces[1], 1)
    return put_back(group, [near_pieces[0], near_back, far_back[1], far_back[0]], tokens.shape)


def solution(mesh):
    in_specs = (P("tm", "agent", None),) + (P(),) * 10 + (P("agent"), P("agent"))
    return jax.shard_map(
        per_device, mesh=mesh, in_specs=in_specs, out_specs=P("tm", "agent", None), check_vma=False
    )
```

```python
import functools

import jax
import jax.numpy as jnp
from jax import lax
from jax.experimental import pallas as pl
from jax.experimental.pallas import tpu as pltpu
from jax.sharding import PartitionSpec as P

HEAD = 64
CHUNKS = 2
RADIX = 32
EPS = 1e-05
LOG2E = 1.4426950408889634
MIB = 1024 * 1024
VMEM = pl.BlockSpec(memory_space=pltpu.VMEM)
ANY = pl.BlockSpec(memory_space=pl.ANY)
HBM = pl.BlockSpec(memory_space=pltpu.HBM)


def pinned(x):
    return pltpu.with_memory_space_constraint(x, pltpu.VMEM)


def far(x):
    return pltpu.with_memory_space_constraint(x, pltpu.HBM)


def cost(microseconds):
    return pl.CostEstimate(
        flops=int(1.1e9 * microseconds) + 10**6, bytes_accessed=int(3.5e6 * microseconds) + 10**4, transcendentals=0
    )


def dot(a, b):
    return jnp.dot(a, b, preferred_element_type=jnp.float32)


def dot_t(a, b):
    return lax.dot_general(a, b, (((1,), (1,)), ((), ())), preferred_element_type=jnp.float32)


def norm_scale(values):
    return lax.rsqrt(jnp.mean(values * values, axis=-1, keepdims=True) + EPS)


def gelu(x):
    return 0.5 * x * (1.0 + lax.erf(x * 0.7071067811865476))


def split_kernel(parts, tokens, *rest):
    outs, sem = rest[:parts], rest[parts]
    agents = outs[0].shape[1]
    copies = [
        pltpu.make_async_copy(tokens.at[:, pl.ds(j * agents, agents)], outs[j], sem.at[j]) for j in range(parts)
    ]
    for copy in copies:
        copy.start()
    for copy in copies:
        copy.wait()


def split(tokens):
    steps, agents, width = tokens.shape
    return pl.pallas_call(
        functools.partial(split_kernel, CHUNKS),
        out_shape=[pltpu.VMEM((steps, agents // CHUNKS, width), tokens.dtype)] * CHUNKS,
        in_specs=[HBM],
        out_specs=[VMEM] * CHUNKS,
        scratch_shapes=[pltpu.SemaphoreType.DMA((CHUNKS,))],
        compiler_params=pltpu.CompilerParams(vmem_limit_bytes=4 * MIB),
        cost_estimate=cost(30),
        name="split",
    )(far(tokens))


def stage_kernel(parts, count, taps, gain, order, present, *rest):
    tokens, sources = rest[:parts], rest[parts : parts + count]
    rest = rest[parts + count :]
    partials, tail, targets = rest[:parts], rest[parts], rest[parts + 1 : parts + 1 + count]
    taps_here, gain_here, order_here, present_here, normed, facts, sem = rest[parts + 1 + count :]
    pairs = [
        (taps, taps_here),
        (gain, gain_here),
        (order, order_here),
        (present, present_here),
        *zip(sources, targets),
    ]
    copies = [pltpu.make_async_copy(source, target, sem.at[i]) for i, (source, target) in enumerate(pairs)]
    for copy in copies:
        copy.start()
    for copy in copies:
        copy.wait()
    agents = order.shape[1]
    facts[...] = jnp.zeros(facts.shape, jnp.float32)
    facts[0:1, :agents] = (order_here[...] // RADIX).astype(jnp.float32)
    facts[1:2, :agents] = (order_here[...] % RADIX).astype(jnp.float32)
    facts[2:3, :agents] = present_here[...].astype(jnp.float32)
    tail[...] = facts[...].astype(jnp.bfloat16)
    steps, reach = tokens[0].shape[0], taps.shape[0] - 1
    gains = gain_here[...]
    for j in range(parts):
        for step in range(steps):
            values = tokens[j][step].astype(jnp.float32)
            normed[step] = values * norm_scale(values) * gains
            total = values
            for lag in range(min(step, reach) + 1):
                total = total + taps_here[lag : lag + 1, :] * normed[step - lag]
            partials[j][step] = total


def stage(tokens, taps, gain, order, present, arrays):
    steps, part, width = tokens[0].shape
    inputs = (taps, gain, order, present)
    return pl.pallas_call(
        functools.partial(stage_kernel, CHUNKS, len(arrays)),
        out_shape=[pltpu.VMEM((steps, part, width), jnp.float32)] * CHUNKS
        + [pltpu.VMEM((part, 128), jnp.bfloat16)]
        + [pltpu.VMEM(x.shape, x.dtype) for x in arrays],
        in_specs=[HBM] * len(inputs) + [VMEM] * CHUNKS + [HBM] * len(arrays),
        out_specs=[VMEM] * (CHUNKS + 1 + len(arrays)),
        scratch_shapes=[pltpu.VMEM(x.shape, x.dtype) for x in inputs]
        + [
            pltpu.VMEM((steps, part, width), jnp.float32),
            pltpu.VMEM((part, 128), jnp.float32),
            pltpu.SemaphoreType.DMA((len(inputs) + len(arrays),)),
        ],
        compiler_params=pltpu.CompilerParams(vmem_limit_bytes=8 * MIB),
        cost_estimate=cost(0),
        name="stage",
    )(*[far(x) for x in inputs], *[pinned(x) for x in tokens], *[far(x) for x in arrays])


def front_kernel(with_tail, group, halo, partial, taps, gain_first, gain_second, w_in, w_out, *rest):
    tail = rest[0] if with_tail else None
    steps, agents, width = halo.shape
    outs = rest[with_tail : with_tail + steps]
    normed, first, hidden, second = rest[with_tail + steps :]
    reach = taps.shape[0] - 1
    gains = gain_first[...]
    for step in range(steps):
        values = halo[step].astype(jnp.float32)
        normed[step] = values * norm_scale(values) * gains
    for step in range(steps):
        total = partial[step]
        for lag in range(step + 1, reach + 1):
            total = total + taps[lag : lag + 1, :] * normed[steps + step - lag]
        first[step * agents : (step + 1) * agents, :] = total.astype(jnp.bfloat16).astype(jnp.float32)
    rows = first[...]
    inner = (rows * norm_scale(rows) * gain_second[...]).astype(jnp.bfloat16)
    tile = 512
    for start in range(0, w_in.shape[1], tile):
        hidden[:, start : start + tile] = gelu(dot(inner, w_in[:, start : start + tile])).astype(jnp.bfloat16)
    result = (first[...] + dot(hidden[...], w_out[...])).astype(jnp.bfloat16)
    for step in range(steps):
        second[step] = result[step * agents : (step + 1) * agents]
    z = lax.axis_index("agent") // group
    for k in range(steps):
        outs[k][:, :width] = second[z ^ (steps - 1 - k)]
        if with_tail:
            outs[k][:, width:] = tail[...]


def front(group, halo, partial, taps, gains, w_in, w_out, *tails):
    steps, agents, width = halo.shape
    rows = steps * agents
    piece = jax.ShapeDtypeStruct((agents, width + 128 * len(tails)), jnp.bfloat16)
    return pl.pallas_call(
        functools.partial(front_kernel, len(tails), group),
        out_shape=[piece] * steps,
        in_specs=[VMEM] * (7 + len(tails)),
        out_specs=[VMEM] * steps,
        scratch_shapes=[
            pltpu.VMEM((steps, agents, width), jnp.float32),
            pltpu.VMEM((rows, width), jnp.float32),
            pltpu.VMEM((rows, w_in.shape[1]), jnp.bfloat16),
            pltpu.VMEM((steps, agents, width), jnp.bfloat16),
        ],
        compiler_params=pltpu.CompilerParams(vmem_limit_bytes=12 * MIB),
        cost_estimate=cost(0),
        name="front",
    )(halo, *[pinned(x) for x in (partial, taps, *gains, w_in, w_out, *tails)])


def project_kernel(count, with_tail, *refs):
    pieces = refs[:count] if with_tail else refs[:count][::-1]
    gain, w_key, w_value, w_query, query, keyval = refs[count:]
    width = gain.shape[1]
    if with_tail:
        agents = pieces[0].shape[0]
        for k in range(count):
            keyval[agents * k : agents * (k + 1), 2 * width :] = pieces[k][:, width:]
    values = jnp.concatenate([piece[:, :width].astype(jnp.float32) for piece in pieces], axis=0)
    attn_in = (values * norm_scale(values) * gain[...]).astype(jnp.bfloat16)
    keyval[:, :width] = dot(attn_in, w_key[...]).astype(jnp.bfloat16)
    keyval[:, width : 2 * width] = dot(attn_in, w_value[...]).astype(jnp.bfloat16)
    query[...] = dot(attn_in, w_query[...]).astype(jnp.bfloat16)


def project(pieces, gain, weights, microseconds):
    rows = sum(piece.shape[0] for piece in pieces)
    width = gain.shape[1]
    extra = pieces[0].shape[1] - width
    return pl.pallas_call(
        functools.partial(project_kernel, len(pieces), extra > 0),
        out_shape=[
            jax.ShapeDtypeStruct((rows, width), jnp.bfloat16),
            jax.ShapeDtypeStruct((rows, 2 * width + extra), jnp.bfloat16),
        ],
        in_specs=[VMEM] * (len(pieces) + 4),
        out_specs=[VMEM] * 2,
        compiler_params=pltpu.CompilerParams(vmem_limit_bytes=8 * MIB),
        cost_estimate=cost(microseconds),
        name="project",
    )(*(pieces if extra else reversed(pieces)), *[pinned(x) for x in (gain, *weights)])


def mask_kernel(steps, chunks, agents, group, width, *rest):
    blocks, bias = rest[:group], rest[group]
    now = (lax.axis_index("tm") * steps + lax.axis_index("agent") // group).astype(jnp.float32)
    lane = lax.broadcasted_iota(jnp.int32, (agents, 128), 1)
    sublane = lax.broadcasted_iota(jnp.int32, (agents, 128), 0)
    tiles = {}
    for r in range(group):
        for k in range(steps):
            tile = blocks[r][agents * k : agents * (k + 1), 2 * width :].astype(jnp.float32)
            tiles[k, r] = (tile[0:1] * RADIX + tile[1:2], tile[2:3])
    own = jnp.concatenate(
        [
            jnp.sum(jnp.where(lane == sublane + j * agents, tiles[k, 0][0], 0.0), axis=1, keepdims=True)
            for k in range(steps)
            for j in range(chunks)
        ],
        axis=0,
    )
    row_lane = lax.broadcasted_iota(jnp.int32, (1, 128), 1)
    per_tile = 128 // agents
    start = 0
    for r in range(group):
        for j in range(chunks):
            for first in range(0, steps, per_tile):
                both = [None, None]
                for i in range(per_tile):
                    for f in (0, 1):
                        moved = pltpu.roll(tiles[first + i, r][f], ((i - j) * agents) % 128, 1)
                        both[f] = moved if i == 0 else jnp.where(row_lane >= i * agents, moved, both[f])
                order, present = both
                alive = jnp.where(now < present, order, 1e9)
                visible = (alive < own) | (order == own)
                bias[:, start : start + 128] = jnp.where(visible, 0.0, -1e30)
                start += 128


def mask(blocks, steps, agents, width):
    rows, group = steps * agents * CHUNKS, len(blocks)
    return pl.pallas_call(
        functools.partial(mask_kernel, steps, CHUNKS, agents, group, width),
        out_shape=pltpu.VMEM((rows, rows * group), jnp.float32),
        in_specs=[VMEM] * group,
        out_specs=VMEM,
        compiler_params=pltpu.CompilerParams(vmem_limit_bytes=8 * MIB),
        cost_estimate=cost(0),
        name="mask",
    )(*blocks)


def attend_kernel(ks, chunks, count, *refs):
    mine = len(ks) * chunks
    queries, seconds, (w_output, bias) = refs[:chunks], refs[chunks : chunks + mine], refs[chunks + mine : chunks + mine + 2]
    rest = refs[chunks + mine + 2 :]
    blocks, outs, attended = rest[:count], rest[count : count + len(ks)], rest[count + len(ks)]
    width = queries[0].shape[1]
    rows = attended.shape[0]
    agents = rows // (len(ks) * chunks)
    keys = sum(block.shape[0] for block in blocks)
    scale = LOG2E * HEAD ** (-0.5)
    low = lax.broadcasted_iota(jnp.int32, (rows, 128), 1) < HEAD
    ones = jnp.ones((keys, 128), jnp.bfloat16)
    first_row = ks[0] * agents * chunks

    for pair in range(width // 128):
        columns = slice(128 * pair, 128 * pair + 128)
        value_columns = slice(width + 128 * pair, width + 128 * pair + 128)
        here = jnp.concatenate(
            [queries[j][agents * k : agents * (k + 1), columns] for k in ks for j in range(chunks)], axis=0
        )
        zeros = jnp.zeros_like(here)
        stacked = jnp.concatenate([jnp.where(low, here, zeros), jnp.where(low, zeros, here)], axis=0)
        key = jnp.concatenate([block[:, columns] for block in blocks], axis=0)
        value = jnp.concatenate([block[:, value_columns] for block in blocks], axis=0)
        products = dot_t(stacked, key)
        weights = []
        for half in range(2):
            scores = products[half * rows : (half + 1) * rows] * scale + bias[first_row : first_row + rows, :]
            top = jnp.max(scores, axis=1, keepdims=True)
            weights.append(jnp.exp2(scores - top).astype(jnp.bfloat16))
        total = dot(jnp.concatenate(weights, axis=0), jnp.concatenate([value, ones], axis=1))
        ratio = total[:, :128] / total[:, 128:]
        attended[:, columns] = jnp.where(low, ratio[:rows], ratio[rows:]).astype(jnp.bfloat16)
    second = jnp.concatenate([piece[:, :width] for piece in seconds], axis=0).astype(jnp.float32)
    result = second + dot(attended[...], w_output[...])
    for i in range(len(ks)):
        outs[i][...] = result[i * agents * chunks : (i + 1) * agents * chunks].astype(jnp.bfloat16)


def attend(ks, queries, seconds, w_output, bias, blocks, agents, microseconds):
    width = queries[0].shape[1]
    piece = jax.ShapeDtypeStruct((agents, width), jnp.bfloat16)
    return pl.pallas_call(
        functools.partial(attend_kernel, ks, len(queries), len(blocks)),
        out_shape=[piece] * len(ks),
        in_specs=[VMEM] * (len(queries) + len(seconds) + 2 + len(blocks)),
        out_specs=[VMEM] * len(ks),
        scratch_shapes=[pltpu.VMEM((len(ks) * agents, width), jnp.bfloat16)],
        compiler_params=pltpu.CompilerParams(vmem_limit_bytes=16 * MIB),
        cost_estimate=cost(microseconds),
        name="attend",
    )(*queries, *seconds, pinned(w_output), pinned(bias), *blocks)


def put_back_kernel(steps, group, *refs):
    pieces, out, sem = refs[:steps], refs[steps], refs[steps + 1]
    z = lax.axis_index("agent") // group
    copies = [pltpu.make_async_copy(pieces[k], out.at[z ^ k], sem.at[k]) for k in range(steps)]
    for copy in copies:
        copy.start()
    for copy in copies:
        copy.wait()


def put_back(group, pieces, shape):
    return pl.pallas_call(
        functools.partial(put_back_kernel, shape[0], group),
        out_shape=jax.ShapeDtypeStruct(shape, jnp.bfloat16),
        in_specs=[VMEM] * len(pieces),
        out_specs=ANY,
        scratch_shapes=[pltpu.SemaphoreType.DMA((len(pieces),))],
        compiler_params=pltpu.CompilerParams(vmem_limit_bytes=4 * MIB),
        cost_estimate=cost(0),
        name="put_back",
    )(*pieces)


def after(x, *others):
    return lax.optimization_barrier((x, *others))[0]


def per_device(
    tokens,
    conv_taps,
    norm_first,
    norm_second,
    norm_third,
    w_in,
    w_out,
    w_query,
    w_key,
    w_value,
    w_output,
    agent_order,
    present_steps,
):
    steps, agents, width = tokens.shape
    tm_count, count = lax.axis_size("tm"), lax.axis_size("agent")
    group = count // steps
    part = agents // CHUNKS
    assert group * steps == count and steps == 4 and 128 % part == 0

    def across(x, k):
        away = steps - 1 - k
        if away == 0:
            return x
        return lax.ppermute(x, "agent", [(i, ((i // group) ^ away) * group + i % group) for i in range(count)])

    def within(x, r):
        return lax.ppermute(x, "agent", [(i, (i // group) * group + ((i % group) ^ r)) for i in range(count)])

    parts = split(tokens)
    *partials, tail, taps, gain_first, gain_second, gain_third = stage(
        parts,
        conv_taps,
        norm_first.reshape(1, width),
        agent_order.reshape(1, agents),
        present_steps.reshape(1, agents),
        [conv_taps] + [x.reshape(1, width) for x in (norm_first, norm_second, norm_third)],
    )
    halos = [
        lax.ppermute(x if j == 0 else after(x, tail), "tm", [(i, i + 1) for i in range(tm_count - 1)])
        for j, x in enumerate(parts)
    ]
    halos[0] = after(halos[0], tail)
    pieces = []
    for j in range(CHUNKS):
        tails = [tail] if j == 0 else []
        made = list(front(group, halos[j], partials[j], taps, (gain_first, gain_second), w_in, w_out, *tails))
        last = made[-1]
        if j + 1 < CHUNKS:
            halos[j + 1] = after(halos[j + 1], last)
        if j > 0:
            for k in range(steps - 1):
                made[k] = after(made[k], pieces[j - 1][steps - 2 - k])
        pieces.append([across(made[k], k) for k in range(steps)])
    queries, blocks = [], []
    for j in range(CHUNKS):
        here = pieces[j] if j == CHUNKS - 1 else pieces[j][:-1] + [after(pieces[j][-1], last)]
        query, keyval = project(here, gain_third, (w_key, w_value, w_query), 25 if j == CHUNKS - 1 else 0)
        if j > 0:
            keyval = after(keyval, *blocks[j - 1])
        queries.append(query)
        blocks.append([keyval] + [within(keyval, r) for r in range(1, group)])
    bias = mask(blocks[0], steps, part, width)
    blocks = [blocks[j][r] for r in range(group) for j in range(CHUNKS)]

    def rows_of(ks, microseconds):
        seconds = [pieces[j][k] for k in ks for j in range(CHUNKS)]
        return attend(ks, queries, seconds, w_output, bias, blocks, agents, microseconds)

    results = [*rows_of((0, 1), 0), *rows_of((2, 3), 10)]
    return put_back(group, [across(results[k], k) for k in reversed(range(steps))], tokens.shape)


def solution(mesh):
    in_specs = (P("tm", "agent", None),) + (P(),) * 10 + (P("agent"), P("agent"))
    return jax.shard_map(
        per_device, mesh=mesh, in_specs=in_specs, out_specs=P("tm", "agent", None), check_vma=False
    )
```

```python
import functools

import jax
import jax.numpy as jnp
from jax import lax
from jax.experimental import pallas as pl
from jax.experimental.pallas import tpu as pltpu
from jax.sharding import PartitionSpec as P

HEAD = 64
CHUNKS = 2
RADIX = 32
EPS = 1e-05
LOG2E = 1.4426950408889634
MIB = 1024 * 1024
VMEM = pl.BlockSpec(memory_space=pltpu.VMEM)
ANY = pl.BlockSpec(memory_space=pl.ANY)
HBM = pl.BlockSpec(memory_space=pltpu.HBM)


def pinned(x):
    return pltpu.with_memory_space_constraint(x, pltpu.VMEM)


def far(x):
    return pltpu.with_memory_space_constraint(x, pltpu.HBM)


def cost(microseconds):
    return pl.CostEstimate(
        flops=int(1.1e9 * microseconds) + 10**6, bytes_accessed=int(3.5e6 * microseconds) + 10**4, transcendentals=0
    )


def dot(a, b):
    return jnp.dot(a, b, preferred_element_type=jnp.float32)


def dot_t(a, b):
    return lax.dot_general(a, b, (((1,), (1,)), ((), ())), preferred_element_type=jnp.float32)


def norm_scale(values):
    return lax.rsqrt(jnp.mean(values * values, axis=-1, keepdims=True) + EPS)


def gelu(x):
    return 0.5 * x * (1.0 + lax.erf(x * 0.7071067811865476))


def split_kernel(parts, tokens, *rest):
    outs, sem = rest[:parts], rest[parts]
    agents = outs[0].shape[1]
    copies = [
        pltpu.make_async_copy(tokens.at[:, pl.ds(j * agents, agents)], outs[j], sem.at[j]) for j in range(parts)
    ]
    for copy in copies:
        copy.start()
    for copy in copies:
        copy.wait()


def split(tokens):
    steps, agents, width = tokens.shape
    return pl.pallas_call(
        functools.partial(split_kernel, CHUNKS),
        out_shape=[pltpu.VMEM((steps, agents // CHUNKS, width), tokens.dtype)] * CHUNKS,
        in_specs=[HBM],
        out_specs=[VMEM] * CHUNKS,
        scratch_shapes=[pltpu.SemaphoreType.DMA((CHUNKS,))],
        compiler_params=pltpu.CompilerParams(vmem_limit_bytes=4 * MIB),
        cost_estimate=cost(30),
        name="split",
    )(far(tokens))


def stage_kernel(parts, count, taps, gain, order, present, *rest):
    tokens, sources = rest[:parts], rest[parts : parts + count]
    rest = rest[parts + count :]
    partials, tail, targets = rest[:parts], rest[parts], rest[parts + 1 : parts + 1 + count]
    taps_here, gain_here, order_here, present_here, normed, facts, sem = rest[parts + 1 + count :]
    pairs = [
        (taps, taps_here),
        (gain, gain_here),
        (order, order_here),
        (present, present_here),
        *zip(sources, targets),
    ]
    copies = [pltpu.make_async_copy(source, target, sem.at[i]) for i, (source, target) in enumerate(pairs)]
    for copy in copies:
        copy.start()
    for copy in copies:
        copy.wait()
    agents = order.shape[1]
    facts[...] = jnp.zeros(facts.shape, jnp.float32)
    facts[0:1, :agents] = (order_here[...] // RADIX).astype(jnp.float32)
    facts[1:2, :agents] = (order_here[...] % RADIX).astype(jnp.float32)
    facts[2:3, :agents] = present_here[...].astype(jnp.float32)
    tail[...] = facts[...].astype(jnp.bfloat16)
    steps, reach = tokens[0].shape[0], taps.shape[0] - 1
    gains = gain_here[...]
    for j in range(parts):
        for step in range(steps):
            values = tokens[j][step].astype(jnp.float32)
            normed[step] = values * norm_scale(values) * gains
            total = values
            for lag in range(min(step, reach) + 1):
                total = total + taps_here[lag : lag + 1, :] * normed[step - lag]
            partials[j][step] = total


def stage(tokens, taps, gain, order, present, arrays):
    steps, part, width = tokens[0].shape
    inputs = (taps, gain, order, present)
    return pl.pallas_call(
        functools.partial(stage_kernel, CHUNKS, len(arrays)),
        out_shape=[pltpu.VMEM((steps, part, width), jnp.float32)] * CHUNKS
        + [pltpu.VMEM((part, 128), jnp.bfloat16)]
        + [pltpu.VMEM(x.shape, x.dtype) for x in arrays],
        in_specs=[HBM] * len(inputs) + [VMEM] * CHUNKS + [HBM] * len(arrays),
        out_specs=[VMEM] * (CHUNKS + 1 + len(arrays)),
        scratch_shapes=[pltpu.VMEM(x.shape, x.dtype) for x in inputs]
        + [
            pltpu.VMEM((steps, part, width), jnp.float32),
            pltpu.VMEM((part, 128), jnp.float32),
            pltpu.SemaphoreType.DMA((len(inputs) + len(arrays),)),
        ],
        compiler_params=pltpu.CompilerParams(vmem_limit_bytes=8 * MIB),
        cost_estimate=cost(0),
        name="stage",
    )(*[far(x) for x in inputs], *[pinned(x) for x in tokens], *[far(x) for x in arrays])


def front_kernel(with_tail, group, halo, partial, taps, gain_first, gain_second, w_in, w_out, *rest):
    tail = rest[0] if with_tail else None
    steps, agents, width = halo.shape
    outs = rest[with_tail : with_tail + steps]
    normed, first, hidden, second = rest[with_tail + steps :]
    reach = taps.shape[0] - 1
    gains = gain_first[...]
    for step in range(steps):
        values = halo[step].astype(jnp.float32)
        normed[step] = values * norm_scale(values) * gains
    for step in range(steps):
        total = partial[step]
        for lag in range(step + 1, reach + 1):
            total = total + taps[lag : lag + 1, :] * normed[steps + step - lag]
        first[step * agents : (step + 1) * agents, :] = total.astype(jnp.bfloat16).astype(jnp.float32)
    rows = first[...]
    inner = (rows * norm_scale(rows) * gain_second[...]).astype(jnp.bfloat16)
    tile = 512
    for start in range(0, w_in.shape[1], tile):
        hidden[:, start : start + tile] = gelu(dot(inner, w_in[:, start : start + tile])).astype(jnp.bfloat16)
    result = (first[...] + dot(hidden[...], w_out[...])).astype(jnp.bfloat16)
    for step in range(steps):
        second[step] = result[step * agents : (step + 1) * agents]
    z = lax.axis_index("agent") // group
    for k in range(steps):
        outs[k][:, :width] = second[z ^ (steps - 1 - k)]
        if with_tail:
            outs[k][:, width:] = tail[...]


def front(group, halo, partial, taps, gains, w_in, w_out, *tails):
    steps, agents, width = halo.shape
    rows = steps * agents
    piece = jax.ShapeDtypeStruct((agents, width + 128 * len(tails)), jnp.bfloat16)
    return pl.pallas_call(
        functools.partial(front_kernel, len(tails), group),
        out_shape=[piece] * steps,
        in_specs=[VMEM] * (7 + len(tails)),
        out_specs=[VMEM] * steps,
        scratch_shapes=[
            pltpu.VMEM((steps, agents, width), jnp.float32),
            pltpu.VMEM((rows, width), jnp.float32),
            pltpu.VMEM((rows, w_in.shape[1]), jnp.bfloat16),
            pltpu.VMEM((steps, agents, width), jnp.bfloat16),
        ],
        compiler_params=pltpu.CompilerParams(vmem_limit_bytes=12 * MIB),
        cost_estimate=cost(0),
        name="front",
    )(halo, *[pinned(x) for x in (partial, taps, *gains, w_in, w_out, *tails)])


def project_kernel(count, with_tail, *refs):
    pieces = refs[:count] if with_tail else refs[:count][::-1]
    gain, w_key, w_value, w_query, query, keyval = refs[count:]
    width = gain.shape[1]
    if with_tail:
        agents = pieces[0].shape[0]
        for k in range(count):
            keyval[agents * k : agents * (k + 1), 2 * width :] = pieces[k][:, width:]
    values = jnp.concatenate([piece[:, :width].astype(jnp.float32) for piece in pieces], axis=0)
    attn_in = (values * norm_scale(values) * gain[...]).astype(jnp.bfloat16)
    keyval[:, :width] = dot(attn_in, w_key[...]).astype(jnp.bfloat16)
    keyval[:, width : 2 * width] = dot(attn_in, w_value[...]).astype(jnp.bfloat16)
    query[...] = dot(attn_in, w_query[...]).astype(jnp.bfloat16)


def project(pieces, gain, weights, microseconds):
    rows = sum(piece.shape[0] for piece in pieces)
    width = gain.shape[1]
    extra = pieces[0].shape[1] - width
    return pl.pallas_call(
        functools.partial(project_kernel, len(pieces), extra > 0),
        out_shape=[
            jax.ShapeDtypeStruct((rows, width), jnp.bfloat16),
            jax.ShapeDtypeStruct((rows, 2 * width + extra), jnp.bfloat16),
        ],
        in_specs=[VMEM] * (len(pieces) + 4),
        out_specs=[VMEM] * 2,
        compiler_params=pltpu.CompilerParams(vmem_limit_bytes=8 * MIB),
        cost_estimate=cost(microseconds),
        name="project",
    )(*(pieces if extra else reversed(pieces)), *[pinned(x) for x in (gain, *weights)])


def mask_kernel(steps, chunks, agents, group, width, *rest):
    blocks, bias = rest[:group], rest[group]
    now = (lax.axis_index("tm") * steps + lax.axis_index("agent") // group).astype(jnp.float32)
    lane = lax.broadcasted_iota(jnp.int32, (agents, 128), 1)
    sublane = lax.broadcasted_iota(jnp.int32, (agents, 128), 0)
    tiles = {}
    for r in range(group):
        for k in range(steps):
            tile = blocks[r][agents * k : agents * (k + 1), 2 * width :].astype(jnp.float32)
            tiles[k, r] = (tile[0:1] * RADIX + tile[1:2], tile[2:3])
    own = jnp.concatenate(
        [
            jnp.sum(jnp.where(lane == sublane + j * agents, tiles[k, 0][0], 0.0), axis=1, keepdims=True)
            for k in range(steps)
            for j in range(chunks)
        ],
        axis=0,
    )
    row_lane = lax.broadcasted_iota(jnp.int32, (1, 128), 1)
    per_tile = 128 // agents
    start = 0
    for r in range(group):
        for j in range(chunks):
            for first in range(0, steps, per_tile):
                both = [None, None]
                for i in range(per_tile):
                    for f in (0, 1):
                        moved = pltpu.roll(tiles[first + i, r][f], ((i - j) * agents) % 128, 1)
                        both[f] = moved if i == 0 else jnp.where(row_lane >= i * agents, moved, both[f])
                order, present = both
                alive = jnp.where(now < present, order, 1e9)
                visible = (alive < own) | (order == own)
                bias[:, start : start + 128] = jnp.where(visible, 0.0, -1e30)
                start += 128


def mask(blocks, steps, agents, width):
    rows, group = steps * agents * CHUNKS, len(blocks)
    return pl.pallas_call(
        functools.partial(mask_kernel, steps, CHUNKS, agents, group, width),
        out_shape=pltpu.VMEM((rows, rows * group), jnp.float32),
        in_specs=[VMEM] * group,
        out_specs=VMEM,
        compiler_params=pltpu.CompilerParams(vmem_limit_bytes=8 * MIB),
        cost_estimate=cost(0),
        name="mask",
    )(*blocks)


def attend_kernel(ks, chunks, count, *refs):
    mine = len(ks) * chunks
    queries, seconds, (w_output, bias) = refs[:chunks], refs[chunks : chunks + mine], refs[chunks + mine : chunks + mine + 2]
    rest = refs[chunks + mine + 2 :]
    blocks, outs, attended = rest[:count], rest[count : count + len(ks)], rest[count + len(ks)]
    width = queries[0].shape[1]
    rows = attended.shape[0]
    agents = rows // (len(ks) * chunks)
    keys = sum(block.shape[0] for block in blocks)
    scale = LOG2E * HEAD ** (-0.5)
    low = lax.broadcasted_iota(jnp.int32, (rows, 128), 1) < HEAD
    ones = jnp.ones((keys, 128), jnp.bfloat16)
    first_row = ks[0] * agents * chunks

    for pair in range(width // 128):
        columns = slice(128 * pair, 128 * pair + 128)
        value_columns = slice(width + 128 * pair, width + 128 * pair + 128)
        here = jnp.concatenate(
            [queries[j][agents * k : agents * (k + 1), columns] for k in ks for j in range(chunks)], axis=0
        )
        zeros = jnp.zeros_like(here)
        stacked = jnp.concatenate([jnp.where(low, here, zeros), jnp.where(low, zeros, here)], axis=0)
        key = jnp.concatenate([block[:, columns] for block in blocks], axis=0)
        value = jnp.concatenate([block[:, value_columns] for block in blocks], axis=0)
        products = dot_t(stacked, key)
        weights = []
        for half in range(2):
            scores = products[half * rows : (half + 1) * rows] * scale + bias[first_row : first_row + rows, :]
            top = jnp.max(scores, axis=1, keepdims=True)
            weights.append(jnp.exp2(scores - top).astype(jnp.bfloat16))
        total = dot(jnp.concatenate(weights, axis=0), jnp.concatenate([value, ones], axis=1))
        ratio = total[:, :128] / total[:, 128:]
        attended[:, columns] = jnp.where(low, ratio[:rows], ratio[rows:]).astype(jnp.bfloat16)
    second = jnp.concatenate([piece[:, :width] for piece in seconds], axis=0).astype(jnp.float32)
    result = second + dot(attended[...], w_output[...])
    for i in range(len(ks)):
        outs[i][...] = result[i * agents * chunks : (i + 1) * agents * chunks].astype(jnp.bfloat16)


def attend(ks, queries, seconds, w_output, bias, blocks, agents, microseconds):
    width = queries[0].shape[1]
    piece = jax.ShapeDtypeStruct((agents, width), jnp.bfloat16)
    return pl.pallas_call(
        functools.partial(attend_kernel, ks, len(queries), len(blocks)),
        out_shape=[piece] * len(ks),
        in_specs=[VMEM] * (len(queries) + len(seconds) + 2 + len(blocks)),
        out_specs=[VMEM] * len(ks),
        scratch_shapes=[pltpu.VMEM((len(ks) * agents, width), jnp.bfloat16)],
        compiler_params=pltpu.CompilerParams(vmem_limit_bytes=16 * MIB),
        cost_estimate=cost(microseconds),
        name="attend",
    )(*queries, *seconds, pinned(w_output), pinned(bias), *blocks)


def put_back_kernel(steps, group, *refs):
    pieces, out, sem = refs[:steps], refs[steps], refs[steps + 1]
    z = lax.axis_index("agent") // group
    copies = [pltpu.make_async_copy(pieces[k], out.at[z ^ k], sem.at[k]) for k in range(steps)]
    for copy in copies:
        copy.start()
    for copy in copies:
        copy.wait()


def put_back(group, pieces, shape):
    return pl.pallas_call(
        functools.partial(put_back_kernel, shape[0], group),
        out_shape=jax.ShapeDtypeStruct(shape, jnp.bfloat16),
        in_specs=[VMEM] * len(pieces),
        out_specs=ANY,
        scratch_shapes=[pltpu.SemaphoreType.DMA((len(pieces),))],
        compiler_params=pltpu.CompilerParams(vmem_limit_bytes=4 * MIB),
        cost_estimate=cost(0),
        name="put_back",
    )(*pieces)


def after(x, *others):
    return lax.optimization_barrier((x, *others))[0]


def per_device(
    tokens,
    conv_taps,
    norm_first,
    norm_second,
    norm_third,
    w_in,
    w_out,
    w_query,
    w_key,
    w_value,
    w_output,
    agent_order,
    present_steps,
):
    steps, agents, width = tokens.shape
    tm_count, count = lax.axis_size("tm"), lax.axis_size("agent")
    group = count // steps
    part = agents // CHUNKS
    assert group * steps == count and steps == 4 and 128 % part == 0

    def across(x, k):
        away = steps - 1 - k
        if away == 0:
            return x
        return lax.ppermute(x, "agent", [(i, ((i // group) ^ away) * group + i % group) for i in range(count)])

    def within(x, r):
        return lax.ppermute(x, "agent", [(i, (i // group) * group + ((i % group) ^ r)) for i in range(count)])

    parts = split(tokens)
    *partials, tail, taps, gain_first, gain_second, gain_third = stage(
        parts,
        conv_taps,
        norm_first.reshape(1, width),
        agent_order.reshape(1, agents),
        present_steps.reshape(1, agents),
        [conv_taps] + [x.reshape(1, width) for x in (norm_first, norm_second, norm_third)],
    )
    halos = [
        lax.ppermute(x if j == 0 else after(x, tail), "tm", [(i, i + 1) for i in range(tm_count - 1)])
        for j, x in enumerate(parts)
    ]
    halos[0] = after(halos[0], tail)
    pieces = []
    for j in range(CHUNKS):
        tails = [tail] if j == 0 else []
        made = list(front(group, halos[j], partials[j], taps, (gain_first, gain_second), w_in, w_out, *tails))
        last = made[-1]
        if j + 1 < CHUNKS:
            halos[j + 1] = after(halos[j + 1], last)
        if j > 0:
            made[steps - 2] = after(made[steps - 2], pieces[j - 1][0])
        pieces.append([across(made[k], k) for k in range(steps)])
    queries, blocks = [], []
    for j in range(CHUNKS):
        here = pieces[j] if j == CHUNKS - 1 else pieces[j][:-1] + [after(pieces[j][-1], last)]
        query, keyval = project(here, gain_third, (w_key, w_value, w_query), 25 if j == CHUNKS - 1 else 0)
        if j > 0:
            keyval = after(keyval, *blocks[j - 1])
        queries.append(query)
        blocks.append([keyval] + [within(keyval, r) for r in range(1, group)])
    bias = mask(blocks[0], steps, part, width)
    blocks = [blocks[j][r] for r in range(group) for j in range(CHUNKS)]

    def rows_of(ks, microseconds):
        seconds = [pieces[j][k] for k in ks for j in range(CHUNKS)]
        return attend(ks, queries, seconds, w_output, bias, blocks, agents, microseconds)

    results = [*rows_of((0, 1), 0), *rows_of((2, 3), 10)]
    return put_back(group, [across(results[k], k) for k in reversed(range(steps))], tokens.shape)


def solution(mesh):
    in_specs = (P("tm", "agent", None),) + (P(),) * 10 + (P("agent"), P("agent"))
    return jax.shard_map(
        per_device, mesh=mesh, in_specs=in_specs, out_specs=P("tm", "agent", None), check_vma=False
    )
```

```python
import functools

import jax
import jax.numpy as jnp
from jax import lax
from jax.experimental import pallas as pl
from jax.experimental.pallas import tpu as pltpu
from jax.sharding import PartitionSpec as P

HEAD = 64
CHUNKS = 2
RADIX = 32
EPS = 1e-05
LOG2E = 1.4426950408889634
MIB = 1024 * 1024
VMEM = pl.BlockSpec(memory_space=pltpu.VMEM)
ANY = pl.BlockSpec(memory_space=pl.ANY)
HBM = pl.BlockSpec(memory_space=pltpu.HBM)


def pinned(x):
    return pltpu.with_memory_space_constraint(x, pltpu.VMEM)


def far(x):
    return pltpu.with_memory_space_constraint(x, pltpu.HBM)


def cost(microseconds):
    return pl.CostEstimate(
        flops=int(1.1e9 * microseconds) + 10**6, bytes_accessed=int(3.5e6 * microseconds) + 10**4, transcendentals=0
    )


def away(k, steps, member):
    odd = member % 2
    return 0 if k == steps - 1 else (steps - 1 - k) * (1 - odd) + (k + 1) * odd


def dot(a, b):
    return jnp.dot(a, b, preferred_element_type=jnp.float32)


def dot_t(a, b):
    return lax.dot_general(a, b, (((1,), (1,)), ((), ())), preferred_element_type=jnp.float32)


def norm_scale(values):
    return lax.rsqrt(jnp.mean(values * values, axis=-1, keepdims=True) + EPS)


def gelu(x):
    return 0.5 * x * (1.0 + lax.erf(x * 0.7071067811865476))


def split_kernel(parts, tokens, *rest):
    outs, sem = rest[:parts], rest[parts]
    agents = outs[0].shape[1]
    copies = [
        pltpu.make_async_copy(tokens.at[:, pl.ds(j * agents, agents)], outs[j], sem.at[j]) for j in range(parts)
    ]
    for copy in copies:
        copy.start()
    for copy in copies:
        copy.wait()


def split(tokens):
    steps, agents, width = tokens.shape
    return pl.pallas_call(
        functools.partial(split_kernel, CHUNKS),
        out_shape=[pltpu.VMEM((steps, agents // CHUNKS, width), tokens.dtype)] * CHUNKS,
        in_specs=[HBM],
        out_specs=[VMEM] * CHUNKS,
        scratch_shapes=[pltpu.SemaphoreType.DMA((CHUNKS,))],
        compiler_params=pltpu.CompilerParams(vmem_limit_bytes=4 * MIB),
        cost_estimate=cost(30),
        name="split",
    )(far(tokens))


def stage_kernel(parts, count, taps, gain, order, present, *rest):
    tokens, sources = rest[:parts], rest[parts : parts + count]
    rest = rest[parts + count :]
    partials, tail, targets = rest[:parts], rest[parts], rest[parts + 1 : parts + 1 + count]
    taps_here, gain_here, order_here, present_here, normed, facts, sem = rest[parts + 1 + count :]
    pairs = [
        (taps, taps_here),
        (gain, gain_here),
        (order, order_here),
        (present, present_here),
        *zip(sources, targets),
    ]
    copies = [pltpu.make_async_copy(source, target, sem.at[i]) for i, (source, target) in enumerate(pairs)]
    for copy in copies:
        copy.start()
    for copy in copies:
        copy.wait()
    agents = order.shape[1]
    facts[...] = jnp.zeros(facts.shape, jnp.float32)
    facts[0:1, :agents] = (order_here[...] // RADIX).astype(jnp.float32)
    facts[1:2, :agents] = (order_here[...] % RADIX).astype(jnp.float32)
    facts[2:3, :agents] = present_here[...].astype(jnp.float32)
    tail[...] = facts[...].astype(jnp.bfloat16)
    steps, reach = tokens[0].shape[0], taps.shape[0] - 1
    gains = gain_here[...]
    for j in range(parts):
        for step in range(steps):
            values = tokens[j][step].astype(jnp.float32)
            normed[step] = values * norm_scale(values) * gains
            total = values
            for lag in range(min(step, reach) + 1):
                total = total + taps_here[lag : lag + 1, :] * normed[step - lag]
            partials[j][step] = total


def stage(tokens, taps, gain, order, present, arrays):
    steps, part, width = tokens[0].shape
    inputs = (taps, gain, order, present)
    return pl.pallas_call(
        functools.partial(stage_kernel, CHUNKS, len(arrays)),
        out_shape=[pltpu.VMEM((steps, part, width), jnp.float32)] * CHUNKS
        + [pltpu.VMEM((part, 128), jnp.bfloat16)]
        + [pltpu.VMEM(x.shape, x.dtype) for x in arrays],
        in_specs=[HBM] * len(inputs) + [VMEM] * CHUNKS + [HBM] * len(arrays),
        out_specs=[VMEM] * (CHUNKS + 1 + len(arrays)),
        scratch_shapes=[pltpu.VMEM(x.shape, x.dtype) for x in inputs]
        + [
            pltpu.VMEM((steps, part, width), jnp.float32),
            pltpu.VMEM((part, 128), jnp.float32),
            pltpu.SemaphoreType.DMA((len(inputs) + len(arrays),)),
        ],
        compiler_params=pltpu.CompilerParams(vmem_limit_bytes=8 * MIB),
        cost_estimate=cost(0),
        name="stage",
    )(*[far(x) for x in inputs], *[pinned(x) for x in tokens], *[far(x) for x in arrays])


def front_kernel(with_tail, group, halo, partial, taps, gain_first, gain_second, w_in, w_out, *rest):
    tail = rest[0] if with_tail else None
    steps, agents, width = halo.shape
    outs = rest[with_tail : with_tail + steps]
    normed, first, hidden, second = rest[with_tail + steps :]
    reach = taps.shape[0] - 1
    gains = gain_first[...]
    for step in range(steps):
        values = halo[step].astype(jnp.float32)
        normed[step] = values * norm_scale(values) * gains
    for step in range(steps):
        total = partial[step]
        for lag in range(step + 1, reach + 1):
            total = total + taps[lag : lag + 1, :] * normed[steps + step - lag]
        first[step * agents : (step + 1) * agents, :] = total.astype(jnp.bfloat16).astype(jnp.float32)
    rows = first[...]
    inner = (rows * norm_scale(rows) * gain_second[...]).astype(jnp.bfloat16)
    tile = 512
    for start in range(0, w_in.shape[1], tile):
        hidden[:, start : start + tile] = gelu(dot(inner, w_in[:, start : start + tile])).astype(jnp.bfloat16)
    result = (first[...] + dot(hidden[...], w_out[...])).astype(jnp.bfloat16)
    for step in range(steps):
        second[step] = result[step * agents : (step + 1) * agents]
    spot = lax.axis_index("agent")
    for k in range(steps):
        outs[k][:, :width] = second[(spot // group) ^ away(k, steps, spot % group)]
        if with_tail:
            outs[k][:, width:] = tail[...]


def front(group, halo, partial, taps, gains, w_in, w_out, *tails):
    steps, agents, width = halo.shape
    rows = steps * agents
    piece = jax.ShapeDtypeStruct((agents, width + 128 * len(tails)), jnp.bfloat16)
    return pl.pallas_call(
        functools.partial(front_kernel, len(tails), group),
        out_shape=[piece] * steps,
        in_specs=[VMEM] * (7 + len(tails)),
        out_specs=[VMEM] * steps,
        scratch_shapes=[
            pltpu.VMEM((steps, agents, width), jnp.float32),
            pltpu.VMEM((rows, width), jnp.float32),
            pltpu.VMEM((rows, w_in.shape[1]), jnp.bfloat16),
            pltpu.VMEM((steps, agents, width), jnp.bfloat16),
        ],
        compiler_params=pltpu.CompilerParams(vmem_limit_bytes=12 * MIB),
        cost_estimate=cost(0),
        name="front",
    )(halo, *[pinned(x) for x in (partial, taps, *gains, w_in, w_out, *tails)])


def project_kernel(count, with_tail, *refs):
    pieces = refs[:count] if with_tail else refs[:count][::-1]
    gain, w_key, w_value, w_query, query, keyval = refs[count:]
    width = gain.shape[1]
    if with_tail:
        agents = pieces[0].shape[0]
        for k in range(count):
            keyval[agents * k : agents * (k + 1), 2 * width :] = pieces[k][:, width:]
    values = jnp.concatenate([piece[:, :width].astype(jnp.float32) for piece in pieces], axis=0)
    attn_in = (values * norm_scale(values) * gain[...]).astype(jnp.bfloat16)
    keyval[:, :width] = dot(attn_in, w_key[...]).astype(jnp.bfloat16)
    keyval[:, width : 2 * width] = dot(attn_in, w_value[...]).astype(jnp.bfloat16)
    query[...] = dot(attn_in, w_query[...]).astype(jnp.bfloat16)


def project(pieces, gain, weights, microseconds):
    rows = sum(piece.shape[0] for piece in pieces)
    width = gain.shape[1]
    extra = pieces[0].shape[1] - width
    return pl.pallas_call(
        functools.partial(project_kernel, len(pieces), extra > 0),
        out_shape=[
            jax.ShapeDtypeStruct((rows, width), jnp.bfloat16),
            jax.ShapeDtypeStruct((rows, 2 * width + extra), jnp.bfloat16),
        ],
        in_specs=[VMEM] * (len(pieces) + 4),
        out_specs=[VMEM] * 2,
        compiler_params=pltpu.CompilerParams(vmem_limit_bytes=8 * MIB),
        cost_estimate=cost(microseconds),
        name="project",
    )(*(pieces if extra else reversed(pieces)), *[pinned(x) for x in (gain, *weights)])


def mask_kernel(steps, chunks, agents, group, width, *rest):
    blocks, bias = rest[:group], rest[group]
    now = (lax.axis_index("tm") * steps + lax.axis_index("agent") // group).astype(jnp.float32)
    lane = lax.broadcasted_iota(jnp.int32, (agents, 128), 1)
    sublane = lax.broadcasted_iota(jnp.int32, (agents, 128), 0)
    tiles = {}
    for r in range(group):
        for k in range(steps):
            tile = blocks[r][agents * k : agents * (k + 1), 2 * width :].astype(jnp.float32)
            tiles[k, r] = (tile[0:1] * RADIX + tile[1:2], tile[2:3])
    own = jnp.concatenate(
        [
            jnp.sum(jnp.where(lane == sublane + j * agents, tiles[k, 0][0], 0.0), axis=1, keepdims=True)
            for k in range(steps)
            for j in range(chunks)
        ],
        axis=0,
    )
    row_lane = lax.broadcasted_iota(jnp.int32, (1, 128), 1)
    per_tile = 128 // agents
    start = 0
    for r in range(group):
        for j in range(chunks):
            for first in range(0, steps, per_tile):
                both = [None, None]
                for i in range(per_tile):
                    for f in (0, 1):
                        moved = pltpu.roll(tiles[first + i, r][f], ((i - j) * agents) % 128, 1)
                        both[f] = moved if i == 0 else jnp.where(row_lane >= i * agents, moved, both[f])
                order, present = both
                alive = jnp.where(now < present, order, 1e9)
                visible = (alive < own) | (order == own)
                bias[:, start : start + 128] = jnp.where(visible, 0.0, -1e30)
                start += 128


def mask(blocks, steps, agents, width):
    rows, group = steps * agents * CHUNKS, len(blocks)
    return pl.pallas_call(
        functools.partial(mask_kernel, steps, CHUNKS, agents, group, width),
        out_shape=pltpu.VMEM((rows, rows * group), jnp.float32),
        in_specs=[VMEM] * group,
        out_specs=VMEM,
        compiler_params=pltpu.CompilerParams(vmem_limit_bytes=8 * MIB),
        cost_estimate=cost(0),
        name="mask",
    )(*blocks)


def attend_kernel(ks, chunks, count, *refs):
    mine = len(ks) * chunks
    queries, seconds, (w_output, bias) = refs[:chunks], refs[chunks : chunks + mine], refs[chunks + mine : chunks + mine + 2]
    rest = refs[chunks + mine + 2 :]
    blocks, outs, attended = rest[:count], rest[count : count + len(ks)], rest[count + len(ks)]
    width = queries[0].shape[1]
    rows = attended.shape[0]
    agents = rows // (len(ks) * chunks)
    keys = sum(block.shape[0] for block in blocks)
    scale = LOG2E * HEAD ** (-0.5)
    low = lax.broadcasted_iota(jnp.int32, (rows, 128), 1) < HEAD
    ones = jnp.ones((keys, 128), jnp.bfloat16)
    first_row = ks[0] * agents * chunks

    for pair in range(width // 128):
        columns = slice(128 * pair, 128 * pair + 128)
        value_columns = slice(width + 128 * pair, width + 128 * pair + 128)
        here = jnp.concatenate(
            [queries[j][agents * k : agents * (k + 1), columns] for k in ks for j in range(chunks)], axis=0
        )
        zeros = jnp.zeros_like(here)
        stacked = jnp.concatenate([jnp.where(low, here, zeros), jnp.where(low, zeros, here)], axis=0)
        key = jnp.concatenate([block[:, columns] for block in blocks], axis=0)
        value = jnp.concatenate([block[:, value_columns] for block in blocks], axis=0)
        products = dot_t(stacked, key)
        weights = []
        for half in range(2):
            scores = products[half * rows : (half + 1) * rows] * scale + bias[first_row : first_row + rows, :]
            top = jnp.max(scores, axis=1, keepdims=True)
            weights.append(jnp.exp2(scores - top).astype(jnp.bfloat16))
        total = dot(jnp.concatenate(weights, axis=0), jnp.concatenate([value, ones], axis=1))
        ratio = total[:, :128] / total[:, 128:]
        attended[:, columns] = jnp.where(low, ratio[:rows], ratio[rows:]).astype(jnp.bfloat16)
    second = jnp.concatenate([piece[:, :width] for piece in seconds], axis=0).astype(jnp.float32)
    result = second + dot(attended[...], w_output[...])
    for i in range(len(ks)):
        outs[i][...] = result[i * agents * chunks : (i + 1) * agents * chunks].astype(jnp.bfloat16)


def attend(ks, queries, seconds, w_output, bias, blocks, agents, microseconds):
    width = queries[0].shape[1]
    piece = jax.ShapeDtypeStruct((agents, width), jnp.bfloat16)
    return pl.pallas_call(
        functools.partial(attend_kernel, ks, len(queries), len(blocks)),
        out_shape=[piece] * len(ks),
        in_specs=[VMEM] * (len(queries) + len(seconds) + 2 + len(blocks)),
        out_specs=[VMEM] * len(ks),
        scratch_shapes=[pltpu.VMEM((len(ks) * agents, width), jnp.bfloat16)],
        compiler_params=pltpu.CompilerParams(vmem_limit_bytes=16 * MIB),
        cost_estimate=cost(microseconds),
        name="attend",
    )(*queries, *seconds, pinned(w_output), pinned(bias), *blocks)


def put_back_kernel(steps, group, *refs):
    pieces, out, sem = refs[:steps][::-1], refs[steps], refs[steps + 1]
    spot = lax.axis_index("agent")
    copies = [
        pltpu.make_async_copy(pieces[k], out.at[(spot // group) ^ away(k, steps, spot % group)], sem.at[k])
        for k in range(steps)
    ]
    for copy in copies:
        copy.start()
    for copy in copies:
        copy.wait()


def put_back(group, pieces, shape):
    return pl.pallas_call(
        functools.partial(put_back_kernel, shape[0], group),
        out_shape=jax.ShapeDtypeStruct(shape, jnp.bfloat16),
        in_specs=[VMEM] * len(pieces),
        out_specs=ANY,
        scratch_shapes=[pltpu.SemaphoreType.DMA((len(pieces),))],
        compiler_params=pltpu.CompilerParams(vmem_limit_bytes=4 * MIB),
        cost_estimate=cost(0),
        name="put_back",
    )(*pieces)


def after(x, *others):
    return lax.optimization_barrier((x, *others))[0]


def per_device(
    tokens,
    conv_taps,
    norm_first,
    norm_second,
    norm_third,
    w_in,
    w_out,
    w_query,
    w_key,
    w_value,
    w_output,
    agent_order,
    present_steps,
):
    steps, agents, width = tokens.shape
    tm_count, count = lax.axis_size("tm"), lax.axis_size("agent")
    group = count // steps
    part = agents // CHUNKS
    assert group * steps == count and steps == 4 and 128 % part == 0

    def across(x, k):
        if k == steps - 1:
            return x
        pairs = [(i, ((i // group) ^ away(k, steps, i % group)) * group + i % group) for i in range(count)]
        return lax.ppermute(x, "agent", pairs)

    def within(x, r):
        return lax.ppermute(x, "agent", [(i, (i // group) * group + ((i % group) ^ r)) for i in range(count)])

    parts = split(tokens)
    *partials, tail, taps, gain_first, gain_second, gain_third = stage(
        parts,
        conv_taps,
        norm_first.reshape(1, width),
        agent_order.reshape(1, agents),
        present_steps.reshape(1, agents),
        [conv_taps] + [x.reshape(1, width) for x in (norm_first, norm_second, norm_third)],
    )
    halos = [
        lax.ppermute(x if j == 0 else after(x, tail), "tm", [(i, i + 1) for i in range(tm_count - 1)])
        for j, x in enumerate(parts)
    ]
    halos[0] = after(halos[0], tail)
    pieces = []
    for j in range(CHUNKS):
        tails = [tail] if j == 0 else []
        made = list(front(group, halos[j], partials[j], taps, (gain_first, gain_second), w_in, w_out, *tails))
        last = made[-1]
        if j + 1 < CHUNKS:
            halos[j + 1] = after(halos[j + 1], last)
        if j > 0:
            made[steps - 2] = after(made[steps - 2], pieces[j - 1][0])
        pieces.append([across(made[k], k) for k in range(steps)])
    queries, blocks = [], []
    for j in range(CHUNKS):
        here = pieces[j] if j == CHUNKS - 1 else pieces[j][:-1] + [after(pieces[j][-1], last)]
        query, keyval = project(here, gain_third, (w_key, w_value, w_query), 25 if j == CHUNKS - 1 else 0)
        if j > 0:
            keyval = after(keyval, *blocks[j - 1])
        queries.append(query)
        blocks.append([keyval] + [within(keyval, r) for r in range(1, group)])
    bias = mask(blocks[0], steps, part, width)
    blocks = [blocks[j][r] for r in range(group) for j in range(CHUNKS)]

    def rows_of(ks, microseconds):
        seconds = [pieces[j][k] for k in ks for j in range(CHUNKS)]
        return attend(ks, queries, seconds, w_output, bias, blocks, agents, microseconds)

    results = [*rows_of((0, 1), 0), *rows_of((2, 3), 10)]
    return put_back(group, [across(results[k], k) for k in reversed(range(steps))], tokens.shape)


def solution(mesh):
    in_specs = (P("tm", "agent", None),) + (P(),) * 10 + (P("agent"), P("agent"))
    return jax.shard_map(
        per_device, mesh=mesh, in_specs=in_specs, out_specs=P("tm", "agent", None), check_vma=False
    )
```

```python
import functools

import jax
import jax.numpy as jnp
from jax import lax
from jax.experimental import pallas as pl
from jax.experimental.pallas import tpu as pltpu
from jax.sharding import PartitionSpec as P

HEAD = 64
CHUNKS = 2
RADIX = 32
EPS = 1e-05
LOG2E = 1.4426950408889634
MIB = 1024 * 1024
VMEM = pl.BlockSpec(memory_space=pltpu.VMEM)
ANY = pl.BlockSpec(memory_space=pl.ANY)
HBM = pl.BlockSpec(memory_space=pltpu.HBM)


def pinned(x):
    return pltpu.with_memory_space_constraint(x, pltpu.VMEM)


def far(x):
    return pltpu.with_memory_space_constraint(x, pltpu.HBM)


def cost(microseconds):
    return pl.CostEstimate(
        flops=int(1.1e9 * microseconds) + 10**6, bytes_accessed=int(3.5e6 * microseconds) + 10**4, transcendentals=0
    )


def away(k, steps, member):
    odd = member % 2
    return 0 if k == steps - 1 else (steps - 1 - k) * (1 - odd) + (k + 1) * odd


def dot(a, b):
    return jnp.dot(a, b, preferred_element_type=jnp.float32)


def dot_t(a, b):
    return lax.dot_general(a, b, (((1,), (1,)), ((), ())), preferred_element_type=jnp.float32)


def norm_scale(values):
    return lax.rsqrt(jnp.mean(values * values, axis=-1, keepdims=True) + EPS)


def gelu(x):
    return 0.5 * x * (1.0 + lax.erf(x * 0.7071067811865476))


def split_kernel(parts, tokens, *rest):
    outs, sem = rest[:parts], rest[parts]
    steps, agents = outs[0].shape[:2]
    copies = [
        pltpu.make_async_copy(
            tokens.at[step, pl.ds(j * agents, agents)], outs[j].at[step], sem.at[j * steps + step]
        )
        for j in range(parts)
        for step in range(steps)
    ]
    for copy in copies:
        copy.start()
    for copy in copies:
        copy.wait()


def split(tokens):
    steps, agents, width = tokens.shape
    return pl.pallas_call(
        functools.partial(split_kernel, CHUNKS),
        out_shape=[pltpu.VMEM((steps, agents // CHUNKS, width), tokens.dtype)] * CHUNKS,
        in_specs=[HBM],
        out_specs=[VMEM] * CHUNKS,
        scratch_shapes=[pltpu.SemaphoreType.DMA((CHUNKS * steps,))],
        compiler_params=pltpu.CompilerParams(vmem_limit_bytes=4 * MIB),
        cost_estimate=cost(30),
        name="split",
    )(far(tokens))


def stage_kernel(parts, count, taps, gain, order, present, *rest):
    tokens, sources = rest[:parts], rest[parts : parts + count]
    rest = rest[parts + count :]
    partials, tail, targets = rest[:parts], rest[parts], rest[parts + 1 : parts + 1 + count]
    taps_here, gain_here, order_here, present_here, normed, facts, sem = rest[parts + 1 + count :]
    pairs = [
        (taps, taps_here),
        (gain, gain_here),
        (order, order_here),
        (present, present_here),
        *zip(sources, targets),
    ]
    copies = [pltpu.make_async_copy(source, target, sem.at[i]) for i, (source, target) in enumerate(pairs)]
    for copy in copies:
        copy.start()
    for copy in copies:
        copy.wait()
    agents = order.shape[1]
    facts[...] = jnp.zeros(facts.shape, jnp.float32)
    facts[0:1, :agents] = (order_here[...] // RADIX).astype(jnp.float32)
    facts[1:2, :agents] = (order_here[...] % RADIX).astype(jnp.float32)
    facts[2:3, :agents] = present_here[...].astype(jnp.float32)
    tail[...] = facts[...].astype(jnp.bfloat16)
    steps, reach = tokens[0].shape[0], taps.shape[0] - 1
    gains = gain_here[...]
    for j in range(parts):
        for step in range(steps):
            values = tokens[j][step].astype(jnp.float32)
            normed[step] = values * norm_scale(values) * gains
            total = values
            for lag in range(min(step, reach) + 1):
                total = total + taps_here[lag : lag + 1, :] * normed[step - lag]
            partials[j][step] = total


def stage(tokens, taps, gain, order, present, arrays):
    steps, part, width = tokens[0].shape
    inputs = (taps, gain, order, present)
    return pl.pallas_call(
        functools.partial(stage_kernel, CHUNKS, len(arrays)),
        out_shape=[pltpu.VMEM((steps, part, width), jnp.float32)] * CHUNKS
        + [pltpu.VMEM((part, 128), jnp.bfloat16)]
        + [pltpu.VMEM(x.shape, x.dtype) for x in arrays],
        in_specs=[HBM] * len(inputs) + [VMEM] * CHUNKS + [HBM] * len(arrays),
        out_specs=[VMEM] * (CHUNKS + 1 + len(arrays)),
        scratch_shapes=[pltpu.VMEM(x.shape, x.dtype) for x in inputs]
        + [
            pltpu.VMEM((steps, part, width), jnp.float32),
            pltpu.VMEM((part, 128), jnp.float32),
            pltpu.SemaphoreType.DMA((len(inputs) + len(arrays),)),
        ],
        compiler_params=pltpu.CompilerParams(vmem_limit_bytes=8 * MIB),
        cost_estimate=cost(0),
        name="stage",
    )(*[far(x) for x in inputs], *[pinned(x) for x in tokens], *[far(x) for x in arrays])


def mixed_rows(halo, partial, taps, gain, normed, first):
    steps, agents = halo.shape[:2]
    reach = taps.shape[0] - 1
    gains = gain[...]
    for step in range(steps):
        values = halo[step].astype(jnp.float32)
        normed[step] = values * norm_scale(values) * gains
    for step in range(steps):
        total = partial[step]
        for lag in range(step + 1, reach + 1):
            total = total + taps[lag : lag + 1, :] * normed[steps + step - lag]
        first[step * agents : (step + 1) * agents, :] = total.astype(jnp.bfloat16).astype(first.dtype)


def feed_forward(rows, gain, w_in, w_out, hidden):
    inner = (rows * norm_scale(rows) * gain[...]).astype(jnp.bfloat16)
    tile = 512
    for start in range(0, w_in.shape[1], tile):
        hidden[:, start : start + tile] = gelu(dot(inner, w_in[:, start : start + tile])).astype(jnp.bfloat16)
    return (rows + dot(hidden[...], w_out[...])).astype(jnp.bfloat16)


def to_heads(second, gain, w_key, w_value, w_query, query, keyval):
    width = second.shape[1]
    values = second.astype(jnp.float32)
    attn_in = (values * norm_scale(values) * gain[...]).astype(jnp.bfloat16)
    keyval[:, :width] = dot(attn_in, w_key[...]).astype(jnp.bfloat16)
    keyval[:, width : 2 * width] = dot(attn_in, w_value[...]).astype(jnp.bfloat16)
    query[...] = dot(attn_in, w_query[...]).astype(jnp.bfloat16)


def conv_kernel(group, halo, partial, taps, gain, tail, *rest):
    steps, agents, width = halo.shape
    outs = rest[:steps]
    normed, first = rest[steps:]
    mixed_rows(halo, partial, taps, gain, normed, first)
    spot = lax.axis_index("agent")
    for k in range(steps):
        step = (spot // group) ^ away(k, steps, spot % group)
        outs[k][:, :width] = first[pl.ds(pl.multiple_of(step * agents, agents), agents), :].astype(jnp.bfloat16)
        outs[k][:, width:] = tail[...]


def conv(group, halo, partial, taps, gain, tail):
    steps, agents, width = halo.shape
    return pl.pallas_call(
        functools.partial(conv_kernel, group),
        out_shape=[jax.ShapeDtypeStruct((agents, width + tail.shape[1]), jnp.bfloat16)] * steps,
        in_specs=[VMEM] * 5,
        out_specs=[VMEM] * steps,
        scratch_shapes=[
            pltpu.VMEM((steps, agents, width), jnp.float32),
            pltpu.VMEM((steps * agents, width), jnp.float32),
        ],
        compiler_params=pltpu.CompilerParams(vmem_limit_bytes=8 * MIB),
        cost_estimate=cost(0),
        name="conv",
    )(halo, *[pinned(x) for x in (partial, taps, gain, tail)])


def front_kernel(group, halo, partial, taps, gain_first, gain_second, w_in, w_out, *rest):
    steps, agents, width = halo.shape
    outs = rest[:steps]
    normed, first, hidden, second = rest[steps:]
    mixed_rows(halo, partial, taps, gain_first, normed, first)
    result = feed_forward(first[...], gain_second, w_in, w_out, hidden)
    for step in range(steps):
        second[step] = result[step * agents : (step + 1) * agents]
    spot = lax.axis_index("agent")
    for k in range(steps):
        outs[k][...] = second[(spot // group) ^ away(k, steps, spot % group)]


def front(group, halo, partial, taps, gains, w_in, w_out):
    steps, agents, width = halo.shape
    rows = steps * agents
    return pl.pallas_call(
        functools.partial(front_kernel, group),
        out_shape=[jax.ShapeDtypeStruct((agents, width), jnp.bfloat16)] * steps,
        in_specs=[VMEM] * 7,
        out_specs=[VMEM] * steps,
        scratch_shapes=[
            pltpu.VMEM((steps, agents, width), jnp.float32),
            pltpu.VMEM((rows, width), jnp.float32),
            pltpu.VMEM((rows, w_in.shape[1]), jnp.bfloat16),
            pltpu.VMEM((steps, agents, width), jnp.bfloat16),
        ],
        compiler_params=pltpu.CompilerParams(vmem_limit_bytes=12 * MIB),
        cost_estimate=cost(0),
        name="front",
    )(halo, *[pinned(x) for x in (partial, taps, *gains, w_in, w_out)])


def feed_kernel(count, *refs):
    pieces = refs[:count]
    gain_second, gain_third, w_in, w_out, w_key, w_value, w_query = refs[count : count + 7]
    query, keyval, second, hidden = refs[count + 7 :]
    width = gain_second.shape[1]
    agents = pieces[0].shape[0]
    for k in range(count):
        keyval[agents * k : agents * (k + 1), 2 * width :] = pieces[k][:, width:]
    first = jnp.concatenate([piece[:, :width].astype(jnp.float32) for piece in pieces], axis=0)
    result = feed_forward(first, gain_second, w_in, w_out, hidden)
    second[...] = result
    to_heads(result, gain_third, w_key, w_value, w_query, query, keyval)


def feed(pieces, gains, weights):
    rows = sum(piece.shape[0] for piece in pieces)
    width = gains[0].shape[1]
    return pl.pallas_call(
        functools.partial(feed_kernel, len(pieces)),
        out_shape=[
            jax.ShapeDtypeStruct((rows, width), jnp.bfloat16),
            jax.ShapeDtypeStruct((rows, width + pieces[0].shape[1]), jnp.bfloat16),
            jax.ShapeDtypeStruct((rows, width), jnp.bfloat16),
        ],
        in_specs=[VMEM] * (len(pieces) + 7),
        out_specs=[VMEM] * 3,
        scratch_shapes=[pltpu.VMEM((rows, weights[0].shape[1]), jnp.bfloat16)],
        compiler_params=pltpu.CompilerParams(vmem_limit_bytes=12 * MIB),
        cost_estimate=cost(0),
        name="feed",
    )(*pieces, *[pinned(x) for x in (*gains, *weights)])


def project_kernel(count, *refs):
    pieces = refs[:count][::-1]
    gain, w_key, w_value, w_query, query, keyval = refs[count:]
    second = jnp.concatenate([piece[...] for piece in pieces], axis=0)
    to_heads(second, gain, w_key, w_value, w_query, query, keyval)


def project(pieces, gain, weights):
    rows = sum(piece.shape[0] for piece in pieces)
    width = gain.shape[1]
    return pl.pallas_call(
        functools.partial(project_kernel, len(pieces)),
        out_shape=[
            jax.ShapeDtypeStruct((rows, width), jnp.bfloat16),
            jax.ShapeDtypeStruct((rows, 2 * width), jnp.bfloat16),
        ],
        in_specs=[VMEM] * (len(pieces) + 4),
        out_specs=[VMEM] * 2,
        compiler_params=pltpu.CompilerParams(vmem_limit_bytes=8 * MIB),
        cost_estimate=cost(25),
        name="project",
    )(*reversed(pieces), *[pinned(x) for x in (gain, *weights)])


def mask_kernel(steps, chunks, agents, group, width, *rest):
    blocks, bias = rest[:group], rest[group]
    now = (lax.axis_index("tm") * steps + lax.axis_index("agent") // group).astype(jnp.float32)
    lane = lax.broadcasted_iota(jnp.int32, (agents, 128), 1)
    sublane = lax.broadcasted_iota(jnp.int32, (agents, 128), 0)
    tiles = {}
    for r in range(group):
        for k in range(steps):
            tile = blocks[r][agents * k : agents * (k + 1), 2 * width :].astype(jnp.float32)
            tiles[k, r] = (tile[0:1] * RADIX + tile[1:2], tile[2:3])
    own = jnp.concatenate(
        [
            jnp.sum(jnp.where(lane == sublane + j * agents, tiles[k, 0][0], 0.0), axis=1, keepdims=True)
            for k in range(steps)
            for j in range(chunks)
        ],
        axis=0,
    )
    row_lane = lax.broadcasted_iota(jnp.int32, (1, 128), 1)
    per_tile = 128 // agents
    start = 0
    for r in range(group):
        for j in range(chunks):
            for first in range(0, steps, per_tile):
                both = [None, None]
                for i in range(per_tile):
                    for f in (0, 1):
                        moved = pltpu.roll(tiles[first + i, r][f], ((i - j) * agents) % 128, 1)
                        both[f] = moved if i == 0 else jnp.where(row_lane >= i * agents, moved, both[f])
                order, present = both
                alive = jnp.where(now < present, order, 1e9)
                visible = (alive < own) | (order == own)
                bias[:, start : start + 128] = jnp.where(visible, 0.0, -1e30)
                start += 128


def mask(blocks, steps, agents, width):
    rows, group = steps * agents * CHUNKS, len(blocks)
    return pl.pallas_call(
        functools.partial(mask_kernel, steps, CHUNKS, agents, group, width),
        out_shape=pltpu.VMEM((rows, rows * group), jnp.float32),
        in_specs=[VMEM] * group,
        out_specs=VMEM,
        compiler_params=pltpu.CompilerParams(vmem_limit_bytes=8 * MIB),
        cost_estimate=cost(0),
        name="mask",
    )(*blocks)


def attend_kernel(ks, chunks, count, *refs):
    mine = 1 + len(ks) * (chunks - 1)
    queries, seconds, (w_output, bias) = refs[:chunks], refs[chunks : chunks + mine], refs[chunks + mine : chunks + mine + 2]
    rest = refs[chunks + mine + 2 :]
    blocks, outs, attended = rest[:count], rest[count : count + len(ks)], rest[count + len(ks)]
    width = queries[0].shape[1]
    rows = attended.shape[0]
    agents = rows // (len(ks) * chunks)
    keys = sum(block.shape[0] for block in blocks)
    scale = LOG2E * HEAD ** (-0.5)
    low = lax.broadcasted_iota(jnp.int32, (rows, 128), 1) < HEAD
    ones = jnp.ones((keys, 128), jnp.bfloat16)
    first_row = ks[0] * agents * chunks

    for pair in range(width // 128):
        columns = slice(128 * pair, 128 * pair + 128)
        value_columns = slice(width + 128 * pair, width + 128 * pair + 128)
        here = jnp.concatenate(
            [queries[j][agents * k : agents * (k + 1), columns] for k in ks for j in range(chunks)], axis=0
        )
        zeros = jnp.zeros_like(here)
        stacked = jnp.concatenate([jnp.where(low, here, zeros), jnp.where(low, zeros, here)], axis=0)
        key = jnp.concatenate([block[:, columns] for block in blocks], axis=0)
        value = jnp.concatenate([block[:, value_columns] for block in blocks], axis=0)
        products = dot_t(stacked, key)
        weights = []
        for half in range(2):
            scores = products[half * rows : (half + 1) * rows] * scale + bias[first_row : first_row + rows, :]
            top = jnp.max(scores, axis=1, keepdims=True)
            weights.append(jnp.exp2(scores - top).astype(jnp.bfloat16))
        total = dot(jnp.concatenate(weights, axis=0), jnp.concatenate([value, ones], axis=1))
        ratio = total[:, :128] / total[:, 128:]
        attended[:, columns] = jnp.where(low, ratio[:rows], ratio[rows:]).astype(jnp.bfloat16)
    part = agents
    residual = []
    for i, k in enumerate(ks):
        residual += [seconds[0][part * k : part * (k + 1)]]
        residual += [piece[...] for piece in seconds[1 + i * (chunks - 1) : 1 + (i + 1) * (chunks - 1)]]
    second = jnp.concatenate(residual, axis=0).astype(jnp.float32)
    result = second + dot(attended[...], w_output[...])
    for i in range(len(ks)):
        outs[i][...] = result[i * agents * chunks : (i + 1) * agents * chunks].astype(jnp.bfloat16)


def attend(ks, queries, seconds, w_output, bias, blocks, agents, microseconds):
    width = queries[0].shape[1]
    piece = jax.ShapeDtypeStruct((agents, width), jnp.bfloat16)
    return pl.pallas_call(
        functools.partial(attend_kernel, ks, len(queries), len(blocks)),
        out_shape=[piece] * len(ks),
        in_specs=[VMEM] * (len(queries) + len(seconds) + 2 + len(blocks)),
        out_specs=[VMEM] * len(ks),
        scratch_shapes=[pltpu.VMEM((len(ks) * agents, width), jnp.bfloat16)],
        compiler_params=pltpu.CompilerParams(vmem_limit_bytes=16 * MIB),
        cost_estimate=cost(microseconds),
        name="attend",
    )(*queries, *seconds, pinned(w_output), pinned(bias), *blocks)


def put_back_kernel(steps, group, *refs):
    pieces, out, sem = refs[:steps][::-1], refs[steps], refs[steps + 1]
    spot = lax.axis_index("agent")
    half = pieces[0].shape[0] // 2
    copies = []
    for k in range(steps):
        target = out.at[(spot // group) ^ away(k, steps, spot % group)]
        for rows in (pl.ds(0, half), pl.ds(half, half)):
            copies.append(pltpu.make_async_copy(pieces[k].at[rows], target.at[rows], sem.at[len(copies)]))
    for copy in copies:
        copy.start()
    for copy in copies:
        copy.wait()


def put_back(group, pieces, shape):
    return pl.pallas_call(
        functools.partial(put_back_kernel, shape[0], group),
        out_shape=jax.ShapeDtypeStruct(shape, jnp.bfloat16),
        in_specs=[VMEM] * len(pieces),
        out_specs=ANY,
        scratch_shapes=[pltpu.SemaphoreType.DMA((2 * len(pieces),))],
        compiler_params=pltpu.CompilerParams(vmem_limit_bytes=4 * MIB),
        cost_estimate=cost(0),
        name="put_back",
    )(*pieces)


def after(x, *others):
    return lax.optimization_barrier((x, *others))[0]


def per_device(
    tokens,
    conv_taps,
    norm_first,
    norm_second,
    norm_third,
    w_in,
    w_out,
    w_query,
    w_key,
    w_value,
    w_output,
    agent_order,
    present_steps,
):
    steps, agents, width = tokens.shape
    tm_count, count = lax.axis_size("tm"), lax.axis_size("agent")
    group = count // steps
    part = agents // CHUNKS
    assert group * steps == count and steps == 4 and 128 % part == 0

    def across(x, k):
        if k == steps - 1:
            return x
        pairs = [(i, ((i // group) ^ away(k, steps, i % group)) * group + i % group) for i in range(count)]
        return lax.ppermute(x, "agent", pairs)

    def within(x, r):
        return lax.ppermute(x, "agent", [(i, (i // group) * group + ((i % group) ^ r)) for i in range(count)])

    parts = split(tokens)
    *partials, tail, taps, gain_first, gain_second, gain_third = stage(
        parts,
        conv_taps,
        norm_first.reshape(1, width),
        agent_order.reshape(1, agents),
        present_steps.reshape(1, agents),
        [conv_taps] + [x.reshape(1, width) for x in (norm_first, norm_second, norm_third)],
    )
    halos = [
        lax.ppermute(x if j == 0 else after(x, tail), "tm", [(i, i + 1) for i in range(tm_count - 1)])
        for j, x in enumerate(parts)
    ]
    halos[0] = after(halos[0], tail)
    made = conv(group, halos[0], partials[0], taps, gain_first, tail)
    last = made[-1]
    pieces = [[across(made[k], k) for k in range(steps)]]
    for j in range(1, CHUNKS):
        halos[j] = after(halos[j], last)
        made = list(front(group, halos[j], partials[j], taps, (gain_first, gain_second), w_in, w_out))
        last = made[-1]
        made[steps - 2] = after(made[steps - 2], pieces[j - 1][0])
        pieces.append([across(made[k], k) for k in range(steps)])
    pieces[0][-1] = after(pieces[0][-1], last)
    to_attend = (w_key, w_value, w_query)
    query, keyval, second = feed(pieces[0], (gain_second, gain_third), (w_in, w_out, *to_attend))
    queries = [query]
    blocks = [[keyval] + [within(keyval, r) for r in range(1, group)]]
    for j in range(1, CHUNKS):
        query, keyval = project(pieces[j], gain_third, to_attend)
        keyval = after(keyval, *blocks[j - 1])
        queries.append(query)
        blocks.append([keyval] + [within(keyval, r) for r in range(1, group)])
    bias = mask(blocks[0], steps, part, width)
    blocks = [blocks[j][r] for r in range(group) for j in range(CHUNKS)]

    def rows_of(ks, microseconds):
        seconds = [second] + [pieces[j][k] for k in ks for j in range(1, CHUNKS)]
        return attend(ks, queries, seconds, w_output, bias, blocks, agents, microseconds)

    results = [*rows_of((0, 1), 0), *rows_of((2, 3), 10)]
    return put_back(group, [across(results[k], k) for k in reversed(range(steps))], tokens.shape)


def solution(mesh):
    in_specs = (P("tm", "agent", None),) + (P(),) * 10 + (P("agent"), P("agent"))
    return jax.shard_map(
        per_device, mesh=mesh, in_specs=in_specs, out_specs=P("tm", "agent", None), check_vma=False
    )
```

```python
import functools

import jax
import jax.numpy as jnp
from jax import lax
from jax.experimental import pallas as pl
from jax.experimental.pallas import tpu as pltpu
from jax.sharding import PartitionSpec as P

HEAD = 64
CHUNKS = 2
RADIX = 32
EPS = 1e-05
LOG2E = 1.4426950408889634
MIB = 1024 * 1024
VMEM = pl.BlockSpec(memory_space=pltpu.VMEM)
ANY = pl.BlockSpec(memory_space=pl.ANY)
HBM = pl.BlockSpec(memory_space=pltpu.HBM)


def pinned(x):
    return pltpu.with_memory_space_constraint(x, pltpu.VMEM)


def far(x):
    return pltpu.with_memory_space_constraint(x, pltpu.HBM)


def cost(microseconds):
    return pl.CostEstimate(
        flops=int(1.1e9 * microseconds) + 10**6, bytes_accessed=int(3.5e6 * microseconds) + 10**4, transcendentals=0
    )


def away(k, steps, member):
    odd = member % 2
    return 0 if k == steps - 1 else (steps - 1 - k) * (1 - odd) + (k + 1) * odd


def dot(a, b):
    return jnp.dot(a, b, preferred_element_type=jnp.float32)


def dot_t(a, b):
    return lax.dot_general(a, b, (((1,), (1,)), ((), ())), preferred_element_type=jnp.float32)


def norm_scale(values):
    return lax.rsqrt(jnp.mean(values * values, axis=-1, keepdims=True) + EPS)


def gelu(x):
    return 0.5 * x * (1.0 + lax.erf(x * 0.7071067811865476))


def split_kernel(parts, tokens, *rest):
    outs, sem = rest[:parts], rest[parts]
    steps, agents = outs[0].shape[:2]
    copies = [
        pltpu.make_async_copy(
            tokens.at[step, pl.ds(j * agents, agents)], outs[j].at[step], sem.at[j * steps + step]
        )
        for j in range(parts)
        for step in range(steps)
    ]
    for copy in copies:
        copy.start()
    for copy in copies:
        copy.wait()


def split(tokens):
    steps, agents, width = tokens.shape
    return pl.pallas_call(
        functools.partial(split_kernel, CHUNKS),
        out_shape=[pltpu.VMEM((steps, agents // CHUNKS, width), tokens.dtype)] * CHUNKS,
        in_specs=[HBM],
        out_specs=[VMEM] * CHUNKS,
        scratch_shapes=[pltpu.SemaphoreType.DMA((CHUNKS * steps,))],
        compiler_params=pltpu.CompilerParams(vmem_limit_bytes=4 * MIB),
        cost_estimate=cost(30),
        name="split",
    )(far(tokens))


def stage_kernel(parts, count, taps, gain, order, present, *rest):
    tokens, sources = rest[:parts], rest[parts : parts + count]
    rest = rest[parts + count :]
    partials, tail, targets = rest[:parts], rest[parts], rest[parts + 1 : parts + 1 + count]
    taps_here, gain_here, order_here, present_here, normed, facts, sem = rest[parts + 1 + count :]
    pairs = [
        (taps, taps_here),
        (gain, gain_here),
        (order, order_here),
        (present, present_here),
        *zip(sources, targets),
    ]
    copies = [pltpu.make_async_copy(source, target, sem.at[i]) for i, (source, target) in enumerate(pairs)]
    for copy in copies:
        copy.start()
    for copy in copies:
        copy.wait()
    agents = order.shape[1]
    facts[...] = jnp.zeros(facts.shape, jnp.float32)
    facts[0:1, :agents] = (order_here[...] // RADIX).astype(jnp.float32)
    facts[1:2, :agents] = (order_here[...] % RADIX).astype(jnp.float32)
    facts[2:3, :agents] = present_here[...].astype(jnp.float32)
    tail[...] = facts[...].astype(jnp.bfloat16)
    steps, reach = tokens[0].shape[0], taps.shape[0] - 1
    gains = gain_here[...]
    for j in range(parts):
        for step in range(steps):
            values = tokens[j][step].astype(jnp.float32)
            normed[step] = values * norm_scale(values) * gains
            total = values
            for lag in range(min(step, reach) + 1):
                total = total + taps_here[lag : lag + 1, :] * normed[step - lag]
            partials[j][step] = total


def stage(tokens, taps, gain, order, present, arrays):
    steps, part, width = tokens[0].shape
    inputs = (taps, gain, order, present)
    return pl.pallas_call(
        functools.partial(stage_kernel, CHUNKS, len(arrays)),
        out_shape=[pltpu.VMEM((steps, part, width), jnp.float32)] * CHUNKS
        + [pltpu.VMEM((part, 128), jnp.bfloat16)]
        + [pltpu.VMEM(x.shape, x.dtype) for x in arrays],
        in_specs=[HBM] * len(inputs) + [VMEM] * CHUNKS + [HBM] * len(arrays),
        out_specs=[VMEM] * (CHUNKS + 1 + len(arrays)),
        scratch_shapes=[pltpu.VMEM(x.shape, x.dtype) for x in inputs]
        + [
            pltpu.VMEM((steps, part, width), jnp.float32),
            pltpu.VMEM((part, 128), jnp.float32),
            pltpu.SemaphoreType.DMA((len(inputs) + len(arrays),)),
        ],
        compiler_params=pltpu.CompilerParams(vmem_limit_bytes=8 * MIB),
        cost_estimate=cost(0),
        name="stage",
    )(*[far(x) for x in inputs], *[pinned(x) for x in tokens], *[far(x) for x in arrays])


def mixed_rows(halo, partial, taps, gain, normed, first):
    steps, agents = halo.shape[:2]
    reach = taps.shape[0] - 1
    gains = gain[...]
    for step in range(steps):
        values = halo[step].astype(jnp.float32)
        normed[step] = values * norm_scale(values) * gains
    for step in range(steps):
        total = partial[step]
        for lag in range(step + 1, reach + 1):
            total = total + taps[lag : lag + 1, :] * normed[steps + step - lag]
        first[step * agents : (step + 1) * agents, :] = total.astype(jnp.bfloat16).astype(first.dtype)


def feed_forward(rows, gain, w_in, w_out, hidden):
    inner = (rows * norm_scale(rows) * gain[...]).astype(jnp.bfloat16)
    tile = 512
    for start in range(0, w_in.shape[1], tile):
        hidden[:, start : start + tile] = gelu(dot(inner, w_in[:, start : start + tile])).astype(jnp.bfloat16)
    return (rows + dot(hidden[...], w_out[...])).astype(jnp.bfloat16)


def to_keys(second, gain, w_key, w_value, keyval):
    width = second.shape[1]
    values = second.astype(jnp.float32)
    attn_in = (values * norm_scale(values) * gain[...]).astype(jnp.bfloat16)
    keyval[:, :width] = dot(attn_in, w_key[...]).astype(jnp.bfloat16)
    keyval[:, width : 2 * width] = dot(attn_in, w_value[...]).astype(jnp.bfloat16)
    return attn_in


def conv_kernel(group, halo, partial, taps, gain, tail, *rest):
    steps, agents, width = halo.shape
    outs = rest[:steps]
    normed, first = rest[steps:]
    mixed_rows(halo, partial, taps, gain, normed, first)
    spot = lax.axis_index("agent")
    for k in range(steps):
        step = (spot // group) ^ away(k, steps, spot % group)
        outs[k][:, :width] = first[pl.ds(pl.multiple_of(step * agents, agents), agents), :].astype(jnp.bfloat16)
        outs[k][:, width:] = tail[...]


def conv(group, halo, partial, taps, gain, tail):
    steps, agents, width = halo.shape
    return pl.pallas_call(
        functools.partial(conv_kernel, group),
        out_shape=[jax.ShapeDtypeStruct((agents, width + tail.shape[1]), jnp.bfloat16)] * steps,
        in_specs=[VMEM] * 5,
        out_specs=[VMEM] * steps,
        scratch_shapes=[
            pltpu.VMEM((steps, agents, width), jnp.float32),
            pltpu.VMEM((steps * agents, width), jnp.float32),
        ],
        compiler_params=pltpu.CompilerParams(vmem_limit_bytes=8 * MIB),
        cost_estimate=cost(0),
        name="conv",
    )(halo, *[pinned(x) for x in (partial, taps, gain, tail)])


def front_kernel(group, halo, partial, taps, gain_first, gain_second, w_in, w_out, *rest):
    steps, agents, width = halo.shape
    outs = rest[:steps]
    normed, first, hidden, second = rest[steps:]
    mixed_rows(halo, partial, taps, gain_first, normed, first)
    result = feed_forward(first[...], gain_second, w_in, w_out, hidden)
    for step in range(steps):
        second[step] = result[step * agents : (step + 1) * agents]
    spot = lax.axis_index("agent")
    for k in range(steps):
        outs[k][...] = second[(spot // group) ^ away(k, steps, spot % group)]


def front(group, halo, partial, taps, gains, w_in, w_out):
    steps, agents, width = halo.shape
    rows = steps * agents
    return pl.pallas_call(
        functools.partial(front_kernel, group),
        out_shape=[jax.ShapeDtypeStruct((agents, width), jnp.bfloat16)] * steps,
        in_specs=[VMEM] * 7,
        out_specs=[VMEM] * steps,
        scratch_shapes=[
            pltpu.VMEM((steps, agents, width), jnp.float32),
            pltpu.VMEM((rows, width), jnp.float32),
            pltpu.VMEM((rows, w_in.shape[1]), jnp.bfloat16),
            pltpu.VMEM((steps, agents, width), jnp.bfloat16),
        ],
        compiler_params=pltpu.CompilerParams(vmem_limit_bytes=12 * MIB),
        cost_estimate=cost(0),
        name="front",
    )(halo, *[pinned(x) for x in (partial, taps, *gains, w_in, w_out)])


def feed_kernel(count, *refs):
    pieces = refs[:count]
    gain_second, gain_third, w_in, w_out, w_key, w_value, w_query = refs[count : count + 7]
    query, keyval, second, hidden = refs[count + 7 :]
    width = gain_second.shape[1]
    agents = pieces[0].shape[0]
    for k in range(count):
        keyval[agents * k : agents * (k + 1), 2 * width :] = pieces[k][:, width:]
    first = jnp.concatenate([piece[:, :width].astype(jnp.float32) for piece in pieces], axis=0)
    result = feed_forward(first, gain_second, w_in, w_out, hidden)
    second[...] = result
    attn_in = to_keys(result, gain_third, w_key, w_value, keyval)
    query[...] = dot(attn_in, w_query[...]).astype(jnp.bfloat16)


def feed(pieces, gains, weights):
    rows = sum(piece.shape[0] for piece in pieces)
    width = gains[0].shape[1]
    return pl.pallas_call(
        functools.partial(feed_kernel, len(pieces)),
        out_shape=[
            jax.ShapeDtypeStruct((rows, width), jnp.bfloat16),
            jax.ShapeDtypeStruct((rows, width + pieces[0].shape[1]), jnp.bfloat16),
            jax.ShapeDtypeStruct((rows, width), jnp.bfloat16),
        ],
        in_specs=[VMEM] * (len(pieces) + 7),
        out_specs=[VMEM] * 3,
        scratch_shapes=[pltpu.VMEM((rows, weights[0].shape[1]), jnp.bfloat16)],
        compiler_params=pltpu.CompilerParams(vmem_limit_bytes=12 * MIB),
        cost_estimate=cost(0),
        name="feed",
    )(*pieces, *[pinned(x) for x in (*gains, *weights)])


def project_kernel(count, *refs):
    pieces = refs[:count][::-1]
    gain, w_key, w_value, attn_in, keyval = refs[count:]
    second = jnp.concatenate([piece[...] for piece in pieces], axis=0)
    attn_in[...] = to_keys(second, gain, w_key, w_value, keyval)


def project(pieces, gain, weights):
    rows = sum(piece.shape[0] for piece in pieces)
    width = gain.shape[1]
    return pl.pallas_call(
        functools.partial(project_kernel, len(pieces)),
        out_shape=[
            jax.ShapeDtypeStruct((rows, width), jnp.bfloat16),
            jax.ShapeDtypeStruct((rows, 2 * width), jnp.bfloat16),
        ],
        in_specs=[VMEM] * (len(pieces) + 3),
        out_specs=[VMEM] * 2,
        compiler_params=pltpu.CompilerParams(vmem_limit_bytes=8 * MIB),
        cost_estimate=cost(25),
        name="project",
    )(*reversed(pieces), *[pinned(x) for x in (gain, *weights)])


def block_order(group, chunks):
    early = [(r, 0) for r in range(group)] + [(0, j) for j in range(1, chunks)]
    return early + [(r, j) for j in range(1, chunks) for r in range(1, group)]


def mask_kernel(steps, chunks, agents, group, width, *rest):
    blocks, bias = rest[:group], rest[group]
    now = (lax.axis_index("tm") * steps + lax.axis_index("agent") // group).astype(jnp.float32)
    lane = lax.broadcasted_iota(jnp.int32, (agents, 128), 1)
    sublane = lax.broadcasted_iota(jnp.int32, (agents, 128), 0)
    tiles = {}
    for r in range(group):
        for k in range(steps):
            tile = blocks[r][agents * k : agents * (k + 1), 2 * width :].astype(jnp.float32)
            tiles[k, r] = (tile[0:1] * RADIX + tile[1:2], tile[2:3])
    own = jnp.concatenate(
        [
            jnp.sum(jnp.where(lane == sublane + j * agents, tiles[k, 0][0], 0.0), axis=1, keepdims=True)
            for k in range(steps)
            for j in range(chunks)
        ],
        axis=0,
    )
    row_lane = lax.broadcasted_iota(jnp.int32, (1, 128), 1)
    per_tile = 128 // agents
    start = 0
    for r, j in block_order(group, chunks):
        for first in range(0, steps, per_tile):
            both = [None, None]
            for i in range(per_tile):
                for f in (0, 1):
                    moved = pltpu.roll(tiles[first + i, r][f], ((i - j) * agents) % 128, 1)
                    both[f] = moved if i == 0 else jnp.where(row_lane >= i * agents, moved, both[f])
            order, present = both
            alive = jnp.where(now < present, order, 1e9)
            visible = (alive < own) | (order == own)
            bias[:, start : start + 128] = jnp.where(visible, 0.0, -1e30)
            start += 128


def mask(blocks, steps, agents, width):
    rows, group = steps * agents * CHUNKS, len(blocks)
    return pl.pallas_call(
        functools.partial(mask_kernel, steps, CHUNKS, agents, group, width),
        out_shape=pltpu.VMEM((rows, rows * group), jnp.float32),
        in_specs=[VMEM] * group,
        out_specs=VMEM,
        compiler_params=pltpu.CompilerParams(vmem_limit_bytes=8 * MIB),
        cost_estimate=cost(0),
        name="mask",
    )(*blocks)


def rows_of(parts, ks, agents, columns):
    return jnp.concatenate([part[agents * k : agents * (k + 1), columns] for k in ks for part in parts], axis=0)


def pair_weights(queries, blocks, bias, top, pair, low):
    rows, width = queries.shape[0], blocks[0].shape[1] // 2 // 128 * 128
    columns = slice(128 * pair, 128 * pair + 128)
    value_columns = slice(width + 128 * pair, width + 128 * pair + 128)
    zeros = jnp.zeros_like(queries)
    stacked = jnp.concatenate([jnp.where(low, queries, zeros), jnp.where(low, zeros, queries)], axis=0)
    key = jnp.concatenate([block[:, columns] for block in blocks], axis=0)
    value = jnp.concatenate([block[:, value_columns] for block in blocks], axis=0)
    products = dot_t(stacked, key)
    tops, weights = [], []
    for half in range(2):
        scores = products[half * rows : (half + 1) * rows] * (LOG2E * HEAD ** (-0.5)) + bias
        highest = jnp.max(scores, axis=1, keepdims=True)
        if top is not None:
            highest = jnp.maximum(highest, top[:, HEAD * half : HEAD * half + 1])
        tops.append(highest)
        weights.append(jnp.exp2(scores - highest).astype(jnp.bfloat16))
    ones = jnp.ones(value.shape, jnp.bfloat16)
    return tops, dot(jnp.concatenate(weights, axis=0), jnp.concatenate([value, ones], axis=1))


def merged(low, total):
    rows = total.shape[0] // 2
    return jnp.where(low, total[:rows], total[rows:])


def early_kernel(ks, chunks, count, *refs):
    (query, attn_in), (w_query, bias) = refs[:2], refs[2:4]
    blocks, (own_query, number, weight, top) = refs[4 : 4 + count], refs[4 + count :]
    own_query[...] = dot(attn_in[...], w_query[...]).astype(jnp.bfloat16)
    rows, width = number.shape
    agents = rows // (len(ks) * chunks)
    low = lax.broadcasted_iota(jnp.int32, (rows, 128), 1) < HEAD
    keys = sum(block.shape[0] for block in blocks)
    here = bias[ks[0] * agents * chunks : ks[0] * agents * chunks + rows, :keys]
    for pair in range(width // 128):
        columns = slice(128 * pair, 128 * pair + 128)
        queries = rows_of((query, own_query), ks, agents, columns)
        tops, total = pair_weights(queries, blocks, here, None, pair, low)
        number[:, columns] = merged(low, total[:, :128])
        weight[:, columns] = merged(low, total[:, 128:])
        top[:, columns] = jnp.where(low, tops[0], tops[1])


def early(ks, query, attn_in, w_query, bias, blocks):
    width = query.shape[1]
    rows = len(ks) * CHUNKS * query.shape[0] // 4
    state = pltpu.VMEM((rows, width), jnp.float32)
    return pl.pallas_call(
        functools.partial(early_kernel, ks, CHUNKS, len(blocks)),
        out_shape=[jax.ShapeDtypeStruct(query.shape, jnp.bfloat16), state, state, state],
        in_specs=[VMEM] * (4 + len(blocks)),
        out_specs=[VMEM] * 4,
        compiler_params=pltpu.CompilerParams(vmem_limit_bytes=16 * MIB),
        cost_estimate=cost(0),
        name="early",
    )(query, attn_in, pinned(w_query), pinned(bias), *blocks)


def attend_kernel(ks, chunks, count, begun, *refs):
    mine = 1 + len(ks) * (chunks - 1)
    queries, seconds, (w_output, bias) = refs[:chunks], refs[chunks : chunks + mine], refs[chunks + mine : chunks + mine + 2]
    rest = refs[chunks + mine + 2 :]
    blocks, state = rest[:count], rest[count : count + begun]
    outs, attended = rest[count + begun : count + begun + len(ks)], rest[count + begun + len(ks)]
    rows, width = attended.shape
    agents = rows // (len(ks) * chunks)
    low = lax.broadcasted_iota(jnp.int32, (rows, 128), 1) < HEAD
    keys = sum(block.shape[0] for block in blocks)
    here = bias[ks[0] * agents * chunks : ks[0] * agents * chunks + rows, bias.shape[1] - keys :]
    for pair in range(width // 128):
        columns = slice(128 * pair, 128 * pair + 128)
        before = [x[:, columns] for x in state]
        tops, total = pair_weights(
            rows_of(queries, ks, agents, columns), blocks, here, before[2] if begun else None, pair, low
        )
        number, weight = merged(low, total[:, :128]), merged(low, total[:, 128:])
        if begun:
            shrink = jnp.exp2(before[2] - jnp.where(low, tops[0], tops[1]))
            number, weight = number + before[0] * shrink, weight + before[1] * shrink
        attended[:, columns] = (number / weight).astype(jnp.bfloat16)
    residual = []
    for i, k in enumerate(ks):
        residual += [seconds[0][agents * k : agents * (k + 1)]]
        residual += [piece[...] for piece in seconds[1 + i * (chunks - 1) : 1 + (i + 1) * (chunks - 1)]]
    result = jnp.concatenate(residual, axis=0).astype(jnp.float32) + dot(attended[...], w_output[...])
    for i in range(len(ks)):
        outs[i][...] = result[i * agents * chunks : (i + 1) * agents * chunks].astype(jnp.bfloat16)


def attend(ks, queries, seconds, w_output, bias, blocks, state, agents, microseconds):
    width = queries[0].shape[1]
    piece = jax.ShapeDtypeStruct((agents, width), jnp.bfloat16)
    return pl.pallas_call(
        functools.partial(attend_kernel, ks, len(queries), len(blocks), len(state)),
        out_shape=[piece] * len(ks),
        in_specs=[VMEM] * (len(queries) + len(seconds) + 2 + len(blocks) + len(state)),
        out_specs=[VMEM] * len(ks),
        scratch_shapes=[pltpu.VMEM((len(ks) * agents, width), jnp.bfloat16)],
        compiler_params=pltpu.CompilerParams(vmem_limit_bytes=16 * MIB),
        cost_estimate=cost(microseconds),
        name="attend",
    )(*queries, *seconds, pinned(w_output), pinned(bias), *blocks, *[pinned(x) for x in state])


def put_back_kernel(steps, group, *refs):
    pieces, out, sem = refs[:steps][::-1], refs[steps], refs[steps + 1]
    spot = lax.axis_index("agent")
    half = pieces[0].shape[0] // 2
    copies = []
    for k in range(steps):
        target = out.at[(spot // group) ^ away(k, steps, spot % group)]
        for rows in (pl.ds(0, half), pl.ds(half, half)):
            copies.append(pltpu.make_async_copy(pieces[k].at[rows], target.at[rows], sem.at[len(copies)]))
    for copy in copies:
        copy.start()
    for copy in copies:
        copy.wait()


def put_back(group, pieces, shape):
    return pl.pallas_call(
        functools.partial(put_back_kernel, shape[0], group),
        out_shape=jax.ShapeDtypeStruct(shape, jnp.bfloat16),
        in_specs=[VMEM] * len(pieces),
        out_specs=ANY,
        scratch_shapes=[pltpu.SemaphoreType.DMA((2 * len(pieces),))],
        compiler_params=pltpu.CompilerParams(vmem_limit_bytes=4 * MIB),
        cost_estimate=cost(0),
        name="put_back",
    )(*pieces)


def after(x, *others):
    return lax.optimization_barrier((x, *others))[0]


def per_device(
    tokens,
    conv_taps,
    norm_first,
    norm_second,
    norm_third,
    w_in,
    w_out,
    w_query,
    w_key,
    w_value,
    w_output,
    agent_order,
    present_steps,
):
    steps, agents, width = tokens.shape
    tm_count, count = lax.axis_size("tm"), lax.axis_size("agent")
    group = count // steps
    part = agents // CHUNKS
    assert group * steps == count and steps == 4 and 128 % part == 0 and CHUNKS == 2 and group > 1

    def across(x, k):
        if k == steps - 1:
            return x
        pairs = [(i, ((i // group) ^ away(k, steps, i % group)) * group + i % group) for i in range(count)]
        return lax.ppermute(x, "agent", pairs)

    def within(x, r):
        return lax.ppermute(x, "agent", [(i, (i // group) * group + ((i % group) ^ r)) for i in range(count)])

    parts = split(tokens)
    *partials, tail, taps, gain_first, gain_second, gain_third = stage(
        parts,
        conv_taps,
        norm_first.reshape(1, width),
        agent_order.reshape(1, agents),
        present_steps.reshape(1, agents),
        [conv_taps] + [x.reshape(1, width) for x in (norm_first, norm_second, norm_third)],
    )
    halos = [
        lax.ppermute(x if j == 0 else after(x, tail), "tm", [(i, i + 1) for i in range(tm_count - 1)])
        for j, x in enumerate(parts)
    ]
    halos[0] = after(halos[0], tail)
    made = conv(group, halos[0], partials[0], taps, gain_first, tail)
    last = made[-1]
    pieces = [[across(made[k], k) for k in range(steps)]]
    for j in range(1, CHUNKS):
        halos[j] = after(halos[j], last)
        made = list(front(group, halos[j], partials[j], taps, (gain_first, gain_second), w_in, w_out))
        last = made[-1]
        made[steps - 2] = after(made[steps - 2], pieces[j - 1][0])
        pieces.append([across(made[k], k) for k in range(steps)])
    pieces[0][-1] = after(pieces[0][-1], last)
    query, keyval, second = feed(pieces[0], (gain_second, gain_third), (w_in, w_out, w_key, w_value, w_query))
    blocks = {(0, 0): keyval, **{(r, 0): within(keyval, r) for r in range(1, group)}}
    attn_in, keyval = project(pieces[1], gain_third, (w_key, w_value))
    keyval = after(keyval, *blocks.values())
    blocks.update({(0, 1): keyval, **{(r, 1): within(keyval, r) for r in range(1, group)}})
    bias = mask([blocks[r, 0] for r in range(group)], steps, part, width)
    blocks = [blocks[spot] for spot in block_order(group, CHUNKS)]
    ready = group + CHUNKS - 1
    far_ks, near_ks = (0, 1), (2, 3)
    own_query, *state = early(far_ks, query, attn_in, w_query, bias, blocks[:ready])

    def finish(ks, blocks, state, microseconds):
        seconds = [second] + [pieces[j][k] for k in ks for j in range(1, CHUNKS)]
        return attend(ks, (query, own_query), seconds, w_output, bias, blocks, state, agents, microseconds)

    results = [*finish(far_ks, blocks[ready:], state, 0), *finish(near_ks, blocks, [], 10)]
    return put_back(group, [across(results[k], k) for k in reversed(range(steps))], tokens.shape)


def solution(mesh):
    in_specs = (P("tm", "agent", None),) + (P(),) * 10 + (P("agent"), P("agent"))
    return jax.shard_map(
        per_device, mesh=mesh, in_specs=in_specs, out_specs=P("tm", "agent", None), check_vma=False
    )
```

```python
import functools

import jax
import jax.numpy as jnp
from jax import lax
from jax.experimental import pallas as pl
from jax.experimental.pallas import tpu as pltpu
from jax.sharding import PartitionSpec as P

HEAD = 64
CHUNKS = 2
RADIX = 32
EPS = 1e-05
LOG2E = 1.4426950408889634
MIB = 1024 * 1024
VMEM = pl.BlockSpec(memory_space=pltpu.VMEM)
ANY = pl.BlockSpec(memory_space=pl.ANY)
HBM = pl.BlockSpec(memory_space=pltpu.HBM)


def pinned(x):
    return pltpu.with_memory_space_constraint(x, pltpu.VMEM)


def far(x):
    return pltpu.with_memory_space_constraint(x, pltpu.HBM)


def cost(microseconds):
    return pl.CostEstimate(
        flops=int(1.1e9 * microseconds) + 10**6, bytes_accessed=int(3.5e6 * microseconds) + 10**4, transcendentals=0
    )


def away(k, steps, member):
    odd = member % 2
    return 0 if k == steps - 1 else (steps - 1 - k) * (1 - odd) + (k + 1) * odd


def dot(a, b):
    return jnp.dot(a, b, preferred_element_type=jnp.float32)


def dot_t(a, b):
    return lax.dot_general(a, b, (((1,), (1,)), ((), ())), preferred_element_type=jnp.float32)


def norm_scale(values):
    return lax.rsqrt(jnp.mean(values * values, axis=-1, keepdims=True) + EPS)


def gelu(x):
    return 0.5 * x * (1.0 + lax.erf(x * 0.7071067811865476))


def split_kernel(parts, tokens, *rest):
    outs, sem = rest[:parts], rest[parts]
    steps, agents = outs[0].shape[:2]
    copies = [
        pltpu.make_async_copy(
            tokens.at[step, pl.ds(j * agents, agents)], outs[j].at[step], sem.at[j * steps + step]
        )
        for j in range(parts)
        for step in range(steps)
    ]
    for copy in copies:
        copy.start()
    for copy in copies:
        copy.wait()


def split(tokens):
    steps, agents, width = tokens.shape
    return pl.pallas_call(
        functools.partial(split_kernel, CHUNKS),
        out_shape=[pltpu.VMEM((steps, agents // CHUNKS, width), tokens.dtype)] * CHUNKS,
        in_specs=[HBM],
        out_specs=[VMEM] * CHUNKS,
        scratch_shapes=[pltpu.SemaphoreType.DMA((CHUNKS * steps,))],
        compiler_params=pltpu.CompilerParams(vmem_limit_bytes=4 * MIB),
        cost_estimate=cost(30),
        name="split",
    )(far(tokens))


def stage_kernel(parts, count, taps, gain, order, present, *rest):
    tokens, sources = rest[:parts], rest[parts : parts + count]
    rest = rest[parts + count :]
    partials, tail, targets = rest[:parts], rest[parts], rest[parts + 1 : parts + 1 + count]
    taps_here, gain_here, order_here, present_here, normed, facts, sem = rest[parts + 1 + count :]
    pairs = [
        (taps, taps_here),
        (gain, gain_here),
        (order, order_here),
        (present, present_here),
        *zip(sources, targets),
    ]
    copies = [pltpu.make_async_copy(source, target, sem.at[i]) for i, (source, target) in enumerate(pairs)]
    for copy in copies:
        copy.start()
    for copy in copies:
        copy.wait()
    agents = order.shape[1]
    facts[...] = jnp.zeros(facts.shape, jnp.float32)
    facts[0:1, :agents] = (order_here[...] // RADIX).astype(jnp.float32)
    facts[1:2, :agents] = (order_here[...] % RADIX).astype(jnp.float32)
    facts[2:3, :agents] = present_here[...].astype(jnp.float32)
    tail[...] = facts[...].astype(jnp.bfloat16)
    steps, reach = tokens[0].shape[0], taps.shape[0] - 1
    gains = gain_here[...]
    for j in range(parts):
        for step in range(steps):
            values = tokens[j][step].astype(jnp.float32)
            normed[step] = values * norm_scale(values) * gains
            total = values
            for lag in range(min(step, reach) + 1):
                total = total + taps_here[lag : lag + 1, :] * normed[step - lag]
            partials[j][step] = total


def stage(tokens, taps, gain, order, present, arrays):
    steps, part, width = tokens[0].shape
    inputs = (taps, gain, order, present)
    return pl.pallas_call(
        functools.partial(stage_kernel, CHUNKS, len(arrays)),
        out_shape=[pltpu.VMEM((steps, part, width), jnp.float32)] * CHUNKS
        + [pltpu.VMEM((part, 128), jnp.bfloat16)]
        + [pltpu.VMEM(x.shape, x.dtype) for x in arrays],
        in_specs=[HBM] * len(inputs) + [VMEM] * CHUNKS + [HBM] * len(arrays),
        out_specs=[VMEM] * (CHUNKS + 1 + len(arrays)),
        scratch_shapes=[pltpu.VMEM(x.shape, x.dtype) for x in inputs]
        + [
            pltpu.VMEM((steps, part, width), jnp.float32),
            pltpu.VMEM((part, 128), jnp.float32),
            pltpu.SemaphoreType.DMA((len(inputs) + len(arrays),)),
        ],
        compiler_params=pltpu.CompilerParams(vmem_limit_bytes=8 * MIB),
        cost_estimate=cost(0),
        name="stage",
    )(*[far(x) for x in inputs], *[pinned(x) for x in tokens], *[far(x) for x in arrays])


def mixed_rows(halo, partial, taps, gain, normed, first):
    steps, agents = halo.shape[:2]
    reach = taps.shape[0] - 1
    gains = gain[...]
    for step in range(steps):
        values = halo[step].astype(jnp.float32)
        normed[step] = values * norm_scale(values) * gains
    for step in range(steps):
        total = partial[step]
        for lag in range(step + 1, reach + 1):
            total = total + taps[lag : lag + 1, :] * normed[steps + step - lag]
        first[step * agents : (step + 1) * agents, :] = total.astype(jnp.bfloat16).astype(first.dtype)


def feed_forward(rows, gain, w_in, w_out, hidden):
    inner = (rows * norm_scale(rows) * gain[...]).astype(jnp.bfloat16)
    tile = 512
    for start in range(0, w_in.shape[1], tile):
        hidden[:, start : start + tile] = gelu(dot(inner, w_in[:, start : start + tile])).astype(jnp.bfloat16)
    return (rows + dot(hidden[...], w_out[...])).astype(jnp.bfloat16)


def to_keys(second, gain, w_key, w_value, keyval):
    width = second.shape[1]
    values = second.astype(jnp.float32)
    attn_in = (values * norm_scale(values) * gain[...]).astype(jnp.bfloat16)
    keyval[:, :width] = dot(attn_in, w_key[...]).astype(jnp.bfloat16)
    keyval[:, width : 2 * width] = dot(attn_in, w_value[...]).astype(jnp.bfloat16)
    return attn_in


def conv_kernel(group, halo, partial, taps, gain, tail, *rest):
    steps, agents, width = halo.shape
    outs = rest[:steps]
    normed, first = rest[steps:]
    mixed_rows(halo, partial, taps, gain, normed, first)
    spot = lax.axis_index("agent")
    for k in range(steps):
        step = (spot // group) ^ away(k, steps, spot % group)
        outs[k][:, :width] = first[pl.ds(pl.multiple_of(step * agents, agents), agents), :].astype(jnp.bfloat16)
        outs[k][:, width:] = tail[...]


def conv(group, halo, partial, taps, gain, tail):
    steps, agents, width = halo.shape
    return pl.pallas_call(
        functools.partial(conv_kernel, group),
        out_shape=[jax.ShapeDtypeStruct((agents, width + tail.shape[1]), jnp.bfloat16)] * steps,
        in_specs=[VMEM] * 5,
        out_specs=[VMEM] * steps,
        scratch_shapes=[
            pltpu.VMEM((steps, agents, width), jnp.float32),
            pltpu.VMEM((steps * agents, width), jnp.float32),
        ],
        compiler_params=pltpu.CompilerParams(vmem_limit_bytes=8 * MIB),
        cost_estimate=cost(0),
        name="conv",
    )(halo, *[pinned(x) for x in (partial, taps, gain, tail)])


def front_kernel(group, halo, partial, taps, gain_first, gain_second, w_in, w_out, *rest):
    steps, agents, width = halo.shape
    outs = rest[:steps]
    normed, first, hidden, second = rest[steps:]
    mixed_rows(halo, partial, taps, gain_first, normed, first)
    result = feed_forward(first[...], gain_second, w_in, w_out, hidden)
    for step in range(steps):
        second[step] = result[step * agents : (step + 1) * agents]
    spot = lax.axis_index("agent")
    for k in range(steps):
        outs[k][...] = second[(spot // group) ^ away(k, steps, spot % group)]


def front(group, halo, partial, taps, gains, w_in, w_out):
    steps, agents, width = halo.shape
    rows = steps * agents
    return pl.pallas_call(
        functools.partial(front_kernel, group),
        out_shape=[jax.ShapeDtypeStruct((agents, width), jnp.bfloat16)] * steps,
        in_specs=[VMEM] * 7,
        out_specs=[VMEM] * steps,
        scratch_shapes=[
            pltpu.VMEM((steps, agents, width), jnp.float32),
            pltpu.VMEM((rows, width), jnp.float32),
            pltpu.VMEM((rows, w_in.shape[1]), jnp.bfloat16),
            pltpu.VMEM((steps, agents, width), jnp.bfloat16),
        ],
        compiler_params=pltpu.CompilerParams(vmem_limit_bytes=12 * MIB),
        cost_estimate=cost(0),
        name="front",
    )(halo, *[pinned(x) for x in (partial, taps, *gains, w_in, w_out)])


def feed_kernel(count, *refs):
    pieces = refs[:count]
    gain_second, gain_third, w_in, w_out, w_key, w_value, w_query = refs[count : count + 7]
    query, keyval, second, hidden = refs[count + 7 :]
    width = gain_second.shape[1]
    agents = pieces[0].shape[0]
    for k in range(count):
        keyval[agents * k : agents * (k + 1), 2 * width :] = pieces[k][:, width:]
    first = jnp.concatenate([piece[:, :width].astype(jnp.float32) for piece in pieces], axis=0)
    result = feed_forward(first, gain_second, w_in, w_out, hidden)
    second[...] = result
    attn_in = to_keys(result, gain_third, w_key, w_value, keyval)
    query[...] = dot(attn_in, w_query[...]).astype(jnp.bfloat16)


def feed(pieces, gains, weights):
    rows = sum(piece.shape[0] for piece in pieces)
    width = gains[0].shape[1]
    return pl.pallas_call(
        functools.partial(feed_kernel, len(pieces)),
        out_shape=[
            jax.ShapeDtypeStruct((rows, width), jnp.bfloat16),
            jax.ShapeDtypeStruct((rows, width + pieces[0].shape[1]), jnp.bfloat16),
            jax.ShapeDtypeStruct((rows, width), jnp.bfloat16),
        ],
        in_specs=[VMEM] * (len(pieces) + 7),
        out_specs=[VMEM] * 3,
        scratch_shapes=[pltpu.VMEM((rows, weights[0].shape[1]), jnp.bfloat16)],
        compiler_params=pltpu.CompilerParams(vmem_limit_bytes=12 * MIB),
        cost_estimate=cost(0),
        name="feed",
    )(*pieces, *[pinned(x) for x in (*gains, *weights)])


def project_kernel(count, *refs):
    pieces = refs[:count][::-1]
    gain, w_key, w_value, attn_in, keyval = refs[count:]
    second = jnp.concatenate([piece[...] for piece in pieces], axis=0)
    attn_in[...] = to_keys(second, gain, w_key, w_value, keyval)


def project(pieces, gain, weights):
    rows = sum(piece.shape[0] for piece in pieces)
    width = gain.shape[1]
    return pl.pallas_call(
        functools.partial(project_kernel, len(pieces)),
        out_shape=[
            jax.ShapeDtypeStruct((rows, width), jnp.bfloat16),
            jax.ShapeDtypeStruct((rows, 2 * width), jnp.bfloat16),
        ],
        in_specs=[VMEM] * (len(pieces) + 3),
        out_specs=[VMEM] * 2,
        compiler_params=pltpu.CompilerParams(vmem_limit_bytes=8 * MIB),
        cost_estimate=cost(25),
        name="project",
    )(*reversed(pieces), *[pinned(x) for x in (gain, *weights)])


def block_order(group, chunks):
    early = [(r, 0) for r in range(group)] + [(0, j) for j in range(1, chunks)]
    return early + [(r, j) for j in range(1, chunks) for r in range(1, group)]


def mask_kernel(steps, chunks, agents, group, width, *rest):
    blocks, bias = rest[:group], rest[group]
    now = (lax.axis_index("tm") * steps + lax.axis_index("agent") // group).astype(jnp.float32)
    lane = lax.broadcasted_iota(jnp.int32, (agents, 128), 1)
    sublane = lax.broadcasted_iota(jnp.int32, (agents, 128), 0)
    tiles = {}
    for r in range(group):
        for k in range(steps):
            tile = blocks[r][agents * k : agents * (k + 1), 2 * width :].astype(jnp.float32)
            tiles[k, r] = (tile[0:1] * RADIX + tile[1:2], tile[2:3])
    own = jnp.concatenate(
        [
            jnp.sum(jnp.where(lane == sublane + j * agents, tiles[k, 0][0], 0.0), axis=1, keepdims=True)
            for k in range(steps)
            for j in range(chunks)
        ],
        axis=0,
    )
    row_lane = lax.broadcasted_iota(jnp.int32, (1, 128), 1)
    per_tile = 128 // agents
    start = 0
    for r, j in block_order(group, chunks):
        for first in range(0, steps, per_tile):
            both = [None, None]
            for i in range(per_tile):
                for f in (0, 1):
                    moved = pltpu.roll(tiles[first + i, r][f], ((i - j) * agents) % 128, 1)
                    both[f] = moved if i == 0 else jnp.where(row_lane >= i * agents, moved, both[f])
            order, present = both
            alive = jnp.where(now < present, order, 1e9)
            visible = (alive < own) | (order == own)
            bias[:, start : start + 128] = jnp.where(visible, 0.0, -1e30)
            start += 128


def mask(blocks, steps, agents, width):
    rows, group = steps * agents * CHUNKS, len(blocks)
    return pl.pallas_call(
        functools.partial(mask_kernel, steps, CHUNKS, agents, group, width),
        out_shape=pltpu.VMEM((rows, rows * group), jnp.float32),
        in_specs=[VMEM] * group,
        out_specs=VMEM,
        compiler_params=pltpu.CompilerParams(vmem_limit_bytes=8 * MIB),
        cost_estimate=cost(0),
        name="mask",
    )(*blocks)


def rows_of(parts, ks, agents, columns):
    return jnp.concatenate([part[agents * k : agents * (k + 1), columns] for k in ks for part in parts], axis=0)


def run_pairs(pairs, lead, stages):
    held = [{} for _ in stages]
    for turn in range(pairs + lead * (len(stages) - 1)):
        for i, stage in enumerate(stages):
            pair = turn - lead * i
            if 0 <= pair < pairs:
                held[i][pair] = stage(pair, held[i - 1].pop(pair)) if i else stage(pair)


def pair_stages(queries_of, blocks, bias, top_of, low):
    width = blocks[0].shape[1] // 2 // 128 * 128

    def products(pair):
        queries = queries_of(pair)
        zeros = jnp.zeros_like(queries)
        stacked = jnp.concatenate([jnp.where(low, queries, zeros), jnp.where(low, zeros, queries)], axis=0)
        key = jnp.concatenate([block[:, 128 * pair : 128 * pair + 128] for block in blocks], axis=0)
        return dot_t(stacked, key)

    def weigh(pair, scores):
        rows = scores.shape[0] // 2
        tops, weights = [], []
        for half in range(2):
            here = scores[half * rows : (half + 1) * rows] * (LOG2E * HEAD ** (-0.5)) + bias
            highest = jnp.max(here, axis=1, keepdims=True)
            if top_of is not None:
                highest = jnp.maximum(highest, top_of(pair)[:, HEAD * half : HEAD * half + 1])
            tops.append(highest)
            weights.append(jnp.exp2(here - highest).astype(jnp.bfloat16))
        return tops, jnp.concatenate(weights, axis=0)

    def sums(pair, made):
        tops, weights = made
        start = width + 128 * pair
        value = jnp.concatenate([block[:, start : start + 128] for block in blocks], axis=0)
        return tops, dot(weights, jnp.concatenate([value, jnp.ones(value.shape, jnp.bfloat16)], axis=1))

    return [products, weigh, sums]


def merged(low, total):
    rows = total.shape[0] // 2
    return jnp.where(low, total[:rows], total[rows:])


def early_kernel(ks, chunks, count, *refs):
    (query, attn_in), (w_query, bias) = refs[:2], refs[2:4]
    blocks, (own_query, number, weight, top) = refs[4 : 4 + count], refs[4 + count :]
    own_query[...] = dot(attn_in[...], w_query[...]).astype(jnp.bfloat16)
    rows, width = number.shape
    agents = rows // (len(ks) * chunks)
    low = lax.broadcasted_iota(jnp.int32, (rows, 128), 1) < HEAD
    keys = sum(block.shape[0] for block in blocks)
    here = bias[ks[0] * agents * chunks : ks[0] * agents * chunks + rows, :keys]

    def columns(pair):
        return slice(128 * pair, 128 * pair + 128)

    def keep(pair, made):
        tops, total = made
        number[:, columns(pair)] = merged(low, total[:, :128])
        weight[:, columns(pair)] = merged(low, total[:, 128:])
        top[:, columns(pair)] = jnp.where(low, tops[0], tops[1])

    stages = pair_stages(lambda pair: rows_of((query, own_query), ks, agents, columns(pair)), blocks, here, None, low)
    run_pairs(width // 128, 1, [*stages, keep])


def early(ks, query, attn_in, w_query, bias, blocks):
    width = query.shape[1]
    rows = len(ks) * CHUNKS * query.shape[0] // 4
    state = pltpu.VMEM((rows, width), jnp.float32)
    return pl.pallas_call(
        functools.partial(early_kernel, ks, CHUNKS, len(blocks)),
        out_shape=[jax.ShapeDtypeStruct(query.shape, jnp.bfloat16), state, state, state],
        in_specs=[VMEM] * (4 + len(blocks)),
        out_specs=[VMEM] * 4,
        compiler_params=pltpu.CompilerParams(vmem_limit_bytes=16 * MIB),
        cost_estimate=cost(0),
        name="early",
    )(query, attn_in, pinned(w_query), pinned(bias), *blocks)


def attend_kernel(ks, chunks, count, begun, *refs):
    mine = 1 + len(ks) * (chunks - 1)
    queries, seconds, (w_output, bias) = refs[:chunks], refs[chunks : chunks + mine], refs[chunks + mine : chunks + mine + 2]
    rest = refs[chunks + mine + 2 :]
    blocks, state = rest[:count], rest[count : count + begun]
    outs, attended = rest[count + begun : count + begun + len(ks)], rest[count + begun + len(ks)]
    rows, width = attended.shape
    agents = rows // (len(ks) * chunks)
    low = lax.broadcasted_iota(jnp.int32, (rows, 128), 1) < HEAD
    keys = sum(block.shape[0] for block in blocks)
    here = bias[ks[0] * agents * chunks : ks[0] * agents * chunks + rows, bias.shape[1] - keys :]

    def columns(pair):
        return slice(128 * pair, 128 * pair + 128)

    def keep(pair, made):
        tops, total = made
        number, weight = merged(low, total[:, :128]), merged(low, total[:, 128:])
        if begun:
            shrink = jnp.exp2(state[2][:, columns(pair)] - jnp.where(low, tops[0], tops[1]))
            number = number + state[0][:, columns(pair)] * shrink
            weight = weight + state[1][:, columns(pair)] * shrink
        attended[:, columns(pair)] = (number / weight).astype(jnp.bfloat16)

    stages = pair_stages(
        lambda pair: rows_of(queries, ks, agents, columns(pair)),
        blocks,
        here,
        (lambda pair: state[2][:, columns(pair)]) if begun else None,
        low,
    )
    run_pairs(width // 128, width // 128 if begun else 1, [*stages, keep])
    residual = []
    for i, k in enumerate(ks):
        residual += [seconds[0][agents * k : agents * (k + 1)]]
        residual += [piece[...] for piece in seconds[1 + i * (chunks - 1) : 1 + (i + 1) * (chunks - 1)]]
    result = jnp.concatenate(residual, axis=0).astype(jnp.float32) + dot(attended[...], w_output[...])
    for i in range(len(ks)):
        outs[i][...] = result[i * agents * chunks : (i + 1) * agents * chunks].astype(jnp.bfloat16)


def attend(ks, queries, seconds, w_output, bias, blocks, state, agents, microseconds):
    width = queries[0].shape[1]
    piece = jax.ShapeDtypeStruct((agents, width), jnp.bfloat16)
    return pl.pallas_call(
        functools.partial(attend_kernel, ks, len(queries), len(blocks), len(state)),
        out_shape=[piece] * len(ks),
        in_specs=[VMEM] * (len(queries) + len(seconds) + 2 + len(blocks) + len(state)),
        out_specs=[VMEM] * len(ks),
        scratch_shapes=[pltpu.VMEM((len(ks) * agents, width), jnp.bfloat16)],
        compiler_params=pltpu.CompilerParams(vmem_limit_bytes=16 * MIB),
        cost_estimate=cost(microseconds),
        name="attend",
    )(*queries, *seconds, pinned(w_output), pinned(bias), *blocks, *[pinned(x) for x in state])


def put_back_kernel(steps, group, *refs):
    pieces, out, sem = refs[:steps][::-1], refs[steps], refs[steps + 1]
    spot = lax.axis_index("agent")
    half = pieces[0].shape[0] // 2
    copies = []
    for k in range(steps):
        target = out.at[(spot // group) ^ away(k, steps, spot % group)]
        for rows in (pl.ds(0, half), pl.ds(half, half)):
            copies.append(pltpu.make_async_copy(pieces[k].at[rows], target.at[rows], sem.at[len(copies)]))
    for copy in copies:
        copy.start()
    for copy in copies:
        copy.wait()


def put_back(group, pieces, shape):
    return pl.pallas_call(
        functools.partial(put_back_kernel, shape[0], group),
        out_shape=jax.ShapeDtypeStruct(shape, jnp.bfloat16),
        in_specs=[VMEM] * len(pieces),
        out_specs=ANY,
        scratch_shapes=[pltpu.SemaphoreType.DMA((2 * len(pieces),))],
        compiler_params=pltpu.CompilerParams(vmem_limit_bytes=4 * MIB),
        cost_estimate=cost(0),
        name="put_back",
    )(*pieces)


def after(x, *others):
    return lax.optimization_barrier((x, *others))[0]


def per_device(
    tokens,
    conv_taps,
    norm_first,
    norm_second,
    norm_third,
    w_in,
    w_out,
    w_query,
    w_key,
    w_value,
    w_output,
    agent_order,
    present_steps,
):
    steps, agents, width = tokens.shape
    tm_count, count = lax.axis_size("tm"), lax.axis_size("agent")
    group = count // steps
    part = agents // CHUNKS
    assert group * steps == count and steps == 4 and 128 % part == 0 and CHUNKS == 2 and group > 1

    def across(x, k):
        if k == steps - 1:
            return x
        pairs = [(i, ((i // group) ^ away(k, steps, i % group)) * group + i % group) for i in range(count)]
        return lax.ppermute(x, "agent", pairs)

    def within(x, r):
        return lax.ppermute(x, "agent", [(i, (i // group) * group + ((i % group) ^ r)) for i in range(count)])

    parts = split(tokens)
    *partials, tail, taps, gain_first, gain_second, gain_third = stage(
        parts,
        conv_taps,
        norm_first.reshape(1, width),
        agent_order.reshape(1, agents),
        present_steps.reshape(1, agents),
        [conv_taps] + [x.reshape(1, width) for x in (norm_first, norm_second, norm_third)],
    )
    halos = [
        lax.ppermute(x if j == 0 else after(x, tail), "tm", [(i, i + 1) for i in range(tm_count - 1)])
        for j, x in enumerate(parts)
    ]
    halos[0] = after(halos[0], tail)
    made = conv(group, halos[0], partials[0], taps, gain_first, tail)
    last = made[-1]
    pieces = [[across(made[k], k) for k in range(steps)]]
    for j in range(1, CHUNKS):
        halos[j] = after(halos[j], last)
        made = list(front(group, halos[j], partials[j], taps, (gain_first, gain_second), w_in, w_out))
        last = made[-1]
        made[steps - 2] = after(made[steps - 2], pieces[j - 1][0])
        pieces.append([across(made[k], k) for k in range(steps)])
    pieces[0][-1] = after(pieces[0][-1], last)
    query, keyval, second = feed(pieces[0], (gain_second, gain_third), (w_in, w_out, w_key, w_value, w_query))
    blocks = {(0, 0): keyval, **{(r, 0): within(keyval, r) for r in range(1, group)}}
    attn_in, keyval = project(pieces[1], gain_third, (w_key, w_value))
    keyval = after(keyval, *blocks.values())
    blocks.update({(0, 1): keyval, **{(r, 1): within(keyval, r) for r in range(1, group)}})
    bias = mask([blocks[r, 0] for r in range(group)], steps, part, width)
    blocks = [blocks[spot] for spot in block_order(group, CHUNKS)]
    ready = group + CHUNKS - 1
    far_ks, near_ks = (0, 1), (2, 3)
    own_query, *state = early(far_ks, query, attn_in, w_query, bias, blocks[:ready])

    def finish(ks, blocks, state, microseconds):
        seconds = [second] + [pieces[j][k] for k in ks for j in range(1, CHUNKS)]
        return attend(ks, (query, own_query), seconds, w_output, bias, blocks, state, agents, microseconds)

    results = [*finish(far_ks, blocks[ready:], state, 0), *finish(near_ks, blocks, [], 10)]
    return put_back(group, [across(results[k], k) for k in reversed(range(steps))], tokens.shape)


def solution(mesh):
    in_specs = (P("tm", "agent", None),) + (P(),) * 10 + (P("agent"), P("agent"))
    return jax.shard_map(
        per_device, mesh=mesh, in_specs=in_specs, out_specs=P("tm", "agent", None), check_vma=False
    )
```

```python
import functools

import jax
import jax.numpy as jnp
from jax import lax
from jax.experimental import pallas as pl
from jax.experimental.pallas import tpu as pltpu
from jax.sharding import PartitionSpec as P

HEAD = 64
CHUNKS = 2
RADIX = 32
EPS = 1e-05
LOG2E = 1.4426950408889634
MIB = 1024 * 1024
VMEM = pl.BlockSpec(memory_space=pltpu.VMEM)
ANY = pl.BlockSpec(memory_space=pl.ANY)
HBM = pl.BlockSpec(memory_space=pltpu.HBM)


def pinned(x):
    return pltpu.with_memory_space_constraint(x, pltpu.VMEM)


def far(x):
    return pltpu.with_memory_space_constraint(x, pltpu.HBM)


def cost(microseconds):
    return pl.CostEstimate(
        flops=int(1.1e9 * microseconds) + 10**6, bytes_accessed=int(3.5e6 * microseconds) + 10**4, transcendentals=0
    )


def away(k, steps, member):
    odd = member % 2
    return 0 if k == steps - 1 else (steps - 1 - k) * (1 - odd) + (k + 1) * odd


def dot(a, b):
    return jnp.dot(a, b, preferred_element_type=jnp.float32)


def dot_t(a, b):
    return lax.dot_general(a, b, (((1,), (1,)), ((), ())), preferred_element_type=jnp.float32)


def norm_scale(values):
    return lax.rsqrt(jnp.mean(values * values, axis=-1, keepdims=True) + EPS)


def gelu(x):
    return 0.5 * x * (1.0 + lax.erf(x * 0.7071067811865476))


def part_copies(tokens, part, target, sem):
    steps, agents = target.shape[:2]
    return [
        pltpu.make_async_copy(tokens.at[step, pl.ds(part * agents, agents)], target.at[step], sem.at[step])
        for step in range(steps)
    ]


def split_kernel(tokens, out, sem):
    copies = part_copies(tokens, 0, out, sem)
    for copy in copies:
        copy.start()
    for copy in copies:
        copy.wait()


def split(tokens):
    steps, agents, width = tokens.shape
    return pl.pallas_call(
        split_kernel,
        out_shape=pltpu.VMEM((steps, agents // CHUNKS, width), tokens.dtype),
        in_specs=[HBM],
        out_specs=VMEM,
        scratch_shapes=[pltpu.SemaphoreType.DMA((steps,))],
        compiler_params=pltpu.CompilerParams(vmem_limit_bytes=4 * MIB),
        cost_estimate=cost(30),
        name="split",
    )(far(tokens))


def stage_kernel(count, taps, gain, order, present, tokens, first_part, *rest):
    sources, rest = rest[:count], rest[count:]
    second_part, partials, tail, targets = rest[0], rest[1:3], rest[3], rest[4 : 4 + count]
    taps_here, gain_here, order_here, present_here, normed, facts, part_sem, sem = rest[4 + count :]
    pairs = [
        (taps, taps_here),
        (gain, gain_here),
        (order, order_here),
        (present, present_here),
        *zip(sources, targets),
    ]
    copies = [pltpu.make_async_copy(source, target, sem.at[i]) for i, (source, target) in enumerate(pairs)]
    later = part_copies(tokens, 1, second_part, part_sem)
    for copy in copies + later:
        copy.start()
    for copy in copies:
        copy.wait()
    agents = order.shape[1]
    facts[...] = jnp.zeros(facts.shape, jnp.float32)
    facts[0:1, :agents] = (order_here[...] // RADIX).astype(jnp.float32)
    facts[1:2, :agents] = (order_here[...] % RADIX).astype(jnp.float32)
    facts[2:3, :agents] = present_here[...].astype(jnp.float32)
    tail[...] = facts[...].astype(jnp.bfloat16)
    steps, reach = first_part.shape[0], taps.shape[0] - 1
    gains = gain_here[...]
    for j, part in enumerate((first_part, second_part)):
        for step in range(steps):
            if j == 1:
                later[step].wait()
            values = part[step].astype(jnp.float32)
            normed[step] = values * norm_scale(values) * gains
            total = values
            for lag in range(min(step, reach) + 1):
                total = total + taps_here[lag : lag + 1, :] * normed[step - lag]
            partials[j][step] = total


def stage(tokens, first_part, taps, gain, order, present, arrays):
    steps, part, width = first_part.shape
    inputs = (taps, gain, order, present)
    return pl.pallas_call(
        functools.partial(stage_kernel, len(arrays)),
        out_shape=[pltpu.VMEM(first_part.shape, first_part.dtype)]
        + [pltpu.VMEM((steps, part, width), jnp.float32)] * CHUNKS
        + [pltpu.VMEM((part, 128), jnp.bfloat16)]
        + [pltpu.VMEM(x.shape, x.dtype) for x in arrays],
        in_specs=[HBM] * (len(inputs) + 1) + [VMEM] + [HBM] * len(arrays),
        out_specs=[VMEM] * (CHUNKS + 2 + len(arrays)),
        scratch_shapes=[pltpu.VMEM(x.shape, x.dtype) for x in inputs]
        + [
            pltpu.VMEM((steps, part, width), jnp.float32),
            pltpu.VMEM((part, 128), jnp.float32),
            pltpu.SemaphoreType.DMA((steps,)),
            pltpu.SemaphoreType.DMA((len(inputs) + len(arrays),)),
        ],
        compiler_params=pltpu.CompilerParams(vmem_limit_bytes=8 * MIB),
        cost_estimate=cost(0),
        name="stage",
    )(*[far(x) for x in (*inputs, tokens)], pinned(first_part), *[far(x) for x in arrays])


def run_pairs(pairs, lead, stages):
    held = [{} for _ in stages]
    for turn in range(pairs + lead * (len(stages) - 1)):
        for i, stage in enumerate(stages):
            pair = turn - lead * i
            if 0 <= pair < pairs:
                held[i][pair] = stage(pair, held[i - 1].pop(pair)) if i else stage(pair)


def mixed_rows(halo, partial, taps, gain, normed, first):
    steps, agents = halo.shape[:2]
    reach = taps.shape[0] - 1
    gains = gain[...]
    for step in range(steps):
        values = halo[step].astype(jnp.float32)
        normed[step] = values * norm_scale(values) * gains
    for step in range(steps):
        total = partial[step]
        for lag in range(step + 1, reach + 1):
            total = total + taps[lag : lag + 1, :] * normed[steps + step - lag]
        first[step * agents : (step + 1) * agents, :] = total.astype(jnp.bfloat16).astype(first.dtype)


def feed_forward(rows, gain, w_in, w_out):
    inner = (rows * norm_scale(rows) * gain[...]).astype(jnp.bfloat16)
    tile, total = 512, [rows]

    def enter(i):
        return dot(inner, w_in[:, i * tile : (i + 1) * tile])

    def activate(i, products):
        return gelu(products).astype(jnp.bfloat16)

    def leave(i, hidden):
        total[0] = total[0] + dot(hidden, w_out[i * tile : (i + 1) * tile, :])

    run_pairs(w_in.shape[1] // tile, 1, [enter, activate, leave])
    return total[0].astype(jnp.bfloat16)


def to_keys(second, gain, w_key, w_value, keyval):
    width = second.shape[1]
    values = second.astype(jnp.float32)
    attn_in = (values * norm_scale(values) * gain[...]).astype(jnp.bfloat16)
    keyval[:, :width] = dot(attn_in, w_key[...]).astype(jnp.bfloat16)
    keyval[:, width : 2 * width] = dot(attn_in, w_value[...]).astype(jnp.bfloat16)
    return attn_in


def conv_kernel(group, halo, partial, taps, gain, tail, *rest):
    steps, agents, width = halo.shape
    outs = rest[:steps]
    normed, first = rest[steps:]
    mixed_rows(halo, partial, taps, gain, normed, first)
    spot = lax.axis_index("agent")
    for k in range(steps):
        step = (spot // group) ^ away(k, steps, spot % group)
        outs[k][:, :width] = first[pl.ds(pl.multiple_of(step * agents, agents), agents), :].astype(jnp.bfloat16)
        outs[k][:, width:] = tail[...]


def conv(group, halo, partial, taps, gain, tail):
    steps, agents, width = halo.shape
    return pl.pallas_call(
        functools.partial(conv_kernel, group),
        out_shape=[jax.ShapeDtypeStruct((agents, width + tail.shape[1]), jnp.bfloat16)] * steps,
        in_specs=[VMEM] * 5,
        out_specs=[VMEM] * steps,
        scratch_shapes=[
            pltpu.VMEM((steps, agents, width), jnp.float32),
            pltpu.VMEM((steps * agents, width), jnp.float32),
        ],
        compiler_params=pltpu.CompilerParams(vmem_limit_bytes=8 * MIB),
        cost_estimate=cost(0),
        name="conv",
    )(halo, *[pinned(x) for x in (partial, taps, gain, tail)])


def front_kernel(group, halo, partial, taps, gain_first, gain_second, w_in, w_out, *rest):
    steps, agents, width = halo.shape
    outs = rest[:steps]
    normed, first, second = rest[steps:]
    mixed_rows(halo, partial, taps, gain_first, normed, first)
    result = feed_forward(first[...], gain_second, w_in, w_out)
    for step in range(steps):
        second[step] = result[step * agents : (step + 1) * agents]
    spot = lax.axis_index("agent")
    for k in range(steps):
        outs[k][...] = second[(spot // group) ^ away(k, steps, spot % group)]


def front(group, halo, partial, taps, gains, w_in, w_out):
    steps, agents, width = halo.shape
    rows = steps * agents
    return pl.pallas_call(
        functools.partial(front_kernel, group),
        out_shape=[jax.ShapeDtypeStruct((agents, width), jnp.bfloat16)] * steps,
        in_specs=[VMEM] * 7,
        out_specs=[VMEM] * steps,
        scratch_shapes=[
            pltpu.VMEM((steps, agents, width), jnp.float32),
            pltpu.VMEM((rows, width), jnp.float32),
            pltpu.VMEM((steps, agents, width), jnp.bfloat16),
        ],
        compiler_params=pltpu.CompilerParams(vmem_limit_bytes=12 * MIB),
        cost_estimate=cost(0),
        name="front",
    )(halo, *[pinned(x) for x in (partial, taps, *gains, w_in, w_out)])


def feed_kernel(count, *refs):
    pieces = refs[:count]
    gain_second, gain_third, w_in, w_out, w_key, w_value, w_query = refs[count : count + 7]
    query, keyval, second = refs[count + 7 :]
    width = gain_second.shape[1]
    agents = pieces[0].shape[0]
    for k in range(count):
        keyval[agents * k : agents * (k + 1), 2 * width :] = pieces[k][:, width:]
    first = jnp.concatenate([piece[:, :width].astype(jnp.float32) for piece in pieces], axis=0)
    result = feed_forward(first, gain_second, w_in, w_out)
    second[...] = result
    attn_in = to_keys(result, gain_third, w_key, w_value, keyval)
    query[...] = dot(attn_in, w_query[...]).astype(jnp.bfloat16)


def feed(pieces, gains, weights):
    rows = sum(piece.shape[0] for piece in pieces)
    width = gains[0].shape[1]
    return pl.pallas_call(
        functools.partial(feed_kernel, len(pieces)),
        out_shape=[
            jax.ShapeDtypeStruct((rows, width), jnp.bfloat16),
            jax.ShapeDtypeStruct((rows, width + pieces[0].shape[1]), jnp.bfloat16),
            jax.ShapeDtypeStruct((rows, width), jnp.bfloat16),
        ],
        in_specs=[VMEM] * (len(pieces) + 7),
        out_specs=[VMEM] * 3,
        compiler_params=pltpu.CompilerParams(vmem_limit_bytes=12 * MIB),
        cost_estimate=cost(0),
        name="feed",
    )(*pieces, *[pinned(x) for x in (*gains, *weights)])


def project_kernel(count, *refs):
    pieces = refs[:count][::-1]
    gain, w_key, w_value, attn_in, keyval = refs[count:]
    second = jnp.concatenate([piece[...] for piece in pieces], axis=0)
    attn_in[...] = to_keys(second, gain, w_key, w_value, keyval)


def project(pieces, gain, weights):
    rows = sum(piece.shape[0] for piece in pieces)
    width = gain.shape[1]
    return pl.pallas_call(
        functools.partial(project_kernel, len(pieces)),
        out_shape=[
            jax.ShapeDtypeStruct((rows, width), jnp.bfloat16),
            jax.ShapeDtypeStruct((rows, 2 * width), jnp.bfloat16),
        ],
        in_specs=[VMEM] * (len(pieces) + 3),
        out_specs=[VMEM] * 2,
        compiler_params=pltpu.CompilerParams(vmem_limit_bytes=8 * MIB),
        cost_estimate=cost(25),
        name="project",
    )(*reversed(pieces), *[pinned(x) for x in (gain, *weights)])


def block_order(group, chunks):
    early = [(r, 0) for r in range(group)] + [(0, j) for j in range(1, chunks)]
    return early + [(r, j) for j in range(1, chunks) for r in range(1, group)]


def mask_kernel(steps, chunks, agents, group, width, *rest):
    blocks, bias = rest[:group], rest[group]
    now = (lax.axis_index("tm") * steps + lax.axis_index("agent") // group).astype(jnp.float32)
    lane = lax.broadcasted_iota(jnp.int32, (agents, 128), 1)
    sublane = lax.broadcasted_iota(jnp.int32, (agents, 128), 0)
    tiles = {}
    for r in range(group):
        for k in range(steps):
            tile = blocks[r][agents * k : agents * (k + 1), 2 * width :].astype(jnp.float32)
            tiles[k, r] = (tile[0:1] * RADIX + tile[1:2], tile[2:3])
    own = jnp.concatenate(
        [
            jnp.sum(jnp.where(lane == sublane + j * agents, tiles[k, 0][0], 0.0), axis=1, keepdims=True)
            for k in range(steps)
            for j in range(chunks)
        ],
        axis=0,
    )
    row_lane = lax.broadcasted_iota(jnp.int32, (1, 128), 1)
    per_tile = 128 // agents
    start = 0
    for r, j in block_order(group, chunks):
        for first in range(0, steps, per_tile):
            both = [None, None]
            for i in range(per_tile):
                for f in (0, 1):
                    moved = pltpu.roll(tiles[first + i, r][f], ((i - j) * agents) % 128, 1)
                    both[f] = moved if i == 0 else jnp.where(row_lane >= i * agents, moved, both[f])
            order, present = both
            alive = jnp.where(now < present, order, 1e9)
            visible = (alive < own) | (order == own)
            bias[:, start : start + 128] = jnp.where(visible, 0.0, -1e30)
            start += 128


def mask(blocks, steps, agents, width):
    rows, group = steps * agents * CHUNKS, len(blocks)
    return pl.pallas_call(
        functools.partial(mask_kernel, steps, CHUNKS, agents, group, width),
        out_shape=pltpu.VMEM((rows, rows * group), jnp.float32),
        in_specs=[VMEM] * group,
        out_specs=VMEM,
        compiler_params=pltpu.CompilerParams(vmem_limit_bytes=8 * MIB),
        cost_estimate=cost(0),
        name="mask",
    )(*blocks)


def rows_of(parts, ks, agents, columns):
    return jnp.concatenate([part[agents * k : agents * (k + 1), columns] for k in ks for part in parts], axis=0)


def pair_stages(queries_of, blocks, bias, top_of, low):
    width = blocks[0].shape[1] // 2 // 128 * 128

    def products(pair):
        queries = queries_of(pair)
        zeros = jnp.zeros_like(queries)
        stacked = jnp.concatenate([jnp.where(low, queries, zeros), jnp.where(low, zeros, queries)], axis=0)
        key = jnp.concatenate([block[:, 128 * pair : 128 * pair + 128] for block in blocks], axis=0)
        return dot_t(stacked, key)

    def weigh(pair, scores):
        rows = scores.shape[0] // 2
        tops, weights = [], []
        for half in range(2):
            here = scores[half * rows : (half + 1) * rows] * (LOG2E * HEAD ** (-0.5)) + bias
            highest = jnp.max(here, axis=1, keepdims=True)
            if top_of is not None:
                highest = jnp.maximum(highest, top_of(pair)[:, HEAD * half : HEAD * half + 1])
            tops.append(highest)
            weights.append(jnp.exp2(here - highest).astype(jnp.bfloat16))
        return tops, jnp.concatenate(weights, axis=0)

    def sums(pair, made):
        tops, weights = made
        start = width + 128 * pair
        value = jnp.concatenate([block[:, start : start + 128] for block in blocks], axis=0)
        return tops, dot(weights, jnp.concatenate([value, jnp.ones(value.shape, jnp.bfloat16)], axis=1))

    return [products, weigh, sums]


def merged(low, total):
    rows = total.shape[0] // 2
    return jnp.where(low, total[:rows], total[rows:])


def early_kernel(ks, chunks, count, *refs):
    (query, attn_in), (w_query, bias) = refs[:2], refs[2:4]
    blocks, (own_query, number, weight, top) = refs[4 : 4 + count], refs[4 + count :]
    own_query[...] = dot(attn_in[...], w_query[...]).astype(jnp.bfloat16)
    rows, width = number.shape
    agents = rows // (len(ks) * chunks)
    low = lax.broadcasted_iota(jnp.int32, (rows, 128), 1) < HEAD
    keys = sum(block.shape[0] for block in blocks)
    here = bias[ks[0] * agents * chunks : ks[0] * agents * chunks + rows, :keys]

    def columns(pair):
        return slice(128 * pair, 128 * pair + 128)

    def keep(pair, made):
        tops, total = made
        number[:, columns(pair)] = merged(low, total[:, :128])
        weight[:, columns(pair)] = merged(low, total[:, 128:])
        top[:, columns(pair)] = jnp.where(low, tops[0], tops[1])

    stages = pair_stages(lambda pair: rows_of((query, own_query), ks, agents, columns(pair)), blocks, here, None, low)
    run_pairs(width // 128, 1, [*stages, keep])


def early(ks, query, attn_in, w_query, bias, blocks):
    width = query.shape[1]
    rows = len(ks) * CHUNKS * query.shape[0] // 4
    state = pltpu.VMEM((rows, width), jnp.float32)
    return pl.pallas_call(
        functools.partial(early_kernel, ks, CHUNKS, len(blocks)),
        out_shape=[jax.ShapeDtypeStruct(query.shape, jnp.bfloat16), state, state, state],
        in_specs=[VMEM] * (4 + len(blocks)),
        out_specs=[VMEM] * 4,
        compiler_params=pltpu.CompilerParams(vmem_limit_bytes=16 * MIB),
        cost_estimate=cost(0),
        name="early",
    )(query, attn_in, pinned(w_query), pinned(bias), *blocks)


def attend_kernel(ks, chunks, count, begun, skipped, *refs):
    mine = 1 + len(ks) * (chunks - 1)
    queries, seconds, (w_output, bias) = refs[:chunks], refs[chunks : chunks + mine], refs[chunks + mine : chunks + mine + 2]
    rest = refs[chunks + mine + 2 :]
    blocks, state = rest[:count], rest[count : count + begun]
    outs, attended = rest[count + begun : count + begun + len(ks)], rest[count + begun + len(ks)]
    rows, width = attended.shape
    agents = rows // (len(ks) * chunks)
    low = lax.broadcasted_iota(jnp.int32, (rows, 128), 1) < HEAD
    keys = sum(block.shape[0] for block in blocks)
    here = bias[ks[0] * agents * chunks : ks[0] * agents * chunks + rows, bias.shape[1] - keys :]
    begun_rows = slice(skipped, skipped + rows)

    def columns(pair):
        return slice(128 * pair, 128 * pair + 128)

    def keep(pair, made):
        tops, total = made
        number, weight = merged(low, total[:, :128]), merged(low, total[:, 128:])
        if begun:
            shrink = jnp.exp2(state[2][begun_rows, columns(pair)] - jnp.where(low, tops[0], tops[1]))
            number = number + state[0][begun_rows, columns(pair)] * shrink
            weight = weight + state[1][begun_rows, columns(pair)] * shrink
        attended[:, columns(pair)] = (number / weight).astype(jnp.bfloat16)

    stages = pair_stages(
        lambda pair: rows_of(queries, ks, agents, columns(pair)),
        blocks,
        here,
        (lambda pair: state[2][begun_rows, columns(pair)]) if begun else None,
        low,
    )
    run_pairs(width // 128, width // 128 if begun else 1, [*stages, keep])
    residual = []
    for i, k in enumerate(ks):
        residual += [seconds[0][agents * k : agents * (k + 1)]]
        residual += [piece[...] for piece in seconds[1 + i * (chunks - 1) : 1 + (i + 1) * (chunks - 1)]]
    result = jnp.concatenate(residual, axis=0).astype(jnp.float32) + dot(attended[...], w_output[...])
    for i in range(len(ks)):
        outs[i][...] = result[i * agents * chunks : (i + 1) * agents * chunks].astype(jnp.bfloat16)


def attend(ks, queries, seconds, w_output, bias, blocks, state, skipped, agents, microseconds):
    width = queries[0].shape[1]
    piece = jax.ShapeDtypeStruct((agents, width), jnp.bfloat16)
    return pl.pallas_call(
        functools.partial(attend_kernel, ks, len(queries), len(blocks), len(state), skipped),
        out_shape=[piece] * len(ks),
        in_specs=[VMEM] * (len(queries) + len(seconds) + 2 + len(blocks) + len(state)),
        out_specs=[VMEM] * len(ks),
        scratch_shapes=[pltpu.VMEM((len(ks) * agents, width), jnp.bfloat16)],
        compiler_params=pltpu.CompilerParams(vmem_limit_bytes=16 * MIB),
        cost_estimate=cost(microseconds),
        name="attend",
    )(*queries, *seconds, pinned(w_output), pinned(bias), *blocks, *[pinned(x) for x in state])


def put_back_kernel(steps, group, *refs):
    pieces, out, sem = refs[:steps][::-1], refs[steps], refs[steps + 1]
    spot = lax.axis_index("agent")
    half = pieces[0].shape[0] // 2
    copies = []
    for k in range(steps):
        target = out.at[(spot // group) ^ away(k, steps, spot % group)]
        for rows in (pl.ds(0, half), pl.ds(half, half)):
            copies.append(pltpu.make_async_copy(pieces[k].at[rows], target.at[rows], sem.at[len(copies)]))
    for copy in copies:
        copy.start()
    for copy in copies:
        copy.wait()


def put_back(group, pieces, shape):
    return pl.pallas_call(
        functools.partial(put_back_kernel, shape[0], group),
        out_shape=jax.ShapeDtypeStruct(shape, jnp.bfloat16),
        in_specs=[VMEM] * len(pieces),
        out_specs=ANY,
        scratch_shapes=[pltpu.SemaphoreType.DMA((2 * len(pieces),))],
        compiler_params=pltpu.CompilerParams(vmem_limit_bytes=4 * MIB),
        cost_estimate=cost(0),
        name="put_back",
    )(*pieces)


def after(x, *others):
    return lax.optimization_barrier((x, *others))[0]


def per_device(
    tokens,
    conv_taps,
    norm_first,
    norm_second,
    norm_third,
    w_in,
    w_out,
    w_query,
    w_key,
    w_value,
    w_output,
    agent_order,
    present_steps,
):
    steps, agents, width = tokens.shape
    tm_count, count = lax.axis_size("tm"), lax.axis_size("agent")
    group = count // steps
    part = agents // CHUNKS
    assert group * steps == count and steps == 4 and 128 % part == 0 and CHUNKS == 2 and group > 1

    def across(x, k):
        if k == steps - 1:
            return x
        pairs = [(i, ((i // group) ^ away(k, steps, i % group)) * group + i % group) for i in range(count)]
        return lax.ppermute(x, "agent", pairs)

    def within(x, r):
        return lax.ppermute(x, "agent", [(i, (i // group) * group + ((i % group) ^ r)) for i in range(count)])

    first_part = split(tokens)
    second_part, *partials, tail, taps, gain_first, gain_second, gain_third = stage(
        tokens,
        first_part,
        conv_taps,
        norm_first.reshape(1, width),
        agent_order.reshape(1, agents),
        present_steps.reshape(1, agents),
        [conv_taps] + [x.reshape(1, width) for x in (norm_first, norm_second, norm_third)],
    )
    halos = [lax.ppermute(x, "tm", [(i, i + 1) for i in range(tm_count - 1)]) for x in (first_part, second_part)]
    halos[0] = after(halos[0], tail)
    made = conv(group, halos[0], partials[0], taps, gain_first, tail)
    last = made[-1]
    pieces = [[across(made[k], k) for k in range(steps)]]
    for j in range(1, CHUNKS):
        halos[j] = after(halos[j], last)
        made = list(front(group, halos[j], partials[j], taps, (gain_first, gain_second), w_in, w_out))
        last = made[-1]
        made[steps - 2] = after(made[steps - 2], pieces[j - 1][0])
        pieces.append([across(made[k], k) for k in range(steps)])
    pieces[0][-1] = after(pieces[0][-1], last)
    query, keyval, second = feed(pieces[0], (gain_second, gain_third), (w_in, w_out, w_key, w_value, w_query))
    blocks = {(0, 0): keyval, **{(r, 0): within(keyval, r) for r in range(1, group)}}
    attn_in, keyval = project(pieces[1], gain_third, (w_key, w_value))
    keyval = after(keyval, *blocks.values())
    blocks.update({(0, 1): keyval, **{(r, 1): within(keyval, r) for r in range(1, group)}})
    bias = mask([blocks[r, 0] for r in range(group)], steps, part, width)
    blocks = [blocks[spot] for spot in block_order(group, CHUNKS)]
    ready = group + CHUNKS - 1
    far_ks, near_ks = (0, 1), (2, 3)
    own_query, *state = early(far_ks, query, attn_in, w_query, bias, blocks[:ready])

    def finish(ks, blocks, state, skipped, microseconds):
        seconds = [second] + [pieces[j][k] for k in ks for j in range(1, CHUNKS)]
        return attend(
            ks, (query, own_query), seconds, w_output, bias, blocks, state, skipped, agents, microseconds
        )

    late = blocks[ready:]
    results = [finish((k,), late, state, k * agents, 0)[0] for k in far_ks] + list(finish(near_ks, blocks, [], 0, 10))
    return put_back(group, [across(results[k], k) for k in reversed(range(steps))], tokens.shape)


def solution(mesh):
    in_specs = (P("tm", "agent", None),) + (P(),) * 10 + (P("agent"), P("agent"))
    return jax.shard_map(
        per_device, mesh=mesh, in_specs=in_specs, out_specs=P("tm", "agent", None), check_vma=False
    )
```

```python
import functools

import jax
import jax.numpy as jnp
from jax import lax
from jax.experimental import pallas as pl
from jax.experimental.pallas import tpu as pltpu
from jax.sharding import PartitionSpec as P

HEAD = 64
CHUNKS = 2
RADIX = 32
EPS = 1e-05
LOG2E = 1.4426950408889634
MIB = 1024 * 1024
VMEM = pl.BlockSpec(memory_space=pltpu.VMEM)
ANY = pl.BlockSpec(memory_space=pl.ANY)
HBM = pl.BlockSpec(memory_space=pltpu.HBM)


def pinned(x):
    return pltpu.with_memory_space_constraint(x, pltpu.VMEM)


def far(x):
    return pltpu.with_memory_space_constraint(x, pltpu.HBM)


def cost(microseconds):
    return pl.CostEstimate(
        flops=int(1.1e9 * microseconds) + 10**6, bytes_accessed=int(3.5e6 * microseconds) + 10**4, transcendentals=0
    )


def away(k, steps, member):
    odd = member % 2
    even_order, odd_order = (2, 3, 1), (2, 1, 3)
    return 0 if k == steps - 1 else even_order[k] * (1 - odd) + odd_order[k] * odd


def dot(a, b):
    return jnp.dot(a, b, preferred_element_type=jnp.float32)


def dot_t(a, b):
    return lax.dot_general(a, b, (((1,), (1,)), ((), ())), preferred_element_type=jnp.float32)


def norm_scale(values):
    return lax.rsqrt(jnp.mean(values * values, axis=-1, keepdims=True) + EPS)


def gelu(x):
    return 0.5 * x * (1.0 + lax.erf(x * 0.7071067811865476))


def part_copies(tokens, part, target, sem):
    steps, agents = target.shape[:2]
    return [
        pltpu.make_async_copy(tokens.at[step, pl.ds(part * agents, agents)], target.at[step], sem.at[step])
        for step in range(steps)
    ]


def split_kernel(tokens, out, sem):
    copies = part_copies(tokens, 0, out, sem)
    for copy in copies:
        copy.start()
    for copy in copies:
        copy.wait()


def split(tokens):
    steps, agents, width = tokens.shape
    return pl.pallas_call(
        split_kernel,
        out_shape=pltpu.VMEM((steps, agents // CHUNKS, width), tokens.dtype),
        in_specs=[HBM],
        out_specs=VMEM,
        scratch_shapes=[pltpu.SemaphoreType.DMA((steps,))],
        compiler_params=pltpu.CompilerParams(vmem_limit_bytes=4 * MIB),
        cost_estimate=cost(30),
        name="split",
    )(far(tokens))


def stage_kernel(count, taps, gain, order, present, tokens, first_part, *rest):
    sources, rest = rest[:count], rest[count:]
    second_part, partials, tail, targets = rest[0], rest[1:3], rest[3], rest[4 : 4 + count]
    taps_here, gain_here, order_here, present_here, normed, facts, part_sem, sem = rest[4 + count :]
    pairs = [
        (taps, taps_here),
        (gain, gain_here),
        (order, order_here),
        (present, present_here),
        *zip(sources, targets),
    ]
    copies = [pltpu.make_async_copy(source, target, sem.at[i]) for i, (source, target) in enumerate(pairs)]
    later = part_copies(tokens, 1, second_part, part_sem)
    for copy in copies + later:
        copy.start()
    for copy in copies:
        copy.wait()
    agents = order.shape[1]
    facts[...] = jnp.zeros(facts.shape, jnp.float32)
    facts[0:1, :agents] = (order_here[...] // RADIX).astype(jnp.float32)
    facts[1:2, :agents] = (order_here[...] % RADIX).astype(jnp.float32)
    facts[2:3, :agents] = present_here[...].astype(jnp.float32)
    tail[...] = facts[...].astype(jnp.bfloat16)
    steps, reach = first_part.shape[0], taps.shape[0] - 1
    gains = gain_here[...]
    for j, part in enumerate((first_part, second_part)):
        for step in range(steps):
            if j == 1:
                later[step].wait()
            values = part[step].astype(jnp.float32)
            normed[step] = values * norm_scale(values) * gains
            total = values
            for lag in range(min(step, reach) + 1):
                total = total + taps_here[lag : lag + 1, :] * normed[step - lag]
            partials[j][step] = total


def stage(tokens, first_part, taps, gain, order, present, arrays):
    steps, part, width = first_part.shape
    inputs = (taps, gain, order, present)
    return pl.pallas_call(
        functools.partial(stage_kernel, len(arrays)),
        out_shape=[pltpu.VMEM(first_part.shape, first_part.dtype)]
        + [pltpu.VMEM((steps, part, width), jnp.float32)] * CHUNKS
        + [pltpu.VMEM((part, 128), jnp.bfloat16)]
        + [pltpu.VMEM(x.shape, x.dtype) for x in arrays],
        in_specs=[HBM] * (len(inputs) + 1) + [VMEM] + [HBM] * len(arrays),
        out_specs=[VMEM] * (CHUNKS + 2 + len(arrays)),
        scratch_shapes=[pltpu.VMEM(x.shape, x.dtype) for x in inputs]
        + [
            pltpu.VMEM((steps, part, width), jnp.float32),
            pltpu.VMEM((part, 128), jnp.float32),
            pltpu.SemaphoreType.DMA((steps,)),
            pltpu.SemaphoreType.DMA((len(inputs) + len(arrays),)),
        ],
        compiler_params=pltpu.CompilerParams(vmem_limit_bytes=8 * MIB),
        cost_estimate=cost(0),
        name="stage",
    )(*[far(x) for x in (*inputs, tokens)], pinned(first_part), *[far(x) for x in arrays])


def run_pairs(pairs, lead, stages):
    held = [{} for _ in stages]
    for turn in range(pairs + lead * (len(stages) - 1)):
        for i, stage in enumerate(stages):
            pair = turn - lead * i
            if 0 <= pair < pairs:
                held[i][pair] = stage(pair, held[i - 1].pop(pair)) if i else stage(pair)


def mixed_rows(halo, partial, taps, gain, normed, first):
    steps, agents = halo.shape[:2]
    reach = taps.shape[0] - 1
    gains = gain[...]
    for step in range(steps):
        values = halo[step].astype(jnp.float32)
        normed[step] = values * norm_scale(values) * gains
    for step in range(steps):
        total = partial[step]
        for lag in range(step + 1, reach + 1):
            total = total + taps[lag : lag + 1, :] * normed[steps + step - lag]
        first[step * agents : (step + 1) * agents, :] = total.astype(jnp.bfloat16).astype(first.dtype)


def feed_forward(rows, gain, w_in, w_out):
    inner = (rows * norm_scale(rows) * gain[...]).astype(jnp.bfloat16)
    tile, total = 512, [rows]

    def enter(i):
        return dot(inner, w_in[:, i * tile : (i + 1) * tile])

    def activate(i, products):
        return gelu(products).astype(jnp.bfloat16)

    def leave(i, hidden):
        total[0] = total[0] + dot(hidden, w_out[i * tile : (i + 1) * tile, :])

    run_pairs(w_in.shape[1] // tile, 1, [enter, activate, leave])
    return total[0].astype(jnp.bfloat16)


def to_keys(second, gain, w_key, w_value, keyval):
    width = second.shape[1]
    values = second.astype(jnp.float32)
    attn_in = (values * norm_scale(values) * gain[...]).astype(jnp.bfloat16)
    keyval[:, :width] = dot(attn_in, w_key[...]).astype(jnp.bfloat16)
    keyval[:, width : 2 * width] = dot(attn_in, w_value[...]).astype(jnp.bfloat16)
    return attn_in


def conv_kernel(group, halo, partial, taps, gain, tail, *rest):
    steps, agents, width = halo.shape
    outs = rest[:steps]
    normed, first = rest[steps:]
    mixed_rows(halo, partial, taps, gain, normed, first)
    spot = lax.axis_index("agent")
    for k in range(steps):
        step = (spot // group) ^ away(k, steps, spot % group)
        outs[k][:, :width] = first[pl.ds(pl.multiple_of(step * agents, agents), agents), :].astype(jnp.bfloat16)
        outs[k][:, width:] = tail[...]


def conv(group, halo, partial, taps, gain, tail):
    steps, agents, width = halo.shape
    return pl.pallas_call(
        functools.partial(conv_kernel, group),
        out_shape=[jax.ShapeDtypeStruct((agents, width + tail.shape[1]), jnp.bfloat16)] * steps,
        in_specs=[VMEM] * 5,
        out_specs=[VMEM] * steps,
        scratch_shapes=[
            pltpu.VMEM((steps, agents, width), jnp.float32),
            pltpu.VMEM((steps * agents, width), jnp.float32),
        ],
        compiler_params=pltpu.CompilerParams(vmem_limit_bytes=8 * MIB),
        cost_estimate=cost(0),
        name="conv",
    )(halo, *[pinned(x) for x in (partial, taps, gain, tail)])


def front_kernel(group, halo, partial, taps, gain_first, gain_second, w_in, w_out, *rest):
    steps, agents, width = halo.shape
    outs = rest[:steps]
    normed, first, second = rest[steps:]
    mixed_rows(halo, partial, taps, gain_first, normed, first)
    result = feed_forward(first[...], gain_second, w_in, w_out)
    for step in range(steps):
        second[step] = result[step * agents : (step + 1) * agents]
    spot = lax.axis_index("agent")
    for k in range(steps):
        outs[k][...] = second[(spot // group) ^ away(k, steps, spot % group)]


def front(group, halo, partial, taps, gains, w_in, w_out):
    steps, agents, width = halo.shape
    rows = steps * agents
    return pl.pallas_call(
        functools.partial(front_kernel, group),
        out_shape=[jax.ShapeDtypeStruct((agents, width), jnp.bfloat16)] * steps,
        in_specs=[VMEM] * 7,
        out_specs=[VMEM] * steps,
        scratch_shapes=[
            pltpu.VMEM((steps, agents, width), jnp.float32),
            pltpu.VMEM((rows, width), jnp.float32),
            pltpu.VMEM((steps, agents, width), jnp.bfloat16),
        ],
        compiler_params=pltpu.CompilerParams(vmem_limit_bytes=12 * MIB),
        cost_estimate=cost(0),
        name="front",
    )(halo, *[pinned(x) for x in (partial, taps, *gains, w_in, w_out)])


def feed_kernel(count, *refs):
    pieces = refs[:count]
    gain_second, gain_third, w_in, w_out, w_key, w_value, w_query = refs[count : count + 7]
    query, keyval, second = refs[count + 7 :]
    width = gain_second.shape[1]
    agents = pieces[0].shape[0]
    for k in range(count):
        keyval[agents * k : agents * (k + 1), 2 * width :] = pieces[k][:, width:]
    first = jnp.concatenate([piece[:, :width].astype(jnp.float32) for piece in pieces], axis=0)
    result = feed_forward(first, gain_second, w_in, w_out)
    second[...] = result
    attn_in = to_keys(result, gain_third, w_key, w_value, keyval)
    query[...] = dot(attn_in, w_query[...]).astype(jnp.bfloat16)


def feed(pieces, gains, weights):
    rows = sum(piece.shape[0] for piece in pieces)
    width = gains[0].shape[1]
    return pl.pallas_call(
        functools.partial(feed_kernel, len(pieces)),
        out_shape=[
            jax.ShapeDtypeStruct((rows, width), jnp.bfloat16),
            jax.ShapeDtypeStruct((rows, width + pieces[0].shape[1]), jnp.bfloat16),
            jax.ShapeDtypeStruct((rows, width), jnp.bfloat16),
        ],
        in_specs=[VMEM] * (len(pieces) + 7),
        out_specs=[VMEM] * 3,
        compiler_params=pltpu.CompilerParams(vmem_limit_bytes=12 * MIB),
        cost_estimate=cost(0),
        name="feed",
    )(*pieces, *[pinned(x) for x in (*gains, *weights)])


def project_kernel(count, *refs):
    pieces = refs[:count][::-1]
    gain, w_key, w_value, attn_in, keyval = refs[count:]
    second = jnp.concatenate([piece[...] for piece in pieces], axis=0)
    attn_in[...] = to_keys(second, gain, w_key, w_value, keyval)


def project(pieces, gain, weights):
    rows = sum(piece.shape[0] for piece in pieces)
    width = gain.shape[1]
    return pl.pallas_call(
        functools.partial(project_kernel, len(pieces)),
        out_shape=[
            jax.ShapeDtypeStruct((rows, width), jnp.bfloat16),
            jax.ShapeDtypeStruct((rows, 2 * width), jnp.bfloat16),
        ],
        in_specs=[VMEM] * (len(pieces) + 3),
        out_specs=[VMEM] * 2,
        compiler_params=pltpu.CompilerParams(vmem_limit_bytes=8 * MIB),
        cost_estimate=cost(25),
        name="project",
    )(*reversed(pieces), *[pinned(x) for x in (gain, *weights)])


def block_order(group, chunks):
    early = [(r, 0) for r in range(group)] + [(0, j) for j in range(1, chunks)]
    return early + [(r, j) for j in range(1, chunks) for r in range(1, group)]


def write_mask(steps, chunks, agents, width, blocks, bias):
    group = len(blocks)
    now = (lax.axis_index("tm") * steps + lax.axis_index("agent") // group).astype(jnp.float32)
    lane = lax.broadcasted_iota(jnp.int32, (agents, 128), 1)
    sublane = lax.broadcasted_iota(jnp.int32, (agents, 128), 0)
    tiles = {}
    for r in range(group):
        for k in range(steps):
            tile = blocks[r][agents * k : agents * (k + 1), 2 * width :].astype(jnp.float32)
            tiles[k, r] = (tile[0:1] * RADIX + tile[1:2], tile[2:3])
    own = jnp.concatenate(
        [
            jnp.sum(jnp.where(lane == sublane + j * agents, tiles[k, 0][0], 0.0), axis=1, keepdims=True)
            for k in range(steps)
            for j in range(chunks)
        ],
        axis=0,
    )
    row_lane = lax.broadcasted_iota(jnp.int32, (1, 128), 1)
    per_tile = 128 // agents
    start = 0
    for r, j in block_order(group, chunks):
        for first in range(0, steps, per_tile):
            both = [None, None]
            for i in range(per_tile):
                for f in (0, 1):
                    moved = pltpu.roll(tiles[first + i, r][f], ((i - j) * agents) % 128, 1)
                    both[f] = moved if i == 0 else jnp.where(row_lane >= i * agents, moved, both[f])
            order, present = both
            alive = jnp.where(now < present, order, 1e9)
            visible = (alive < own) | (order == own)
            bias[:, start : start + 128] = jnp.where(visible, 0.0, -1e30)
            start += 128


def rows_of(parts, ks, agents, columns):
    return jnp.concatenate([part[agents * k : agents * (k + 1), columns] for k in ks for part in parts], axis=0)


def pair_stages(queries_of, blocks, bias, top_of, low):
    width = blocks[0].shape[1] // 2 // 128 * 128

    def products(pair):
        queries = queries_of(pair)
        zeros = jnp.zeros_like(queries)
        stacked = jnp.concatenate([jnp.where(low, queries, zeros), jnp.where(low, zeros, queries)], axis=0)
        key = jnp.concatenate([block[:, 128 * pair : 128 * pair + 128] for block in blocks], axis=0)
        return dot_t(stacked, key)

    def weigh(pair, scores):
        rows = scores.shape[0] // 2
        tops, weights = [], []
        for half in range(2):
            here = scores[half * rows : (half + 1) * rows] * (LOG2E * HEAD ** (-0.5)) + bias
            highest = jnp.max(here, axis=1, keepdims=True)
            if top_of is not None:
                highest = jnp.maximum(highest, top_of(pair)[:, HEAD * half : HEAD * half + 1])
            tops.append(highest)
            weights.append(jnp.exp2(here - highest).astype(jnp.bfloat16))
        return tops, jnp.concatenate(weights, axis=0)

    def sums(pair, made):
        tops, weights = made
        start = width + 128 * pair
        value = jnp.concatenate([block[:, start : start + 128] for block in blocks], axis=0)
        return tops, dot(weights, jnp.concatenate([value, jnp.ones(value.shape, jnp.bfloat16)], axis=1))

    return [products, weigh, sums]


def merged(low, total):
    rows = total.shape[0] // 2
    return jnp.where(low, total[:rows], total[rows:])


def early_kernel(ks, steps, chunks, group, query, attn_in, w_query, *refs):
    count = group + chunks - 1
    blocks, (own_query, bias, number, weight, top) = refs[:count], refs[count:]
    own_query[...] = dot(attn_in[...], w_query[...]).astype(jnp.bfloat16)
    rows, width = number.shape
    write_mask(steps, chunks, query.shape[0] // steps, width, blocks[:group], bias)
    agents = rows // (len(ks) * chunks)
    low = lax.broadcasted_iota(jnp.int32, (rows, 128), 1) < HEAD
    keys = sum(block.shape[0] for block in blocks)
    here = bias[ks[0] * agents * chunks : ks[0] * agents * chunks + rows, :keys]

    def columns(pair):
        return slice(128 * pair, 128 * pair + 128)

    def keep(pair, made):
        tops, total = made
        number[:, columns(pair)] = merged(low, total[:, :128])
        weight[:, columns(pair)] = merged(low, total[:, 128:])
        top[:, columns(pair)] = jnp.where(low, tops[0], tops[1])

    stages = pair_stages(lambda pair: rows_of((query, own_query), ks, agents, columns(pair)), blocks, here, None, low)
    run_pairs(width // 128, 1, [*stages, keep])


def early(ks, steps, group, query, attn_in, w_query, blocks):
    count, width = query.shape
    rows = count * CHUNKS
    state = pltpu.VMEM((len(ks) * rows // steps, width), jnp.float32)
    return pl.pallas_call(
        functools.partial(early_kernel, ks, steps, CHUNKS, group),
        out_shape=[jax.ShapeDtypeStruct(query.shape, jnp.bfloat16), pltpu.VMEM((rows, rows * group), jnp.float32)]
        + [state] * 3,
        in_specs=[VMEM] * (3 + len(blocks)),
        out_specs=[VMEM] * 5,
        compiler_params=pltpu.CompilerParams(vmem_limit_bytes=16 * MIB),
        cost_estimate=cost(0),
        name="early",
    )(query, attn_in, pinned(w_query), *blocks)


def attend_kernel(ks, chunks, count, begun, skipped, *refs):
    mine = 1 + len(ks) * (chunks - 1)
    queries, seconds, (w_output, bias) = refs[:chunks], refs[chunks : chunks + mine], refs[chunks + mine : chunks + mine + 2]
    rest = refs[chunks + mine + 2 :]
    blocks, state = rest[:count], rest[count : count + begun]
    outs, attended = rest[count + begun : count + begun + len(ks)], rest[count + begun + len(ks)]
    rows, width = attended.shape
    agents = rows // (len(ks) * chunks)
    low = lax.broadcasted_iota(jnp.int32, (rows, 128), 1) < HEAD
    keys = sum(block.shape[0] for block in blocks)
    here = bias[ks[0] * agents * chunks : ks[0] * agents * chunks + rows, bias.shape[1] - keys :]
    begun_rows = slice(skipped, skipped + rows)

    def columns(pair):
        return slice(128 * pair, 128 * pair + 128)

    def keep(pair, made):
        tops, total = made
        number, weight = merged(low, total[:, :128]), merged(low, total[:, 128:])
        if begun:
            shrink = jnp.exp2(state[2][begun_rows, columns(pair)] - jnp.where(low, tops[0], tops[1]))
            number = number + state[0][begun_rows, columns(pair)] * shrink
            weight = weight + state[1][begun_rows, columns(pair)] * shrink
        attended[:, columns(pair)] = (number / weight).astype(jnp.bfloat16)

    stages = pair_stages(
        lambda pair: rows_of(queries, ks, agents, columns(pair)),
        blocks,
        here,
        (lambda pair: state[2][begun_rows, columns(pair)]) if begun else None,
        low,
    )
    run_pairs(width // 128, width // 128 if begun else 1, [*stages, keep])
    residual = []
    for i, k in enumerate(ks):
        residual += [seconds[0][agents * k : agents * (k + 1)]]
        residual += [piece[...] for piece in seconds[1 + i * (chunks - 1) : 1 + (i + 1) * (chunks - 1)]]
    result = jnp.concatenate(residual, axis=0).astype(jnp.float32) + dot(attended[...], w_output[...])
    for i in range(len(ks)):
        outs[i][...] = result[i * agents * chunks : (i + 1) * agents * chunks].astype(jnp.bfloat16)


def attend(ks, queries, seconds, w_output, bias, blocks, state, skipped, agents, microseconds):
    width = queries[0].shape[1]
    piece = jax.ShapeDtypeStruct((agents, width), jnp.bfloat16)
    return pl.pallas_call(
        functools.partial(attend_kernel, ks, len(queries), len(blocks), len(state), skipped),
        out_shape=[piece] * len(ks),
        in_specs=[VMEM] * (len(queries) + len(seconds) + 2 + len(blocks) + len(state)),
        out_specs=[VMEM] * len(ks),
        scratch_shapes=[pltpu.VMEM((len(ks) * agents, width), jnp.bfloat16)],
        compiler_params=pltpu.CompilerParams(vmem_limit_bytes=16 * MIB),
        cost_estimate=cost(microseconds),
        name="attend",
    )(*queries, *seconds, pinned(w_output), pinned(bias), *blocks, *[pinned(x) for x in state])


def put_back_kernel(steps, group, *refs):
    pieces, out, sem = refs[:steps][::-1], refs[steps], refs[steps + 1]
    spot = lax.axis_index("agent")
    half = pieces[0].shape[0] // 2
    copies = []
    for k in range(steps):
        target = out.at[(spot // group) ^ away(k, steps, spot % group)]
        for rows in (pl.ds(0, half), pl.ds(half, half)):
            copies.append(pltpu.make_async_copy(pieces[k].at[rows], target.at[rows], sem.at[len(copies)]))
    for copy in copies:
        copy.start()
    for copy in copies:
        copy.wait()


def put_back(group, pieces, shape):
    return pl.pallas_call(
        functools.partial(put_back_kernel, shape[0], group),
        out_shape=jax.ShapeDtypeStruct(shape, jnp.bfloat16),
        in_specs=[VMEM] * len(pieces),
        out_specs=ANY,
        scratch_shapes=[pltpu.SemaphoreType.DMA((2 * len(pieces),))],
        compiler_params=pltpu.CompilerParams(vmem_limit_bytes=4 * MIB),
        cost_estimate=cost(0),
        name="put_back",
    )(*pieces)


def after(x, *others):
    return lax.optimization_barrier((x, *others))[0]


def per_device(
    tokens,
    conv_taps,
    norm_first,
    norm_second,
    norm_third,
    w_in,
    w_out,
    w_query,
    w_key,
    w_value,
    w_output,
    agent_order,
    present_steps,
):
    steps, agents, width = tokens.shape
    tm_count, count = lax.axis_size("tm"), lax.axis_size("agent")
    group = count // steps
    part = agents // CHUNKS
    assert group * steps == count and steps == 4 and 128 % part == 0 and CHUNKS == 2 and group > 1

    def across(x, k):
        if k == steps - 1:
            return x
        pairs = [(i, ((i // group) ^ away(k, steps, i % group)) * group + i % group) for i in range(count)]
        return lax.ppermute(x, "agent", pairs)

    def within(x, r):
        return lax.ppermute(x, "agent", [(i, (i // group) * group + ((i % group) ^ r)) for i in range(count)])

    first_part = split(tokens)
    second_part, *partials, tail, taps, gain_first, gain_second, gain_third = stage(
        tokens,
        first_part,
        conv_taps,
        norm_first.reshape(1, width),
        agent_order.reshape(1, agents),
        present_steps.reshape(1, agents),
        [conv_taps] + [x.reshape(1, width) for x in (norm_first, norm_second, norm_third)],
    )
    halos = [lax.ppermute(x, "tm", [(i, i + 1) for i in range(tm_count - 1)]) for x in (first_part, second_part)]
    halos[0] = after(halos[0], tail)
    made = conv(group, halos[0], partials[0], taps, gain_first, tail)
    last = made[-1]
    pieces = [[across(made[k], k) for k in range(steps)]]
    for j in range(1, CHUNKS):
        halos[j] = after(halos[j], last)
        made = list(front(group, halos[j], partials[j], taps, (gain_first, gain_second), w_in, w_out))
        last = made[-1]
        made[steps - 2] = after(made[steps - 2], pieces[j - 1][0])
        pieces.append([across(made[k], k) for k in range(steps)])
    pieces[0][-1] = after(pieces[0][-1], last)
    query, keyval, second = feed(pieces[0], (gain_second, gain_third), (w_in, w_out, w_key, w_value, w_query))
    blocks = {(0, 0): keyval, **{(r, 0): within(keyval, r) for r in range(1, group)}}
    attn_in, keyval = project(pieces[1], gain_third, (w_key, w_value))
    keyval = after(keyval, *blocks.values())
    blocks.update({(0, 1): keyval, **{(r, 1): within(keyval, r) for r in range(1, group)}})
    blocks = [blocks[spot] for spot in block_order(group, CHUNKS)]
    ready = group + CHUNKS - 1
    far_ks, near_ks = (0, 1), (2, 3)
    own_query, bias, *state = early(far_ks, steps, group, query, attn_in, w_query, blocks[:ready])

    def finish(ks, blocks, state, skipped, microseconds):
        seconds = [second] + [pieces[j][k] for k in ks for j in range(1, CHUNKS)]
        return attend(
            ks, (query, own_query), seconds, w_output, bias, blocks, state, skipped, agents, microseconds
        )

    late = blocks[ready:]
    results = [*finish(far_ks, late, state, 0, 0), *finish(near_ks, blocks, [], 0, 10)]
    return put_back(group, [across(results[k], k) for k in reversed(range(steps))], tokens.shape)


def solution(mesh):
    in_specs = (P("tm", "agent", None),) + (P(),) * 10 + (P("agent"), P("agent"))
    return jax.shard_map(
        per_device, mesh=mesh, in_specs=in_specs, out_specs=P("tm", "agent", None), check_vma=False
    )
```

```python
import functools

import jax
import jax.numpy as jnp
from jax import lax
from jax.experimental import pallas as pl
from jax.experimental.pallas import tpu as pltpu
from jax.sharding import PartitionSpec as P

HEAD = 64
CHUNKS = 2
RADIX = 32
EPS = 1e-05
LOG2E = 1.4426950408889634
MIB = 1024 * 1024
VMEM = pl.BlockSpec(memory_space=pltpu.VMEM)
ANY = pl.BlockSpec(memory_space=pl.ANY)
HBM = pl.BlockSpec(memory_space=pltpu.HBM)


def pinned(x):
    return pltpu.with_memory_space_constraint(x, pltpu.VMEM)


def far(x):
    return pltpu.with_memory_space_constraint(x, pltpu.HBM)


def cost(microseconds):
    return pl.CostEstimate(
        flops=int(1.1e9 * microseconds) + 10**6, bytes_accessed=int(3.5e6 * microseconds) + 10**4, transcendentals=0
    )


def away(k, steps, member):
    odd = member % 2
    even_order, odd_order = (2, 3, 1), (2, 1, 3)
    return 0 if k == steps - 1 else even_order[k] * (1 - odd) + odd_order[k] * odd


def dot(a, b):
    return jnp.dot(a, b, preferred_element_type=jnp.float32)


def dot_t(a, b):
    return lax.dot_general(a, b, (((1,), (1,)), ((), ())), preferred_element_type=jnp.float32)


def norm_scale(values):
    return lax.rsqrt(jnp.mean(values * values, axis=-1, keepdims=True) + EPS)


def gelu(x):
    return 0.5 * x * (1.0 + lax.erf(x * 0.7071067811865476))


def part_copies(tokens, part, target, sem):
    steps, agents = target.shape[:2]
    return [
        pltpu.make_async_copy(tokens.at[step, pl.ds(part * agents, agents)], target.at[step], sem.at[step])
        for step in range(steps)
    ]


def split_kernel(tokens, out, sem):
    copies = part_copies(tokens, 0, out, sem)
    for copy in copies:
        copy.start()
    for copy in copies:
        copy.wait()


def split(tokens):
    steps, agents, width = tokens.shape
    return pl.pallas_call(
        split_kernel,
        out_shape=pltpu.VMEM((steps, agents // CHUNKS, width), tokens.dtype),
        in_specs=[HBM],
        out_specs=VMEM,
        scratch_shapes=[pltpu.SemaphoreType.DMA((steps,))],
        compiler_params=pltpu.CompilerParams(vmem_limit_bytes=4 * MIB),
        cost_estimate=cost(30),
        name="split",
    )(far(tokens))


def stage_kernel(count, taps, gain, order, present, tokens, first_part, *rest):
    sources, rest = rest[:count], rest[count:]
    second_part, partials, tail, targets = rest[0], rest[1:3], rest[3], rest[4 : 4 + count]
    taps_here, gain_here, order_here, present_here, normed, facts, part_sem, sem = rest[4 + count :]
    pairs = [
        (taps, taps_here),
        (gain, gain_here),
        (order, order_here),
        (present, present_here),
        *zip(sources, targets),
    ]
    copies = [pltpu.make_async_copy(source, target, sem.at[i]) for i, (source, target) in enumerate(pairs)]
    later = part_copies(tokens, 1, second_part, part_sem)
    for copy in copies + later:
        copy.start()
    for copy in copies:
        copy.wait()
    agents = order.shape[1]
    facts[...] = jnp.zeros(facts.shape, jnp.float32)
    facts[0:1, :agents] = (order_here[...] // RADIX).astype(jnp.float32)
    facts[1:2, :agents] = (order_here[...] % RADIX).astype(jnp.float32)
    facts[2:3, :agents] = present_here[...].astype(jnp.float32)
    tail[...] = facts[...].astype(jnp.bfloat16)
    steps, reach = first_part.shape[0], taps.shape[0] - 1
    gains = gain_here[...]
    for j, part in enumerate((first_part, second_part)):
        for step in range(steps):
            if j == 1:
                later[step].wait()
            values = part[step].astype(jnp.float32)
            normed[step] = values * norm_scale(values) * gains
            total = values
            for lag in range(min(step, reach) + 1):
                total = total + taps_here[lag : lag + 1, :] * normed[step - lag]
            partials[j][step] = total


def stage(tokens, first_part, taps, gain, order, present, arrays):
    steps, part, width = first_part.shape
    inputs = (taps, gain, order, present)
    return pl.pallas_call(
        functools.partial(stage_kernel, len(arrays)),
        out_shape=[pltpu.VMEM(first_part.shape, first_part.dtype)]
        + [pltpu.VMEM((steps, part, width), jnp.float32)] * CHUNKS
        + [pltpu.VMEM((part, 128), jnp.bfloat16)]
        + [pltpu.VMEM(x.shape, x.dtype) for x in arrays],
        in_specs=[HBM] * (len(inputs) + 1) + [VMEM] + [HBM] * len(arrays),
        out_specs=[VMEM] * (CHUNKS + 2 + len(arrays)),
        scratch_shapes=[pltpu.VMEM(x.shape, x.dtype) for x in inputs]
        + [
            pltpu.VMEM((steps, part, width), jnp.float32),
            pltpu.VMEM((part, 128), jnp.float32),
            pltpu.SemaphoreType.DMA((steps,)),
            pltpu.SemaphoreType.DMA((len(inputs) + len(arrays),)),
        ],
        compiler_params=pltpu.CompilerParams(vmem_limit_bytes=8 * MIB),
        cost_estimate=cost(0),
        name="stage",
    )(*[far(x) for x in (*inputs, tokens)], pinned(first_part), *[far(x) for x in arrays])


def run_pairs(pairs, lead, stages):
    held = [{} for _ in stages]
    for turn in range(pairs + lead * (len(stages) - 1)):
        for i, stage in enumerate(stages):
            pair = turn - lead * i
            if 0 <= pair < pairs:
                held[i][pair] = stage(pair, held[i - 1].pop(pair)) if i else stage(pair)


def mixed_rows(halo, partial, taps, gain, normed, first):
    steps, agents = halo.shape[:2]
    reach = taps.shape[0] - 1
    gains = gain[...] * (lax.axis_index("tm") > 0).astype(jnp.float32)
    for step in range(steps):
        values = halo[step].astype(jnp.float32)
        normed[step] = values * norm_scale(values) * gains
    for step in range(steps):
        total = partial[step]
        for lag in range(step + 1, reach + 1):
            total = total + taps[lag : lag + 1, :] * normed[steps + step - lag]
        first[step * agents : (step + 1) * agents, :] = total.astype(jnp.bfloat16).astype(first.dtype)


def feed_forward(rows, gain, w_in, w_out):
    inner = (rows * norm_scale(rows) * gain[...]).astype(jnp.bfloat16)
    tile, total = 512, [rows]

    def enter(i):
        return dot(inner, w_in[:, i * tile : (i + 1) * tile])

    def activate(i, products):
        return gelu(products).astype(jnp.bfloat16)

    def leave(i, hidden):
        total[0] = total[0] + dot(hidden, w_out[i * tile : (i + 1) * tile, :])

    run_pairs(w_in.shape[1] // tile, 1, [enter, activate, leave])
    return total[0].astype(jnp.bfloat16)


def to_keys(second, gain, w_key, w_value, keyval):
    width = second.shape[1]
    values = second.astype(jnp.float32)
    attn_in = (values * norm_scale(values) * gain[...]).astype(jnp.bfloat16)
    keyval[:, :width] = dot(attn_in, w_key[...]).astype(jnp.bfloat16)
    keyval[:, width : 2 * width] = dot(attn_in, w_value[...]).astype(jnp.bfloat16)
    return attn_in


def conv_kernel(group, halo, partial, taps, gain, tail, *rest):
    steps, agents, width = halo.shape
    outs = rest[:steps]
    normed, first = rest[steps:]
    mixed_rows(halo, partial, taps, gain, normed, first)
    spot = lax.axis_index("agent")
    for k in range(steps):
        step = (spot // group) ^ away(k, steps, spot % group)
        outs[k][:, :width] = first[pl.ds(pl.multiple_of(step * agents, agents), agents), :].astype(jnp.bfloat16)
        outs[k][:, width:] = tail[...]


def conv(group, halo, partial, taps, gain, tail):
    steps, agents, width = halo.shape
    return pl.pallas_call(
        functools.partial(conv_kernel, group),
        out_shape=[jax.ShapeDtypeStruct((agents, width + tail.shape[1]), jnp.bfloat16)] * steps,
        in_specs=[VMEM] * 5,
        out_specs=[VMEM] * steps,
        scratch_shapes=[
            pltpu.VMEM((steps, agents, width), jnp.float32),
            pltpu.VMEM((steps * agents, width), jnp.float32),
        ],
        compiler_params=pltpu.CompilerParams(vmem_limit_bytes=8 * MIB),
        cost_estimate=cost(0),
        name="conv",
    )(halo, *[pinned(x) for x in (partial, taps, gain, tail)])


def front_kernel(group, halo, partial, taps, gain_first, gain_second, w_in, w_out, *rest):
    steps, agents, width = halo.shape
    outs = rest[:steps]
    normed, first, second = rest[steps:]
    mixed_rows(halo, partial, taps, gain_first, normed, first)
    result = feed_forward(first[...], gain_second, w_in, w_out)
    for step in range(steps):
        second[step] = result[step * agents : (step + 1) * agents]
    spot = lax.axis_index("agent")
    for k in range(steps):
        outs[k][...] = second[(spot // group) ^ away(k, steps, spot % group)]


def front(group, halo, partial, taps, gains, w_in, w_out):
    steps, agents, width = halo.shape
    rows = steps * agents
    return pl.pallas_call(
        functools.partial(front_kernel, group),
        out_shape=[jax.ShapeDtypeStruct((agents, width), jnp.bfloat16)] * steps,
        in_specs=[VMEM] * 7,
        out_specs=[VMEM] * steps,
        scratch_shapes=[
            pltpu.VMEM((steps, agents, width), jnp.float32),
            pltpu.VMEM((rows, width), jnp.float32),
            pltpu.VMEM((steps, agents, width), jnp.bfloat16),
        ],
        compiler_params=pltpu.CompilerParams(vmem_limit_bytes=12 * MIB),
        cost_estimate=cost(0),
        name="front",
    )(halo, *[pinned(x) for x in (partial, taps, *gains, w_in, w_out)])


def feed_kernel(count, *refs):
    pieces = refs[:count]
    gain_second, gain_third, w_in, w_out, w_key, w_value, w_query = refs[count : count + 7]
    query, keyval, second = refs[count + 7 :]
    width = gain_second.shape[1]
    agents = pieces[0].shape[0]
    for k in range(count):
        keyval[agents * k : agents * (k + 1), 2 * width :] = pieces[k][:, width:]
    first = jnp.concatenate([piece[:, :width].astype(jnp.float32) for piece in pieces], axis=0)
    result = feed_forward(first, gain_second, w_in, w_out)
    second[...] = result
    attn_in = to_keys(result, gain_third, w_key, w_value, keyval)
    query[...] = dot(attn_in, w_query[...]).astype(jnp.bfloat16)


def feed(pieces, gains, weights):
    rows = sum(piece.shape[0] for piece in pieces)
    width = gains[0].shape[1]
    return pl.pallas_call(
        functools.partial(feed_kernel, len(pieces)),
        out_shape=[
            jax.ShapeDtypeStruct((rows, width), jnp.bfloat16),
            jax.ShapeDtypeStruct((rows, width + pieces[0].shape[1]), jnp.bfloat16),
            jax.ShapeDtypeStruct((rows, width), jnp.bfloat16),
        ],
        in_specs=[VMEM] * (len(pieces) + 7),
        out_specs=[VMEM] * 3,
        compiler_params=pltpu.CompilerParams(vmem_limit_bytes=12 * MIB),
        cost_estimate=cost(0),
        name="feed",
    )(*pieces, *[pinned(x) for x in (*gains, *weights)])


def project_kernel(count, *refs):
    pieces = refs[:count][::-1]
    gain, w_key, w_value, attn_in, keyval = refs[count:]
    second = jnp.concatenate([piece[...] for piece in pieces], axis=0)
    attn_in[...] = to_keys(second, gain, w_key, w_value, keyval)


def project(pieces, gain, weights):
    rows = sum(piece.shape[0] for piece in pieces)
    width = gain.shape[1]
    return pl.pallas_call(
        functools.partial(project_kernel, len(pieces)),
        out_shape=[
            jax.ShapeDtypeStruct((rows, width), jnp.bfloat16),
            jax.ShapeDtypeStruct((rows, 2 * width), jnp.bfloat16),
        ],
        in_specs=[VMEM] * (len(pieces) + 3),
        out_specs=[VMEM] * 2,
        compiler_params=pltpu.CompilerParams(vmem_limit_bytes=8 * MIB),
        cost_estimate=cost(25),
        name="project",
    )(*reversed(pieces), *[pinned(x) for x in (gain, *weights)])


def block_order(group, chunks):
    early = [(r, 0) for r in range(group)] + [(0, j) for j in range(1, chunks)]
    return early + [(r, j) for j in range(1, chunks) for r in range(1, group)]


def write_mask(steps, chunks, agents, width, blocks, bias):
    group = len(blocks)
    now = (lax.axis_index("tm") * steps + lax.axis_index("agent") // group).astype(jnp.float32)
    lane = lax.broadcasted_iota(jnp.int32, (agents, 128), 1)
    sublane = lax.broadcasted_iota(jnp.int32, (agents, 128), 0)
    tiles = {}
    for r in range(group):
        for k in range(steps):
            tile = blocks[r][agents * k : agents * (k + 1), 2 * width :].astype(jnp.float32)
            tiles[k, r] = (tile[0:1] * RADIX + tile[1:2], tile[2:3])
    own = jnp.concatenate(
        [
            jnp.sum(jnp.where(lane == sublane + j * agents, tiles[k, 0][0], 0.0), axis=1, keepdims=True)
            for k in range(steps)
            for j in range(chunks)
        ],
        axis=0,
    )
    row_lane = lax.broadcasted_iota(jnp.int32, (1, 128), 1)
    per_tile = 128 // agents
    start = 0
    for r, j in block_order(group, chunks):
        for first in range(0, steps, per_tile):
            both = [None, None]
            for i in range(per_tile):
                for f in (0, 1):
                    moved = pltpu.roll(tiles[first + i, r][f], ((i - j) * agents) % 128, 1)
                    both[f] = moved if i == 0 else jnp.where(row_lane >= i * agents, moved, both[f])
            order, present = both
            alive = jnp.where(now < present, order, 1e9)
            visible = (alive < own) | (order == own)
            bias[:, start : start + 128] = jnp.where(visible, 0.0, -1e30)
            start += 128


def rows_of(parts, ks, agents, columns):
    return jnp.concatenate([part[agents * k : agents * (k + 1), columns] for k in ks for part in parts], axis=0)


def pair_stages(queries_of, blocks, bias, top_of, low):
    width = blocks[0].shape[1] // 2 // 128 * 128

    def products(pair):
        queries = queries_of(pair)
        zeros = jnp.zeros_like(queries)
        stacked = jnp.concatenate([jnp.where(low, queries, zeros), jnp.where(low, zeros, queries)], axis=0)
        key = jnp.concatenate([block[:, 128 * pair : 128 * pair + 128] for block in blocks], axis=0)
        return dot_t(stacked, key)

    def weigh(pair, scores):
        rows = scores.shape[0] // 2
        tops, weights = [], []
        for half in range(2):
            here = scores[half * rows : (half + 1) * rows] * (LOG2E * HEAD ** (-0.5)) + bias
            highest = jnp.max(here, axis=1, keepdims=True)
            if top_of is not None:
                highest = jnp.maximum(highest, top_of(pair)[:, HEAD * half : HEAD * half + 1])
            tops.append(highest)
            weights.append(jnp.exp2(here - highest).astype(jnp.bfloat16))
        return tops, jnp.concatenate(weights, axis=0)

    def sums(pair, made):
        tops, weights = made
        start = width + 128 * pair
        value = jnp.concatenate([block[:, start : start + 128] for block in blocks], axis=0)
        return tops, dot(weights, jnp.concatenate([value, jnp.ones(value.shape, jnp.bfloat16)], axis=1))

    return [products, weigh, sums]


def merged(low, total):
    rows = total.shape[0] // 2
    return jnp.where(low, total[:rows], total[rows:])


def early_kernel(ks, steps, chunks, group, query, attn_in, w_query, *refs):
    count = group + chunks - 1
    blocks, (own_query, bias, number, weight, top) = refs[:count], refs[count:]
    own_query[...] = dot(attn_in[...], w_query[...]).astype(jnp.bfloat16)
    rows, width = number.shape
    write_mask(steps, chunks, query.shape[0] // steps, width, blocks[:group], bias)
    agents = rows // (len(ks) * chunks)
    low = lax.broadcasted_iota(jnp.int32, (rows, 128), 1) < HEAD
    keys = sum(block.shape[0] for block in blocks)
    here = bias[ks[0] * agents * chunks : ks[0] * agents * chunks + rows, :keys]

    def columns(pair):
        return slice(128 * pair, 128 * pair + 128)

    def keep(pair, made):
        tops, total = made
        number[:, columns(pair)] = merged(low, total[:, :128])
        weight[:, columns(pair)] = merged(low, total[:, 128:])
        top[:, columns(pair)] = jnp.where(low, tops[0], tops[1])

    stages = pair_stages(lambda pair: rows_of((query, own_query), ks, agents, columns(pair)), blocks, here, None, low)
    run_pairs(width // 128, 1, [*stages, keep])


def early(ks, steps, group, query, attn_in, w_query, blocks):
    count, width = query.shape
    rows = count * CHUNKS
    state = pltpu.VMEM((len(ks) * rows // steps, width), jnp.float32)
    return pl.pallas_call(
        functools.partial(early_kernel, ks, steps, CHUNKS, group),
        out_shape=[jax.ShapeDtypeStruct(query.shape, jnp.bfloat16), pltpu.VMEM((rows, rows * group), jnp.float32)]
        + [state] * 3,
        in_specs=[VMEM] * (3 + len(blocks)),
        out_specs=[VMEM] * 5,
        compiler_params=pltpu.CompilerParams(vmem_limit_bytes=16 * MIB),
        cost_estimate=cost(0),
        name="early",
    )(query, attn_in, pinned(w_query), *blocks)


def attend_kernel(ks, chunks, count, begun, skipped, *refs):
    mine = 1 + len(ks) * (chunks - 1)
    queries, seconds, (w_output, bias) = refs[:chunks], refs[chunks : chunks + mine], refs[chunks + mine : chunks + mine + 2]
    rest = refs[chunks + mine + 2 :]
    blocks, state = rest[:count], rest[count : count + begun]
    outs, attended = rest[count + begun : count + begun + len(ks)], rest[count + begun + len(ks)]
    rows, width = attended.shape
    agents = rows // (len(ks) * chunks)
    low = lax.broadcasted_iota(jnp.int32, (rows, 128), 1) < HEAD
    keys = sum(block.shape[0] for block in blocks)
    here = bias[ks[0] * agents * chunks : ks[0] * agents * chunks + rows, bias.shape[1] - keys :]
    begun_rows = slice(skipped, skipped + rows)

    def columns(pair):
        return slice(128 * pair, 128 * pair + 128)

    def keep(pair, made):
        tops, total = made
        number, weight = merged(low, total[:, :128]), merged(low, total[:, 128:])
        if begun:
            shrink = jnp.exp2(state[2][begun_rows, columns(pair)] - jnp.where(low, tops[0], tops[1]))
            number = number + state[0][begun_rows, columns(pair)] * shrink
            weight = weight + state[1][begun_rows, columns(pair)] * shrink
        attended[:, columns(pair)] = (number / weight).astype(jnp.bfloat16)

    stages = pair_stages(
        lambda pair: rows_of(queries, ks, agents, columns(pair)),
        blocks,
        here,
        (lambda pair: state[2][begun_rows, columns(pair)]) if begun else None,
        low,
    )
    run_pairs(width // 128, width // 128 if begun else 1, [*stages, keep])
    residual = []
    for i, k in enumerate(ks):
        residual += [seconds[0][agents * k : agents * (k + 1)]]
        residual += [piece[...] for piece in seconds[1 + i * (chunks - 1) : 1 + (i + 1) * (chunks - 1)]]
    result = jnp.concatenate(residual, axis=0).astype(jnp.float32) + dot(attended[...], w_output[...])
    for i in range(len(ks)):
        outs[i][...] = result[i * agents * chunks : (i + 1) * agents * chunks].astype(jnp.bfloat16)


def attend(ks, queries, seconds, w_output, bias, blocks, state, skipped, agents, microseconds):
    width = queries[0].shape[1]
    piece = jax.ShapeDtypeStruct((agents, width), jnp.bfloat16)
    return pl.pallas_call(
        functools.partial(attend_kernel, ks, len(queries), len(blocks), len(state), skipped),
        out_shape=[piece] * len(ks),
        in_specs=[VMEM] * (len(queries) + len(seconds) + 2 + len(blocks) + len(state)),
        out_specs=[VMEM] * len(ks),
        scratch_shapes=[pltpu.VMEM((len(ks) * agents, width), jnp.bfloat16)],
        compiler_params=pltpu.CompilerParams(vmem_limit_bytes=16 * MIB),
        cost_estimate=cost(microseconds),
        name="attend",
    )(*queries, *seconds, pinned(w_output), pinned(bias), *blocks, *[pinned(x) for x in state])


def put_back_kernel(steps, group, *refs):
    pieces, out, sem = refs[:steps][::-1], refs[steps], refs[steps + 1]
    spot = lax.axis_index("agent")
    half = pieces[0].shape[0] // 2
    copies = []
    for k in range(steps):
        target = out.at[(spot // group) ^ away(k, steps, spot % group)]
        for rows in (pl.ds(0, half), pl.ds(half, half)):
            copies.append(pltpu.make_async_copy(pieces[k].at[rows], target.at[rows], sem.at[len(copies)]))
    for copy in copies:
        copy.start()
    for copy in copies:
        copy.wait()


def put_back(group, pieces, shape):
    return pl.pallas_call(
        functools.partial(put_back_kernel, shape[0], group),
        out_shape=jax.ShapeDtypeStruct(shape, jnp.bfloat16),
        in_specs=[VMEM] * len(pieces),
        out_specs=ANY,
        scratch_shapes=[pltpu.SemaphoreType.DMA((2 * len(pieces),))],
        compiler_params=pltpu.CompilerParams(vmem_limit_bytes=4 * MIB),
        cost_estimate=cost(0),
        name="put_back",
    )(*pieces)


def after(x, *others):
    return lax.optimization_barrier((x, *others))[0]


def per_device(
    tokens,
    conv_taps,
    norm_first,
    norm_second,
    norm_third,
    w_in,
    w_out,
    w_query,
    w_key,
    w_value,
    w_output,
    agent_order,
    present_steps,
):
    steps, agents, width = tokens.shape
    tm_count, count = lax.axis_size("tm"), lax.axis_size("agent")
    group = count // steps
    part = agents // CHUNKS
    assert group * steps == count and steps == 4 and 128 % part == 0 and CHUNKS == 2 and group > 1

    def across(x, k):
        if k == steps - 1:
            return x
        pairs = [(i, ((i // group) ^ away(k, steps, i % group)) * group + i % group) for i in range(count)]
        return lax.ppermute(x, "agent", pairs)

    def within(x, r):
        return lax.ppermute(x, "agent", [(i, (i // group) * group + ((i % group) ^ r)) for i in range(count)])

    first_part = split(tokens)
    second_part, *partials, tail, taps, gain_first, gain_second, gain_third = stage(
        tokens,
        first_part,
        conv_taps,
        norm_first.reshape(1, width),
        agent_order.reshape(1, agents),
        present_steps.reshape(1, agents),
        [conv_taps] + [x.reshape(1, width) for x in (norm_first, norm_second, norm_third)],
    )
    halos = [lax.ppermute(x, "tm", [(i, (i + 1) % tm_count) for i in range(tm_count)]) for x in (first_part, second_part)]
    halos[0] = after(halos[0], tail)
    made = conv(group, halos[0], partials[0], taps, gain_first, tail)
    last = made[-1]
    pieces = [[across(made[k], k) for k in range(steps)]]
    for j in range(1, CHUNKS):
        halos[j] = after(halos[j], last)
        made = list(front(group, halos[j], partials[j], taps, (gain_first, gain_second), w_in, w_out))
        last = made[-1]
        made[steps - 2] = after(made[steps - 2], pieces[j - 1][0])
        pieces.append([across(made[k], k) for k in range(steps)])
    pieces[0][-1] = after(pieces[0][-1], last)
    query, keyval, second = feed(pieces[0], (gain_second, gain_third), (w_in, w_out, w_key, w_value, w_query))
    blocks = {(0, 0): keyval, **{(r, 0): within(keyval, r) for r in range(1, group)}}
    attn_in, keyval = project(pieces[1], gain_third, (w_key, w_value))
    keyval = after(keyval, *blocks.values())
    blocks.update({(0, 1): keyval, **{(r, 1): within(keyval, r) for r in range(1, group)}})
    blocks = [blocks[spot] for spot in block_order(group, CHUNKS)]
    ready = group + CHUNKS - 1
    far_ks, near_ks = (0, 1), (2, 3)
    own_query, bias, *state = early(far_ks, steps, group, query, attn_in, w_query, blocks[:ready])

    def finish(ks, blocks, state, skipped, microseconds):
        seconds = [second] + [pieces[j][k] for k in ks for j in range(1, CHUNKS)]
        return attend(
            ks, (query, own_query), seconds, w_output, bias, blocks, state, skipped, agents, microseconds
        )

    late = blocks[ready:]
    results = [*finish(far_ks, late, state, 0, 0), *finish(near_ks, blocks, [], 0, 10)]
    return put_back(group, [across(results[k], k) for k in reversed(range(steps))], tokens.shape)


def solution(mesh):
    in_specs = (P("tm", "agent", None),) + (P(),) * 10 + (P("agent"), P("agent"))
    return jax.shard_map(
        per_device, mesh=mesh, in_specs=in_specs, out_specs=P("tm", "agent", None), check_vma=False
    )
```

```python
import functools

import jax
import jax.numpy as jnp
from jax import lax
from jax.experimental import pallas as pl
from jax.experimental.pallas import tpu as pltpu
from jax.sharding import PartitionSpec as P

HEAD = 64
CHUNKS = 2
RADIX = 32
EPS = 1e-05
LOG2E = 1.4426950408889634
MIB = 1024 * 1024
VMEM = pl.BlockSpec(memory_space=pltpu.VMEM)
ANY = pl.BlockSpec(memory_space=pl.ANY)
HBM = pl.BlockSpec(memory_space=pltpu.HBM)


def pinned(x):
    return pltpu.with_memory_space_constraint(x, pltpu.VMEM)


def far(x):
    return pltpu.with_memory_space_constraint(x, pltpu.HBM)


def cost(microseconds):
    return pl.CostEstimate(
        flops=int(1.1e9 * microseconds) + 10**6, bytes_accessed=int(3.5e6 * microseconds) + 10**4, transcendentals=0
    )


def away(k, steps, member):
    odd = member % 2
    even_order, odd_order = (2, 3, 1), (2, 1, 3)
    return 0 if k == steps - 1 else even_order[k] * (1 - odd) + odd_order[k] * odd


def dot(a, b):
    return jnp.dot(a, b, preferred_element_type=jnp.float32)


def dot_t(a, b):
    return lax.dot_general(a, b, (((1,), (1,)), ((), ())), preferred_element_type=jnp.float32)


def norm_scale(values):
    return lax.rsqrt(jnp.mean(values * values, axis=-1, keepdims=True) + EPS)


def gelu(x):
    return 0.5 * x * (1.0 + lax.erf(x * 0.7071067811865476))


def part_copies(tokens, part, target, sem):
    steps, agents = target.shape[:2]
    return [
        pltpu.make_async_copy(tokens.at[step, pl.ds(part * agents, agents)], target.at[step], sem.at[step])
        for step in range(steps)
    ]


def split_kernel(tokens, out, sem):
    copies = part_copies(tokens, 0, out, sem)
    for copy in copies:
        copy.start()
    for copy in copies:
        copy.wait()


def split(tokens):
    steps, agents, width = tokens.shape
    return pl.pallas_call(
        split_kernel,
        out_shape=pltpu.VMEM((steps, agents // CHUNKS, width), tokens.dtype),
        in_specs=[HBM],
        out_specs=VMEM,
        scratch_shapes=[pltpu.SemaphoreType.DMA((steps,))],
        compiler_params=pltpu.CompilerParams(vmem_limit_bytes=4 * MIB),
        cost_estimate=cost(0),
        name="split",
    )(far(tokens))


def stage_kernel(count, taps, gain, order, present, tokens, first_part, *rest):
    sources, rest = rest[:count], rest[count:]
    second_part, partials, tail, targets = rest[0], rest[1:3], rest[3], rest[4 : 4 + count]
    taps_here, gain_here, order_here, present_here, normed, facts, part_sem, sem = rest[4 + count :]
    pairs = [
        (taps, taps_here),
        (gain, gain_here),
        (order, order_here),
        (present, present_here),
        *zip(sources, targets),
    ]
    copies = [pltpu.make_async_copy(source, target, sem.at[i]) for i, (source, target) in enumerate(pairs)]
    later = part_copies(tokens, 1, second_part, part_sem)
    for copy in copies + later:
        copy.start()
    for copy in copies:
        copy.wait()
    agents = order.shape[1]
    facts[...] = jnp.zeros(facts.shape, jnp.float32)
    facts[0:1, :agents] = (order_here[...] // RADIX).astype(jnp.float32)
    facts[1:2, :agents] = (order_here[...] % RADIX).astype(jnp.float32)
    facts[2:3, :agents] = present_here[...].astype(jnp.float32)
    tail[...] = facts[...].astype(jnp.bfloat16)
    steps, reach = first_part.shape[0], taps.shape[0] - 1
    gains = gain_here[...]
    for j, part in enumerate((first_part, second_part)):
        for step in range(steps):
            if j == 1:
                later[step].wait()
            values = part[step].astype(jnp.float32)
            normed[step] = values * norm_scale(values) * gains
            total = values
            for lag in range(min(step, reach) + 1):
                total = total + taps_here[lag : lag + 1, :] * normed[step - lag]
            partials[j][step] = total


def stage(tokens, first_part, taps, gain, order, present, arrays):
    steps, part, width = first_part.shape
    inputs = (taps, gain, order, present)
    return pl.pallas_call(
        functools.partial(stage_kernel, len(arrays)),
        out_shape=[pltpu.VMEM(first_part.shape, first_part.dtype)]
        + [pltpu.VMEM((steps, part, width), jnp.float32)] * CHUNKS
        + [pltpu.VMEM((part, 128), jnp.bfloat16)]
        + [pltpu.VMEM(x.shape, x.dtype) for x in arrays],
        in_specs=[HBM] * (len(inputs) + 1) + [VMEM] + [HBM] * len(arrays),
        out_specs=[VMEM] * (CHUNKS + 2 + len(arrays)),
        scratch_shapes=[pltpu.VMEM(x.shape, x.dtype) for x in inputs]
        + [
            pltpu.VMEM((steps, part, width), jnp.float32),
            pltpu.VMEM((part, 128), jnp.float32),
            pltpu.SemaphoreType.DMA((steps,)),
            pltpu.SemaphoreType.DMA((len(inputs) + len(arrays),)),
        ],
        compiler_params=pltpu.CompilerParams(vmem_limit_bytes=8 * MIB),
        cost_estimate=cost(30),
        name="stage",
    )(*[far(x) for x in (*inputs, tokens)], pinned(first_part), *[far(x) for x in arrays])


def run_pairs(pairs, lead, stages):
    held = [{} for _ in stages]
    for turn in range(pairs + lead * (len(stages) - 1)):
        for i, stage in enumerate(stages):
            pair = turn - lead * i
            if 0 <= pair < pairs:
                held[i][pair] = stage(pair, held[i - 1].pop(pair)) if i else stage(pair)


def mixed_rows(halo, partial, taps, gain, normed, first):
    steps, agents = halo.shape[:2]
    reach = taps.shape[0] - 1
    gains = gain[...] * (lax.axis_index("tm") > 0).astype(jnp.float32)
    for step in range(steps):
        values = halo[step].astype(jnp.float32)
        normed[step] = values * norm_scale(values) * gains
    for step in range(steps):
        total = partial[step]
        for lag in range(step + 1, reach + 1):
            total = total + taps[lag : lag + 1, :] * normed[steps + step - lag]
        first[step * agents : (step + 1) * agents, :] = total.astype(jnp.bfloat16).astype(first.dtype)


def feed_forward(rows, gain, w_in, w_out):
    inner = (rows * norm_scale(rows) * gain[...]).astype(jnp.bfloat16)
    tile, total = 512, [rows]

    def enter(i):
        return dot(inner, w_in[:, i * tile : (i + 1) * tile])

    def activate(i, products):
        return gelu(products).astype(jnp.bfloat16)

    def leave(i, hidden):
        total[0] = total[0] + dot(hidden, w_out[i * tile : (i + 1) * tile, :])

    run_pairs(w_in.shape[1] // tile, 1, [enter, activate, leave])
    return total[0].astype(jnp.bfloat16)


def to_keys(second, gain, w_key, w_value, keyval):
    width = second.shape[1]
    values = second.astype(jnp.float32)
    attn_in = (values * norm_scale(values) * gain[...]).astype(jnp.bfloat16)
    keyval[:, :width] = dot(attn_in, w_key[...]).astype(jnp.bfloat16)
    keyval[:, width : 2 * width] = dot(attn_in, w_value[...]).astype(jnp.bfloat16)
    return attn_in


def conv_kernel(group, halo, partial, taps, gain, tail, *rest):
    steps, agents, width = halo.shape
    outs = rest[:steps]
    normed, first = rest[steps:]
    mixed_rows(halo, partial, taps, gain, normed, first)
    spot = lax.axis_index("agent")
    for k in range(steps):
        step = (spot // group) ^ away(k, steps, spot % group)
        outs[k][:, :width] = first[pl.ds(pl.multiple_of(step * agents, agents), agents), :].astype(jnp.bfloat16)
        outs[k][:, width:] = tail[...]


def conv(group, halo, partial, taps, gain, tail):
    steps, agents, width = halo.shape
    return pl.pallas_call(
        functools.partial(conv_kernel, group),
        out_shape=[jax.ShapeDtypeStruct((agents, width + tail.shape[1]), jnp.bfloat16)] * steps,
        in_specs=[VMEM] * 5,
        out_specs=[VMEM] * steps,
        scratch_shapes=[
            pltpu.VMEM((steps, agents, width), jnp.float32),
            pltpu.VMEM((steps * agents, width), jnp.float32),
        ],
        compiler_params=pltpu.CompilerParams(vmem_limit_bytes=8 * MIB),
        cost_estimate=cost(0),
        name="conv",
    )(halo, *[pinned(x) for x in (partial, taps, gain, tail)])


def front_kernel(group, halo, partial, taps, gain_first, gain_second, w_in, w_out, *rest):
    steps, agents, width = halo.shape
    outs = rest[:steps]
    normed, first, second = rest[steps:]
    mixed_rows(halo, partial, taps, gain_first, normed, first)
    result = feed_forward(first[...], gain_second, w_in, w_out)
    for step in range(steps):
        second[step] = result[step * agents : (step + 1) * agents]
    spot = lax.axis_index("agent")
    for k in range(steps):
        outs[k][...] = second[(spot // group) ^ away(k, steps, spot % group)]


def front(group, halo, partial, taps, gains, w_in, w_out):
    steps, agents, width = halo.shape
    rows = steps * agents
    return pl.pallas_call(
        functools.partial(front_kernel, group),
        out_shape=[jax.ShapeDtypeStruct((agents, width), jnp.bfloat16)] * steps,
        in_specs=[VMEM] * 7,
        out_specs=[VMEM] * steps,
        scratch_shapes=[
            pltpu.VMEM((steps, agents, width), jnp.float32),
            pltpu.VMEM((rows, width), jnp.float32),
            pltpu.VMEM((steps, agents, width), jnp.bfloat16),
        ],
        compiler_params=pltpu.CompilerParams(vmem_limit_bytes=12 * MIB),
        cost_estimate=cost(0),
        name="front",
    )(halo, *[pinned(x) for x in (partial, taps, *gains, w_in, w_out)])


def feed_kernel(count, *refs):
    pieces = refs[:count]
    gain_second, gain_third, w_in, w_out, w_key, w_value, w_query = refs[count : count + 7]
    query, keyval, second = refs[count + 7 :]
    width = gain_second.shape[1]
    agents = pieces[0].shape[0]
    for k in range(count):
        keyval[agents * k : agents * (k + 1), 2 * width :] = pieces[k][:, width:]
    first = jnp.concatenate([piece[:, :width].astype(jnp.float32) for piece in pieces], axis=0)
    result = feed_forward(first, gain_second, w_in, w_out)
    second[...] = result
    attn_in = to_keys(result, gain_third, w_key, w_value, keyval)
    query[...] = dot(attn_in, w_query[...]).astype(jnp.bfloat16)


def feed(pieces, gains, weights):
    rows = sum(piece.shape[0] for piece in pieces)
    width = gains[0].shape[1]
    return pl.pallas_call(
        functools.partial(feed_kernel, len(pieces)),
        out_shape=[
            jax.ShapeDtypeStruct((rows, width), jnp.bfloat16),
            jax.ShapeDtypeStruct((rows, width + pieces[0].shape[1]), jnp.bfloat16),
            jax.ShapeDtypeStruct((rows, width), jnp.bfloat16),
        ],
        in_specs=[VMEM] * (len(pieces) + 7),
        out_specs=[VMEM] * 3,
        compiler_params=pltpu.CompilerParams(vmem_limit_bytes=12 * MIB),
        cost_estimate=cost(0),
        name="feed",
    )(*pieces, *[pinned(x) for x in (*gains, *weights)])


def project_kernel(count, *refs):
    pieces = refs[:count][::-1]
    gain, w_key, w_value, attn_in, keyval = refs[count:]
    second = jnp.concatenate([piece[...] for piece in pieces], axis=0)
    attn_in[...] = to_keys(second, gain, w_key, w_value, keyval)


def project(pieces, gain, weights):
    rows = sum(piece.shape[0] for piece in pieces)
    width = gain.shape[1]
    return pl.pallas_call(
        functools.partial(project_kernel, len(pieces)),
        out_shape=[
            jax.ShapeDtypeStruct((rows, width), jnp.bfloat16),
            jax.ShapeDtypeStruct((rows, 2 * width), jnp.bfloat16),
        ],
        in_specs=[VMEM] * (len(pieces) + 3),
        out_specs=[VMEM] * 2,
        compiler_params=pltpu.CompilerParams(vmem_limit_bytes=8 * MIB),
        cost_estimate=cost(25),
        name="project",
    )(*reversed(pieces), *[pinned(x) for x in (gain, *weights)])


def block_order(group, chunks):
    early = [(r, 0) for r in range(group)] + [(0, j) for j in range(1, chunks)]
    return early + [(r, j) for j in range(1, chunks) for r in range(1, group)]


def write_mask(steps, chunks, agents, width, blocks, bias):
    group = len(blocks)
    now = (lax.axis_index("tm") * steps + lax.axis_index("agent") // group).astype(jnp.float32)
    lane = lax.broadcasted_iota(jnp.int32, (agents, 128), 1)
    sublane = lax.broadcasted_iota(jnp.int32, (agents, 128), 0)
    tiles = {}
    for r in range(group):
        for k in range(steps):
            tile = blocks[r][agents * k : agents * (k + 1), 2 * width :].astype(jnp.float32)
            tiles[k, r] = (tile[0:1] * RADIX + tile[1:2], tile[2:3])
    own = jnp.concatenate(
        [
            jnp.sum(jnp.where(lane == sublane + j * agents, tiles[k, 0][0], 0.0), axis=1, keepdims=True)
            for k in range(steps)
            for j in range(chunks)
        ],
        axis=0,
    )
    row_lane = lax.broadcasted_iota(jnp.int32, (1, 128), 1)
    per_tile = 128 // agents
    start = 0
    for r, j in block_order(group, chunks):
        for first in range(0, steps, per_tile):
            both = [None, None]
            for i in range(per_tile):
                for f in (0, 1):
                    moved = pltpu.roll(tiles[first + i, r][f], ((i - j) * agents) % 128, 1)
                    both[f] = moved if i == 0 else jnp.where(row_lane >= i * agents, moved, both[f])
            order, present = both
            alive = jnp.where(now < present, order, 1e9)
            visible = (alive < own) | (order == own)
            bias[:, start : start + 128] = jnp.where(visible, 0.0, -1e30)
            start += 128


def rows_of(parts, ks, agents, columns):
    return jnp.concatenate([part[agents * k : agents * (k + 1), columns] for k in ks for part in parts], axis=0)


def pair_stages(queries_of, blocks, bias, top_of, low):
    width = blocks[0].shape[1] // 2 // 128 * 128

    def products(pair):
        queries = queries_of(pair)
        zeros = jnp.zeros_like(queries)
        stacked = jnp.concatenate([jnp.where(low, queries, zeros), jnp.where(low, zeros, queries)], axis=0)
        key = jnp.concatenate([block[:, 128 * pair : 128 * pair + 128] for block in blocks], axis=0)
        return dot_t(stacked, key)

    def weigh(pair, scores):
        rows = scores.shape[0] // 2
        tops, weights = [], []
        for half in range(2):
            here = scores[half * rows : (half + 1) * rows] * (LOG2E * HEAD ** (-0.5)) + bias
            highest = jnp.max(here, axis=1, keepdims=True)
            if top_of is not None:
                highest = jnp.maximum(highest, top_of(pair)[:, HEAD * half : HEAD * half + 1])
            tops.append(highest)
            weights.append(jnp.exp2(here - highest).astype(jnp.bfloat16))
        return tops, jnp.concatenate(weights, axis=0)

    def sums(pair, made):
        tops, weights = made
        start = width + 128 * pair
        value = jnp.concatenate([block[:, start : start + 128] for block in blocks], axis=0)
        return tops, dot(weights, jnp.concatenate([value, jnp.ones(value.shape, jnp.bfloat16)], axis=1))

    return [products, weigh, sums]


def merged(low, total):
    rows = total.shape[0] // 2
    return jnp.where(low, total[:rows], total[rows:])


def early_kernel(ks, steps, chunks, group, query, attn_in, w_query, *refs):
    count = group + chunks - 1
    blocks, (own_query, bias, number, weight, top) = refs[:count], refs[count:]
    own_query[...] = dot(attn_in[...], w_query[...]).astype(jnp.bfloat16)
    rows, width = number.shape
    write_mask(steps, chunks, query.shape[0] // steps, width, blocks[:group], bias)
    agents = rows // (len(ks) * chunks)
    low = lax.broadcasted_iota(jnp.int32, (rows, 128), 1) < HEAD
    keys = sum(block.shape[0] for block in blocks)
    here = bias[ks[0] * agents * chunks : ks[0] * agents * chunks + rows, :keys]

    def columns(pair):
        return slice(128 * pair, 128 * pair + 128)

    def keep(pair, made):
        tops, total = made
        number[:, columns(pair)] = merged(low, total[:, :128])
        weight[:, columns(pair)] = merged(low, total[:, 128:])
        top[:, columns(pair)] = jnp.where(low, tops[0], tops[1])

    stages = pair_stages(lambda pair: rows_of((query, own_query), ks, agents, columns(pair)), blocks, here, None, low)
    run_pairs(width // 128, 1, [*stages, keep])


def early(ks, steps, group, query, attn_in, w_query, blocks):
    count, width = query.shape
    rows = count * CHUNKS
    state = pltpu.VMEM((len(ks) * rows // steps, width), jnp.float32)
    return pl.pallas_call(
        functools.partial(early_kernel, ks, steps, CHUNKS, group),
        out_shape=[jax.ShapeDtypeStruct(query.shape, jnp.bfloat16), pltpu.VMEM((rows, rows * group), jnp.float32)]
        + [state] * 3,
        in_specs=[VMEM] * (3 + len(blocks)),
        out_specs=[VMEM] * 5,
        compiler_params=pltpu.CompilerParams(vmem_limit_bytes=16 * MIB),
        cost_estimate=cost(0),
        name="early",
    )(query, attn_in, pinned(w_query), *blocks)


def attend_kernel(ks, chunks, count, begun, skipped, *refs):
    mine = 1 + len(ks) * (chunks - 1)
    queries, seconds, (w_output, bias) = refs[:chunks], refs[chunks : chunks + mine], refs[chunks + mine : chunks + mine + 2]
    rest = refs[chunks + mine + 2 :]
    blocks, state = rest[:count], rest[count : count + begun]
    outs = rest[count + begun :]
    width, agents = w_output.shape[1], queries[0].shape[0] // 4
    rows = len(ks) * chunks * agents
    low = lax.broadcasted_iota(jnp.int32, (rows, 128), 1) < HEAD
    keys = sum(block.shape[0] for block in blocks)
    here = bias[ks[0] * agents * chunks : ks[0] * agents * chunks + rows, bias.shape[1] - keys :]
    begun_rows = slice(skipped, skipped + rows)

    def columns(pair):
        return slice(128 * pair, 128 * pair + 128)

    residual = []
    for i, k in enumerate(ks):
        residual += [seconds[0][agents * k : agents * (k + 1)]]
        residual += [piece[...] for piece in seconds[1 + i * (chunks - 1) : 1 + (i + 1) * (chunks - 1)]]
    result = [jnp.concatenate(residual, axis=0).astype(jnp.float32)]

    def keep(pair, made):
        tops, total = made
        number, weight = merged(low, total[:, :128]), merged(low, total[:, 128:])
        if begun:
            shrink = jnp.exp2(state[2][begun_rows, columns(pair)] - jnp.where(low, tops[0], tops[1]))
            number = number + state[0][begun_rows, columns(pair)] * shrink
            weight = weight + state[1][begun_rows, columns(pair)] * shrink
        return (number / weight).astype(jnp.bfloat16)

    waiting = []

    def output(pair, attended):
        waiting.append(attended)
        if len(waiting) == 2:
            features = slice(128 * (pair - 1), 128 * (pair + 1))
            result[0] = result[0] + dot(jnp.concatenate(waiting, axis=1), w_output[features, :])
            waiting.clear()

    stages = pair_stages(
        lambda pair: rows_of(queries, ks, agents, columns(pair)),
        blocks,
        here,
        (lambda pair: state[2][begun_rows, columns(pair)]) if begun else None,
        low,
    )
    run_pairs(width // 128, width // 128 if begun else 1, [*stages, keep, output])
    for i in range(len(ks)):
        outs[i][...] = result[0][i * agents * chunks : (i + 1) * agents * chunks].astype(jnp.bfloat16)


def attend(ks, queries, seconds, w_output, bias, blocks, state, skipped, agents, microseconds):
    width = queries[0].shape[1]
    piece = jax.ShapeDtypeStruct((agents, width), jnp.bfloat16)
    return pl.pallas_call(
        functools.partial(attend_kernel, ks, len(queries), len(blocks), len(state), skipped),
        out_shape=[piece] * len(ks),
        in_specs=[VMEM] * (len(queries) + len(seconds) + 2 + len(blocks) + len(state)),
        out_specs=[VMEM] * len(ks),
        compiler_params=pltpu.CompilerParams(vmem_limit_bytes=16 * MIB),
        cost_estimate=cost(microseconds),
        name="attend",
    )(*queries, *seconds, pinned(w_output), pinned(bias), *blocks, *[pinned(x) for x in state])


def put_back_kernel(steps, group, *refs):
    pieces, out, sem = refs[:steps][::-1], refs[steps], refs[steps + 1]
    spot = lax.axis_index("agent")
    half = pieces[0].shape[0] // 2
    copies = []
    for k in range(steps):
        target = out.at[(spot // group) ^ away(k, steps, spot % group)]
        for rows in (pl.ds(0, half), pl.ds(half, half)):
            copies.append(pltpu.make_async_copy(pieces[k].at[rows], target.at[rows], sem.at[len(copies)]))
    for copy in copies:
        copy.start()
    for copy in copies:
        copy.wait()


def put_back(group, pieces, shape):
    return pl.pallas_call(
        functools.partial(put_back_kernel, shape[0], group),
        out_shape=jax.ShapeDtypeStruct(shape, jnp.bfloat16),
        in_specs=[VMEM] * len(pieces),
        out_specs=ANY,
        scratch_shapes=[pltpu.SemaphoreType.DMA((2 * len(pieces),))],
        compiler_params=pltpu.CompilerParams(vmem_limit_bytes=4 * MIB),
        cost_estimate=cost(0),
        name="put_back",
    )(*pieces)


def after(x, *others):
    return lax.optimization_barrier((x, *others))[0]


def per_device(
    tokens,
    conv_taps,
    norm_first,
    norm_second,
    norm_third,
    w_in,
    w_out,
    w_query,
    w_key,
    w_value,
    w_output,
    agent_order,
    present_steps,
):
    steps, agents, width = tokens.shape
    tm_count, count = lax.axis_size("tm"), lax.axis_size("agent")
    group = count // steps
    part = agents // CHUNKS
    assert group * steps == count and steps == 4 and 128 % part == 0 and CHUNKS == 2 and group > 1

    def across(x, k):
        if k == steps - 1:
            return x
        pairs = [(i, ((i // group) ^ away(k, steps, i % group)) * group + i % group) for i in range(count)]
        return lax.ppermute(x, "agent", pairs)

    def within(x, r):
        return lax.ppermute(x, "agent", [(i, (i // group) * group + ((i % group) ^ r)) for i in range(count)])

    first_part = split(tokens)
    second_part, *partials, tail, taps, gain_first, gain_second, gain_third = stage(
        tokens,
        first_part,
        conv_taps,
        norm_first.reshape(1, width),
        agent_order.reshape(1, agents),
        present_steps.reshape(1, agents),
        [conv_taps] + [x.reshape(1, width) for x in (norm_first, norm_second, norm_third)],
    )
    halos = [lax.ppermute(x, "tm", [(i, (i + 1) % tm_count) for i in range(tm_count)]) for x in (first_part, second_part)]
    halos[0] = after(halos[0], tail)
    made = conv(group, halos[0], partials[0], taps, gain_first, tail)
    last = made[-1]
    pieces = [[across(made[k], k) for k in range(steps)]]
    for j in range(1, CHUNKS):
        halos[j] = after(halos[j], last)
        made = list(front(group, halos[j], partials[j], taps, (gain_first, gain_second), w_in, w_out))
        last = made[-1]
        made[steps - 2] = after(made[steps - 2], pieces[j - 1][0])
        pieces.append([across(made[k], k) for k in range(steps)])
    pieces[0][-1] = after(pieces[0][-1], last)
    query, keyval, second = feed(pieces[0], (gain_second, gain_third), (w_in, w_out, w_key, w_value, w_query))
    blocks = {(0, 0): keyval, **{(r, 0): within(keyval, r) for r in range(1, group)}}
    attn_in, keyval = project(pieces[1], gain_third, (w_key, w_value))
    keyval = after(keyval, *blocks.values())
    blocks.update({(0, 1): keyval, **{(r, 1): within(keyval, r) for r in range(1, group)}})
    blocks = [blocks[spot] for spot in block_order(group, CHUNKS)]
    ready = group + CHUNKS - 1
    far_ks, near_ks = (0, 1), (2, 3)
    own_query, bias, *state = early(far_ks, steps, group, query, attn_in, w_query, blocks[:ready])

    def finish(ks, blocks, state, skipped, microseconds):
        seconds = [second] + [pieces[j][k] for k in ks for j in range(1, CHUNKS)]
        return attend(
            ks, (query, own_query), seconds, w_output, bias, blocks, state, skipped, agents, microseconds
        )

    late = blocks[ready:]
    results = [*finish(far_ks, late, state, 0, 0), *finish(near_ks, blocks, [], 0, 10)]
    return put_back(group, [across(results[k], k) for k in reversed(range(steps))], tokens.shape)


def solution(mesh):
    in_specs = (P("tm", "agent", None),) + (P(),) * 10 + (P("agent"), P("agent"))
    return jax.shard_map(
        per_device, mesh=mesh, in_specs=in_specs, out_specs=P("tm", "agent", None), check_vma=False
    )
```

```python
import functools

import jax
import jax.numpy as jnp
from jax import lax
from jax.experimental import pallas as pl
from jax.experimental.pallas import tpu as pltpu
from jax.sharding import PartitionSpec as P

HEAD = 64
CHUNKS = 2
RADIX = 32
EPS = 1e-05
LOG2E = 1.4426950408889634
MIB = 1024 * 1024
VMEM = pl.BlockSpec(memory_space=pltpu.VMEM)
ANY = pl.BlockSpec(memory_space=pl.ANY)
HBM = pl.BlockSpec(memory_space=pltpu.HBM)


def pinned(x):
    return pltpu.with_memory_space_constraint(x, pltpu.VMEM)


def far(x):
    return pltpu.with_memory_space_constraint(x, pltpu.HBM)


def cost(microseconds):
    return pl.CostEstimate(
        flops=int(1.1e9 * microseconds) + 10**6, bytes_accessed=int(3.5e6 * microseconds) + 10**4, transcendentals=0
    )


def away(k, steps, member):
    odd = member % 2
    even_order, odd_order = (2, 3, 1), (2, 1, 3)
    return 0 if k == steps - 1 else even_order[k] * (1 - odd) + odd_order[k] * odd


def dot(a, b):
    return jnp.dot(a, b, preferred_element_type=jnp.float32)


def dot_t(a, b):
    return lax.dot_general(a, b, (((1,), (1,)), ((), ())), preferred_element_type=jnp.float32)


def norm_scale(values):
    return lax.rsqrt(jnp.mean(values * values, axis=-1, keepdims=True) + EPS)


def gelu(x):
    return 0.5 * x * (1.0 + lax.erf(x * 0.7071067811865476))


def part_copies(tokens, part, target, sem):
    steps, agents = target.shape[:2]
    return [
        pltpu.make_async_copy(tokens.at[step, pl.ds(part * agents, agents)], target.at[step], sem.at[step])
        for step in range(steps)
    ]


def split_kernel(tokens, out, sem):
    copies = part_copies(tokens, 0, out, sem)
    for copy in copies:
        copy.start()
    for copy in copies:
        copy.wait()


def split(tokens):
    steps, agents, width = tokens.shape
    return pl.pallas_call(
        split_kernel,
        out_shape=pltpu.VMEM((steps, agents // CHUNKS, width), tokens.dtype),
        in_specs=[HBM],
        out_specs=VMEM,
        scratch_shapes=[pltpu.SemaphoreType.DMA((steps,))],
        compiler_params=pltpu.CompilerParams(vmem_limit_bytes=4 * MIB),
        cost_estimate=cost(0),
        name="split",
    )(far(tokens))


def stage_kernel(count, taps, gain, order, present, tokens, first_part, *rest):
    sources, rest = rest[:count], rest[count:]
    second_part, partials, tail, targets = rest[0], rest[1:3], rest[3], rest[4 : 4 + count]
    taps_here, gain_here, order_here, present_here, normed, facts, part_sem, sem = rest[4 + count :]
    pairs = [
        (taps, taps_here),
        (gain, gain_here),
        (order, order_here),
        (present, present_here),
        *zip(sources, targets),
    ]
    copies = [pltpu.make_async_copy(source, target, sem.at[i]) for i, (source, target) in enumerate(pairs)]
    later = part_copies(tokens, 1, second_part, part_sem)
    for copy in copies + later:
        copy.start()
    for copy in copies:
        copy.wait()
    agents = order.shape[1]
    facts[...] = jnp.zeros(facts.shape, jnp.float32)
    facts[0:1, :agents] = (order_here[...] // RADIX).astype(jnp.float32)
    facts[1:2, :agents] = (order_here[...] % RADIX).astype(jnp.float32)
    facts[2:3, :agents] = present_here[...].astype(jnp.float32)
    tail[...] = facts[...].astype(jnp.bfloat16)
    steps, reach = first_part.shape[0], taps.shape[0] - 1
    gains = gain_here[...]
    for j, part in enumerate((first_part, second_part)):
        for step in range(steps):
            if j == 1:
                later[step].wait()
            values = part[step].astype(jnp.float32)
            normed[step] = values * norm_scale(values) * gains
            total = values
            for lag in range(min(step, reach) + 1):
                total = total + taps_here[lag : lag + 1, :] * normed[step - lag]
            partials[j][step] = total


def stage(tokens, first_part, taps, gain, order, present, arrays):
    steps, part, width = first_part.shape
    inputs = (taps, gain, order, present)
    return pl.pallas_call(
        functools.partial(stage_kernel, len(arrays)),
        out_shape=[pltpu.VMEM(first_part.shape, first_part.dtype)]
        + [pltpu.VMEM((steps, part, width), jnp.float32)] * CHUNKS
        + [pltpu.VMEM((part, 128), jnp.bfloat16)]
        + [pltpu.VMEM(x.shape, x.dtype) for x in arrays],
        in_specs=[HBM] * (len(inputs) + 1) + [VMEM] + [HBM] * len(arrays),
        out_specs=[VMEM] * (CHUNKS + 2 + len(arrays)),
        scratch_shapes=[pltpu.VMEM(x.shape, x.dtype) for x in inputs]
        + [
            pltpu.VMEM((steps, part, width), jnp.float32),
            pltpu.VMEM((part, 128), jnp.float32),
            pltpu.SemaphoreType.DMA((steps,)),
            pltpu.SemaphoreType.DMA((len(inputs) + len(arrays),)),
        ],
        compiler_params=pltpu.CompilerParams(vmem_limit_bytes=8 * MIB),
        cost_estimate=cost(30),
        name="stage",
    )(*[far(x) for x in (*inputs, tokens)], pinned(first_part), *[far(x) for x in arrays])


def run_pairs(pairs, lead, stages):
    held = [{} for _ in stages]
    for turn in range(pairs + lead * (len(stages) - 1)):
        for i, stage in enumerate(stages):
            pair = turn - lead * i
            if 0 <= pair < pairs:
                held[i][pair] = stage(pair, held[i - 1].pop(pair)) if i else stage(pair)


def mixed_rows(halo, partial, taps, gain, normed, first):
    steps, agents = halo.shape[:2]
    reach = taps.shape[0] - 1
    gains = gain[...] * (lax.axis_index("tm") > 0).astype(jnp.float32)
    for step in range(steps):
        values = halo[step].astype(jnp.float32)
        normed[step] = values * norm_scale(values) * gains
    for step in range(steps):
        total = partial[step]
        for lag in range(step + 1, reach + 1):
            total = total + taps[lag : lag + 1, :] * normed[steps + step - lag]
        first[step * agents : (step + 1) * agents, :] = total.astype(jnp.bfloat16).astype(first.dtype)


def feed_forward(rows, gain, w_in, w_out):
    inner = (rows * norm_scale(rows) * gain[...]).astype(jnp.bfloat16)
    tile, total = 512, [rows]

    def enter(i):
        return dot(inner, w_in[:, i * tile : (i + 1) * tile])

    def activate(i, products):
        return gelu(products).astype(jnp.bfloat16)

    def leave(i, hidden):
        total[0] = total[0] + dot(hidden, w_out[i * tile : (i + 1) * tile, :])

    run_pairs(w_in.shape[1] // tile, 1, [enter, activate, leave])
    return total[0].astype(jnp.bfloat16)


def to_keys(second, gain, w_key, w_value, keyval):
    width = second.shape[1]
    values = second.astype(jnp.float32)
    attn_in = (values * norm_scale(values) * gain[...]).astype(jnp.bfloat16)
    keyval[:, :width] = dot(attn_in, w_key[...]).astype(jnp.bfloat16)
    keyval[:, width : 2 * width] = dot(attn_in, w_value[...]).astype(jnp.bfloat16)
    return attn_in


def conv_kernel(group, halo, partial, taps, gain, tail, *rest):
    steps, agents, width = halo.shape
    outs = rest[:steps]
    normed, first = rest[steps:]
    mixed_rows(halo, partial, taps, gain, normed, first)
    spot = lax.axis_index("agent")
    for k in range(steps):
        step = (spot // group) ^ away(k, steps, spot % group)
        outs[k][:, :width] = first[pl.ds(pl.multiple_of(step * agents, agents), agents), :].astype(jnp.bfloat16)
        outs[k][:, width:] = tail[...]


def conv(group, halo, partial, taps, gain, tail):
    steps, agents, width = halo.shape
    return pl.pallas_call(
        functools.partial(conv_kernel, group),
        out_shape=[jax.ShapeDtypeStruct((agents, width + tail.shape[1]), jnp.bfloat16)] * steps,
        in_specs=[VMEM] * 5,
        out_specs=[VMEM] * steps,
        scratch_shapes=[
            pltpu.VMEM((steps, agents, width), jnp.float32),
            pltpu.VMEM((steps * agents, width), jnp.float32),
        ],
        compiler_params=pltpu.CompilerParams(vmem_limit_bytes=8 * MIB),
        cost_estimate=cost(0),
        name="conv",
    )(halo, *[pinned(x) for x in (partial, taps, gain, tail)])


def front_kernel(group, halo, partial, taps, gain_first, gain_second, w_in, w_out, *rest):
    steps, agents, width = halo.shape
    outs = rest[:steps]
    normed, first, second = rest[steps:]
    mixed_rows(halo, partial, taps, gain_first, normed, first)
    result = feed_forward(first[...], gain_second, w_in, w_out)
    for step in range(steps):
        second[step] = result[step * agents : (step + 1) * agents]
    spot = lax.axis_index("agent")
    for k in range(steps):
        outs[k][...] = second[(spot // group) ^ away(k, steps, spot % group)]


def front(group, halo, partial, taps, gains, w_in, w_out):
    steps, agents, width = halo.shape
    rows = steps * agents
    return pl.pallas_call(
        functools.partial(front_kernel, group),
        out_shape=[jax.ShapeDtypeStruct((agents, width), jnp.bfloat16)] * steps,
        in_specs=[VMEM] * 7,
        out_specs=[VMEM] * steps,
        scratch_shapes=[
            pltpu.VMEM((steps, agents, width), jnp.float32),
            pltpu.VMEM((rows, width), jnp.float32),
            pltpu.VMEM((steps, agents, width), jnp.bfloat16),
        ],
        compiler_params=pltpu.CompilerParams(vmem_limit_bytes=12 * MIB),
        cost_estimate=cost(0),
        name="front",
    )(halo, *[pinned(x) for x in (partial, taps, *gains, w_in, w_out)])


def feed_kernel(count, *refs):
    pieces = refs[:count]
    gain_second, gain_third, w_in, w_out, w_key, w_value, w_query = refs[count : count + 7]
    query, keyval, second = refs[count + 7 :]
    width = gain_second.shape[1]
    agents = pieces[0].shape[0]
    for k in range(count):
        keyval[agents * k : agents * (k + 1), 2 * width :] = pieces[k][:, width:]
    first = jnp.concatenate([piece[:, :width].astype(jnp.float32) for piece in pieces], axis=0)
    result = feed_forward(first, gain_second, w_in, w_out)
    second[...] = result
    attn_in = to_keys(result, gain_third, w_key, w_value, keyval)
    query[...] = dot(attn_in, w_query[...]).astype(jnp.bfloat16)


def feed(pieces, gains, weights):
    rows = sum(piece.shape[0] for piece in pieces)
    width = gains[0].shape[1]
    return pl.pallas_call(
        functools.partial(feed_kernel, len(pieces)),
        out_shape=[
            jax.ShapeDtypeStruct((rows, width), jnp.bfloat16),
            jax.ShapeDtypeStruct((rows, width + pieces[0].shape[1]), jnp.bfloat16),
            jax.ShapeDtypeStruct((rows, width), jnp.bfloat16),
        ],
        in_specs=[VMEM] * (len(pieces) + 7),
        out_specs=[VMEM] * 3,
        compiler_params=pltpu.CompilerParams(vmem_limit_bytes=12 * MIB),
        cost_estimate=cost(0),
        name="feed",
    )(*pieces, *[pinned(x) for x in (*gains, *weights)])


def project_kernel(count, *refs):
    pieces = refs[:count][::-1]
    gain, w_key, w_value, attn_in, keyval = refs[count:]
    second = jnp.concatenate([piece[...] for piece in pieces], axis=0)
    attn_in[...] = to_keys(second, gain, w_key, w_value, keyval)


def project(pieces, gain, weights):
    rows = sum(piece.shape[0] for piece in pieces)
    width = gain.shape[1]
    return pl.pallas_call(
        functools.partial(project_kernel, len(pieces)),
        out_shape=[
            jax.ShapeDtypeStruct((rows, width), jnp.bfloat16),
            jax.ShapeDtypeStruct((rows, 2 * width), jnp.bfloat16),
        ],
        in_specs=[VMEM] * (len(pieces) + 3),
        out_specs=[VMEM] * 2,
        compiler_params=pltpu.CompilerParams(vmem_limit_bytes=8 * MIB),
        cost_estimate=cost(25),
        name="project",
    )(*reversed(pieces), *[pinned(x) for x in (gain, *weights)])


def block_order(group, chunks):
    early = [(r, 0) for r in range(group)] + [(0, j) for j in range(1, chunks)]
    return early + [(r, j) for j in range(1, chunks) for r in range(1, group)]


def write_mask(steps, chunks, agents, width, blocks, bias):
    group = len(blocks)
    now = (lax.axis_index("tm") * steps + lax.axis_index("agent") // group).astype(jnp.float32)
    lane = lax.broadcasted_iota(jnp.int32, (agents, 128), 1)
    sublane = lax.broadcasted_iota(jnp.int32, (agents, 128), 0)
    tiles = {}
    for r in range(group):
        for k in range(steps):
            tile = blocks[r][agents * k : agents * (k + 1), 2 * width :].astype(jnp.float32)
            tiles[k, r] = (tile[0:1] * RADIX + tile[1:2], tile[2:3])
    own = jnp.concatenate(
        [
            jnp.sum(jnp.where(lane == sublane + j * agents, tiles[k, 0][0], 0.0), axis=1, keepdims=True)
            for k in range(steps)
            for j in range(chunks)
        ],
        axis=0,
    )
    row_lane = lax.broadcasted_iota(jnp.int32, (1, 128), 1)
    per_tile = 128 // agents
    start = 0
    for r, j in block_order(group, chunks):
        for first in range(0, steps, per_tile):
            both = [None, None]
            for i in range(per_tile):
                for f in (0, 1):
                    moved = pltpu.roll(tiles[first + i, r][f], ((i - j) * agents) % 128, 1)
                    both[f] = moved if i == 0 else jnp.where(row_lane >= i * agents, moved, both[f])
            order, present = both
            alive = jnp.where(now < present, order, 1e9)
            visible = (alive < own) | (order == own)
            bias[:, start : start + 128] = jnp.where(visible, 0.0, -1e30)
            start += 128


def rows_of(parts, ks, agents, columns):
    return jnp.concatenate([part[agents * k : agents * (k + 1), columns] for k in ks for part in parts], axis=0)


def pair_stages(queries_of, blocks, bias, top_of, low):
    width = blocks[0].shape[1] // 2 // 128 * 128

    def products(pair):
        queries = queries_of(pair)
        zeros = jnp.zeros_like(queries)
        stacked = jnp.concatenate([jnp.where(low, queries, zeros), jnp.where(low, zeros, queries)], axis=0)
        key = jnp.concatenate([block[:, 128 * pair : 128 * pair + 128] for block in blocks], axis=0)
        return dot_t(stacked, key)

    def weigh(pair, scores):
        rows, keys = scores.shape[0] // 2, scores.shape[1]
        tops, weights = [], []
        for half in range(2):
            here = scores[half * rows : (half + 1) * rows] * (LOG2E * HEAD ** (-0.5)) + bias
            highest = jnp.broadcast_to(jnp.max(here, axis=1, keepdims=True), (rows, 128))
            if top_of is not None:
                highest = jnp.maximum(highest, top_of(pair, half))
            tops.append(highest)
            wide = jnp.concatenate([highest] * (keys // 128), axis=1)
            weights.append(jnp.exp2(here - wide).astype(jnp.bfloat16))
        return tops, jnp.concatenate(weights, axis=0)

    def sums(pair, made):
        tops, weights = made
        start = width + 128 * pair
        value = jnp.concatenate([block[:, start : start + 128] for block in blocks], axis=0)
        return tops, dot(weights, jnp.concatenate([value, jnp.ones(value.shape, jnp.bfloat16)], axis=1))

    return [products, weigh, sums]


def merged(low, total):
    rows = total.shape[0] // 2
    return jnp.where(low, total[:rows], total[rows:])


def early_kernel(ks, steps, chunks, group, query, attn_in, w_query, *refs):
    count = group + chunks - 1
    blocks, (own_query, bias, number, weight, top_low, top_high) = refs[:count], refs[count:]
    own_query[...] = dot(attn_in[...], w_query[...]).astype(jnp.bfloat16)
    rows, width = number.shape
    write_mask(steps, chunks, query.shape[0] // steps, width, blocks[:group], bias)
    agents = rows // (len(ks) * chunks)
    low = lax.broadcasted_iota(jnp.int32, (rows, 128), 1) < HEAD
    keys = sum(block.shape[0] for block in blocks)
    here = bias[ks[0] * agents * chunks : ks[0] * agents * chunks + rows, :keys]

    def columns(pair):
        return slice(128 * pair, 128 * pair + 128)

    def keep(pair, made):
        tops, total = made
        number[:, columns(pair)] = merged(low, total[:, :128])
        weight[:, columns(pair)] = merged(low, total[:, 128:])
        top_low[:, columns(pair)] = tops[0]
        top_high[:, columns(pair)] = tops[1]

    stages = pair_stages(lambda pair: rows_of((query, own_query), ks, agents, columns(pair)), blocks, here, None, low)
    run_pairs(width // 128, 1, [*stages, keep])


def early(ks, steps, group, query, attn_in, w_query, blocks):
    count, width = query.shape
    rows = count * CHUNKS
    state = pltpu.VMEM((len(ks) * rows // steps, width), jnp.float32)
    return pl.pallas_call(
        functools.partial(early_kernel, ks, steps, CHUNKS, group),
        out_shape=[jax.ShapeDtypeStruct(query.shape, jnp.bfloat16), pltpu.VMEM((rows, rows * group), jnp.float32)]
        + [state] * 4,
        in_specs=[VMEM] * (3 + len(blocks)),
        out_specs=[VMEM] * 6,
        compiler_params=pltpu.CompilerParams(vmem_limit_bytes=16 * MIB),
        cost_estimate=cost(0),
        name="early",
    )(query, attn_in, pinned(w_query), *blocks)


def attend_kernel(ks, chunks, count, begun, skipped, *refs):
    mine = 1 + len(ks) * (chunks - 1)
    queries, seconds, (w_output, bias) = refs[:chunks], refs[chunks : chunks + mine], refs[chunks + mine : chunks + mine + 2]
    rest = refs[chunks + mine + 2 :]
    blocks, state = rest[:count], rest[count : count + begun]
    outs = rest[count + begun :]
    width, agents = w_output.shape[1], queries[0].shape[0] // 4
    rows = len(ks) * chunks * agents
    low = lax.broadcasted_iota(jnp.int32, (rows, 128), 1) < HEAD
    keys = sum(block.shape[0] for block in blocks)
    here = bias[ks[0] * agents * chunks : ks[0] * agents * chunks + rows, bias.shape[1] - keys :]
    begun_rows = slice(skipped, skipped + rows)

    def columns(pair):
        return slice(128 * pair, 128 * pair + 128)

    residual = []
    for i, k in enumerate(ks):
        residual += [seconds[0][agents * k : agents * (k + 1)]]
        residual += [piece[...] for piece in seconds[1 + i * (chunks - 1) : 1 + (i + 1) * (chunks - 1)]]
    result = [jnp.concatenate(residual, axis=0).astype(jnp.float32)]

    def keep(pair, made):
        tops, total = made
        number, weight = merged(low, total[:, :128]), merged(low, total[:, 128:])
        if begun:
            drop = [state[2 + half][begun_rows, columns(pair)] - tops[half] for half in range(2)]
            shrink = jnp.exp2(jnp.where(low, *drop))
            number = number + state[0][begun_rows, columns(pair)] * shrink
            weight = weight + state[1][begun_rows, columns(pair)] * shrink
        return (number / weight).astype(jnp.bfloat16)

    waiting = []

    def output(pair, attended):
        waiting.append(attended)
        if len(waiting) == 2:
            features = slice(128 * (pair - 1), 128 * (pair + 1))
            result[0] = result[0] + dot(jnp.concatenate(waiting, axis=1), w_output[features, :])
            waiting.clear()

    stages = pair_stages(
        lambda pair: rows_of(queries, ks, agents, columns(pair)),
        blocks,
        here,
        (lambda pair, half: state[2 + half][begun_rows, columns(pair)]) if begun else None,
        low,
    )
    run_pairs(width // 128, 2 if begun else 1, [*stages, keep, output])
    for i in range(len(ks)):
        outs[i][...] = result[0][i * agents * chunks : (i + 1) * agents * chunks].astype(jnp.bfloat16)


def attend(ks, queries, seconds, w_output, bias, blocks, state, skipped, agents, microseconds):
    width = queries[0].shape[1]
    piece = jax.ShapeDtypeStruct((agents, width), jnp.bfloat16)
    return pl.pallas_call(
        functools.partial(attend_kernel, ks, len(queries), len(blocks), len(state), skipped),
        out_shape=[piece] * len(ks),
        in_specs=[VMEM] * (len(queries) + len(seconds) + 2 + len(blocks) + len(state)),
        out_specs=[VMEM] * len(ks),
        compiler_params=pltpu.CompilerParams(vmem_limit_bytes=16 * MIB),
        cost_estimate=cost(microseconds),
        name="attend",
    )(*queries, *seconds, pinned(w_output), pinned(bias), *blocks, *[pinned(x) for x in state])


def put_back_kernel(steps, group, *refs):
    pieces, out, sem = refs[:steps][::-1], refs[steps], refs[steps + 1]
    spot = lax.axis_index("agent")
    half = pieces[0].shape[0] // 2
    copies = []
    for k in range(steps):
        target = out.at[(spot // group) ^ away(k, steps, spot % group)]
        for rows in (pl.ds(0, half), pl.ds(half, half)):
            copies.append(pltpu.make_async_copy(pieces[k].at[rows], target.at[rows], sem.at[len(copies)]))
    for copy in copies:
        copy.start()
    for copy in copies:
        copy.wait()


def put_back(group, pieces, shape):
    return pl.pallas_call(
        functools.partial(put_back_kernel, shape[0], group),
        out_shape=jax.ShapeDtypeStruct(shape, jnp.bfloat16),
        in_specs=[VMEM] * len(pieces),
        out_specs=ANY,
        scratch_shapes=[pltpu.SemaphoreType.DMA((2 * len(pieces),))],
        compiler_params=pltpu.CompilerParams(vmem_limit_bytes=4 * MIB),
        cost_estimate=cost(0),
        name="put_back",
    )(*pieces)


def after(x, *others):
    return lax.optimization_barrier((x, *others))[0]


def per_device(
    tokens,
    conv_taps,
    norm_first,
    norm_second,
    norm_third,
    w_in,
    w_out,
    w_query,
    w_key,
    w_value,
    w_output,
    agent_order,
    present_steps,
):
    steps, agents, width = tokens.shape
    tm_count, count = lax.axis_size("tm"), lax.axis_size("agent")
    group = count // steps
    part = agents // CHUNKS
    assert group * steps == count and steps == 4 and 128 % part == 0 and CHUNKS == 2 and group > 1

    def across(x, k):
        if k == steps - 1:
            return x
        pairs = [(i, ((i // group) ^ away(k, steps, i % group)) * group + i % group) for i in range(count)]
        return lax.ppermute(x, "agent", pairs)

    def within(x, r):
        return lax.ppermute(x, "agent", [(i, (i // group) * group + ((i % group) ^ r)) for i in range(count)])

    first_part = split(tokens)
    second_part, *partials, tail, taps, gain_first, gain_second, gain_third = stage(
        tokens,
        first_part,
        conv_taps,
        norm_first.reshape(1, width),
        agent_order.reshape(1, agents),
        present_steps.reshape(1, agents),
        [conv_taps] + [x.reshape(1, width) for x in (norm_first, norm_second, norm_third)],
    )
    halos = [lax.ppermute(x, "tm", [(i, (i + 1) % tm_count) for i in range(tm_count)]) for x in (first_part, second_part)]
    halos[0] = after(halos[0], tail)
    made = conv(group, halos[0], partials[0], taps, gain_first, tail)
    last = made[-1]
    pieces = [[across(made[k], k) for k in range(steps)]]
    for j in range(1, CHUNKS):
        halos[j] = after(halos[j], last)
        made = list(front(group, halos[j], partials[j], taps, (gain_first, gain_second), w_in, w_out))
        last = made[-1]
        made[steps - 2] = after(made[steps - 2], pieces[j - 1][0])
        pieces.append([across(made[k], k) for k in range(steps)])
    pieces[0][-1] = after(pieces[0][-1], last)
    query, keyval, second = feed(pieces[0], (gain_second, gain_third), (w_in, w_out, w_key, w_value, w_query))
    blocks = {(0, 0): keyval, **{(r, 0): within(keyval, r) for r in range(1, group)}}
    attn_in, keyval = project(pieces[1], gain_third, (w_key, w_value))
    keyval = after(keyval, *blocks.values())
    blocks.update({(0, 1): keyval, **{(r, 1): within(keyval, r) for r in range(1, group)}})
    blocks = [blocks[spot] for spot in block_order(group, CHUNKS)]
    ready = group + CHUNKS - 1
    far_ks, near_ks = (0, 1), (2, 3)
    own_query, bias, *state = early(far_ks, steps, group, query, attn_in, w_query, blocks[:ready])

    def finish(ks, blocks, state, skipped, microseconds):
        seconds = [second] + [pieces[j][k] for k in ks for j in range(1, CHUNKS)]
        return attend(
            ks, (query, own_query), seconds, w_output, bias, blocks, state, skipped, agents, microseconds
        )

    late = blocks[ready:]
    results = [*finish(far_ks, late, state, 0, 0), *finish(near_ks, blocks, [], 0, 10)]
    return put_back(group, [across(results[k], k) for k in reversed(range(steps))], tokens.shape)


def solution(mesh):
    in_specs = (P("tm", "agent", None),) + (P(),) * 10 + (P("agent"), P("agent"))
    return jax.shard_map(
        per_device, mesh=mesh, in_specs=in_specs, out_specs=P("tm", "agent", None), check_vma=False
    )
```

```python
import functools

import jax
import jax.numpy as jnp
from jax import lax
from jax.experimental import pallas as pl
from jax.experimental.pallas import tpu as pltpu
from jax.sharding import PartitionSpec as P

HEAD = 64
CHUNKS = 2
RADIX = 32
EPS = 1e-05
LOG2E = 1.4426950408889634
MIB = 1024 * 1024
VMEM = pl.BlockSpec(memory_space=pltpu.VMEM)
ANY = pl.BlockSpec(memory_space=pl.ANY)
HBM = pl.BlockSpec(memory_space=pltpu.HBM)


def pinned(x):
    return pltpu.with_memory_space_constraint(x, pltpu.VMEM)


def far(x):
    return pltpu.with_memory_space_constraint(x, pltpu.HBM)


def cost(microseconds):
    return pl.CostEstimate(
        flops=int(1.1e9 * microseconds) + 10**6, bytes_accessed=int(3.5e6 * microseconds) + 10**4, transcendentals=0
    )


def away(k, steps, member):
    odd = member % 2
    even_order, odd_order = (3, 2, 1), (2, 1, 3)
    return 0 if k == steps - 1 else even_order[k] * (1 - odd) + odd_order[k] * odd


def dot(a, b):
    return jnp.dot(a, b, preferred_element_type=jnp.float32)


def dot_t(a, b):
    return lax.dot_general(a, b, (((1,), (1,)), ((), ())), preferred_element_type=jnp.float32)


def norm_scale(values):
    return lax.rsqrt(jnp.mean(values * values, axis=-1, keepdims=True) + EPS)


def gelu(x):
    return 0.5 * x * (1.0 + lax.erf(x * 0.7071067811865476))


def part_copies(tokens, part, target, sem):
    steps, agents = target.shape[:2]
    return [
        pltpu.make_async_copy(tokens.at[step, pl.ds(part * agents, agents)], target.at[step], sem.at[step])
        for step in range(steps)
    ]


def split_kernel(tokens, out, sem):
    copies = part_copies(tokens, 0, out, sem)
    for copy in copies:
        copy.start()
    for copy in copies:
        copy.wait()


def split(tokens):
    steps, agents, width = tokens.shape
    return pl.pallas_call(
        split_kernel,
        out_shape=pltpu.VMEM((steps, agents // CHUNKS, width), tokens.dtype),
        in_specs=[HBM],
        out_specs=VMEM,
        scratch_shapes=[pltpu.SemaphoreType.DMA((steps,))],
        compiler_params=pltpu.CompilerParams(vmem_limit_bytes=4 * MIB),
        cost_estimate=cost(0),
        name="split",
    )(far(tokens))


def stage_kernel(count, taps, gain, order, present, tokens, first_part, *rest):
    sources, rest = rest[:count], rest[count:]
    second_part, partials, tail, targets = rest[0], rest[1:3], rest[3], rest[4 : 4 + count]
    taps_here, gain_here, order_here, present_here, normed, facts, part_sem, sem = rest[4 + count :]
    pairs = [
        (taps, taps_here),
        (gain, gain_here),
        (order, order_here),
        (present, present_here),
        *zip(sources, targets),
    ]
    copies = [pltpu.make_async_copy(source, target, sem.at[i]) for i, (source, target) in enumerate(pairs)]
    later = part_copies(tokens, 1, second_part, part_sem)
    for copy in copies + later:
        copy.start()
    for copy in copies:
        copy.wait()
    agents = order.shape[1]
    facts[...] = jnp.zeros(facts.shape, jnp.float32)
    facts[0:1, :agents] = (order_here[...] // RADIX).astype(jnp.float32)
    facts[1:2, :agents] = (order_here[...] % RADIX).astype(jnp.float32)
    facts[2:3, :agents] = present_here[...].astype(jnp.float32)
    tail[...] = facts[...].astype(jnp.bfloat16)
    steps, reach = first_part.shape[0], taps.shape[0] - 1
    gains = gain_here[...]
    for j, part in enumerate((first_part, second_part)):
        for step in range(steps):
            if j == 1:
                later[step].wait()
            values = part[step].astype(jnp.float32)
            normed[step] = values * norm_scale(values) * gains
            total = values
            for lag in range(min(step, reach) + 1):
                total = total + taps_here[lag : lag + 1, :] * normed[step - lag]
            partials[j][step] = total


def stage(tokens, first_part, taps, gain, order, present, arrays):
    steps, part, width = first_part.shape
    inputs = (taps, gain, order, present)
    return pl.pallas_call(
        functools.partial(stage_kernel, len(arrays)),
        out_shape=[pltpu.VMEM(first_part.shape, first_part.dtype)]
        + [pltpu.VMEM((steps, part, width), jnp.float32)] * CHUNKS
        + [pltpu.VMEM((part, 128), jnp.bfloat16)]
        + [pltpu.VMEM(x.shape, x.dtype) for x in arrays],
        in_specs=[HBM] * (len(inputs) + 1) + [VMEM] + [HBM] * len(arrays),
        out_specs=[VMEM] * (CHUNKS + 2 + len(arrays)),
        scratch_shapes=[pltpu.VMEM(x.shape, x.dtype) for x in inputs]
        + [
            pltpu.VMEM((steps, part, width), jnp.float32),
            pltpu.VMEM((part, 128), jnp.float32),
            pltpu.SemaphoreType.DMA((steps,)),
            pltpu.SemaphoreType.DMA((len(inputs) + len(arrays),)),
        ],
        compiler_params=pltpu.CompilerParams(vmem_limit_bytes=8 * MIB),
        cost_estimate=cost(30),
        name="stage",
    )(*[far(x) for x in (*inputs, tokens)], pinned(first_part), *[far(x) for x in arrays])


def run_pairs(pairs, lead, stages):
    held = [{} for _ in stages]
    for turn in range(pairs + lead * (len(stages) - 1)):
        for i, stage in enumerate(stages):
            pair = turn - lead * i
            if 0 <= pair < pairs:
                held[i][pair] = stage(pair, held[i - 1].pop(pair)) if i else stage(pair)


def mixed_rows(halo, partial, taps, gain, normed, first):
    steps, agents = halo.shape[:2]
    reach = taps.shape[0] - 1
    gains = gain[...] * (lax.axis_index("tm") > 0).astype(jnp.float32)
    for step in range(steps):
        values = halo[step].astype(jnp.float32)
        normed[step] = values * norm_scale(values) * gains
    for step in range(steps):
        total = partial[step]
        for lag in range(step + 1, reach + 1):
            total = total + taps[lag : lag + 1, :] * normed[steps + step - lag]
        first[step * agents : (step + 1) * agents, :] = total.astype(jnp.bfloat16).astype(first.dtype)


def feed_forward(rows, gain, w_in, w_out):
    inner = (rows * norm_scale(rows) * gain[...]).astype(jnp.bfloat16)
    tile, total = 512, [rows]

    def enter(i):
        return dot(inner, w_in[:, i * tile : (i + 1) * tile])

    def activate(i, products):
        return gelu(products).astype(jnp.bfloat16)

    def leave(i, hidden):
        total[0] = total[0] + dot(hidden, w_out[i * tile : (i + 1) * tile, :])

    run_pairs(w_in.shape[1] // tile, 1, [enter, activate, leave])
    return total[0].astype(jnp.bfloat16)


def to_keys(second, gain, w_key, w_value, keyval):
    width = second.shape[1]
    values = second.astype(jnp.float32)
    attn_in = (values * norm_scale(values) * gain[...]).astype(jnp.bfloat16)
    keyval[:, :width] = dot(attn_in, w_key[...]).astype(jnp.bfloat16)
    keyval[:, width : 2 * width] = dot(attn_in, w_value[...]).astype(jnp.bfloat16)
    return attn_in


def conv_kernel(group, halo, partial, taps, gain, tail, *rest):
    steps, agents, width = halo.shape
    outs = rest[:steps]
    normed, first = rest[steps:]
    mixed_rows(halo, partial, taps, gain, normed, first)
    spot = lax.axis_index("agent")
    for k in range(steps):
        step = (spot // group) ^ away(k, steps, spot % group)
        outs[k][:, :width] = first[pl.ds(pl.multiple_of(step * agents, agents), agents), :].astype(jnp.bfloat16)
        outs[k][:, width:] = tail[...]


def conv(group, halo, partial, taps, gain, tail):
    steps, agents, width = halo.shape
    return pl.pallas_call(
        functools.partial(conv_kernel, group),
        out_shape=[jax.ShapeDtypeStruct((agents, width + tail.shape[1]), jnp.bfloat16)] * steps,
        in_specs=[VMEM] * 5,
        out_specs=[VMEM] * steps,
        scratch_shapes=[
            pltpu.VMEM((steps, agents, width), jnp.float32),
            pltpu.VMEM((steps * agents, width), jnp.float32),
        ],
        compiler_params=pltpu.CompilerParams(vmem_limit_bytes=8 * MIB),
        cost_estimate=cost(0),
        name="conv",
    )(halo, *[pinned(x) for x in (partial, taps, gain, tail)])


def front_kernel(group, halo, partial, taps, gain_first, gain_second, w_in, w_out, *rest):
    steps, agents, width = halo.shape
    outs = rest[:steps]
    normed, first, second = rest[steps:]
    mixed_rows(halo, partial, taps, gain_first, normed, first)
    result = feed_forward(first[...], gain_second, w_in, w_out)
    for step in range(steps):
        second[step] = result[step * agents : (step + 1) * agents]
    spot = lax.axis_index("agent")
    for k in range(steps):
        outs[k][...] = second[(spot // group) ^ away(k, steps, spot % group)]


def front(group, halo, partial, taps, gains, w_in, w_out):
    steps, agents, width = halo.shape
    rows = steps * agents
    return pl.pallas_call(
        functools.partial(front_kernel, group),
        out_shape=[jax.ShapeDtypeStruct((agents, width), jnp.bfloat16)] * steps,
        in_specs=[VMEM] * 7,
        out_specs=[VMEM] * steps,
        scratch_shapes=[
            pltpu.VMEM((steps, agents, width), jnp.float32),
            pltpu.VMEM((rows, width), jnp.float32),
            pltpu.VMEM((steps, agents, width), jnp.bfloat16),
        ],
        compiler_params=pltpu.CompilerParams(vmem_limit_bytes=12 * MIB),
        cost_estimate=cost(0),
        name="front",
    )(halo, *[pinned(x) for x in (partial, taps, *gains, w_in, w_out)])


def feed_kernel(count, *refs):
    pieces = refs[:count]
    gain_second, gain_third, w_in, w_out, w_key, w_value, w_query = refs[count : count + 7]
    query, keyval, second = refs[count + 7 :]
    width = gain_second.shape[1]
    agents = pieces[0].shape[0]
    for k in range(count):
        keyval[agents * k : agents * (k + 1), 2 * width :] = pieces[k][:, width:]
    first = jnp.concatenate([piece[:, :width].astype(jnp.float32) for piece in pieces], axis=0)
    result = feed_forward(first, gain_second, w_in, w_out)
    second[...] = result
    attn_in = to_keys(result, gain_third, w_key, w_value, keyval)
    query[...] = dot(attn_in, w_query[...]).astype(jnp.bfloat16)


def feed(pieces, gains, weights):
    rows = sum(piece.shape[0] for piece in pieces)
    width = gains[0].shape[1]
    return pl.pallas_call(
        functools.partial(feed_kernel, len(pieces)),
        out_shape=[
            jax.ShapeDtypeStruct((rows, width), jnp.bfloat16),
            jax.ShapeDtypeStruct((rows, width + pieces[0].shape[1]), jnp.bfloat16),
            jax.ShapeDtypeStruct((rows, width), jnp.bfloat16),
        ],
        in_specs=[VMEM] * (len(pieces) + 7),
        out_specs=[VMEM] * 3,
        compiler_params=pltpu.CompilerParams(vmem_limit_bytes=12 * MIB),
        cost_estimate=cost(0),
        name="feed",
    )(*pieces, *[pinned(x) for x in (*gains, *weights)])


def project_kernel(count, *refs):
    pieces = refs[:count][::-1]
    gain, w_key, w_value, attn_in, keyval = refs[count:]
    second = jnp.concatenate([piece[...] for piece in pieces], axis=0)
    attn_in[...] = to_keys(second, gain, w_key, w_value, keyval)


def project(pieces, gain, weights):
    rows = sum(piece.shape[0] for piece in pieces)
    width = gain.shape[1]
    return pl.pallas_call(
        functools.partial(project_kernel, len(pieces)),
        out_shape=[
            jax.ShapeDtypeStruct((rows, width), jnp.bfloat16),
            jax.ShapeDtypeStruct((rows, 2 * width), jnp.bfloat16),
        ],
        in_specs=[VMEM] * (len(pieces) + 3),
        out_specs=[VMEM] * 2,
        compiler_params=pltpu.CompilerParams(vmem_limit_bytes=8 * MIB),
        cost_estimate=cost(25),
        name="project",
    )(*reversed(pieces), *[pinned(x) for x in (gain, *weights)])


def block_order(group, chunks):
    early = [(r, 0) for r in range(group)] + [(0, j) for j in range(1, chunks)]
    return early + [(r, j) for j in range(1, chunks) for r in range(1, group)]


def write_mask(steps, chunks, agents, width, blocks, bias):
    group = len(blocks)
    now = (lax.axis_index("tm") * steps + lax.axis_index("agent") // group).astype(jnp.float32)
    lane = lax.broadcasted_iota(jnp.int32, (agents, 128), 1)
    sublane = lax.broadcasted_iota(jnp.int32, (agents, 128), 0)
    tiles = {}
    for r in range(group):
        for k in range(steps):
            tile = blocks[r][agents * k : agents * (k + 1), 2 * width :].astype(jnp.float32)
            tiles[k, r] = (tile[0:1] * RADIX + tile[1:2], tile[2:3])
    own = jnp.concatenate(
        [
            jnp.sum(jnp.where(lane == sublane + j * agents, tiles[k, 0][0], 0.0), axis=1, keepdims=True)
            for k in range(steps)
            for j in range(chunks)
        ],
        axis=0,
    )
    row_lane = lax.broadcasted_iota(jnp.int32, (1, 128), 1)
    per_tile = 128 // agents
    start = 0
    for r, j in block_order(group, chunks):
        for first in range(0, steps, per_tile):
            both = [None, None]
            for i in range(per_tile):
                for f in (0, 1):
                    moved = pltpu.roll(tiles[first + i, r][f], ((i - j) * agents) % 128, 1)
                    both[f] = moved if i == 0 else jnp.where(row_lane >= i * agents, moved, both[f])
            order, present = both
            alive = jnp.where(now < present, order, 1e9)
            visible = (alive < own) | (order == own)
            bias[:, start : start + 128] = jnp.where(visible, 0.0, -1e30)
            start += 128


def rows_of(parts, ks, agents, columns):
    return jnp.concatenate([part[agents * k : agents * (k + 1), columns] for k in ks for part in parts], axis=0)


def pair_stages(queries_of, blocks, bias, top_of, low):
    width = blocks[0].shape[1] // 2 // 128 * 128

    def products(pair):
        queries = queries_of(pair)
        zeros = jnp.zeros_like(queries)
        stacked = jnp.concatenate([jnp.where(low, queries, zeros), jnp.where(low, zeros, queries)], axis=0)
        key = jnp.concatenate([block[:, 128 * pair : 128 * pair + 128] for block in blocks], axis=0)
        return dot_t(stacked, key)

    def weigh(pair, scores):
        rows, keys = scores.shape[0] // 2, scores.shape[1]
        tops, weights = [], []
        for half in range(2):
            here = scores[half * rows : (half + 1) * rows] * (LOG2E * HEAD ** (-0.5)) + bias
            highest = jnp.broadcast_to(jnp.max(here, axis=1, keepdims=True), (rows, 128))
            if top_of is not None:
                highest = jnp.maximum(highest, top_of(pair, half))
            tops.append(highest)
            wide = jnp.concatenate([highest] * (keys // 128), axis=1)
            weights.append(jnp.exp2(here - wide).astype(jnp.bfloat16))
        return tops, jnp.concatenate(weights, axis=0)

    def sums(pair, made):
        tops, weights = made
        start = width + 128 * pair
        value = jnp.concatenate([block[:, start : start + 128] for block in blocks], axis=0)
        return tops, dot(weights, jnp.concatenate([value, jnp.ones(value.shape, jnp.bfloat16)], axis=1))

    return [products, weigh, sums]


def merged(low, total):
    rows = total.shape[0] // 2
    return jnp.where(low, total[:rows], total[rows:])


def early_kernel(ks, steps, chunks, group, query, attn_in, w_query, *refs):
    count = group + chunks - 1
    blocks, (own_query, bias, number, weight, top_low, top_high) = refs[:count], refs[count:]
    own_query[...] = dot(attn_in[...], w_query[...]).astype(jnp.bfloat16)
    rows, width = number.shape
    write_mask(steps, chunks, query.shape[0] // steps, width, blocks[:group], bias)
    agents = rows // (len(ks) * chunks)
    low = lax.broadcasted_iota(jnp.int32, (rows, 128), 1) < HEAD
    keys = sum(block.shape[0] for block in blocks)
    here = bias[ks[0] * agents * chunks : ks[0] * agents * chunks + rows, :keys]

    def columns(pair):
        return slice(128 * pair, 128 * pair + 128)

    def keep(pair, made):
        tops, total = made
        number[:, columns(pair)] = merged(low, total[:, :128])
        weight[:, columns(pair)] = merged(low, total[:, 128:])
        top_low[:, columns(pair)] = tops[0]
        top_high[:, columns(pair)] = tops[1]

    stages = pair_stages(lambda pair: rows_of((query, own_query), ks, agents, columns(pair)), blocks, here, None, low)
    run_pairs(width // 128, 1, [*stages, keep])


def early(ks, steps, group, query, attn_in, w_query, blocks):
    count, width = query.shape
    rows = count * CHUNKS
    state = pltpu.VMEM((len(ks) * rows // steps, width), jnp.float32)
    return pl.pallas_call(
        functools.partial(early_kernel, ks, steps, CHUNKS, group),
        out_shape=[jax.ShapeDtypeStruct(query.shape, jnp.bfloat16), pltpu.VMEM((rows, rows * group), jnp.float32)]
        + [state] * 4,
        in_specs=[VMEM] * (3 + len(blocks)),
        out_specs=[VMEM] * 6,
        compiler_params=pltpu.CompilerParams(vmem_limit_bytes=16 * MIB),
        cost_estimate=cost(0),
        name="early",
    )(query, attn_in, pinned(w_query), *blocks)


def attend_kernel(ks, chunks, count, begun, skipped, *refs):
    mine = 1 + len(ks) * (chunks - 1)
    queries, seconds, (w_output, bias) = refs[:chunks], refs[chunks : chunks + mine], refs[chunks + mine : chunks + mine + 2]
    rest = refs[chunks + mine + 2 :]
    blocks, state = rest[:count], rest[count : count + begun]
    outs = rest[count + begun :]
    width, agents = w_output.shape[1], queries[0].shape[0] // 4
    rows = len(ks) * chunks * agents
    low = lax.broadcasted_iota(jnp.int32, (rows, 128), 1) < HEAD
    keys = sum(block.shape[0] for block in blocks)
    here = bias[ks[0] * agents * chunks : ks[0] * agents * chunks + rows, bias.shape[1] - keys :]
    begun_rows = slice(skipped, skipped + rows)

    def columns(pair):
        return slice(128 * pair, 128 * pair + 128)

    residual = []
    for i, k in enumerate(ks):
        residual += [seconds[0][agents * k : agents * (k + 1)]]
        residual += [piece[...] for piece in seconds[1 + i * (chunks - 1) : 1 + (i + 1) * (chunks - 1)]]
    result = [jnp.concatenate(residual, axis=0).astype(jnp.float32)]

    def keep(pair, made):
        tops, total = made
        number, weight = merged(low, total[:, :128]), merged(low, total[:, 128:])
        if begun:
            drop = [state[2 + half][begun_rows, columns(pair)] - tops[half] for half in range(2)]
            shrink = jnp.exp2(jnp.where(low, *drop))
            number = number + state[0][begun_rows, columns(pair)] * shrink
            weight = weight + state[1][begun_rows, columns(pair)] * shrink
        return (number / weight).astype(jnp.bfloat16)

    waiting, together = [], 2 if begun else width // 128

    def output(pair, attended):
        waiting.append(attended)
        if len(waiting) == together:
            features = slice(128 * (pair + 1 - together), 128 * (pair + 1))
            result[0] = result[0] + dot(jnp.concatenate(waiting, axis=1), w_output[features, :])
            waiting.clear()

    stages = pair_stages(
        lambda pair: rows_of(queries, ks, agents, columns(pair)),
        blocks,
        here,
        (lambda pair, half: state[2 + half][begun_rows, columns(pair)]) if begun else None,
        low,
    )
    run_pairs(width // 128, 2 if begun else 1, [*stages, keep, output])
    for i in range(len(ks)):
        outs[i][...] = result[0][i * agents * chunks : (i + 1) * agents * chunks].astype(jnp.bfloat16)


def attend(ks, queries, seconds, w_output, bias, blocks, state, skipped, agents, microseconds):
    width = queries[0].shape[1]
    piece = jax.ShapeDtypeStruct((agents, width), jnp.bfloat16)
    return pl.pallas_call(
        functools.partial(attend_kernel, ks, len(queries), len(blocks), len(state), skipped),
        out_shape=[piece] * len(ks),
        in_specs=[VMEM] * (len(queries) + len(seconds) + 2 + len(blocks) + len(state)),
        out_specs=[VMEM] * len(ks),
        compiler_params=pltpu.CompilerParams(vmem_limit_bytes=16 * MIB),
        cost_estimate=cost(microseconds),
        name="attend",
    )(*queries, *seconds, pinned(w_output), pinned(bias), *blocks, *[pinned(x) for x in state])


def put_back_kernel(steps, group, *refs):
    pieces, out, sem = refs[:steps][::-1], refs[steps], refs[steps + 1]
    spot = lax.axis_index("agent")
    half = pieces[0].shape[0] // 2
    copies = []
    for k in range(steps):
        target = out.at[(spot // group) ^ away(k, steps, spot % group)]
        for rows in (pl.ds(0, half), pl.ds(half, half)):
            copies.append(pltpu.make_async_copy(pieces[k].at[rows], target.at[rows], sem.at[len(copies)]))
    for copy in copies:
        copy.start()
    for copy in copies:
        copy.wait()


def put_back(group, pieces, shape):
    return pl.pallas_call(
        functools.partial(put_back_kernel, shape[0], group),
        out_shape=jax.ShapeDtypeStruct(shape, jnp.bfloat16),
        in_specs=[VMEM] * len(pieces),
        out_specs=ANY,
        scratch_shapes=[pltpu.SemaphoreType.DMA((2 * len(pieces),))],
        compiler_params=pltpu.CompilerParams(vmem_limit_bytes=4 * MIB),
        cost_estimate=cost(0),
        name="put_back",
    )(*pieces)


def after(x, *others):
    return lax.optimization_barrier((x, *others))[0]


def per_device(
    tokens,
    conv_taps,
    norm_first,
    norm_second,
    norm_third,
    w_in,
    w_out,
    w_query,
    w_key,
    w_value,
    w_output,
    agent_order,
    present_steps,
):
    steps, agents, width = tokens.shape
    tm_count, count = lax.axis_size("tm"), lax.axis_size("agent")
    group = count // steps
    part = agents // CHUNKS
    assert group * steps == count and steps == 4 and 128 % part == 0 and CHUNKS == 2 and group > 1

    def across(x, k):
        if k == steps - 1:
            return x
        pairs = [(i, ((i // group) ^ away(k, steps, i % group)) * group + i % group) for i in range(count)]
        return lax.ppermute(x, "agent", pairs)

    def within(x, r):
        return lax.ppermute(x, "agent", [(i, (i // group) * group + ((i % group) ^ r)) for i in range(count)])

    first_part = split(tokens)
    second_part, *partials, tail, taps, gain_first, gain_second, gain_third = stage(
        tokens,
        first_part,
        conv_taps,
        norm_first.reshape(1, width),
        agent_order.reshape(1, agents),
        present_steps.reshape(1, agents),
        [conv_taps] + [x.reshape(1, width) for x in (norm_first, norm_second, norm_third)],
    )
    halos = [lax.ppermute(x, "tm", [(i, (i + 1) % tm_count) for i in range(tm_count)]) for x in (first_part, second_part)]
    halos[0] = after(halos[0], tail)
    made = conv(group, halos[0], partials[0], taps, gain_first, tail)
    last = made[-1]
    pieces = [[across(made[k], k) for k in range(steps)]]
    for j in range(1, CHUNKS):
        halos[j] = after(halos[j], last)
        made = list(front(group, halos[j], partials[j], taps, (gain_first, gain_second), w_in, w_out))
        last = made[-1]
        made[steps - 2] = after(made[steps - 2], pieces[j - 1][0])
        pieces.append([across(made[k], k) for k in range(steps)])
    pieces[0][-1] = after(pieces[0][-1], last)
    query, keyval, second = feed(pieces[0], (gain_second, gain_third), (w_in, w_out, w_key, w_value, w_query))
    blocks = {(0, 0): keyval, **{(r, 0): within(keyval, r) for r in range(1, group)}}
    attn_in, keyval = project(pieces[1], gain_third, (w_key, w_value))
    keyval = after(keyval, *blocks.values())
    blocks.update({(0, 1): keyval, **{(r, 1): within(keyval, r) for r in range(1, group)}})
    blocks = [blocks[spot] for spot in block_order(group, CHUNKS)]
    ready = group + CHUNKS - 1
    far_ks, near_ks = (0, 1), (2, 3)
    own_query, bias, *state = early(far_ks, steps, group, query, attn_in, w_query, blocks[:ready])

    def finish(ks, blocks, state, skipped, microseconds):
        seconds = [second] + [pieces[j][k] for k in ks for j in range(1, CHUNKS)]
        return attend(
            ks, (query, own_query), seconds, w_output, bias, blocks, state, skipped, agents, microseconds
        )

    late = blocks[ready:]
    results = [*finish(far_ks, late, state, 0, 0), *finish(near_ks, blocks, [], 0, 10)]
    return put_back(group, [across(results[k], k) for k in reversed(range(steps))], tokens.shape)


def solution(mesh):
    in_specs = (P("tm", "agent", None),) + (P(),) * 10 + (P("agent"), P("agent"))
    return jax.shard_map(
        per_device, mesh=mesh, in_specs=in_specs, out_specs=P("tm", "agent", None), check_vma=False
    )
```

```python
import functools

import jax
import jax.numpy as jnp
from jax import lax
from jax.experimental import pallas as pl
from jax.experimental.pallas import tpu as pltpu
from jax.sharding import PartitionSpec as P

HEAD = 64
CHUNKS = 2
RADIX = 32
EPS = 1e-05
LOG2E = 1.4426950408889634
MIB = 1024 * 1024
VMEM = pl.BlockSpec(memory_space=pltpu.VMEM)
ANY = pl.BlockSpec(memory_space=pl.ANY)
HBM = pl.BlockSpec(memory_space=pltpu.HBM)


def pinned(x):
    return pltpu.with_memory_space_constraint(x, pltpu.VMEM)


def far(x):
    return pltpu.with_memory_space_constraint(x, pltpu.HBM)


def cost(microseconds):
    return pl.CostEstimate(
        flops=int(1.1e9 * microseconds) + 10**6, bytes_accessed=int(3.5e6 * microseconds) + 10**4, transcendentals=0
    )


def away(k, steps, member, line):
    if k == steps - 1:
        return 0
    odd, first = member % 2, 1 - jnp.minimum(line, 1) if isinstance(line, jax.Array) else int(line == 0)
    first_order, even_order, odd_order = (3, 2, 1), (2, 3, 1), (2, 1, 3)
    return (first_order[k] * first + even_order[k] * (1 - first)) * (1 - odd) + odd_order[k] * odd


def dot(a, b):
    return jnp.dot(a, b, preferred_element_type=jnp.float32)


def dot_t(a, b):
    return lax.dot_general(a, b, (((1,), (1,)), ((), ())), preferred_element_type=jnp.float32)


def norm_scale(values):
    return lax.rsqrt(jnp.mean(values * values, axis=-1, keepdims=True) + EPS)


def gelu(x):
    return 0.5 * x * (1.0 + lax.erf(x * 0.7071067811865476))


def part_copies(tokens, part, target, sem):
    steps, agents = target.shape[:2]
    return [
        pltpu.make_async_copy(tokens.at[step, pl.ds(part * agents, agents)], target.at[step], sem.at[step])
        for step in range(steps)
    ]


def split_kernel(tokens, out, sem):
    copies = part_copies(tokens, 0, out, sem)
    for copy in copies:
        copy.start()
    for copy in copies:
        copy.wait()


def split(tokens):
    steps, agents, width = tokens.shape
    return pl.pallas_call(
        split_kernel,
        out_shape=pltpu.VMEM((steps, agents // CHUNKS, width), tokens.dtype),
        in_specs=[HBM],
        out_specs=VMEM,
        scratch_shapes=[pltpu.SemaphoreType.DMA((steps,))],
        compiler_params=pltpu.CompilerParams(vmem_limit_bytes=4 * MIB),
        cost_estimate=cost(0),
        name="split",
    )(far(tokens))


def stage_kernel(count, taps, gain, order, present, tokens, first_part, *rest):
    sources, rest = rest[:count], rest[count:]
    second_part, partials, tail, targets = rest[0], rest[1:3], rest[3], rest[4 : 4 + count]
    taps_here, gain_here, order_here, present_here, normed, facts, part_sem, sem = rest[4 + count :]
    pairs = [
        (taps, taps_here),
        (gain, gain_here),
        (order, order_here),
        (present, present_here),
        *zip(sources, targets),
    ]
    copies = [pltpu.make_async_copy(source, target, sem.at[i]) for i, (source, target) in enumerate(pairs)]
    later = part_copies(tokens, 1, second_part, part_sem)
    for copy in copies + later:
        copy.start()
    for copy in copies:
        copy.wait()
    agents = order.shape[1]
    facts[...] = jnp.zeros(facts.shape, jnp.float32)
    facts[0:1, :agents] = (order_here[...] // RADIX).astype(jnp.float32)
    facts[1:2, :agents] = (order_here[...] % RADIX).astype(jnp.float32)
    facts[2:3, :agents] = present_here[...].astype(jnp.float32)
    tail[...] = facts[...].astype(jnp.bfloat16)
    steps, reach = first_part.shape[0], taps.shape[0] - 1
    gains = gain_here[...]
    for j, part in enumerate((first_part, second_part)):
        for step in range(steps):
            if j == 1:
                later[step].wait()
            values = part[step].astype(jnp.float32)
            normed[step] = values * norm_scale(values) * gains
            total = values
            for lag in range(min(step, reach) + 1):
                total = total + taps_here[lag : lag + 1, :] * normed[step - lag]
            partials[j][step] = total


def stage(tokens, first_part, taps, gain, order, present, arrays):
    steps, part, width = first_part.shape
    inputs = (taps, gain, order, present)
    return pl.pallas_call(
        functools.partial(stage_kernel, len(arrays)),
        out_shape=[pltpu.VMEM(first_part.shape, first_part.dtype)]
        + [pltpu.VMEM((steps, part, width), jnp.float32)] * CHUNKS
        + [pltpu.VMEM((part, 128), jnp.bfloat16)]
        + [pltpu.VMEM(x.shape, x.dtype) for x in arrays],
        in_specs=[HBM] * (len(inputs) + 1) + [VMEM] + [HBM] * len(arrays),
        out_specs=[VMEM] * (CHUNKS + 2 + len(arrays)),
        scratch_shapes=[pltpu.VMEM(x.shape, x.dtype) for x in inputs]
        + [
            pltpu.VMEM((steps, part, width), jnp.float32),
            pltpu.VMEM((part, 128), jnp.float32),
            pltpu.SemaphoreType.DMA((steps,)),
            pltpu.SemaphoreType.DMA((len(inputs) + len(arrays),)),
        ],
        compiler_params=pltpu.CompilerParams(vmem_limit_bytes=8 * MIB),
        cost_estimate=cost(30),
        name="stage",
    )(*[far(x) for x in (*inputs, tokens)], pinned(first_part), *[far(x) for x in arrays])


def run_pairs(pairs, lead, stages):
    held = [{} for _ in stages]
    for turn in range(pairs + lead * (len(stages) - 1)):
        for i, stage in enumerate(stages):
            pair = turn - lead * i
            if 0 <= pair < pairs:
                held[i][pair] = stage(pair, held[i - 1].pop(pair)) if i else stage(pair)


def mixed_rows(halo, partial, taps, gain, normed, first):
    steps, agents = halo.shape[:2]
    reach = taps.shape[0] - 1
    gains = gain[...] * (lax.axis_index("tm") > 0).astype(jnp.float32)
    for step in range(steps):
        values = halo[step].astype(jnp.float32)
        normed[step] = values * norm_scale(values) * gains
    for step in range(steps):
        total = partial[step]
        for lag in range(step + 1, reach + 1):
            total = total + taps[lag : lag + 1, :] * normed[steps + step - lag]
        first[step * agents : (step + 1) * agents, :] = total.astype(jnp.bfloat16).astype(first.dtype)


def feed_forward(rows, gain, w_in, w_out):
    inner = (rows * norm_scale(rows) * gain[...]).astype(jnp.bfloat16)
    tile, total = 512, [rows]

    def enter(i):
        return dot(inner, w_in[:, i * tile : (i + 1) * tile])

    def activate(i, products):
        return gelu(products).astype(jnp.bfloat16)

    def leave(i, hidden):
        total[0] = total[0] + dot(hidden, w_out[i * tile : (i + 1) * tile, :])

    run_pairs(w_in.shape[1] // tile, 1, [enter, activate, leave])
    return total[0].astype(jnp.bfloat16)


def to_keys(second, gain, w_key, w_value, keyval):
    width = second.shape[1]
    values = second.astype(jnp.float32)
    attn_in = (values * norm_scale(values) * gain[...]).astype(jnp.bfloat16)
    keyval[:, :width] = dot(attn_in, w_key[...]).astype(jnp.bfloat16)
    keyval[:, width : 2 * width] = dot(attn_in, w_value[...]).astype(jnp.bfloat16)
    return attn_in


def conv_kernel(group, halo, partial, taps, gain, tail, *rest):
    steps, agents, width = halo.shape
    outs = rest[:steps]
    normed, first = rest[steps:]
    mixed_rows(halo, partial, taps, gain, normed, first)
    spot = lax.axis_index("agent")
    for k in range(steps):
        step = (spot // group) ^ away(k, steps, spot % group, lax.axis_index("tm"))
        outs[k][:, :width] = first[pl.ds(pl.multiple_of(step * agents, agents), agents), :].astype(jnp.bfloat16)
        outs[k][:, width:] = tail[...]


def conv(group, halo, partial, taps, gain, tail):
    steps, agents, width = halo.shape
    return pl.pallas_call(
        functools.partial(conv_kernel, group),
        out_shape=[jax.ShapeDtypeStruct((agents, width + tail.shape[1]), jnp.bfloat16)] * steps,
        in_specs=[VMEM] * 5,
        out_specs=[VMEM] * steps,
        scratch_shapes=[
            pltpu.VMEM((steps, agents, width), jnp.float32),
            pltpu.VMEM((steps * agents, width), jnp.float32),
        ],
        compiler_params=pltpu.CompilerParams(vmem_limit_bytes=8 * MIB),
        cost_estimate=cost(0),
        name="conv",
    )(halo, *[pinned(x) for x in (partial, taps, gain, tail)])


def front_kernel(group, halo, partial, taps, gain_first, gain_second, w_in, w_out, *rest):
    steps, agents, width = halo.shape
    outs = rest[:steps]
    normed, first, second = rest[steps:]
    mixed_rows(halo, partial, taps, gain_first, normed, first)
    result = feed_forward(first[...], gain_second, w_in, w_out)
    for step in range(steps):
        second[step] = result[step * agents : (step + 1) * agents]
    spot = lax.axis_index("agent")
    for k in range(steps):
        outs[k][...] = second[(spot // group) ^ away(k, steps, spot % group, lax.axis_index("tm"))]


def front(group, halo, partial, taps, gains, w_in, w_out):
    steps, agents, width = halo.shape
    rows = steps * agents
    return pl.pallas_call(
        functools.partial(front_kernel, group),
        out_shape=[jax.ShapeDtypeStruct((agents, width), jnp.bfloat16)] * steps,
        in_specs=[VMEM] * 7,
        out_specs=[VMEM] * steps,
        scratch_shapes=[
            pltpu.VMEM((steps, agents, width), jnp.float32),
            pltpu.VMEM((rows, width), jnp.float32),
            pltpu.VMEM((steps, agents, width), jnp.bfloat16),
        ],
        compiler_params=pltpu.CompilerParams(vmem_limit_bytes=12 * MIB),
        cost_estimate=cost(0),
        name="front",
    )(halo, *[pinned(x) for x in (partial, taps, *gains, w_in, w_out)])


def feed_kernel(count, *refs):
    pieces = refs[:count]
    gain_second, gain_third, w_in, w_out, w_key, w_value, w_query = refs[count : count + 7]
    query, keyval, second = refs[count + 7 :]
    width = gain_second.shape[1]
    agents = pieces[0].shape[0]
    for k in range(count):
        keyval[agents * k : agents * (k + 1), 2 * width :] = pieces[k][:, width:]
    first = jnp.concatenate([piece[:, :width].astype(jnp.float32) for piece in pieces], axis=0)
    result = feed_forward(first, gain_second, w_in, w_out)
    second[...] = result
    attn_in = to_keys(result, gain_third, w_key, w_value, keyval)
    query[...] = dot(attn_in, w_query[...]).astype(jnp.bfloat16)


def feed(pieces, gains, weights):
    rows = sum(piece.shape[0] for piece in pieces)
    width = gains[0].shape[1]
    return pl.pallas_call(
        functools.partial(feed_kernel, len(pieces)),
        out_shape=[
            jax.ShapeDtypeStruct((rows, width), jnp.bfloat16),
            jax.ShapeDtypeStruct((rows, width + pieces[0].shape[1]), jnp.bfloat16),
            jax.ShapeDtypeStruct((rows, width), jnp.bfloat16),
        ],
        in_specs=[VMEM] * (len(pieces) + 7),
        out_specs=[VMEM] * 3,
        compiler_params=pltpu.CompilerParams(vmem_limit_bytes=12 * MIB),
        cost_estimate=cost(0),
        name="feed",
    )(*pieces, *[pinned(x) for x in (*gains, *weights)])


def project_kernel(count, *refs):
    pieces = refs[:count][::-1]
    gain, w_key, w_value, attn_in, keyval = refs[count:]
    second = jnp.concatenate([piece[...] for piece in pieces], axis=0)
    attn_in[...] = to_keys(second, gain, w_key, w_value, keyval)


def project(pieces, gain, weights):
    rows = sum(piece.shape[0] for piece in pieces)
    width = gain.shape[1]
    return pl.pallas_call(
        functools.partial(project_kernel, len(pieces)),
        out_shape=[
            jax.ShapeDtypeStruct((rows, width), jnp.bfloat16),
            jax.ShapeDtypeStruct((rows, 2 * width), jnp.bfloat16),
        ],
        in_specs=[VMEM] * (len(pieces) + 3),
        out_specs=[VMEM] * 2,
        compiler_params=pltpu.CompilerParams(vmem_limit_bytes=8 * MIB),
        cost_estimate=cost(25),
        name="project",
    )(*reversed(pieces), *[pinned(x) for x in (gain, *weights)])


def block_order(group, chunks):
    early = [(r, 0) for r in range(group)] + [(0, j) for j in range(1, chunks)]
    return early + [(r, j) for j in range(1, chunks) for r in range(1, group)]


def write_mask(steps, chunks, agents, width, blocks, bias):
    group = len(blocks)
    now = (lax.axis_index("tm") * steps + lax.axis_index("agent") // group).astype(jnp.float32)
    lane = lax.broadcasted_iota(jnp.int32, (agents, 128), 1)
    sublane = lax.broadcasted_iota(jnp.int32, (agents, 128), 0)
    tiles = {}
    for r in range(group):
        for k in range(steps):
            tile = blocks[r][agents * k : agents * (k + 1), 2 * width :].astype(jnp.float32)
            tiles[k, r] = (tile[0:1] * RADIX + tile[1:2], tile[2:3])
    own = jnp.concatenate(
        [
            jnp.sum(jnp.where(lane == sublane + j * agents, tiles[k, 0][0], 0.0), axis=1, keepdims=True)
            for k in range(steps)
            for j in range(chunks)
        ],
        axis=0,
    )
    row_lane = lax.broadcasted_iota(jnp.int32, (1, 128), 1)
    per_tile = 128 // agents
    start = 0
    for r, j in block_order(group, chunks):
        for first in range(0, steps, per_tile):
            both = [None, None]
            for i in range(per_tile):
                for f in (0, 1):
                    moved = pltpu.roll(tiles[first + i, r][f], ((i - j) * agents) % 128, 1)
                    both[f] = moved if i == 0 else jnp.where(row_lane >= i * agents, moved, both[f])
            order, present = both
            alive = jnp.where(now < present, order, 1e9)
            visible = (alive < own) | (order == own)
            bias[:, start : start + 128] = jnp.where(visible, 0.0, -1e30)
            start += 128


def rows_of(parts, ks, agents, columns):
    return jnp.concatenate([part[agents * k : agents * (k + 1), columns] for k in ks for part in parts], axis=0)


def pair_stages(queries_of, blocks, bias, top_of, low):
    width = blocks[0].shape[1] // 2 // 128 * 128

    def products(pair):
        queries = queries_of(pair)
        zeros = jnp.zeros_like(queries)
        stacked = jnp.concatenate([jnp.where(low, queries, zeros), jnp.where(low, zeros, queries)], axis=0)
        key = jnp.concatenate([block[:, 128 * pair : 128 * pair + 128] for block in blocks], axis=0)
        return dot_t(stacked, key)

    def weigh(pair, scores):
        rows, keys = scores.shape[0] // 2, scores.shape[1]
        tops, weights = [], []
        for half in range(2):
            here = scores[half * rows : (half + 1) * rows] * (LOG2E * HEAD ** (-0.5)) + bias
            highest = jnp.broadcast_to(jnp.max(here, axis=1, keepdims=True), (rows, 128))
            if top_of is not None:
                highest = jnp.maximum(highest, top_of(pair, half))
            tops.append(highest)
            wide = jnp.concatenate([highest] * (keys // 128), axis=1)
            weights.append(jnp.exp2(here - wide).astype(jnp.bfloat16))
        return tops, jnp.concatenate(weights, axis=0)

    def sums(pair, made):
        tops, weights = made
        start = width + 128 * pair
        value = jnp.concatenate([block[:, start : start + 128] for block in blocks], axis=0)
        return tops, dot(weights, jnp.concatenate([value, jnp.ones(value.shape, jnp.bfloat16)], axis=1))

    return [products, weigh, sums]


def merged(low, total):
    rows = total.shape[0] // 2
    return jnp.where(low, total[:rows], total[rows:])


def early_kernel(ks, steps, chunks, group, query, attn_in, w_query, *refs):
    count = group + chunks - 1
    blocks, (own_query, bias, number, weight, top_low, top_high) = refs[:count], refs[count:]
    own_query[...] = dot(attn_in[...], w_query[...]).astype(jnp.bfloat16)
    rows, width = number.shape
    write_mask(steps, chunks, query.shape[0] // steps, width, blocks[:group], bias)
    agents = rows // (len(ks) * chunks)
    low = lax.broadcasted_iota(jnp.int32, (rows, 128), 1) < HEAD
    keys = sum(block.shape[0] for block in blocks)
    here = bias[ks[0] * agents * chunks : ks[0] * agents * chunks + rows, :keys]

    def columns(pair):
        return slice(128 * pair, 128 * pair + 128)

    def keep(pair, made):
        tops, total = made
        number[:, columns(pair)] = merged(low, total[:, :128])
        weight[:, columns(pair)] = merged(low, total[:, 128:])
        top_low[:, columns(pair)] = tops[0]
        top_high[:, columns(pair)] = tops[1]

    stages = pair_stages(lambda pair: rows_of((query, own_query), ks, agents, columns(pair)), blocks, here, None, low)
    run_pairs(width // 128, 1, [*stages, keep])


def early(ks, steps, group, query, attn_in, w_query, blocks):
    count, width = query.shape
    rows = count * CHUNKS
    state = pltpu.VMEM((len(ks) * rows // steps, width), jnp.float32)
    return pl.pallas_call(
        functools.partial(early_kernel, ks, steps, CHUNKS, group),
        out_shape=[jax.ShapeDtypeStruct(query.shape, jnp.bfloat16), pltpu.VMEM((rows, rows * group), jnp.float32)]
        + [state] * 4,
        in_specs=[VMEM] * (3 + len(blocks)),
        out_specs=[VMEM] * 6,
        compiler_params=pltpu.CompilerParams(vmem_limit_bytes=16 * MIB),
        cost_estimate=cost(0),
        name="early",
    )(query, attn_in, pinned(w_query), *blocks)


def attend_kernel(ks, chunks, count, begun, skipped, *refs):
    mine = 1 + len(ks) * (chunks - 1)
    queries, seconds, (w_output, bias) = refs[:chunks], refs[chunks : chunks + mine], refs[chunks + mine : chunks + mine + 2]
    rest = refs[chunks + mine + 2 :]
    blocks, state = rest[:count], rest[count : count + begun]
    outs = rest[count + begun :]
    width, agents = w_output.shape[1], queries[0].shape[0] // 4
    rows = len(ks) * chunks * agents
    low = lax.broadcasted_iota(jnp.int32, (rows, 128), 1) < HEAD
    keys = sum(block.shape[0] for block in blocks)
    here = bias[ks[0] * agents * chunks : ks[0] * agents * chunks + rows, bias.shape[1] - keys :]
    begun_rows = slice(skipped, skipped + rows)

    def columns(pair):
        return slice(128 * pair, 128 * pair + 128)

    residual = []
    for i, k in enumerate(ks):
        residual += [seconds[0][agents * k : agents * (k + 1)]]
        residual += [piece[...] for piece in seconds[1 + i * (chunks - 1) : 1 + (i + 1) * (chunks - 1)]]
    result = [jnp.concatenate(residual, axis=0).astype(jnp.float32)]

    def keep(pair, made):
        tops, total = made
        number, weight = merged(low, total[:, :128]), merged(low, total[:, 128:])
        if begun:
            drop = [state[2 + half][begun_rows, columns(pair)] - tops[half] for half in range(2)]
            shrink = jnp.exp2(jnp.where(low, *drop))
            number = number + state[0][begun_rows, columns(pair)] * shrink
            weight = weight + state[1][begun_rows, columns(pair)] * shrink
        return (number / weight).astype(jnp.bfloat16)

    waiting, together = [], 2 if begun else width // 128

    def output(pair, attended):
        waiting.append(attended)
        if len(waiting) == together:
            features = slice(128 * (pair + 1 - together), 128 * (pair + 1))
            result[0] = result[0] + dot(jnp.concatenate(waiting, axis=1), w_output[features, :])
            waiting.clear()

    stages = pair_stages(
        lambda pair: rows_of(queries, ks, agents, columns(pair)),
        blocks,
        here,
        (lambda pair, half: state[2 + half][begun_rows, columns(pair)]) if begun else None,
        low,
    )
    run_pairs(width // 128, 2 if begun else 1, [*stages, keep, output])
    for i in range(len(ks)):
        outs[i][...] = result[0][i * agents * chunks : (i + 1) * agents * chunks].astype(jnp.bfloat16)


def attend(ks, queries, seconds, w_output, bias, blocks, state, skipped, agents, microseconds):
    width = queries[0].shape[1]
    piece = jax.ShapeDtypeStruct((agents, width), jnp.bfloat16)
    return pl.pallas_call(
        functools.partial(attend_kernel, ks, len(queries), len(blocks), len(state), skipped),
        out_shape=[piece] * len(ks),
        in_specs=[VMEM] * (len(queries) + len(seconds) + 2 + len(blocks) + len(state)),
        out_specs=[VMEM] * len(ks),
        compiler_params=pltpu.CompilerParams(vmem_limit_bytes=16 * MIB),
        cost_estimate=cost(microseconds),
        name="attend",
    )(*queries, *seconds, pinned(w_output), pinned(bias), *blocks, *[pinned(x) for x in state])


def put_back_kernel(steps, group, *refs):
    pieces, out, sem = refs[:steps][::-1], refs[steps], refs[steps + 1]
    spot = lax.axis_index("agent")
    half = pieces[0].shape[0] // 2
    copies = []
    for k in range(steps):
        target = out.at[(spot // group) ^ away(k, steps, spot % group, lax.axis_index("tm"))]
        for rows in (pl.ds(0, half), pl.ds(half, half)):
            copies.append(pltpu.make_async_copy(pieces[k].at[rows], target.at[rows], sem.at[len(copies)]))
    for copy in copies:
        copy.start()
    for copy in copies:
        copy.wait()


def put_back(group, pieces, shape):
    return pl.pallas_call(
        functools.partial(put_back_kernel, shape[0], group),
        out_shape=jax.ShapeDtypeStruct(shape, jnp.bfloat16),
        in_specs=[VMEM] * len(pieces),
        out_specs=ANY,
        scratch_shapes=[pltpu.SemaphoreType.DMA((2 * len(pieces),))],
        compiler_params=pltpu.CompilerParams(vmem_limit_bytes=4 * MIB),
        cost_estimate=cost(0),
        name="put_back",
    )(*pieces)


def after(x, *others):
    return lax.optimization_barrier((x, *others))[0]


def per_device(
    tokens,
    conv_taps,
    norm_first,
    norm_second,
    norm_third,
    w_in,
    w_out,
    w_query,
    w_key,
    w_value,
    w_output,
    agent_order,
    present_steps,
):
    steps, agents, width = tokens.shape
    tm_count, count = lax.axis_size("tm"), lax.axis_size("agent")
    group = count // steps
    part = agents // CHUNKS
    assert group * steps == count and steps == 4 and 128 % part == 0 and CHUNKS == 2 and group > 1

    def across(x, k):
        if k == steps - 1:
            return x
        pairs = [
            (line * count + i, line * count + ((i // group) ^ away(k, steps, i % group, line)) * group + i % group)
            for line in range(tm_count)
            for i in range(count)
        ]
        return lax.ppermute(x, ("tm", "agent"), pairs)

    def within(x, r):
        return lax.ppermute(x, "agent", [(i, (i // group) * group + ((i % group) ^ r)) for i in range(count)])

    first_part = split(tokens)
    second_part, *partials, tail, taps, gain_first, gain_second, gain_third = stage(
        tokens,
        first_part,
        conv_taps,
        norm_first.reshape(1, width),
        agent_order.reshape(1, agents),
        present_steps.reshape(1, agents),
        [conv_taps] + [x.reshape(1, width) for x in (norm_first, norm_second, norm_third)],
    )
    halos = [lax.ppermute(x, "tm", [(i, (i + 1) % tm_count) for i in range(tm_count)]) for x in (first_part, second_part)]
    halos[0] = after(halos[0], tail)
    made = conv(group, halos[0], partials[0], taps, gain_first, tail)
    last = made[-1]
    pieces = [[across(made[k], k) for k in range(steps)]]
    for j in range(1, CHUNKS):
        halos[j] = after(halos[j], last)
        made = list(front(group, halos[j], partials[j], taps, (gain_first, gain_second), w_in, w_out))
        last = made[-1]
        made[steps - 2] = after(made[steps - 2], pieces[j - 1][0])
        pieces.append([across(made[k], k) for k in range(steps)])
    pieces[0][-1] = after(pieces[0][-1], last)
    query, keyval, second = feed(pieces[0], (gain_second, gain_third), (w_in, w_out, w_key, w_value, w_query))
    blocks = {(0, 0): keyval, **{(r, 0): within(keyval, r) for r in range(1, group)}}
    attn_in, keyval = project(pieces[1], gain_third, (w_key, w_value))
    keyval = after(keyval, *blocks.values())
    blocks.update({(0, 1): keyval, **{(r, 1): within(keyval, r) for r in range(1, group)}})
    blocks = [blocks[spot] for spot in block_order(group, CHUNKS)]
    ready = group + CHUNKS - 1
    far_ks, near_ks = (0, 1), (2, 3)
    own_query, bias, *state = early(far_ks, steps, group, query, attn_in, w_query, blocks[:ready])

    def finish(ks, blocks, state, skipped, microseconds):
        seconds = [second] + [pieces[j][k] for k in ks for j in range(1, CHUNKS)]
        return attend(
            ks, (query, own_query), seconds, w_output, bias, blocks, state, skipped, agents, microseconds
        )

    late = blocks[ready:]
    results = [*finish(far_ks, late, state, 0, 0), *finish(near_ks, blocks, [], 0, 10)]
    return put_back(group, [across(results[k], k) for k in reversed(range(steps))], tokens.shape)


def solution(mesh):
    in_specs = (P("tm", "agent", None),) + (P(),) * 10 + (P("agent"), P("agent"))
    return jax.shard_map(
        per_device, mesh=mesh, in_specs=in_specs, out_specs=P("tm", "agent", None), check_vma=False
    )
```

```python
import functools

import jax
import jax.numpy as jnp
from jax import lax
from jax.experimental import pallas as pl
from jax.experimental.pallas import tpu as pltpu
from jax.sharding import PartitionSpec as P

HEAD = 64
CHUNKS = 2
RADIX = 32
EPS = 1e-05
LOG2E = 1.4426950408889634
MIB = 1024 * 1024
VMEM = pl.BlockSpec(memory_space=pltpu.VMEM)
ANY = pl.BlockSpec(memory_space=pl.ANY)
HBM = pl.BlockSpec(memory_space=pltpu.HBM)


def pinned(x):
    return pltpu.with_memory_space_constraint(x, pltpu.VMEM)


def far(x):
    return pltpu.with_memory_space_constraint(x, pltpu.HBM)


def cost(microseconds):
    return pl.CostEstimate(
        flops=int(1.1e9 * microseconds) + 10**6, bytes_accessed=int(3.5e6 * microseconds) + 10**4, transcendentals=0
    )


def away(k, steps, member, line):
    if k == steps - 1:
        return 0
    odd, first = member % 2, 1 - jnp.minimum(line, 1) if isinstance(line, jax.Array) else int(line == 0)
    first_order, even_order, odd_order = (3, 2, 1), (2, 3, 1), (2, 1, 3)
    return (first_order[k] * first + even_order[k] * (1 - first)) * (1 - odd) + odd_order[k] * odd


def dot(a, b):
    return jnp.dot(a, b, preferred_element_type=jnp.float32)


def dot_t(a, b):
    return lax.dot_general(a, b, (((1,), (1,)), ((), ())), preferred_element_type=jnp.float32)


def norm_scale(values):
    return lax.rsqrt(jnp.mean(values * values, axis=-1, keepdims=True) + EPS)


def gelu(x):
    return 0.5 * x * (1.0 + lax.erf(x * 0.7071067811865476))


def part_copies(tokens, part, target, sem):
    steps, agents = target.shape[:2]
    return [
        pltpu.make_async_copy(tokens.at[step, pl.ds(part * agents, agents)], target.at[step], sem.at[step])
        for step in range(steps)
    ]


def stage_kernel(count, taps, gain, order, present, tokens, first_part, *rest):
    sources, rest = rest[:count], rest[count:]
    second_part, partials, tail, targets = rest[0], rest[1:3], rest[3], rest[4 : 4 + count]
    taps_here, gain_here, order_here, present_here, normed, facts, part_sem, sem = rest[4 + count :]
    pairs = [
        (taps, taps_here),
        (gain, gain_here),
        (order, order_here),
        (present, present_here),
        *zip(sources, targets),
    ]
    copies = [pltpu.make_async_copy(source, target, sem.at[i]) for i, (source, target) in enumerate(pairs)]
    later = part_copies(tokens, 1, second_part, part_sem)
    for copy in copies + later:
        copy.start()
    for copy in copies:
        copy.wait()
    agents = order.shape[1]
    facts[...] = jnp.zeros(facts.shape, jnp.float32)
    facts[0:1, :agents] = (order_here[...] // RADIX).astype(jnp.float32)
    facts[1:2, :agents] = (order_here[...] % RADIX).astype(jnp.float32)
    facts[2:3, :agents] = present_here[...].astype(jnp.float32)
    tail[...] = facts[...].astype(jnp.bfloat16)
    steps, reach = first_part.shape[0], taps.shape[0] - 1
    gains = gain_here[...]
    for j, part in enumerate((first_part, second_part)):
        for step in range(steps):
            if j == 1:
                later[step].wait()
            values = part[step].astype(jnp.float32)
            normed[step] = values * norm_scale(values) * gains
            total = values
            for lag in range(min(step, reach) + 1):
                total = total + taps_here[lag : lag + 1, :] * normed[step - lag]
            partials[j][step] = total


def stage(tokens, first_part, taps, gain, order, present, arrays):
    steps, part, width = first_part.shape
    inputs = (taps, gain, order, present)
    return pl.pallas_call(
        functools.partial(stage_kernel, len(arrays)),
        out_shape=[pltpu.VMEM(first_part.shape, first_part.dtype)]
        + [pltpu.VMEM((steps, part, width), jnp.float32)] * CHUNKS
        + [pltpu.VMEM((part, 128), jnp.bfloat16)]
        + [pltpu.VMEM(x.shape, x.dtype) for x in arrays],
        in_specs=[HBM] * (len(inputs) + 1) + [VMEM] + [HBM] * len(arrays),
        out_specs=[VMEM] * (CHUNKS + 2 + len(arrays)),
        scratch_shapes=[pltpu.VMEM(x.shape, x.dtype) for x in inputs]
        + [
            pltpu.VMEM((steps, part, width), jnp.float32),
            pltpu.VMEM((part, 128), jnp.float32),
            pltpu.SemaphoreType.DMA((steps,)),
            pltpu.SemaphoreType.DMA((len(inputs) + len(arrays),)),
        ],
        compiler_params=pltpu.CompilerParams(vmem_limit_bytes=8 * MIB),
        cost_estimate=cost(30),
        name="stage",
    )(*[far(x) for x in (*inputs, tokens)], pinned(first_part), *[far(x) for x in arrays])


def run_pairs(pairs, lead, stages):
    held = [{} for _ in stages]
    for turn in range(pairs + lead * (len(stages) - 1)):
        for i, stage in enumerate(stages):
            pair = turn - lead * i
            if 0 <= pair < pairs:
                held[i][pair] = stage(pair, held[i - 1].pop(pair)) if i else stage(pair)


def mixed_rows(halo, partial, taps, gain, normed, first):
    steps, agents = halo.shape[:2]
    reach = taps.shape[0] - 1
    gains = gain[...] * (lax.axis_index("tm") > 0).astype(jnp.float32)
    for step in range(steps):
        values = halo[step].astype(jnp.float32)
        normed[step] = values * norm_scale(values) * gains
    for step in range(steps):
        total = partial[step]
        for lag in range(step + 1, reach + 1):
            total = total + taps[lag : lag + 1, :] * normed[steps + step - lag]
        first[step * agents : (step + 1) * agents, :] = total.astype(jnp.bfloat16).astype(first.dtype)


def feed_forward(rows, gain, w_in, w_out):
    inner = (rows * norm_scale(rows) * gain[...]).astype(jnp.bfloat16)
    tile, total = 512, [rows]

    def enter(i):
        return dot(inner, w_in[:, i * tile : (i + 1) * tile])

    def activate(i, products):
        return gelu(products).astype(jnp.bfloat16)

    def leave(i, hidden):
        total[0] = total[0] + dot(hidden, w_out[i * tile : (i + 1) * tile, :])

    run_pairs(w_in.shape[1] // tile, 1, [enter, activate, leave])
    return total[0].astype(jnp.bfloat16)


def to_keys(second, gain, w_key, w_value, keyval):
    width = second.shape[1]
    values = second.astype(jnp.float32)
    attn_in = (values * norm_scale(values) * gain[...]).astype(jnp.bfloat16)
    keyval[:, :width] = dot(attn_in, w_key[...]).astype(jnp.bfloat16)
    keyval[:, width : 2 * width] = dot(attn_in, w_value[...]).astype(jnp.bfloat16)
    return attn_in


def conv_kernel(group, halo, partial, taps, gain, tail, *rest):
    steps, agents, width = halo.shape
    outs = rest[:steps]
    normed, first = rest[steps:]
    mixed_rows(halo, partial, taps, gain, normed, first)
    spot = lax.axis_index("agent")
    for k in range(steps):
        step = (spot // group) ^ away(k, steps, spot % group, lax.axis_index("tm"))
        outs[k][:, :width] = first[pl.ds(pl.multiple_of(step * agents, agents), agents), :].astype(jnp.bfloat16)
        outs[k][:, width:] = tail[...]


def conv(group, halo, partial, taps, gain, tail):
    steps, agents, width = halo.shape
    return pl.pallas_call(
        functools.partial(conv_kernel, group),
        out_shape=[jax.ShapeDtypeStruct((agents, width + tail.shape[1]), jnp.bfloat16)] * steps,
        in_specs=[VMEM] * 5,
        out_specs=[VMEM] * steps,
        scratch_shapes=[
            pltpu.VMEM((steps, agents, width), jnp.float32),
            pltpu.VMEM((steps * agents, width), jnp.float32),
        ],
        compiler_params=pltpu.CompilerParams(vmem_limit_bytes=8 * MIB),
        cost_estimate=cost(0),
        name="conv",
    )(halo, *[pinned(x) for x in (partial, taps, gain, tail)])


def front_kernel(group, halo, partial, taps, gain_first, gain_second, w_in, w_out, *rest):
    steps, agents, width = halo.shape
    outs = rest[:steps]
    normed, first, second = rest[steps:]
    mixed_rows(halo, partial, taps, gain_first, normed, first)
    result = feed_forward(first[...], gain_second, w_in, w_out)
    for step in range(steps):
        second[step] = result[step * agents : (step + 1) * agents]
    spot = lax.axis_index("agent")
    for k in range(steps):
        outs[k][...] = second[(spot // group) ^ away(k, steps, spot % group, lax.axis_index("tm"))]


def front(group, halo, partial, taps, gains, w_in, w_out):
    steps, agents, width = halo.shape
    rows = steps * agents
    return pl.pallas_call(
        functools.partial(front_kernel, group),
        out_shape=[jax.ShapeDtypeStruct((agents, width), jnp.bfloat16)] * steps,
        in_specs=[VMEM] * 7,
        out_specs=[VMEM] * steps,
        scratch_shapes=[
            pltpu.VMEM((steps, agents, width), jnp.float32),
            pltpu.VMEM((rows, width), jnp.float32),
            pltpu.VMEM((steps, agents, width), jnp.bfloat16),
        ],
        compiler_params=pltpu.CompilerParams(vmem_limit_bytes=12 * MIB),
        cost_estimate=cost(0),
        name="front",
    )(halo, *[pinned(x) for x in (partial, taps, *gains, w_in, w_out)])


def feed_kernel(count, *refs):
    pieces = refs[:count]
    gain_second, gain_third, w_in, w_out, w_key, w_value = refs[count : count + 6]
    query_in, keyval, second = refs[count + 6 :]
    width = gain_second.shape[1]
    agents = pieces[0].shape[0]
    for k in range(count):
        keyval[agents * k : agents * (k + 1), 2 * width :] = pieces[k][:, width:]
    first = jnp.concatenate([piece[:, :width].astype(jnp.float32) for piece in pieces], axis=0)
    result = feed_forward(first, gain_second, w_in, w_out)
    second[...] = result
    query_in[...] = to_keys(result, gain_third, w_key, w_value, keyval)


def feed(pieces, gains, weights):
    rows = sum(piece.shape[0] for piece in pieces)
    width = gains[0].shape[1]
    return pl.pallas_call(
        functools.partial(feed_kernel, len(pieces)),
        out_shape=[
            jax.ShapeDtypeStruct((rows, width), jnp.bfloat16),
            jax.ShapeDtypeStruct((rows, width + pieces[0].shape[1]), jnp.bfloat16),
            jax.ShapeDtypeStruct((rows, width), jnp.bfloat16),
        ],
        in_specs=[VMEM] * (len(pieces) + 6),
        out_specs=[VMEM] * 3,
        compiler_params=pltpu.CompilerParams(vmem_limit_bytes=12 * MIB),
        cost_estimate=cost(0),
        name="feed",
    )(*pieces, *[pinned(x) for x in (*gains, *weights)])


def project_kernel(count, *refs):
    pieces = refs[:count][::-1]
    gain, w_key, w_value, attn_in, keyval = refs[count:]
    second = jnp.concatenate([piece[...] for piece in pieces], axis=0)
    attn_in[...] = to_keys(second, gain, w_key, w_value, keyval)


def project(pieces, gain, weights):
    rows = sum(piece.shape[0] for piece in pieces)
    width = gain.shape[1]
    return pl.pallas_call(
        functools.partial(project_kernel, len(pieces)),
        out_shape=[
            jax.ShapeDtypeStruct((rows, width), jnp.bfloat16),
            jax.ShapeDtypeStruct((rows, 2 * width), jnp.bfloat16),
        ],
        in_specs=[VMEM] * (len(pieces) + 3),
        out_specs=[VMEM] * 2,
        compiler_params=pltpu.CompilerParams(vmem_limit_bytes=8 * MIB),
        cost_estimate=cost(25),
        name="project",
    )(*reversed(pieces), *[pinned(x) for x in (gain, *weights)])


def block_order(group, chunks):
    early = [(r, 0) for r in range(group)] + [(0, j) for j in range(1, chunks)]
    return early + [(r, j) for j in range(1, chunks) for r in range(1, group)]


def write_mask(steps, chunks, agents, width, blocks, bias):
    group = len(blocks)
    now = (lax.axis_index("tm") * steps + lax.axis_index("agent") // group).astype(jnp.float32)
    lane = lax.broadcasted_iota(jnp.int32, (agents, 128), 1)
    sublane = lax.broadcasted_iota(jnp.int32, (agents, 128), 0)
    tiles = {}
    for r in range(group):
        for k in range(steps):
            tile = blocks[r][agents * k : agents * (k + 1), 2 * width :].astype(jnp.float32)
            tiles[k, r] = (tile[0:1] * RADIX + tile[1:2], tile[2:3])
    own = jnp.concatenate(
        [
            jnp.sum(jnp.where(lane == sublane + j * agents, tiles[k, 0][0], 0.0), axis=1, keepdims=True)
            for k in range(steps)
            for j in range(chunks)
        ],
        axis=0,
    )
    row_lane = lax.broadcasted_iota(jnp.int32, (1, 128), 1)
    per_tile = 128 // agents
    start = 0
    for r, j in block_order(group, chunks):
        for first in range(0, steps, per_tile):
            both = [None, None]
            for i in range(per_tile):
                for f in (0, 1):
                    moved = pltpu.roll(tiles[first + i, r][f], ((i - j) * agents) % 128, 1)
                    both[f] = moved if i == 0 else jnp.where(row_lane >= i * agents, moved, both[f])
            order, present = both
            alive = jnp.where(now < present, order, 1e9)
            visible = (alive < own) | (order == own)
            bias[:, start : start + 128] = jnp.where(visible, 0.0, -1e30)
            start += 128


def rows_of(parts, ks, agents, columns):
    return jnp.concatenate([part[agents * k : agents * (k + 1), columns] for k in ks for part in parts], axis=0)


def pair_stages(queries_of, blocks, bias, top_of, low):
    width = blocks[0].shape[1] // 2 // 128 * 128

    def products(pair):
        queries = queries_of(pair)
        zeros = jnp.zeros_like(queries)
        stacked = jnp.concatenate([jnp.where(low, queries, zeros), jnp.where(low, zeros, queries)], axis=0)
        key = jnp.concatenate([block[:, 128 * pair : 128 * pair + 128] for block in blocks], axis=0)
        return dot_t(stacked, key)

    def weigh(pair, scores):
        rows, keys = scores.shape[0] // 2, scores.shape[1]
        tops, weights = [], []
        for half in range(2):
            here = scores[half * rows : (half + 1) * rows] * (LOG2E * HEAD ** (-0.5)) + bias
            highest = jnp.broadcast_to(jnp.max(here, axis=1, keepdims=True), (rows, 128))
            if top_of is not None:
                highest = jnp.maximum(highest, top_of(pair, half))
            tops.append(highest)
            wide = jnp.concatenate([highest] * (keys // 128), axis=1)
            weights.append(jnp.exp2(here - wide).astype(jnp.bfloat16))
        return tops, jnp.concatenate(weights, axis=0)

    def sums(pair, made):
        tops, weights = made
        start = width + 128 * pair
        value = jnp.concatenate([block[:, start : start + 128] for block in blocks], axis=0)
        return tops, dot(weights, jnp.concatenate([value, jnp.ones(value.shape, jnp.bfloat16)], axis=1))

    return [products, weigh, sums]


def merged(low, total):
    rows = total.shape[0] // 2
    return jnp.where(low, total[:rows], total[rows:])


def early_kernel(ks, steps, chunks, group, first_in, second_in, w_query, *refs):
    count = group + chunks - 1
    blocks, (first_query, second_query, bias, number, weight, top_low, top_high) = refs[:count], refs[count:]
    rows, width = number.shape
    queries = dot(jnp.concatenate([first_in[...], second_in[...]], axis=0), w_query[...]).astype(jnp.bfloat16)
    first_query[...] = queries[: first_in.shape[0]]
    second_query[...] = queries[first_in.shape[0] :]
    write_mask(steps, chunks, first_in.shape[0] // steps, width, blocks[:group], bias)
    agents = rows // (len(ks) * chunks)
    low = lax.broadcasted_iota(jnp.int32, (rows, 128), 1) < HEAD
    keys = sum(block.shape[0] for block in blocks)
    here = bias[ks[0] * agents * chunks : ks[0] * agents * chunks + rows, :keys]

    def columns(pair):
        return slice(128 * pair, 128 * pair + 128)

    def keep(pair, made):
        tops, total = made
        number[:, columns(pair)] = merged(low, total[:, :128])
        weight[:, columns(pair)] = merged(low, total[:, 128:])
        top_low[:, columns(pair)] = tops[0]
        top_high[:, columns(pair)] = tops[1]

    stages = pair_stages(lambda pair: rows_of((first_query, second_query), ks, agents, columns(pair)), blocks, here, None, low)
    run_pairs(width // 128, 1, [*stages, keep])


def early(ks, steps, group, first_in, second_in, w_query, blocks):
    count, width = first_in.shape
    rows = count * CHUNKS
    state = pltpu.VMEM((len(ks) * rows // steps, width), jnp.float32)
    return pl.pallas_call(
        functools.partial(early_kernel, ks, steps, CHUNKS, group),
        out_shape=[jax.ShapeDtypeStruct(first_in.shape, jnp.bfloat16)] * 2
        + [pltpu.VMEM((rows, rows * group), jnp.float32)]
        + [state] * 4,
        in_specs=[VMEM] * (3 + len(blocks)),
        out_specs=[VMEM] * 7,
        compiler_params=pltpu.CompilerParams(vmem_limit_bytes=16 * MIB),
        cost_estimate=cost(0),
        name="early",
    )(first_in, second_in, pinned(w_query), *blocks)


def attend_kernel(ks, chunks, count, begun, skipped, *refs):
    mine = 1 + len(ks) * (chunks - 1)
    queries, seconds, (w_output, bias) = refs[:chunks], refs[chunks : chunks + mine], refs[chunks + mine : chunks + mine + 2]
    rest = refs[chunks + mine + 2 :]
    blocks, state = rest[:count], rest[count : count + begun]
    outs = rest[count + begun :]
    width, agents = w_output.shape[1], queries[0].shape[0] // 4
    rows = len(ks) * chunks * agents
    low = lax.broadcasted_iota(jnp.int32, (rows, 128), 1) < HEAD
    keys = sum(block.shape[0] for block in blocks)
    here = bias[ks[0] * agents * chunks : ks[0] * agents * chunks + rows, bias.shape[1] - keys :]
    begun_rows = slice(skipped, skipped + rows)

    def columns(pair):
        return slice(128 * pair, 128 * pair + 128)

    residual = []
    for i, k in enumerate(ks):
        residual += [seconds[0][agents * k : agents * (k + 1)]]
        residual += [piece[...] for piece in seconds[1 + i * (chunks - 1) : 1 + (i + 1) * (chunks - 1)]]
    result = [jnp.concatenate(residual, axis=0).astype(jnp.float32)]

    def keep(pair, made):
        tops, total = made
        number, weight = merged(low, total[:, :128]), merged(low, total[:, 128:])
        if begun:
            drop = [state[2 + half][begun_rows, columns(pair)] - tops[half] for half in range(2)]
            shrink = jnp.exp2(jnp.where(low, *drop))
            number = number + state[0][begun_rows, columns(pair)] * shrink
            weight = weight + state[1][begun_rows, columns(pair)] * shrink
        return (number / weight).astype(jnp.bfloat16)

    waiting, together = [], 2 if begun else width // 128

    def output(pair, attended):
        waiting.append(attended)
        if len(waiting) == together:
            features = slice(128 * (pair + 1 - together), 128 * (pair + 1))
            result[0] = result[0] + dot(jnp.concatenate(waiting, axis=1), w_output[features, :])
            waiting.clear()

    stages = pair_stages(
        lambda pair: rows_of(queries, ks, agents, columns(pair)),
        blocks,
        here,
        (lambda pair, half: state[2 + half][begun_rows, columns(pair)]) if begun else None,
        low,
    )
    run_pairs(width // 128, 2 if begun else 1, [*stages, keep, output])
    for i in range(len(ks)):
        outs[i][...] = result[0][i * agents * chunks : (i + 1) * agents * chunks].astype(jnp.bfloat16)


def attend(ks, queries, seconds, w_output, bias, blocks, state, skipped, agents, microseconds):
    width = queries[0].shape[1]
    piece = jax.ShapeDtypeStruct((agents, width), jnp.bfloat16)
    return pl.pallas_call(
        functools.partial(attend_kernel, ks, len(queries), len(blocks), len(state), skipped),
        out_shape=[piece] * len(ks),
        in_specs=[VMEM] * (len(queries) + len(seconds) + 2 + len(blocks) + len(state)),
        out_specs=[VMEM] * len(ks),
        compiler_params=pltpu.CompilerParams(vmem_limit_bytes=16 * MIB),
        cost_estimate=cost(microseconds),
        name="attend",
    )(*queries, *seconds, pinned(w_output), pinned(bias), *blocks, *[pinned(x) for x in state])


def put_back_kernel(steps, group, *refs):
    pieces, out, sem = refs[:steps][::-1], refs[steps], refs[steps + 1]
    spot = lax.axis_index("agent")
    half = pieces[0].shape[0] // 2
    copies = []
    for k in range(steps):
        target = out.at[(spot // group) ^ away(k, steps, spot % group, lax.axis_index("tm"))]
        for rows in (pl.ds(0, half), pl.ds(half, half)):
            copies.append(pltpu.make_async_copy(pieces[k].at[rows], target.at[rows], sem.at[len(copies)]))
    for copy in copies:
        copy.start()
    for copy in copies:
        copy.wait()


def put_back(group, pieces, shape):
    return pl.pallas_call(
        functools.partial(put_back_kernel, shape[0], group),
        out_shape=jax.ShapeDtypeStruct(shape, jnp.bfloat16),
        in_specs=[VMEM] * len(pieces),
        out_specs=ANY,
        scratch_shapes=[pltpu.SemaphoreType.DMA((2 * len(pieces),))],
        compiler_params=pltpu.CompilerParams(vmem_limit_bytes=4 * MIB),
        cost_estimate=cost(0),
        name="put_back",
    )(*pieces)


def after(x, *others):
    return lax.optimization_barrier((x, *others))[0]


def per_device(
    tokens,
    conv_taps,
    norm_first,
    norm_second,
    norm_third,
    w_in,
    w_out,
    w_query,
    w_key,
    w_value,
    w_output,
    agent_order,
    present_steps,
):
    steps, agents, width = tokens.shape
    tm_count, count = lax.axis_size("tm"), lax.axis_size("agent")
    group = count // steps
    part = agents // CHUNKS
    assert group * steps == count and steps == 4 and 128 % part == 0 and CHUNKS == 2 and group > 1

    def across(x, k):
        if k == steps - 1:
            return x
        pairs = [
            (line * count + i, line * count + ((i // group) ^ away(k, steps, i % group, line)) * group + i % group)
            for line in range(tm_count)
            for i in range(count)
        ]
        return lax.ppermute(x, ("tm", "agent"), pairs)

    def within(x, r):
        return lax.ppermute(x, "agent", [(i, (i // group) * group + ((i % group) ^ r)) for i in range(count)])

    first_part = tokens[:, :part]
    second_part, *partials, tail, taps, gain_first, gain_second, gain_third = stage(
        tokens,
        first_part,
        conv_taps,
        norm_first.reshape(1, width),
        agent_order.reshape(1, agents),
        present_steps.reshape(1, agents),
        [conv_taps] + [x.reshape(1, width) for x in (norm_first, norm_second, norm_third)],
    )
    halos = [lax.ppermute(x, "tm", [(i, (i + 1) % tm_count) for i in range(tm_count)]) for x in (first_part, second_part)]
    halos[0] = after(halos[0], tail)
    made = conv(group, halos[0], partials[0], taps, gain_first, tail)
    last = made[-1]
    pieces = [[across(made[k], k) for k in range(steps)]]
    for j in range(1, CHUNKS):
        halos[j] = after(halos[j], last)
        made = list(front(group, halos[j], partials[j], taps, (gain_first, gain_second), w_in, w_out))
        last = made[-1]
        made[steps - 2] = after(made[steps - 2], pieces[j - 1][0])
        pieces.append([across(made[k], k) for k in range(steps)])
    pieces[0][-1] = after(pieces[0][-1], last)
    first_in, keyval, second = feed(pieces[0], (gain_second, gain_third), (w_in, w_out, w_key, w_value))
    blocks = {(0, 0): keyval, **{(r, 0): within(keyval, r) for r in range(1, group)}}
    second_in, keyval = project(pieces[1], gain_third, (w_key, w_value))
    keyval = after(keyval, *blocks.values())
    blocks.update({(0, 1): keyval, **{(r, 1): within(keyval, r) for r in range(1, group)}})
    blocks = [blocks[spot] for spot in block_order(group, CHUNKS)]
    ready = group + CHUNKS - 1
    far_ks, near_ks = (0, 1), (2, 3)
    first_query, second_query, bias, *state = early(
        far_ks, steps, group, first_in, second_in, w_query, blocks[:ready]
    )

    def finish(ks, blocks, state, skipped, microseconds):
        seconds = [second] + [pieces[j][k] for k in ks for j in range(1, CHUNKS)]
        return attend(
            ks, (first_query, second_query), seconds, w_output, bias, blocks, state, skipped, agents, microseconds
        )

    late = blocks[ready:]
    results = [*finish(far_ks, late, state, 0, 0), *finish(near_ks, blocks, [], 0, 10)]
    return put_back(group, [across(results[k], k) for k in reversed(range(steps))], tokens.shape)


def solution(mesh):
    in_specs = (P("tm", "agent", None),) + (P(),) * 10 + (P("agent"), P("agent"))
    return jax.shard_map(
        per_device, mesh=mesh, in_specs=in_specs, out_specs=P("tm", "agent", None), check_vma=False
    )
```

```python
import functools

import jax
import jax.numpy as jnp
from jax import lax
from jax.experimental import pallas as pl
from jax.experimental.pallas import tpu as pltpu
from jax.sharding import PartitionSpec as P

HEAD = 64
CHUNKS = 2
RADIX = 32
EPS = 1e-05
LOG2E = 1.4426950408889634
MIB = 1024 * 1024
VMEM = pl.BlockSpec(memory_space=pltpu.VMEM)
ANY = pl.BlockSpec(memory_space=pl.ANY)
HBM = pl.BlockSpec(memory_space=pltpu.HBM)


def pinned(x):
    return pltpu.with_memory_space_constraint(x, pltpu.VMEM)


def far(x):
    return pltpu.with_memory_space_constraint(x, pltpu.HBM)


def cost(microseconds):
    return pl.CostEstimate(
        flops=int(1.1e9 * microseconds) + 10**6, bytes_accessed=int(3.5e6 * microseconds) + 10**4, transcendentals=0
    )


def away(k, steps, member, line):
    if k == steps - 1:
        return 0
    odd, first = member % 2, 1 - jnp.minimum(line, 1) if isinstance(line, jax.Array) else int(line == 0)
    first_orders, orders = ((2, 1, 3), (3, 2, 1)), ((2, 3, 1), (2, 1, 3))
    even, odd_away = (a[k] * first + b[k] * (1 - first) for a, b in zip(first_orders, orders))
    return even * (1 - odd) + odd_away * odd


def dot(a, b):
    return jnp.dot(a, b, preferred_element_type=jnp.float32)


def dot_t(a, b):
    return lax.dot_general(a, b, (((1,), (1,)), ((), ())), preferred_element_type=jnp.float32)


def norm_scale(values):
    return lax.rsqrt(jnp.mean(values * values, axis=-1, keepdims=True) + EPS)


def gelu(x):
    return 0.5 * x * (1.0 + lax.erf(x * 0.7071067811865476))


def part_copies(tokens, part, target, sem):
    steps, agents = target.shape[:2]
    return [
        pltpu.make_async_copy(tokens.at[step, pl.ds(part * agents, agents)], target.at[step], sem.at[step])
        for step in range(steps)
    ]


def split_kernel(tokens, out, sem):
    copies = part_copies(tokens, 0, out, sem)
    for copy in copies:
        copy.start()
    for copy in copies:
        copy.wait()


def split(tokens):
    steps, agents, width = tokens.shape
    return pl.pallas_call(
        split_kernel,
        out_shape=pltpu.VMEM((steps, agents // CHUNKS, width), tokens.dtype),
        in_specs=[HBM],
        out_specs=VMEM,
        scratch_shapes=[pltpu.SemaphoreType.DMA((steps,))],
        compiler_params=pltpu.CompilerParams(vmem_limit_bytes=4 * MIB),
        cost_estimate=cost(0),
        name="split",
    )(far(tokens))


def stage_kernel(count, taps, gain, order, present, tokens, first_part, *rest):
    sources, rest = rest[:count], rest[count:]
    second_part, partials, tail, targets = rest[0], rest[1:3], rest[3], rest[4 : 4 + count]
    taps_here, gain_here, order_here, present_here, normed, facts, part_sem, sem = rest[4 + count :]
    pairs = [
        (taps, taps_here),
        (gain, gain_here),
        (order, order_here),
        (present, present_here),
        *zip(sources, targets),
    ]
    copies = [pltpu.make_async_copy(source, target, sem.at[i]) for i, (source, target) in enumerate(pairs)]
    later = part_copies(tokens, 1, second_part, part_sem)
    for copy in copies + later:
        copy.start()
    for copy in copies:
        copy.wait()
    agents = order.shape[1]
    facts[...] = jnp.zeros(facts.shape, jnp.float32)
    facts[0:1, :agents] = (order_here[...] // RADIX).astype(jnp.float32)
    facts[1:2, :agents] = (order_here[...] % RADIX).astype(jnp.float32)
    facts[2:3, :agents] = present_here[...].astype(jnp.float32)
    tail[...] = facts[...].astype(jnp.bfloat16)
    steps, reach = first_part.shape[0], taps.shape[0] - 1
    gains = gain_here[...]
    for j, part in enumerate((first_part, second_part)):
        for step in range(steps):
            if j == 1:
                later[step].wait()
            values = part[step].astype(jnp.float32)
            normed[step] = values * norm_scale(values) * gains
            total = values
            for lag in range(min(step, reach) + 1):
                total = total + taps_here[lag : lag + 1, :] * normed[step - lag]
            partials[j][step] = total


def stage(tokens, first_part, taps, gain, order, present, arrays):
    steps, part, width = first_part.shape
    inputs = (taps, gain, order, present)
    return pl.pallas_call(
        functools.partial(stage_kernel, len(arrays)),
        out_shape=[pltpu.VMEM(first_part.shape, first_part.dtype)]
        + [pltpu.VMEM((steps, part, width), jnp.float32)] * CHUNKS
        + [pltpu.VMEM((part, 128), jnp.bfloat16)]
        + [pltpu.VMEM(x.shape, x.dtype) for x in arrays],
        in_specs=[HBM] * (len(inputs) + 1) + [VMEM] + [HBM] * len(arrays),
        out_specs=[VMEM] * (CHUNKS + 2 + len(arrays)),
        scratch_shapes=[pltpu.VMEM(x.shape, x.dtype) for x in inputs]
        + [
            pltpu.VMEM((steps, part, width), jnp.float32),
            pltpu.VMEM((part, 128), jnp.float32),
            pltpu.SemaphoreType.DMA((steps,)),
            pltpu.SemaphoreType.DMA((len(inputs) + len(arrays),)),
        ],
        compiler_params=pltpu.CompilerParams(vmem_limit_bytes=8 * MIB),
        cost_estimate=cost(30),
        name="stage",
    )(*[far(x) for x in (*inputs, tokens)], pinned(first_part), *[far(x) for x in arrays])


def run_pairs(pairs, lead, stages):
    held = [{} for _ in stages]
    for turn in range(pairs + lead * (len(stages) - 1)):
        for i, stage in enumerate(stages):
            pair = turn - lead * i
            if 0 <= pair < pairs:
                held[i][pair] = stage(pair, held[i - 1].pop(pair)) if i else stage(pair)


def mixed_rows(halo, partial, taps, gain, normed, first):
    steps, agents = halo.shape[:2]
    reach = taps.shape[0] - 1
    gains = gain[...] * (lax.axis_index("tm") > 0).astype(jnp.float32)
    for step in range(steps):
        values = halo[step].astype(jnp.float32)
        normed[step] = values * norm_scale(values) * gains
    for step in range(steps):
        total = partial[step]
        for lag in range(step + 1, reach + 1):
            total = total + taps[lag : lag + 1, :] * normed[steps + step - lag]
        first[step * agents : (step + 1) * agents, :] = total.astype(jnp.bfloat16).astype(first.dtype)


def feed_forward(rows, gain, w_in, w_out):
    inner = (rows * norm_scale(rows) * gain[...]).astype(jnp.bfloat16)
    tile, total = 512, [rows]

    def enter(i):
        return dot(inner, w_in[:, i * tile : (i + 1) * tile])

    def activate(i, products):
        return gelu(products).astype(jnp.bfloat16)

    def leave(i, hidden):
        total[0] = total[0] + dot(hidden, w_out[i * tile : (i + 1) * tile, :])

    run_pairs(w_in.shape[1] // tile, 1, [enter, activate, leave])
    return total[0].astype(jnp.bfloat16)


def to_keys(second, gain, w_key, w_value, keyval):
    width = second.shape[1]
    values = second.astype(jnp.float32)
    attn_in = (values * norm_scale(values) * gain[...]).astype(jnp.bfloat16)
    keyval[:, :width] = dot(attn_in, w_key[...]).astype(jnp.bfloat16)
    keyval[:, width : 2 * width] = dot(attn_in, w_value[...]).astype(jnp.bfloat16)
    return attn_in


def conv_kernel(group, halo, partial, taps, gain, tail, *rest):
    steps, agents, width = halo.shape
    outs = rest[:steps]
    normed, first = rest[steps:]
    mixed_rows(halo, partial, taps, gain, normed, first)
    spot = lax.axis_index("agent")
    for k in range(steps):
        step = (spot // group) ^ away(k, steps, spot % group, lax.axis_index("tm"))
        outs[k][:, :width] = first[pl.ds(pl.multiple_of(step * agents, agents), agents), :].astype(jnp.bfloat16)
        outs[k][:, width:] = tail[...]


def conv(group, halo, partial, taps, gain, tail):
    steps, agents, width = halo.shape
    return pl.pallas_call(
        functools.partial(conv_kernel, group),
        out_shape=[jax.ShapeDtypeStruct((agents, width + tail.shape[1]), jnp.bfloat16)] * steps,
        in_specs=[VMEM] * 5,
        out_specs=[VMEM] * steps,
        scratch_shapes=[
            pltpu.VMEM((steps, agents, width), jnp.float32),
            pltpu.VMEM((steps * agents, width), jnp.float32),
        ],
        compiler_params=pltpu.CompilerParams(vmem_limit_bytes=8 * MIB),
        cost_estimate=cost(0),
        name="conv",
    )(halo, *[pinned(x) for x in (partial, taps, gain, tail)])


def front_kernel(group, halo, partial, taps, gain_first, gain_second, w_in, w_out, *rest):
    steps, agents, width = halo.shape
    outs = rest[:steps]
    normed, first, second = rest[steps:]
    mixed_rows(halo, partial, taps, gain_first, normed, first)
    result = feed_forward(first[...], gain_second, w_in, w_out)
    for step in range(steps):
        second[step] = result[step * agents : (step + 1) * agents]
    spot = lax.axis_index("agent")
    for k in range(steps):
        outs[k][...] = second[(spot // group) ^ away(k, steps, spot % group, lax.axis_index("tm"))]


def front(group, halo, partial, taps, gains, w_in, w_out):
    steps, agents, width = halo.shape
    rows = steps * agents
    return pl.pallas_call(
        functools.partial(front_kernel, group),
        out_shape=[jax.ShapeDtypeStruct((agents, width), jnp.bfloat16)] * steps,
        in_specs=[VMEM] * 7,
        out_specs=[VMEM] * steps,
        scratch_shapes=[
            pltpu.VMEM((steps, agents, width), jnp.float32),
            pltpu.VMEM((rows, width), jnp.float32),
            pltpu.VMEM((steps, agents, width), jnp.bfloat16),
        ],
        compiler_params=pltpu.CompilerParams(vmem_limit_bytes=12 * MIB),
        cost_estimate=cost(0),
        name="front",
    )(halo, *[pinned(x) for x in (partial, taps, *gains, w_in, w_out)])


def feed_kernel(count, *refs):
    pieces = refs[:count]
    gain_second, gain_third, w_in, w_out, w_key, w_value, w_query = refs[count : count + 7]
    query, keyval, second = refs[count + 7 :]
    width = gain_second.shape[1]
    agents = pieces[0].shape[0]
    for k in range(count):
        keyval[agents * k : agents * (k + 1), 2 * width :] = pieces[k][:, width:]
    first = jnp.concatenate([piece[:, :width].astype(jnp.float32) for piece in pieces], axis=0)
    result = feed_forward(first, gain_second, w_in, w_out)
    second[...] = result
    attn_in = to_keys(result, gain_third, w_key, w_value, keyval)
    query[...] = dot(attn_in, w_query[...]).astype(jnp.bfloat16)


def feed(pieces, gains, weights):
    rows = sum(piece.shape[0] for piece in pieces)
    width = gains[0].shape[1]
    return pl.pallas_call(
        functools.partial(feed_kernel, len(pieces)),
        out_shape=[
            jax.ShapeDtypeStruct((rows, width), jnp.bfloat16),
            jax.ShapeDtypeStruct((rows, width + pieces[0].shape[1]), jnp.bfloat16),
            jax.ShapeDtypeStruct((rows, width), jnp.bfloat16),
        ],
        in_specs=[VMEM] * (len(pieces) + 7),
        out_specs=[VMEM] * 3,
        compiler_params=pltpu.CompilerParams(vmem_limit_bytes=12 * MIB),
        cost_estimate=cost(0),
        name="feed",
    )(*pieces, *[pinned(x) for x in (*gains, *weights)])


def project_kernel(count, *refs):
    pieces = refs[:count][::-1]
    gain, w_key, w_value, attn_in, keyval = refs[count:]
    second = jnp.concatenate([piece[...] for piece in pieces], axis=0)
    attn_in[...] = to_keys(second, gain, w_key, w_value, keyval)


def project(pieces, gain, weights):
    rows = sum(piece.shape[0] for piece in pieces)
    width = gain.shape[1]
    return pl.pallas_call(
        functools.partial(project_kernel, len(pieces)),
        out_shape=[
            jax.ShapeDtypeStruct((rows, width), jnp.bfloat16),
            jax.ShapeDtypeStruct((rows, 2 * width), jnp.bfloat16),
        ],
        in_specs=[VMEM] * (len(pieces) + 3),
        out_specs=[VMEM] * 2,
        compiler_params=pltpu.CompilerParams(vmem_limit_bytes=8 * MIB),
        cost_estimate=cost(25),
        name="project",
    )(*reversed(pieces), *[pinned(x) for x in (gain, *weights)])


def block_order(group, chunks):
    early = [(r, 0) for r in range(group)] + [(0, j) for j in range(1, chunks)]
    return early + [(r, j) for j in range(1, chunks) for r in range(1, group)]


def write_mask(steps, chunks, agents, width, blocks, bias):
    group = len(blocks)
    now = (lax.axis_index("tm") * steps + lax.axis_index("agent") // group).astype(jnp.float32)
    lane = lax.broadcasted_iota(jnp.int32, (agents, 128), 1)
    sublane = lax.broadcasted_iota(jnp.int32, (agents, 128), 0)
    tiles = {}
    for r in range(group):
        for k in range(steps):
            tile = blocks[r][agents * k : agents * (k + 1), 2 * width :].astype(jnp.float32)
            tiles[k, r] = (tile[0:1] * RADIX + tile[1:2], tile[2:3])
    own = jnp.concatenate(
        [
            jnp.sum(jnp.where(lane == sublane + j * agents, tiles[k, 0][0], 0.0), axis=1, keepdims=True)
            for k in range(steps)
            for j in range(chunks)
        ],
        axis=0,
    )
    row_lane = lax.broadcasted_iota(jnp.int32, (1, 128), 1)
    per_tile = 128 // agents
    start = 0
    for r, j in block_order(group, chunks):
        for first in range(0, steps, per_tile):
            both = [None, None]
            for i in range(per_tile):
                for f in (0, 1):
                    moved = pltpu.roll(tiles[first + i, r][f], ((i - j) * agents) % 128, 1)
                    both[f] = moved if i == 0 else jnp.where(row_lane >= i * agents, moved, both[f])
            order, present = both
            alive = jnp.where(now < present, order, 1e9)
            visible = (alive < own) | (order == own)
            bias[:, start : start + 128] = jnp.where(visible, 0.0, -1e30)
            start += 128


def rows_of(parts, ks, agents, columns):
    return jnp.concatenate([part[agents * k : agents * (k + 1), columns] for k in ks for part in parts], axis=0)


def pair_stages(queries_of, blocks, bias, top_of, low):
    width = blocks[0].shape[1] // 2 // 128 * 128

    def products(pair):
        queries = queries_of(pair)
        zeros = jnp.zeros_like(queries)
        stacked = jnp.concatenate([jnp.where(low, queries, zeros), jnp.where(low, zeros, queries)], axis=0)
        key = jnp.concatenate([block[:, 128 * pair : 128 * pair + 128] for block in blocks], axis=0)
        return dot_t(stacked, key)

    def weigh(pair, scores):
        rows, keys = scores.shape[0] // 2, scores.shape[1]
        tops, weights = [], []
        for half in range(2):
            here = scores[half * rows : (half + 1) * rows] * (LOG2E * HEAD ** (-0.5)) + bias
            highest = jnp.broadcast_to(jnp.max(here, axis=1, keepdims=True), (rows, 128))
            if top_of is not None:
                highest = jnp.maximum(highest, top_of(pair, half))
            tops.append(highest)
            wide = jnp.concatenate([highest] * (keys // 128), axis=1)
            weights.append(jnp.exp2(here - wide).astype(jnp.bfloat16))
        return tops, jnp.concatenate(weights, axis=0)

    def sums(pair, made):
        tops, weights = made
        start = width + 128 * pair
        value = jnp.concatenate([block[:, start : start + 128] for block in blocks], axis=0)
        return tops, dot(weights, jnp.concatenate([value, jnp.ones(value.shape, jnp.bfloat16)], axis=1))

    return [products, weigh, sums]


def merged(low, total):
    rows = total.shape[0] // 2
    return jnp.where(low, total[:rows], total[rows:])


def early_kernel(ks, steps, chunks, group, query, attn_in, w_query, *refs):
    count = group + chunks - 1
    blocks, (own_query, bias, number, weight, top_low, top_high) = refs[:count], refs[count:]
    own_query[...] = dot(attn_in[...], w_query[...]).astype(jnp.bfloat16)
    rows, width = number.shape
    write_mask(steps, chunks, query.shape[0] // steps, width, blocks[:group], bias)
    agents = rows // (len(ks) * chunks)
    low = lax.broadcasted_iota(jnp.int32, (rows, 128), 1) < HEAD
    keys = sum(block.shape[0] for block in blocks)
    here = bias[ks[0] * agents * chunks : ks[0] * agents * chunks + rows, :keys]

    def columns(pair):
        return slice(128 * pair, 128 * pair + 128)

    def keep(pair, made):
        tops, total = made
        number[:, columns(pair)] = merged(low, total[:, :128])
        weight[:, columns(pair)] = merged(low, total[:, 128:])
        top_low[:, columns(pair)] = tops[0]
        top_high[:, columns(pair)] = tops[1]

    stages = pair_stages(lambda pair: rows_of((query, own_query), ks, agents, columns(pair)), blocks, here, None, low)
    run_pairs(width // 128, 1, [*stages, keep])


def early(ks, steps, group, query, attn_in, w_query, blocks):
    count, width = query.shape
    rows = count * CHUNKS
    state = pltpu.VMEM((len(ks) * rows // steps, width), jnp.float32)
    return pl.pallas_call(
        functools.partial(early_kernel, ks, steps, CHUNKS, group),
        out_shape=[jax.ShapeDtypeStruct(query.shape, jnp.bfloat16), pltpu.VMEM((rows, rows * group), jnp.float32)]
        + [state] * 4,
        in_specs=[VMEM] * (3 + len(blocks)),
        out_specs=[VMEM] * 6,
        compiler_params=pltpu.CompilerParams(vmem_limit_bytes=16 * MIB),
        cost_estimate=cost(0),
        name="early",
    )(query, attn_in, pinned(w_query), *blocks)


def attend_kernel(ks, chunks, count, begun, skipped, *refs):
    mine = 1 + len(ks) * (chunks - 1)
    queries, seconds, (w_output, bias) = refs[:chunks], refs[chunks : chunks + mine], refs[chunks + mine : chunks + mine + 2]
    rest = refs[chunks + mine + 2 :]
    blocks, state = rest[:count], rest[count : count + begun]
    outs = rest[count + begun :]
    width, agents = w_output.shape[1], queries[0].shape[0] // 4
    rows = len(ks) * chunks * agents
    low = lax.broadcasted_iota(jnp.int32, (rows, 128), 1) < HEAD
    keys = sum(block.shape[0] for block in blocks)
    here = bias[ks[0] * agents * chunks : ks[0] * agents * chunks + rows, bias.shape[1] - keys :]
    begun_rows = slice(skipped, skipped + rows)

    def columns(pair):
        return slice(128 * pair, 128 * pair + 128)

    residual = []
    for i, k in enumerate(ks):
        residual += [seconds[0][agents * k : agents * (k + 1)]]
        residual += [piece[...] for piece in seconds[1 + i * (chunks - 1) : 1 + (i + 1) * (chunks - 1)]]
    result = [jnp.concatenate(residual, axis=0).astype(jnp.float32)]

    def keep(pair, made):
        tops, total = made
        number, weight = merged(low, total[:, :128]), merged(low, total[:, 128:])
        if begun:
            drop = [state[2 + half][begun_rows, columns(pair)] - tops[half] for half in range(2)]
            shrink = jnp.exp2(jnp.where(low, *drop))
            number = number + state[0][begun_rows, columns(pair)] * shrink
            weight = weight + state[1][begun_rows, columns(pair)] * shrink
        return (number / weight).astype(jnp.bfloat16)

    waiting, together = [], 2 if begun else width // 128

    def output(pair, attended):
        waiting.append(attended)
        if len(waiting) == together:
            features = slice(128 * (pair + 1 - together), 128 * (pair + 1))
            result[0] = result[0] + dot(jnp.concatenate(waiting, axis=1), w_output[features, :])
            waiting.clear()

    stages = pair_stages(
        lambda pair: rows_of(queries, ks, agents, columns(pair)),
        blocks,
        here,
        (lambda pair, half: state[2 + half][begun_rows, columns(pair)]) if begun else None,
        low,
    )
    run_pairs(width // 128, 2 if begun else 1, [*stages, keep, output])
    for i in range(len(ks)):
        outs[i][...] = result[0][i * agents * chunks : (i + 1) * agents * chunks].astype(jnp.bfloat16)


def attend(ks, queries, seconds, w_output, bias, blocks, state, skipped, agents, microseconds):
    width = queries[0].shape[1]
    piece = jax.ShapeDtypeStruct((agents, width), jnp.bfloat16)
    return pl.pallas_call(
        functools.partial(attend_kernel, ks, len(queries), len(blocks), len(state), skipped),
        out_shape=[piece] * len(ks),
        in_specs=[VMEM] * (len(queries) + len(seconds) + 2 + len(blocks) + len(state)),
        out_specs=[VMEM] * len(ks),
        compiler_params=pltpu.CompilerParams(vmem_limit_bytes=16 * MIB),
        cost_estimate=cost(microseconds),
        name="attend",
    )(*queries, *seconds, pinned(w_output), pinned(bias), *blocks, *[pinned(x) for x in state])


def put_back_kernel(steps, group, *refs):
    pieces, out, sem = refs[:steps][::-1], refs[steps], refs[steps + 1]
    spot = lax.axis_index("agent")
    half = pieces[0].shape[0] // 2
    copies = []
    for k in range(steps):
        target = out.at[(spot // group) ^ away(k, steps, spot % group, lax.axis_index("tm"))]
        for rows in (pl.ds(0, half), pl.ds(half, half)):
            copies.append(pltpu.make_async_copy(pieces[k].at[rows], target.at[rows], sem.at[len(copies)]))
    for copy in copies:
        copy.start()
    for copy in copies:
        copy.wait()


def put_back(group, pieces, shape):
    return pl.pallas_call(
        functools.partial(put_back_kernel, shape[0], group),
        out_shape=jax.ShapeDtypeStruct(shape, jnp.bfloat16),
        in_specs=[VMEM] * len(pieces),
        out_specs=ANY,
        scratch_shapes=[pltpu.SemaphoreType.DMA((2 * len(pieces),))],
        compiler_params=pltpu.CompilerParams(vmem_limit_bytes=4 * MIB),
        cost_estimate=cost(0),
        name="put_back",
    )(*pieces)


def after(x, *others):
    return lax.optimization_barrier((x, *others))[0]


def per_device(
    tokens,
    conv_taps,
    norm_first,
    norm_second,
    norm_third,
    w_in,
    w_out,
    w_query,
    w_key,
    w_value,
    w_output,
    agent_order,
    present_steps,
):
    steps, agents, width = tokens.shape
    tm_count, count = lax.axis_size("tm"), lax.axis_size("agent")
    group = count // steps
    part = agents // CHUNKS
    assert group * steps == count and steps == 4 and 128 % part == 0 and CHUNKS == 2 and group > 1

    def across(x, k):
        if k == steps - 1:
            return x
        pairs = [
            (line * count + i, line * count + ((i // group) ^ away(k, steps, i % group, line)) * group + i % group)
            for line in range(tm_count)
            for i in range(count)
        ]
        return lax.ppermute(x, ("tm", "agent"), pairs)

    def within(x, r):
        return lax.ppermute(x, "agent", [(i, (i // group) * group + ((i % group) ^ r)) for i in range(count)])

    first_part = split(tokens)
    second_part, *partials, tail, taps, gain_first, gain_second, gain_third = stage(
        tokens,
        first_part,
        conv_taps,
        norm_first.reshape(1, width),
        agent_order.reshape(1, agents),
        present_steps.reshape(1, agents),
        [conv_taps] + [x.reshape(1, width) for x in (norm_first, norm_second, norm_third)],
    )
    halos = [lax.ppermute(x, "tm", [(i, (i + 1) % tm_count) for i in range(tm_count)]) for x in (first_part, second_part)]
    halos[0] = after(halos[0], tail)
    made = conv(group, halos[0], partials[0], taps, gain_first, tail)
    last = made[-1]
    pieces = [[across(made[k], k) for k in range(steps)]]
    for j in range(1, CHUNKS):
        halos[j] = after(halos[j], last)
        made = list(front(group, halos[j], partials[j], taps, (gain_first, gain_second), w_in, w_out))
        last = made[-1]
        made[steps - 2] = after(made[steps - 2], pieces[j - 1][0])
        pieces.append([across(made[k], k) for k in range(steps)])
    pieces[0][-1] = after(pieces[0][-1], last)
    query, keyval, second = feed(pieces[0], (gain_second, gain_third), (w_in, w_out, w_key, w_value, w_query))
    blocks = {(0, 0): keyval, **{(r, 0): within(keyval, r) for r in range(1, group)}}
    attn_in, keyval = project(pieces[1], gain_third, (w_key, w_value))
    keyval = after(keyval, *blocks.values())
    blocks.update({(0, 1): keyval, **{(r, 1): within(keyval, r) for r in range(1, group)}})
    blocks = [blocks[spot] for spot in block_order(group, CHUNKS)]
    ready = group + CHUNKS - 1
    far_ks, near_ks = (0, 1), (2, 3)
    own_query, bias, *state = early(far_ks, steps, group, query, attn_in, w_query, blocks[:ready])

    def finish(ks, blocks, state, skipped, microseconds):
        seconds = [second] + [pieces[j][k] for k in ks for j in range(1, CHUNKS)]
        return attend(
            ks, (query, own_query), seconds, w_output, bias, blocks, state, skipped, agents, microseconds
        )

    late = blocks[ready:]
    results = [*finish(far_ks, late, state, 0, 0), *finish(near_ks, blocks, [], 0, 10)]
    return put_back(group, [across(results[k], k) for k in reversed(range(steps))], tokens.shape)


def solution(mesh):
    in_specs = (P("tm", "agent", None),) + (P(),) * 10 + (P("agent"), P("agent"))
    return jax.shard_map(
        per_device, mesh=mesh, in_specs=in_specs, out_specs=P("tm", "agent", None), check_vma=False
    )
```

```python
import functools

import jax
import jax.numpy as jnp
from jax import lax
from jax.experimental import pallas as pl
from jax.experimental.pallas import tpu as pltpu
from jax.sharding import PartitionSpec as P

HEAD = 64
CHUNKS = 2
RADIX = 32
EPS = 1e-05
LOG2E = 1.4426950408889634
MIB = 1024 * 1024
VMEM = pl.BlockSpec(memory_space=pltpu.VMEM)
ANY = pl.BlockSpec(memory_space=pl.ANY)
HBM = pl.BlockSpec(memory_space=pltpu.HBM)


def pinned(x):
    return pltpu.with_memory_space_constraint(x, pltpu.VMEM)


def far(x):
    return pltpu.with_memory_space_constraint(x, pltpu.HBM)


def cost(microseconds):
    return pl.CostEstimate(
        flops=int(1.1e9 * microseconds) + 10**6, bytes_accessed=int(3.5e6 * microseconds) + 10**4, transcendentals=0
    )


def away(k, steps, member, line):
    if k == steps - 1:
        return 0
    odd, first = member % 2, 1 - jnp.minimum(line, 1) if isinstance(line, jax.Array) else int(line == 0)
    first_orders, orders = ((2, 1, 3), (3, 2, 1)), ((2, 3, 1), (2, 1, 3))
    even, odd_away = (a[k] * first + b[k] * (1 - first) for a, b in zip(first_orders, orders))
    return even * (1 - odd) + odd_away * odd


def dot(a, b):
    return jnp.dot(a, b, preferred_element_type=jnp.float32)


def dot_t(a, b):
    return lax.dot_general(a, b, (((1,), (1,)), ((), ())), preferred_element_type=jnp.float32)


def norm_scale(values):
    return lax.rsqrt(jnp.mean(values * values, axis=-1, keepdims=True) + EPS)


def gelu(x):
    return 0.5 * x * (1.0 + lax.erf(x * 0.7071067811865476))


def part_copies(tokens, part, target, sem):
    steps, agents = target.shape[:2]
    return [
        pltpu.make_async_copy(tokens.at[step, pl.ds(part * agents, agents)], target.at[step], sem.at[step])
        for step in range(steps)
    ]


def split_kernel(tokens, out, sem):
    copies = part_copies(tokens, 0, out, sem)
    for copy in copies:
        copy.start()
    for copy in copies:
        copy.wait()


def split(tokens):
    steps, agents, width = tokens.shape
    return pl.pallas_call(
        split_kernel,
        out_shape=pltpu.VMEM((steps, agents // CHUNKS, width), tokens.dtype),
        in_specs=[HBM],
        out_specs=VMEM,
        scratch_shapes=[pltpu.SemaphoreType.DMA((steps,))],
        compiler_params=pltpu.CompilerParams(vmem_limit_bytes=4 * MIB),
        cost_estimate=cost(0),
        name="split",
    )(far(tokens))


def stage_kernel(count, taps, gain, order, present, tokens, first_part, *rest):
    sources, rest = rest[:count], rest[count:]
    second_part, partials, tail, targets = rest[0], rest[1:3], rest[3], rest[4 : 4 + count]
    taps_here, gain_here, order_here, present_here, normed, facts, part_sem, sem = rest[4 + count :]
    pairs = [
        (taps, taps_here),
        (gain, gain_here),
        (order, order_here),
        (present, present_here),
        *zip(sources, targets),
    ]
    copies = [pltpu.make_async_copy(source, target, sem.at[i]) for i, (source, target) in enumerate(pairs)]
    later = part_copies(tokens, 1, second_part, part_sem)
    for copy in copies + later:
        copy.start()
    for copy in copies:
        copy.wait()
    agents = order.shape[1]
    facts[...] = jnp.zeros(facts.shape, jnp.float32)
    facts[0:1, :agents] = (order_here[...] // RADIX).astype(jnp.float32)
    facts[1:2, :agents] = (order_here[...] % RADIX).astype(jnp.float32)
    facts[2:3, :agents] = present_here[...].astype(jnp.float32)
    tail[...] = facts[...].astype(jnp.bfloat16)
    steps, reach = first_part.shape[0], taps.shape[0] - 1
    gains = gain_here[...]
    for j, part in enumerate((first_part, second_part)):
        for step in range(steps):
            if j == 1:
                later[step].wait()
            values = part[step].astype(jnp.float32)
            normed[step] = values * norm_scale(values) * gains
            total = values
            for lag in range(min(step, reach) + 1):
                total = total + taps_here[lag : lag + 1, :] * normed[step - lag]
            partials[j][step] = total


def stage(tokens, first_part, taps, gain, order, present, arrays):
    steps, part, width = first_part.shape
    inputs = (taps, gain, order, present)
    return pl.pallas_call(
        functools.partial(stage_kernel, len(arrays)),
        out_shape=[pltpu.VMEM(first_part.shape, first_part.dtype)]
        + [pltpu.VMEM((steps, part, width), jnp.float32)] * CHUNKS
        + [pltpu.VMEM((part, 128), jnp.bfloat16)]
        + [pltpu.VMEM(x.shape, x.dtype) for x in arrays],
        in_specs=[HBM] * (len(inputs) + 1) + [VMEM] + [HBM] * len(arrays),
        out_specs=[VMEM] * (CHUNKS + 2 + len(arrays)),
        scratch_shapes=[pltpu.VMEM(x.shape, x.dtype) for x in inputs]
        + [
            pltpu.VMEM((steps, part, width), jnp.float32),
            pltpu.VMEM((part, 128), jnp.float32),
            pltpu.SemaphoreType.DMA((steps,)),
            pltpu.SemaphoreType.DMA((len(inputs) + len(arrays),)),
        ],
        compiler_params=pltpu.CompilerParams(vmem_limit_bytes=8 * MIB),
        cost_estimate=cost(30),
        name="stage",
    )(*[far(x) for x in (*inputs, tokens)], pinned(first_part), *[far(x) for x in arrays])


def run_pairs(pairs, lead, stages):
    held = [{} for _ in stages]
    for turn in range(pairs + lead * (len(stages) - 1)):
        for i, stage in enumerate(stages):
            pair = turn - lead * i
            if 0 <= pair < pairs:
                held[i][pair] = stage(pair, held[i - 1].pop(pair)) if i else stage(pair)


def mixed_rows(halo, partial, taps, gain, normed, first):
    steps, agents = halo.shape[:2]
    reach = taps.shape[0] - 1
    gains = gain[...] * (lax.axis_index("tm") > 0).astype(jnp.float32)
    for step in range(steps):
        values = halo[step].astype(jnp.float32)
        normed[step] = values * norm_scale(values) * gains
    for step in range(steps):
        total = partial[step]
        for lag in range(step + 1, reach + 1):
            total = total + taps[lag : lag + 1, :] * normed[steps + step - lag]
        first[step * agents : (step + 1) * agents, :] = total.astype(jnp.bfloat16).astype(first.dtype)


def feed_forward(rows, gain, w_in, w_out):
    inner = (rows * norm_scale(rows) * gain[...]).astype(jnp.bfloat16)
    tile, total = 512, [rows]

    def enter(i):
        return dot(inner, w_in[:, i * tile : (i + 1) * tile])

    def activate(i, products):
        return gelu(products).astype(jnp.bfloat16)

    def leave(i, hidden):
        total[0] = total[0] + dot(hidden, w_out[i * tile : (i + 1) * tile, :])

    run_pairs(w_in.shape[1] // tile, 1, [enter, activate, leave])
    return total[0].astype(jnp.bfloat16)


def to_keys(second, gain, w_key, w_value, keyval):
    width = second.shape[1]
    values = second.astype(jnp.float32)
    attn_in = (values * norm_scale(values) * gain[...]).astype(jnp.bfloat16)
    keyval[:, :width] = dot(attn_in, w_key[...]).astype(jnp.bfloat16)
    keyval[:, width : 2 * width] = dot(attn_in, w_value[...]).astype(jnp.bfloat16)
    return attn_in


def conv_kernel(group, halo, partial, taps, gain, tail, *rest):
    steps, agents, width = halo.shape
    outs = rest[:steps]
    normed, first = rest[steps:]
    mixed_rows(halo, partial, taps, gain, normed, first)
    spot = lax.axis_index("agent")
    for k in range(steps):
        step = (spot // group) ^ away(k, steps, spot % group, lax.axis_index("tm"))
        outs[k][:, :width] = first[pl.ds(pl.multiple_of(step * agents, agents), agents), :].astype(jnp.bfloat16)
        outs[k][:, width:] = tail[...]


def conv(group, halo, partial, taps, gain, tail):
    steps, agents, width = halo.shape
    return pl.pallas_call(
        functools.partial(conv_kernel, group),
        out_shape=[jax.ShapeDtypeStruct((agents, width + tail.shape[1]), jnp.bfloat16)] * steps,
        in_specs=[VMEM] * 5,
        out_specs=[VMEM] * steps,
        scratch_shapes=[
            pltpu.VMEM((steps, agents, width), jnp.float32),
            pltpu.VMEM((steps * agents, width), jnp.float32),
        ],
        compiler_params=pltpu.CompilerParams(vmem_limit_bytes=8 * MIB),
        cost_estimate=cost(0),
        name="conv",
    )(halo, *[pinned(x) for x in (partial, taps, gain, tail)])


def front_kernel(group, halo, partial, taps, gain_first, gain_second, w_in, w_out, *rest):
    steps, agents, width = halo.shape
    outs = rest[:steps]
    normed, first, second = rest[steps:]
    mixed_rows(halo, partial, taps, gain_first, normed, first)
    result = feed_forward(first[...], gain_second, w_in, w_out)
    for step in range(steps):
        second[step] = result[step * agents : (step + 1) * agents]
    spot = lax.axis_index("agent")
    for k in range(steps):
        outs[k][...] = second[(spot // group) ^ away(k, steps, spot % group, lax.axis_index("tm"))]


def front(group, halo, partial, taps, gains, w_in, w_out):
    steps, agents, width = halo.shape
    rows = steps * agents
    return pl.pallas_call(
        functools.partial(front_kernel, group),
        out_shape=[jax.ShapeDtypeStruct((agents, width), jnp.bfloat16)] * steps,
        in_specs=[VMEM] * 7,
        out_specs=[VMEM] * steps,
        scratch_shapes=[
            pltpu.VMEM((steps, agents, width), jnp.float32),
            pltpu.VMEM((rows, width), jnp.float32),
            pltpu.VMEM((steps, agents, width), jnp.bfloat16),
        ],
        compiler_params=pltpu.CompilerParams(vmem_limit_bytes=12 * MIB),
        cost_estimate=cost(0),
        name="front",
    )(halo, *[pinned(x) for x in (partial, taps, *gains, w_in, w_out)])


def feed_kernel(count, *refs):
    pieces = refs[:count]
    gain_second, gain_third, w_in, w_out, w_key, w_value = refs[count : count + 6]
    attn_in, keyval, second = refs[count + 6 :]
    width = gain_second.shape[1]
    agents = pieces[0].shape[0]
    for k in range(count):
        keyval[agents * k : agents * (k + 1), 2 * width :] = pieces[k][:, width:]
    first = jnp.concatenate([piece[:, :width].astype(jnp.float32) for piece in pieces], axis=0)
    result = feed_forward(first, gain_second, w_in, w_out)
    second[...] = result
    attn_in[...] = to_keys(result, gain_third, w_key, w_value, keyval)


def feed(pieces, gains, weights):
    rows = sum(piece.shape[0] for piece in pieces)
    width = gains[0].shape[1]
    return pl.pallas_call(
        functools.partial(feed_kernel, len(pieces)),
        out_shape=[
            jax.ShapeDtypeStruct((rows, width), jnp.bfloat16),
            jax.ShapeDtypeStruct((rows, width + pieces[0].shape[1]), jnp.bfloat16),
            jax.ShapeDtypeStruct((rows, width), jnp.bfloat16),
        ],
        in_specs=[VMEM] * (len(pieces) + 6),
        out_specs=[VMEM] * 3,
        compiler_params=pltpu.CompilerParams(vmem_limit_bytes=12 * MIB),
        cost_estimate=cost(0),
        name="feed",
    )(*pieces, *[pinned(x) for x in (*gains, *weights)])


def project_kernel(count, *refs):
    pieces = refs[:count][::-1]
    gain, w_key, w_value, earlier_in, w_query, attn_in, keyval, query = refs[count:]
    query[...] = dot(earlier_in[...], w_query[...]).astype(jnp.bfloat16)
    second = jnp.concatenate([piece[...] for piece in pieces], axis=0)
    attn_in[...] = to_keys(second, gain, w_key, w_value, keyval)


def project(pieces, gain, weights, earlier_in, w_query):
    rows = sum(piece.shape[0] for piece in pieces)
    width = gain.shape[1]
    return pl.pallas_call(
        functools.partial(project_kernel, len(pieces)),
        out_shape=[
            jax.ShapeDtypeStruct((rows, width), jnp.bfloat16),
            jax.ShapeDtypeStruct((rows, 2 * width), jnp.bfloat16),
            jax.ShapeDtypeStruct(earlier_in.shape, jnp.bfloat16),
        ],
        in_specs=[VMEM] * (len(pieces) + 5),
        out_specs=[VMEM] * 3,
        compiler_params=pltpu.CompilerParams(vmem_limit_bytes=8 * MIB),
        cost_estimate=cost(25),
        name="project",
    )(*reversed(pieces), *[pinned(x) for x in (gain, *weights)], earlier_in, pinned(w_query))


def block_order(group, chunks):
    early = [(r, 0) for r in range(group)] + [(0, j) for j in range(1, chunks)]
    return early + [(r, j) for j in range(1, chunks) for r in range(1, group)]


def write_mask(steps, chunks, agents, width, blocks, bias):
    group = len(blocks)
    now = (lax.axis_index("tm") * steps + lax.axis_index("agent") // group).astype(jnp.float32)
    lane = lax.broadcasted_iota(jnp.int32, (agents, 128), 1)
    sublane = lax.broadcasted_iota(jnp.int32, (agents, 128), 0)
    tiles = {}
    for r in range(group):
        for k in range(steps):
            tile = blocks[r][agents * k : agents * (k + 1), 2 * width :].astype(jnp.float32)
            tiles[k, r] = (tile[0:1] * RADIX + tile[1:2], tile[2:3])
    own = jnp.concatenate(
        [
            jnp.sum(jnp.where(lane == sublane + j * agents, tiles[k, 0][0], 0.0), axis=1, keepdims=True)
            for k in range(steps)
            for j in range(chunks)
        ],
        axis=0,
    )
    row_lane = lax.broadcasted_iota(jnp.int32, (1, 128), 1)
    per_tile = 128 // agents
    start = 0
    for r, j in block_order(group, chunks):
        for first in range(0, steps, per_tile):
            both = [None, None]
            for i in range(per_tile):
                for f in (0, 1):
                    moved = pltpu.roll(tiles[first + i, r][f], ((i - j) * agents) % 128, 1)
                    both[f] = moved if i == 0 else jnp.where(row_lane >= i * agents, moved, both[f])
            order, present = both
            alive = jnp.where(now < present, order, 1e9)
            visible = (alive < own) | (order == own)
            bias[:, start : start + 128] = jnp.where(visible, 0.0, -1e30)
            start += 128


def rows_of(parts, ks, agents, columns):
    return jnp.concatenate([part[agents * k : agents * (k + 1), columns] for k in ks for part in parts], axis=0)


def pair_stages(queries_of, blocks, bias, top_of, low):
    width = blocks[0].shape[1] // 2 // 128 * 128

    def products(pair):
        queries = queries_of(pair)
        zeros = jnp.zeros_like(queries)
        stacked = jnp.concatenate([jnp.where(low, queries, zeros), jnp.where(low, zeros, queries)], axis=0)
        key = jnp.concatenate([block[:, 128 * pair : 128 * pair + 128] for block in blocks], axis=0)
        return dot_t(stacked, key)

    def weigh(pair, scores):
        rows, keys = scores.shape[0] // 2, scores.shape[1]
        tops, weights = [], []
        for half in range(2):
            here = scores[half * rows : (half + 1) * rows] * (LOG2E * HEAD ** (-0.5)) + bias
            highest = jnp.broadcast_to(jnp.max(here, axis=1, keepdims=True), (rows, 128))
            if top_of is not None:
                highest = jnp.maximum(highest, top_of(pair, half))
            tops.append(highest)
            wide = jnp.concatenate([highest] * (keys // 128), axis=1)
            weights.append(jnp.exp2(here - wide).astype(jnp.bfloat16))
        return tops, jnp.concatenate(weights, axis=0)

    def sums(pair, made):
        tops, weights = made
        start = width + 128 * pair
        value = jnp.concatenate([block[:, start : start + 128] for block in blocks], axis=0)
        return tops, dot(weights, jnp.concatenate([value, jnp.ones(value.shape, jnp.bfloat16)], axis=1))

    return [products, weigh, sums]


def merged(low, total):
    rows = total.shape[0] // 2
    return jnp.where(low, total[:rows], total[rows:])


def early_kernel(ks, steps, chunks, group, query, attn_in, w_query, *refs):
    count = group + chunks - 1
    blocks, (own_query, bias, number, weight, top_low, top_high) = refs[:count], refs[count:]
    own_query[...] = dot(attn_in[...], w_query[...]).astype(jnp.bfloat16)
    rows, width = number.shape
    write_mask(steps, chunks, query.shape[0] // steps, width, blocks[:group], bias)
    agents = rows // (len(ks) * chunks)
    low = lax.broadcasted_iota(jnp.int32, (rows, 128), 1) < HEAD
    keys = sum(block.shape[0] for block in blocks)
    here = bias[ks[0] * agents * chunks : ks[0] * agents * chunks + rows, :keys]

    def columns(pair):
        return slice(128 * pair, 128 * pair + 128)

    def keep(pair, made):
        tops, total = made
        number[:, columns(pair)] = merged(low, total[:, :128])
        weight[:, columns(pair)] = merged(low, total[:, 128:])
        top_low[:, columns(pair)] = tops[0]
        top_high[:, columns(pair)] = tops[1]

    stages = pair_stages(lambda pair: rows_of((query, own_query), ks, agents, columns(pair)), blocks, here, None, low)
    run_pairs(width // 128, 1, [*stages, keep])


def early(ks, steps, group, query, attn_in, w_query, blocks):
    count, width = query.shape
    rows = count * CHUNKS
    state = pltpu.VMEM((len(ks) * rows // steps, width), jnp.float32)
    return pl.pallas_call(
        functools.partial(early_kernel, ks, steps, CHUNKS, group),
        out_shape=[jax.ShapeDtypeStruct(query.shape, jnp.bfloat16), pltpu.VMEM((rows, rows * group), jnp.float32)]
        + [state] * 4,
        in_specs=[VMEM] * (3 + len(blocks)),
        out_specs=[VMEM] * 6,
        compiler_params=pltpu.CompilerParams(vmem_limit_bytes=16 * MIB),
        cost_estimate=cost(0),
        name="early",
    )(query, attn_in, pinned(w_query), *blocks)


def attend_kernel(ks, chunks, count, begun, skipped, *refs):
    mine = 1 + len(ks) * (chunks - 1)
    queries, seconds, (w_output, bias) = refs[:chunks], refs[chunks : chunks + mine], refs[chunks + mine : chunks + mine + 2]
    rest = refs[chunks + mine + 2 :]
    blocks, state = rest[:count], rest[count : count + begun]
    outs = rest[count + begun :]
    width, agents = w_output.shape[1], queries[0].shape[0] // 4
    rows = len(ks) * chunks * agents
    low = lax.broadcasted_iota(jnp.int32, (rows, 128), 1) < HEAD
    keys = sum(block.shape[0] for block in blocks)
    here = bias[ks[0] * agents * chunks : ks[0] * agents * chunks + rows, bias.shape[1] - keys :]
    begun_rows = slice(skipped, skipped + rows)

    def columns(pair):
        return slice(128 * pair, 128 * pair + 128)

    residual = []
    for i, k in enumerate(ks):
        residual += [seconds[0][agents * k : agents * (k + 1)]]
        residual += [piece[...] for piece in seconds[1 + i * (chunks - 1) : 1 + (i + 1) * (chunks - 1)]]
    result = [jnp.concatenate(residual, axis=0).astype(jnp.float32)]

    def keep(pair, made):
        tops, total = made
        number, weight = merged(low, total[:, :128]), merged(low, total[:, 128:])
        if begun:
            drop = [state[2 + half][begun_rows, columns(pair)] - tops[half] for half in range(2)]
            shrink = jnp.exp2(jnp.where(low, *drop))
            number = number + state[0][begun_rows, columns(pair)] * shrink
            weight = weight + state[1][begun_rows, columns(pair)] * shrink
        return (number / weight).astype(jnp.bfloat16)

    waiting, together = [], 2 if begun else width // 128

    def output(pair, attended):
        waiting.append(attended)
        if len(waiting) == together:
            features = slice(128 * (pair + 1 - together), 128 * (pair + 1))
            result[0] = result[0] + dot(jnp.concatenate(waiting, axis=1), w_output[features, :])
            waiting.clear()

    stages = pair_stages(
        lambda pair: rows_of(queries, ks, agents, columns(pair)),
        blocks,
        here,
        (lambda pair, half: state[2 + half][begun_rows, columns(pair)]) if begun else None,
        low,
    )
    run_pairs(width // 128, 2 if begun else 1, [*stages, keep, output])
    for i in range(len(ks)):
        outs[i][...] = result[0][i * agents * chunks : (i + 1) * agents * chunks].astype(jnp.bfloat16)


def attend(ks, queries, seconds, w_output, bias, blocks, state, skipped, agents, microseconds):
    width = queries[0].shape[1]
    piece = jax.ShapeDtypeStruct((agents, width), jnp.bfloat16)
    return pl.pallas_call(
        functools.partial(attend_kernel, ks, len(queries), len(blocks), len(state), skipped),
        out_shape=[piece] * len(ks),
        in_specs=[VMEM] * (len(queries) + len(seconds) + 2 + len(blocks) + len(state)),
        out_specs=[VMEM] * len(ks),
        compiler_params=pltpu.CompilerParams(vmem_limit_bytes=16 * MIB),
        cost_estimate=cost(microseconds),
        name="attend",
    )(*queries, *seconds, pinned(w_output), pinned(bias), *blocks, *[pinned(x) for x in state])


def put_back_kernel(steps, group, *refs):
    pieces, out, sem = refs[:steps][::-1], refs[steps], refs[steps + 1]
    spot = lax.axis_index("agent")
    half = pieces[0].shape[0] // 2
    copies = []
    for k in range(steps):
        target = out.at[(spot // group) ^ away(k, steps, spot % group, lax.axis_index("tm"))]
        for rows in (pl.ds(0, half), pl.ds(half, half)):
            copies.append(pltpu.make_async_copy(pieces[k].at[rows], target.at[rows], sem.at[len(copies)]))
    for copy in copies:
        copy.start()
    for copy in copies:
        copy.wait()


def put_back(group, pieces, shape):
    return pl.pallas_call(
        functools.partial(put_back_kernel, shape[0], group),
        out_shape=jax.ShapeDtypeStruct(shape, jnp.bfloat16),
        in_specs=[VMEM] * len(pieces),
        out_specs=ANY,
        scratch_shapes=[pltpu.SemaphoreType.DMA((2 * len(pieces),))],
        compiler_params=pltpu.CompilerParams(vmem_limit_bytes=4 * MIB),
        cost_estimate=cost(0),
        name="put_back",
    )(*pieces)


def after(x, *others):
    return lax.optimization_barrier((x, *others))[0]


def per_device(
    tokens,
    conv_taps,
    norm_first,
    norm_second,
    norm_third,
    w_in,
    w_out,
    w_query,
    w_key,
    w_value,
    w_output,
    agent_order,
    present_steps,
):
    steps, agents, width = tokens.shape
    tm_count, count = lax.axis_size("tm"), lax.axis_size("agent")
    group = count // steps
    part = agents // CHUNKS
    assert group * steps == count and steps == 4 and 128 % part == 0 and CHUNKS == 2 and group > 1

    def across(x, k):
        if k == steps - 1:
            return x
        pairs = [
            (line * count + i, line * count + ((i // group) ^ away(k, steps, i % group, line)) * group + i % group)
            for line in range(tm_count)
            for i in range(count)
        ]
        return lax.ppermute(x, ("tm", "agent"), pairs)

    def within(x, r):
        return lax.ppermute(x, "agent", [(i, (i // group) * group + ((i % group) ^ r)) for i in range(count)])

    first_part = split(tokens)
    second_part, *partials, tail, taps, gain_first, gain_second, gain_third = stage(
        tokens,
        first_part,
        conv_taps,
        norm_first.reshape(1, width),
        agent_order.reshape(1, agents),
        present_steps.reshape(1, agents),
        [conv_taps] + [x.reshape(1, width) for x in (norm_first, norm_second, norm_third)],
    )
    halos = [lax.ppermute(x, "tm", [(i, (i + 1) % tm_count) for i in range(tm_count)]) for x in (first_part, second_part)]
    halos[0] = after(halos[0], tail)
    made = conv(group, halos[0], partials[0], taps, gain_first, tail)
    last = made[-1]
    pieces = [[across(made[k], k) for k in range(steps)]]
    for j in range(1, CHUNKS):
        halos[j] = after(halos[j], last)
        made = list(front(group, halos[j], partials[j], taps, (gain_first, gain_second), w_in, w_out))
        last = made[-1]
        made[steps - 2] = after(made[steps - 2], pieces[j - 1][0])
        pieces.append([across(made[k], k) for k in range(steps)])
    pieces[0][-1] = after(pieces[0][-1], last)
    first_in, keyval, second = feed(pieces[0], (gain_second, gain_third), (w_in, w_out, w_key, w_value))
    blocks = {(0, 0): keyval, **{(r, 0): within(keyval, r) for r in range(1, group)}}
    attn_in, keyval, query = project(pieces[1], gain_third, (w_key, w_value), first_in, w_query)
    keyval = after(keyval, *blocks.values())
    blocks.update({(0, 1): keyval, **{(r, 1): within(keyval, r) for r in range(1, group)}})
    blocks = [blocks[spot] for spot in block_order(group, CHUNKS)]
    ready = group + CHUNKS - 1
    far_ks, near_ks = (0, 1), (2, 3)
    own_query, bias, *state = early(far_ks, steps, group, query, attn_in, w_query, blocks[:ready])

    def finish(ks, blocks, state, skipped, microseconds):
        seconds = [second] + [pieces[j][k] for k in ks for j in range(1, CHUNKS)]
        return attend(
            ks, (query, own_query), seconds, w_output, bias, blocks, state, skipped, agents, microseconds
        )

    late = blocks[ready:]
    results = [*finish(far_ks, late, state, 0, 0), *finish(near_ks, blocks, [], 0, 10)]
    return put_back(group, [across(results[k], k) for k in reversed(range(steps))], tokens.shape)


def solution(mesh):
    in_specs = (P("tm", "agent", None),) + (P(),) * 10 + (P("agent"), P("agent"))
    return jax.shard_map(
        per_device, mesh=mesh, in_specs=in_specs, out_specs=P("tm", "agent", None), check_vma=False
    )
```

```python
import functools

import jax
import jax.numpy as jnp
from jax import lax
from jax.experimental import pallas as pl
from jax.experimental.pallas import tpu as pltpu
from jax.sharding import PartitionSpec as P

HEAD = 64
CHUNKS = 2
RADIX = 32
EPS = 1e-05
LOG2E = 1.4426950408889634
MIB = 1024 * 1024
VMEM = pl.BlockSpec(memory_space=pltpu.VMEM)
ANY = pl.BlockSpec(memory_space=pl.ANY)
HBM = pl.BlockSpec(memory_space=pltpu.HBM)


def pinned(x):
    return pltpu.with_memory_space_constraint(x, pltpu.VMEM)


def far(x):
    return pltpu.with_memory_space_constraint(x, pltpu.HBM)


def cost(microseconds):
    return pl.CostEstimate(
        flops=int(1.1e9 * microseconds) + 10**6, bytes_accessed=int(3.5e6 * microseconds) + 10**4, transcendentals=0
    )


def away(k, steps, member, line):
    if k == steps - 1:
        return 0
    odd, first = member % 2, 1 - jnp.minimum(line, 1) if isinstance(line, jax.Array) else int(line == 0)
    first_orders, orders = ((3, 1, 2), (3, 2, 1)), ((2, 3, 1), (2, 1, 3))
    even, odd_away = (a[k] * first + b[k] * (1 - first) for a, b in zip(first_orders, orders))
    return even * (1 - odd) + odd_away * odd


def dot(a, b):
    return jnp.dot(a, b, preferred_element_type=jnp.float32)


def dot_t(a, b):
    return lax.dot_general(a, b, (((1,), (1,)), ((), ())), preferred_element_type=jnp.float32)


def norm_scale(values):
    return lax.rsqrt(jnp.mean(values * values, axis=-1, keepdims=True) + EPS)


def gelu(x):
    return 0.5 * x * (1.0 + lax.erf(x * 0.7071067811865476))


def part_copies(tokens, part, target, sem):
    steps, agents = target.shape[:2]
    return [
        pltpu.make_async_copy(tokens.at[step, pl.ds(part * agents, agents)], target.at[step], sem.at[step])
        for step in range(steps)
    ]


def split_kernel(tokens, out, sem):
    copies = part_copies(tokens, 0, out, sem)
    for copy in copies:
        copy.start()
    for copy in copies:
        copy.wait()


def split(tokens):
    steps, agents, width = tokens.shape
    return pl.pallas_call(
        split_kernel,
        out_shape=pltpu.VMEM((steps, agents // CHUNKS, width), tokens.dtype),
        in_specs=[HBM],
        out_specs=VMEM,
        scratch_shapes=[pltpu.SemaphoreType.DMA((steps,))],
        compiler_params=pltpu.CompilerParams(vmem_limit_bytes=4 * MIB),
        cost_estimate=cost(0),
        name="split",
    )(far(tokens))


def stage_kernel(count, taps, gain, order, present, tokens, first_part, *rest):
    sources, rest = rest[:count], rest[count:]
    second_part, partials, tail, targets = rest[0], rest[1:3], rest[3], rest[4 : 4 + count]
    taps_here, gain_here, order_here, present_here, normed, facts, part_sem, sem = rest[4 + count :]
    pairs = [
        (taps, taps_here),
        (gain, gain_here),
        (order, order_here),
        (present, present_here),
        *zip(sources, targets),
    ]
    copies = [pltpu.make_async_copy(source, target, sem.at[i]) for i, (source, target) in enumerate(pairs)]
    later = part_copies(tokens, 1, second_part, part_sem)
    for copy in copies + later:
        copy.start()
    for copy in copies:
        copy.wait()
    agents = order.shape[1]
    facts[...] = jnp.zeros(facts.shape, jnp.float32)
    facts[0:1, :agents] = (order_here[...] // RADIX).astype(jnp.float32)
    facts[1:2, :agents] = (order_here[...] % RADIX).astype(jnp.float32)
    facts[2:3, :agents] = present_here[...].astype(jnp.float32)
    tail[...] = facts[...].astype(jnp.bfloat16)
    steps, reach = first_part.shape[0], taps.shape[0] - 1
    gains = gain_here[...]
    for j, part in enumerate((first_part, second_part)):
        for step in range(steps):
            if j == 1:
                later[step].wait()
            values = part[step].astype(jnp.float32)
            normed[step] = values * norm_scale(values) * gains
            total = values
            for lag in range(min(step, reach) + 1):
                total = total + taps_here[lag : lag + 1, :] * normed[step - lag]
            partials[j][step] = total


def stage(tokens, first_part, taps, gain, order, present, arrays):
    steps, part, width = first_part.shape
    inputs = (taps, gain, order, present)
    return pl.pallas_call(
        functools.partial(stage_kernel, len(arrays)),
        out_shape=[pltpu.VMEM(first_part.shape, first_part.dtype)]
        + [pltpu.VMEM((steps, part, width), jnp.float32)] * CHUNKS
        + [pltpu.VMEM((part, 128), jnp.bfloat16)]
        + [pltpu.VMEM(x.shape, x.dtype) for x in arrays],
        in_specs=[HBM] * (len(inputs) + 1) + [VMEM] + [HBM] * len(arrays),
        out_specs=[VMEM] * (CHUNKS + 2 + len(arrays)),
        scratch_shapes=[pltpu.VMEM(x.shape, x.dtype) for x in inputs]
        + [
            pltpu.VMEM((steps, part, width), jnp.float32),
            pltpu.VMEM((part, 128), jnp.float32),
            pltpu.SemaphoreType.DMA((steps,)),
            pltpu.SemaphoreType.DMA((len(inputs) + len(arrays),)),
        ],
        compiler_params=pltpu.CompilerParams(vmem_limit_bytes=8 * MIB),
        cost_estimate=cost(30),
        name="stage",
    )(*[far(x) for x in (*inputs, tokens)], pinned(first_part), *[far(x) for x in arrays])


def run_pairs(pairs, lead, stages):
    held = [{} for _ in stages]
    for turn in range(pairs + lead * (len(stages) - 1)):
        for i, stage in enumerate(stages):
            pair = turn - lead * i
            if 0 <= pair < pairs:
                held[i][pair] = stage(pair, held[i - 1].pop(pair)) if i else stage(pair)


def mixed_rows(halo, partial, taps, gain, normed, first):
    steps, agents = halo.shape[:2]
    reach = taps.shape[0] - 1
    gains = gain[...] * (lax.axis_index("tm") > 0).astype(jnp.float32)
    for step in range(steps):
        values = halo[step].astype(jnp.float32)
        normed[step] = values * norm_scale(values) * gains
    for step in range(steps):
        total = partial[step]
        for lag in range(step + 1, reach + 1):
            total = total + taps[lag : lag + 1, :] * normed[steps + step - lag]
        first[step * agents : (step + 1) * agents, :] = total.astype(jnp.bfloat16).astype(first.dtype)


def feed_forward(rows, gain, w_in, w_out):
    inner = (rows * norm_scale(rows) * gain[...]).astype(jnp.bfloat16)
    tile, total = 512, [rows]

    def enter(i):
        return dot(inner, w_in[:, i * tile : (i + 1) * tile])

    def activate(i, products):
        return gelu(products).astype(jnp.bfloat16)

    def leave(i, hidden):
        total[0] = total[0] + dot(hidden, w_out[i * tile : (i + 1) * tile, :])

    run_pairs(w_in.shape[1] // tile, 1, [enter, activate, leave])
    return total[0].astype(jnp.bfloat16)


def to_keys(second, gain, w_key, w_value, keyval):
    width = second.shape[1]
    values = second.astype(jnp.float32)
    attn_in = (values * norm_scale(values) * gain[...]).astype(jnp.bfloat16)
    keyval[:, :width] = dot(attn_in, w_key[...]).astype(jnp.bfloat16)
    keyval[:, width : 2 * width] = dot(attn_in, w_value[...]).astype(jnp.bfloat16)
    return attn_in


def conv_kernel(group, halo, partial, taps, gain, tail, *rest):
    steps, agents, width = halo.shape
    outs = rest[:steps]
    normed, first = rest[steps:]
    mixed_rows(halo, partial, taps, gain, normed, first)
    spot = lax.axis_index("agent")
    for k in range(steps):
        step = (spot // group) ^ away(k, steps, spot % group, lax.axis_index("tm"))
        outs[k][:, :width] = first[pl.ds(pl.multiple_of(step * agents, agents), agents), :].astype(jnp.bfloat16)
        outs[k][:, width:] = tail[...]


def conv(group, halo, partial, taps, gain, tail):
    steps, agents, width = halo.shape
    return pl.pallas_call(
        functools.partial(conv_kernel, group),
        out_shape=[jax.ShapeDtypeStruct((agents, width + tail.shape[1]), jnp.bfloat16)] * steps,
        in_specs=[VMEM] * 5,
        out_specs=[VMEM] * steps,
        scratch_shapes=[
            pltpu.VMEM((steps, agents, width), jnp.float32),
            pltpu.VMEM((steps * agents, width), jnp.float32),
        ],
        compiler_params=pltpu.CompilerParams(vmem_limit_bytes=8 * MIB),
        cost_estimate=cost(0),
        name="conv",
    )(halo, *[pinned(x) for x in (partial, taps, gain, tail)])


def front_kernel(group, halo, partial, taps, gain_first, gain_second, w_in, w_out, *rest):
    steps, agents, width = halo.shape
    outs = rest[:steps]
    normed, first, second = rest[steps:]
    mixed_rows(halo, partial, taps, gain_first, normed, first)
    result = feed_forward(first[...], gain_second, w_in, w_out)
    for step in range(steps):
        second[step] = result[step * agents : (step + 1) * agents]
    spot = lax.axis_index("agent")
    for k in range(steps):
        outs[k][...] = second[(spot // group) ^ away(k, steps, spot % group, lax.axis_index("tm"))]


def front(group, halo, partial, taps, gains, w_in, w_out):
    steps, agents, width = halo.shape
    rows = steps * agents
    return pl.pallas_call(
        functools.partial(front_kernel, group),
        out_shape=[jax.ShapeDtypeStruct((agents, width), jnp.bfloat16)] * steps,
        in_specs=[VMEM] * 7,
        out_specs=[VMEM] * steps,
        scratch_shapes=[
            pltpu.VMEM((steps, agents, width), jnp.float32),
            pltpu.VMEM((rows, width), jnp.float32),
            pltpu.VMEM((steps, agents, width), jnp.bfloat16),
        ],
        compiler_params=pltpu.CompilerParams(vmem_limit_bytes=12 * MIB),
        cost_estimate=cost(0),
        name="front",
    )(halo, *[pinned(x) for x in (partial, taps, *gains, w_in, w_out)])


def feed_kernel(count, *refs):
    pieces = refs[:count]
    gain_second, gain_third, w_in, w_out, w_key, w_value, w_query = refs[count : count + 7]
    query, keyval, second = refs[count + 7 :]
    width = gain_second.shape[1]
    agents = pieces[0].shape[0]
    for k in range(count):
        keyval[agents * k : agents * (k + 1), 2 * width :] = pieces[k][:, width:]
    first = jnp.concatenate([piece[:, :width].astype(jnp.float32) for piece in pieces], axis=0)
    result = feed_forward(first, gain_second, w_in, w_out)
    second[...] = result
    attn_in = to_keys(result, gain_third, w_key, w_value, keyval)
    query[...] = dot(attn_in, w_query[...]).astype(jnp.bfloat16)


def feed(pieces, gains, weights):
    rows = sum(piece.shape[0] for piece in pieces)
    width = gains[0].shape[1]
    return pl.pallas_call(
        functools.partial(feed_kernel, len(pieces)),
        out_shape=[
            jax.ShapeDtypeStruct((rows, width), jnp.bfloat16),
            jax.ShapeDtypeStruct((rows, width + pieces[0].shape[1]), jnp.bfloat16),
            jax.ShapeDtypeStruct((rows, width), jnp.bfloat16),
        ],
        in_specs=[VMEM] * (len(pieces) + 7),
        out_specs=[VMEM] * 3,
        compiler_params=pltpu.CompilerParams(vmem_limit_bytes=12 * MIB),
        cost_estimate=cost(0),
        name="feed",
    )(*pieces, *[pinned(x) for x in (*gains, *weights)])


def project_kernel(count, *refs):
    pieces = refs[:count][::-1]
    gain, w_key, w_value, attn_in, keyval = refs[count:]
    second = jnp.concatenate([piece[...] for piece in pieces], axis=0)
    attn_in[...] = to_keys(second, gain, w_key, w_value, keyval)


def project(pieces, gain, weights):
    rows = sum(piece.shape[0] for piece in pieces)
    width = gain.shape[1]
    return pl.pallas_call(
        functools.partial(project_kernel, len(pieces)),
        out_shape=[
            jax.ShapeDtypeStruct((rows, width), jnp.bfloat16),
            jax.ShapeDtypeStruct((rows, 2 * width), jnp.bfloat16),
        ],
        in_specs=[VMEM] * (len(pieces) + 3),
        out_specs=[VMEM] * 2,
        compiler_params=pltpu.CompilerParams(vmem_limit_bytes=8 * MIB),
        cost_estimate=cost(25),
        name="project",
    )(*reversed(pieces), *[pinned(x) for x in (gain, *weights)])


def block_order(group, chunks):
    early = [(r, 0) for r in range(group)] + [(0, j) for j in range(1, chunks)]
    return early + [(r, j) for j in range(1, chunks) for r in range(1, group)]


def write_mask(steps, chunks, agents, width, blocks, bias):
    group = len(blocks)
    now = (lax.axis_index("tm") * steps + lax.axis_index("agent") // group).astype(jnp.float32)
    lane = lax.broadcasted_iota(jnp.int32, (agents, 128), 1)
    sublane = lax.broadcasted_iota(jnp.int32, (agents, 128), 0)
    tiles = {}
    for r in range(group):
        for k in range(steps):
            tile = blocks[r][agents * k : agents * (k + 1), 2 * width :].astype(jnp.float32)
            tiles[k, r] = (tile[0:1] * RADIX + tile[1:2], tile[2:3])
    own = jnp.concatenate(
        [
            jnp.sum(jnp.where(lane == sublane + j * agents, tiles[k, 0][0], 0.0), axis=1, keepdims=True)
            for k in range(steps)
            for j in range(chunks)
        ],
        axis=0,
    )
    row_lane = lax.broadcasted_iota(jnp.int32, (1, 128), 1)
    per_tile = 128 // agents
    start = 0
    for r, j in block_order(group, chunks):
        for first in range(0, steps, per_tile):
            both = [None, None]
            for i in range(per_tile):
                for f in (0, 1):
                    moved = pltpu.roll(tiles[first + i, r][f], ((i - j) * agents) % 128, 1)
                    both[f] = moved if i == 0 else jnp.where(row_lane >= i * agents, moved, both[f])
            order, present = both
            alive = jnp.where(now < present, order, 1e9)
            visible = (alive < own) | (order == own)
            bias[:, start : start + 128] = jnp.where(visible, 0.0, -1e30)
            start += 128


def rows_of(parts, ks, agents, columns):
    return jnp.concatenate([part[agents * k : agents * (k + 1), columns] for k in ks for part in parts], axis=0)


def pair_stages(queries_of, blocks, bias, top_of, low):
    width = blocks[0].shape[1] // 2 // 128 * 128

    def products(pair):
        queries = queries_of(pair)
        zeros = jnp.zeros_like(queries)
        stacked = jnp.concatenate([jnp.where(low, queries, zeros), jnp.where(low, zeros, queries)], axis=0)
        key = jnp.concatenate([block[:, 128 * pair : 128 * pair + 128] for block in blocks], axis=0)
        return dot_t(stacked, key)

    def weigh(pair, scores):
        rows, keys = scores.shape[0] // 2, scores.shape[1]
        tops, weights = [], []
        for half in range(2):
            here = scores[half * rows : (half + 1) * rows] * (LOG2E * HEAD ** (-0.5)) + bias
            highest = jnp.broadcast_to(jnp.max(here, axis=1, keepdims=True), (rows, 128))
            if top_of is not None:
                highest = jnp.maximum(highest, top_of(pair, half))
            tops.append(highest)
            wide = jnp.concatenate([highest] * (keys // 128), axis=1)
            weights.append(jnp.exp2(here - wide).astype(jnp.bfloat16))
        return tops, jnp.concatenate(weights, axis=0)

    def sums(pair, made):
        tops, weights = made
        start = width + 128 * pair
        value = jnp.concatenate([block[:, start : start + 128] for block in blocks], axis=0)
        return tops, dot(weights, jnp.concatenate([value, jnp.ones(value.shape, jnp.bfloat16)], axis=1))

    return [products, weigh, sums]


def merged(low, total):
    rows = total.shape[0] // 2
    return jnp.where(low, total[:rows], total[rows:])


def early_kernel(ks, steps, chunks, group, query, attn_in, w_query, *refs):
    count = group + chunks - 1
    blocks, (own_query, bias, number, weight, top_low, top_high) = refs[:count], refs[count:]
    own_query[...] = dot(attn_in[...], w_query[...]).astype(jnp.bfloat16)
    rows, width = number.shape
    write_mask(steps, chunks, query.shape[0] // steps, width, blocks[:group], bias)
    agents = rows // (len(ks) * chunks)
    low = lax.broadcasted_iota(jnp.int32, (rows, 128), 1) < HEAD
    keys = sum(block.shape[0] for block in blocks)
    here = bias[ks[0] * agents * chunks : ks[0] * agents * chunks + rows, :keys]

    def columns(pair):
        return slice(128 * pair, 128 * pair + 128)

    def keep(pair, made):
        tops, total = made
        number[:, columns(pair)] = merged(low, total[:, :128])
        weight[:, columns(pair)] = merged(low, total[:, 128:])
        top_low[:, columns(pair)] = tops[0]
        top_high[:, columns(pair)] = tops[1]

    stages = pair_stages(lambda pair: rows_of((query, own_query), ks, agents, columns(pair)), blocks, here, None, low)
    run_pairs(width // 128, 1, [*stages, keep])


def early(ks, steps, group, query, attn_in, w_query, blocks):
    count, width = query.shape
    rows = count * CHUNKS
    state = pltpu.VMEM((len(ks) * rows // steps, width), jnp.float32)
    return pl.pallas_call(
        functools.partial(early_kernel, ks, steps, CHUNKS, group),
        out_shape=[jax.ShapeDtypeStruct(query.shape, jnp.bfloat16), pltpu.VMEM((rows, rows * group), jnp.float32)]
        + [state] * 4,
        in_specs=[VMEM] * (3 + len(blocks)),
        out_specs=[VMEM] * 6,
        compiler_params=pltpu.CompilerParams(vmem_limit_bytes=16 * MIB),
        cost_estimate=cost(0),
        name="early",
    )(query, attn_in, pinned(w_query), *blocks)


def attend_kernel(ks, chunks, count, begun, skipped, *refs):
    mine = 1 + len(ks) * (chunks - 1)
    queries, seconds, (w_output, bias) = refs[:chunks], refs[chunks : chunks + mine], refs[chunks + mine : chunks + mine + 2]
    rest = refs[chunks + mine + 2 :]
    blocks, state = rest[:count], rest[count : count + begun]
    outs = rest[count + begun :]
    width, agents = w_output.shape[1], queries[0].shape[0] // 4
    rows = len(ks) * chunks * agents
    low = lax.broadcasted_iota(jnp.int32, (rows, 128), 1) < HEAD
    keys = sum(block.shape[0] for block in blocks)
    here = bias[ks[0] * agents * chunks : ks[0] * agents * chunks + rows, bias.shape[1] - keys :]
    begun_rows = slice(skipped, skipped + rows)

    def columns(pair):
        return slice(128 * pair, 128 * pair + 128)

    residual = []
    for i, k in enumerate(ks):
        residual += [seconds[0][agents * k : agents * (k + 1)]]
        residual += [piece[...] for piece in seconds[1 + i * (chunks - 1) : 1 + (i + 1) * (chunks - 1)]]
    result = [jnp.concatenate(residual, axis=0).astype(jnp.float32)]

    def keep(pair, made):
        tops, total = made
        number, weight = merged(low, total[:, :128]), merged(low, total[:, 128:])
        if begun:
            drop = [state[2 + half][begun_rows, columns(pair)] - tops[half] for half in range(2)]
            shrink = jnp.exp2(jnp.where(low, *drop))
            number = number + state[0][begun_rows, columns(pair)] * shrink
            weight = weight + state[1][begun_rows, columns(pair)] * shrink
        return (number / weight).astype(jnp.bfloat16)

    waiting, together = [], 2 if begun else width // 128

    def output(pair, attended):
        waiting.append(attended)
        if len(waiting) == together:
            features = slice(128 * (pair + 1 - together), 128 * (pair + 1))
            result[0] = result[0] + dot(jnp.concatenate(waiting, axis=1), w_output[features, :])
            waiting.clear()

    stages = pair_stages(
        lambda pair: rows_of(queries, ks, agents, columns(pair)),
        blocks,
        here,
        (lambda pair, half: state[2 + half][begun_rows, columns(pair)]) if begun else None,
        low,
    )
    run_pairs(width // 128, 2 if begun else 1, [*stages, keep, output])
    for i in range(len(ks)):
        outs[i][...] = result[0][i * agents * chunks : (i + 1) * agents * chunks].astype(jnp.bfloat16)


def attend(ks, queries, seconds, w_output, bias, blocks, state, skipped, agents, microseconds):
    width = queries[0].shape[1]
    piece = jax.ShapeDtypeStruct((agents, width), jnp.bfloat16)
    return pl.pallas_call(
        functools.partial(attend_kernel, ks, len(queries), len(blocks), len(state), skipped),
        out_shape=[piece] * len(ks),
        in_specs=[VMEM] * (len(queries) + len(seconds) + 2 + len(blocks) + len(state)),
        out_specs=[VMEM] * len(ks),
        compiler_params=pltpu.CompilerParams(vmem_limit_bytes=16 * MIB),
        cost_estimate=cost(microseconds),
        name="attend",
    )(*queries, *seconds, pinned(w_output), pinned(bias), *blocks, *[pinned(x) for x in state])


def put_back_kernel(steps, group, *refs):
    pieces, out, sem = refs[:steps][::-1], refs[steps], refs[steps + 1]
    spot = lax.axis_index("agent")
    half = pieces[0].shape[0] // 2
    copies = []
    for k in range(steps):
        target = out.at[(spot // group) ^ away(k, steps, spot % group, lax.axis_index("tm"))]
        for rows in (pl.ds(0, half), pl.ds(half, half)):
            copies.append(pltpu.make_async_copy(pieces[k].at[rows], target.at[rows], sem.at[len(copies)]))
    for copy in copies:
        copy.start()
    for copy in copies:
        copy.wait()


def put_back(group, pieces, shape):
    return pl.pallas_call(
        functools.partial(put_back_kernel, shape[0], group),
        out_shape=jax.ShapeDtypeStruct(shape, jnp.bfloat16),
        in_specs=[VMEM] * len(pieces),
        out_specs=ANY,
        scratch_shapes=[pltpu.SemaphoreType.DMA((2 * len(pieces),))],
        compiler_params=pltpu.CompilerParams(vmem_limit_bytes=4 * MIB),
        cost_estimate=cost(0),
        name="put_back",
    )(*pieces)


def after(x, *others):
    return lax.optimization_barrier((x, *others))[0]


def per_device(
    tokens,
    conv_taps,
    norm_first,
    norm_second,
    norm_third,
    w_in,
    w_out,
    w_query,
    w_key,
    w_value,
    w_output,
    agent_order,
    present_steps,
):
    steps, agents, width = tokens.shape
    tm_count, count = lax.axis_size("tm"), lax.axis_size("agent")
    group = count // steps
    part = agents // CHUNKS
    assert group * steps == count and steps == 4 and 128 % part == 0 and CHUNKS == 2 and group > 1

    def across(x, k):
        if k == steps - 1:
            return x
        pairs = [
            (line * count + i, line * count + ((i // group) ^ away(k, steps, i % group, line)) * group + i % group)
            for line in range(tm_count)
            for i in range(count)
        ]
        return lax.ppermute(x, ("tm", "agent"), pairs)

    def within(x, r):
        return lax.ppermute(x, "agent", [(i, (i // group) * group + ((i % group) ^ r)) for i in range(count)])

    first_part = split(tokens)
    second_part, *partials, tail, taps, gain_first, gain_second, gain_third = stage(
        tokens,
        first_part,
        conv_taps,
        norm_first.reshape(1, width),
        agent_order.reshape(1, agents),
        present_steps.reshape(1, agents),
        [conv_taps] + [x.reshape(1, width) for x in (norm_first, norm_second, norm_third)],
    )
    halos = [lax.ppermute(x, "tm", [(i, (i + 1) % tm_count) for i in range(tm_count)]) for x in (first_part, second_part)]
    halos[0] = after(halos[0], tail)
    made = conv(group, halos[0], partials[0], taps, gain_first, tail)
    last = made[-1]
    pieces = [[across(made[k], k) for k in range(steps)]]
    for j in range(1, CHUNKS):
        halos[j] = after(halos[j], last)
        made = list(front(group, halos[j], partials[j], taps, (gain_first, gain_second), w_in, w_out))
        last = made[-1]
        made[steps - 2] = after(made[steps - 2], pieces[j - 1][0])
        pieces.append([across(made[k], k) for k in range(steps)])
    pieces[0][-1] = after(pieces[0][-1], last)
    query, keyval, second = feed(pieces[0], (gain_second, gain_third), (w_in, w_out, w_key, w_value, w_query))
    blocks = {(0, 0): keyval, **{(r, 0): within(keyval, r) for r in range(1, group)}}
    attn_in, keyval = project(pieces[1], gain_third, (w_key, w_value))
    keyval = after(keyval, *blocks.values())
    blocks.update({(0, 1): keyval, **{(r, 1): within(keyval, r) for r in range(1, group)}})
    blocks = [blocks[spot] for spot in block_order(group, CHUNKS)]
    ready = group + CHUNKS - 1
    far_ks, near_ks = (0, 1), (2, 3)
    own_query, bias, *state = early(far_ks, steps, group, query, attn_in, w_query, blocks[:ready])

    def finish(ks, blocks, state, skipped, microseconds):
        seconds = [second] + [pieces[j][k] for k in ks for j in range(1, CHUNKS)]
        return attend(
            ks, (query, own_query), seconds, w_output, bias, blocks, state, skipped, agents, microseconds
        )

    late = blocks[ready:]
    results = [*finish(far_ks, late, state, 0, 0), *finish(near_ks, blocks, [], 0, 10)]
    return put_back(group, [across(results[k], k) for k in reversed(range(steps))], tokens.shape)


def solution(mesh):
    in_specs = (P("tm", "agent", None),) + (P(),) * 10 + (P("agent"), P("agent"))
    return jax.shard_map(
        per_device, mesh=mesh, in_specs=in_specs, out_specs=P("tm", "agent", None), check_vma=False
    )
```

```python
import functools

import jax
import jax.numpy as jnp
from jax import lax
from jax.experimental import pallas as pl
from jax.experimental.pallas import tpu as pltpu
from jax.sharding import PartitionSpec as P

HEAD = 64
CHUNKS = 2
RADIX = 32
EPS = 1e-05
LOG2E = 1.4426950408889634
MIB = 1024 * 1024
VMEM = pl.BlockSpec(memory_space=pltpu.VMEM)
ANY = pl.BlockSpec(memory_space=pl.ANY)
HBM = pl.BlockSpec(memory_space=pltpu.HBM)


def pinned(x):
    return pltpu.with_memory_space_constraint(x, pltpu.VMEM)


def far(x):
    return pltpu.with_memory_space_constraint(x, pltpu.HBM)


def cost(microseconds):
    return pl.CostEstimate(
        flops=int(1.1e9 * microseconds) + 10**6, bytes_accessed=int(3.5e6 * microseconds) + 10**4, transcendentals=0
    )


def away(k, steps, member, line):
    if k == steps - 1:
        return 0
    odd, first = member % 2, 1 - jnp.minimum(line, 1) if isinstance(line, jax.Array) else int(line == 0)
    first_orders, orders = ((2, 1, 3), (3, 2, 1)), ((2, 3, 1), (2, 1, 3))
    even, odd_away = (a[k] * first + b[k] * (1 - first) for a, b in zip(first_orders, orders))
    return even * (1 - odd) + odd_away * odd


def dot(a, b):
    return jnp.dot(a, b, preferred_element_type=jnp.float32)


def dot_t(a, b):
    return lax.dot_general(a, b, (((1,), (1,)), ((), ())), preferred_element_type=jnp.float32)


def norm_scale(values):
    return lax.rsqrt(jnp.mean(values * values, axis=-1, keepdims=True) + EPS)


def gelu(x):
    return 0.5 * x * (1.0 + lax.erf(x * 0.7071067811865476))


def part_copies(tokens, part, target, sem):
    steps, agents = target.shape[:2]
    return [
        pltpu.make_async_copy(tokens.at[step, pl.ds(part * agents, agents)], target.at[step], sem.at[step])
        for step in range(steps)
    ]


def split_kernel(tokens, out, sem):
    copies = part_copies(tokens, 0, out, sem)
    for copy in copies:
        copy.start()
    for copy in copies:
        copy.wait()


def split(tokens):
    steps, agents, width = tokens.shape
    return pl.pallas_call(
        split_kernel,
        out_shape=pltpu.VMEM((steps, agents // CHUNKS, width), tokens.dtype),
        in_specs=[HBM],
        out_specs=VMEM,
        scratch_shapes=[pltpu.SemaphoreType.DMA((steps,))],
        compiler_params=pltpu.CompilerParams(vmem_limit_bytes=4 * MIB),
        cost_estimate=cost(0),
        name="split",
    )(far(tokens))


def stage_kernel(count, taps, gain, order, present, tokens, first_part, *rest):
    sources, rest = rest[:count], rest[count:]
    second_part, partials, tail, targets = rest[0], rest[1:3], rest[3], rest[4 : 4 + count]
    taps_here, gain_here, order_here, present_here, normed, facts, part_sem, sem = rest[4 + count :]
    pairs = [
        (taps, taps_here),
        (gain, gain_here),
        (order, order_here),
        (present, present_here),
        *zip(sources, targets),
    ]
    copies = [pltpu.make_async_copy(source, target, sem.at[i]) for i, (source, target) in enumerate(pairs)]
    later = part_copies(tokens, 1, second_part, part_sem)
    for copy in copies + later:
        copy.start()
    for copy in copies:
        copy.wait()
    agents = order.shape[1]
    facts[...] = jnp.zeros(facts.shape, jnp.float32)
    facts[0:1, :agents] = (order_here[...] // RADIX).astype(jnp.float32)
    facts[1:2, :agents] = (order_here[...] % RADIX).astype(jnp.float32)
    facts[2:3, :agents] = present_here[...].astype(jnp.float32)
    tail[...] = facts[...].astype(jnp.bfloat16)
    steps, reach = first_part.shape[0], taps.shape[0] - 1
    gains = gain_here[...]
    for j, part in enumerate((first_part, second_part)):
        for step in range(steps):
            if j == 1:
                later[step].wait()
            values = part[step].astype(jnp.float32)
            normed[step] = values * norm_scale(values) * gains
            total = values
            for lag in range(min(step, reach) + 1):
                total = total + taps_here[lag : lag + 1, :] * normed[step - lag]
            partials[j][step] = total


def stage(tokens, first_part, taps, gain, order, present, arrays):
    steps, part, width = first_part.shape
    inputs = (taps, gain, order, present)
    return pl.pallas_call(
        functools.partial(stage_kernel, len(arrays)),
        out_shape=[pltpu.VMEM(first_part.shape, first_part.dtype)]
        + [pltpu.VMEM((steps, part, width), jnp.float32)] * CHUNKS
        + [pltpu.VMEM((part, 128), jnp.bfloat16)]
        + [pltpu.VMEM(x.shape, x.dtype) for x in arrays],
        in_specs=[HBM] * (len(inputs) + 1) + [VMEM] + [HBM] * len(arrays),
        out_specs=[VMEM] * (CHUNKS + 2 + len(arrays)),
        scratch_shapes=[pltpu.VMEM(x.shape, x.dtype) for x in inputs]
        + [
            pltpu.VMEM((steps, part, width), jnp.float32),
            pltpu.VMEM((part, 128), jnp.float32),
            pltpu.SemaphoreType.DMA((steps,)),
            pltpu.SemaphoreType.DMA((len(inputs) + len(arrays),)),
        ],
        compiler_params=pltpu.CompilerParams(vmem_limit_bytes=8 * MIB),
        cost_estimate=cost(30),
        name="stage",
    )(*[far(x) for x in (*inputs, tokens)], pinned(first_part), *[far(x) for x in arrays])


def run_pairs(pairs, lead, stages):
    held = [{} for _ in stages]
    for turn in range(pairs + lead * (len(stages) - 1)):
        for i, stage in enumerate(stages):
            pair = turn - lead * i
            if 0 <= pair < pairs:
                held[i][pair] = stage(pair, held[i - 1].pop(pair)) if i else stage(pair)


def mixed_rows(halo, partial, taps, gain, normed, first):
    steps, agents = halo.shape[:2]
    reach = taps.shape[0] - 1
    gains = gain[...] * (lax.axis_index("tm") > 0).astype(jnp.float32)
    for step in range(steps):
        values = halo[step].astype(jnp.float32)
        normed[step] = values * norm_scale(values) * gains
    for step in range(steps):
        total = partial[step]
        for lag in range(step + 1, reach + 1):
            total = total + taps[lag : lag + 1, :] * normed[steps + step - lag]
        first[step * agents : (step + 1) * agents, :] = total.astype(jnp.bfloat16).astype(first.dtype)


def feed_forward(rows, gain, w_in, w_out):
    inner = (rows * norm_scale(rows) * gain[...]).astype(jnp.bfloat16)
    tile, total = 512, [rows]

    def enter(i):
        return dot(inner, w_in[:, i * tile : (i + 1) * tile])

    def activate(i, products):
        return gelu(products).astype(jnp.bfloat16)

    def leave(i, hidden):
        total[0] = total[0] + dot(hidden, w_out[i * tile : (i + 1) * tile, :])

    run_pairs(w_in.shape[1] // tile, 1, [enter, activate, leave])
    return total[0].astype(jnp.bfloat16)


def to_keys(second, gain, w_key, w_value, keyval):
    width = second.shape[1]
    values = second.astype(jnp.float32)
    attn_in = (values * norm_scale(values) * gain[...]).astype(jnp.bfloat16)
    keyval[:, :width] = dot(attn_in, w_key[...]).astype(jnp.bfloat16)
    keyval[:, width : 2 * width] = dot(attn_in, w_value[...]).astype(jnp.bfloat16)
    return attn_in


def conv_kernel(group, halo, partial, taps, gain, tail, *rest):
    steps, agents, width = halo.shape
    outs = rest[:steps]
    normed, first = rest[steps:]
    mixed_rows(halo, partial, taps, gain, normed, first)
    spot = lax.axis_index("agent")
    for k in range(steps):
        step = (spot // group) ^ away(k, steps, spot % group, lax.axis_index("tm"))
        outs[k][:, :width] = first[pl.ds(pl.multiple_of(step * agents, agents), agents), :].astype(jnp.bfloat16)
        outs[k][:, width:] = tail[...]


def conv(group, halo, partial, taps, gain, tail):
    steps, agents, width = halo.shape
    return pl.pallas_call(
        functools.partial(conv_kernel, group),
        out_shape=[jax.ShapeDtypeStruct((agents, width + tail.shape[1]), jnp.bfloat16)] * steps,
        in_specs=[VMEM] * 5,
        out_specs=[VMEM] * steps,
        scratch_shapes=[
            pltpu.VMEM((steps, agents, width), jnp.float32),
            pltpu.VMEM((steps * agents, width), jnp.float32),
        ],
        compiler_params=pltpu.CompilerParams(vmem_limit_bytes=8 * MIB),
        cost_estimate=cost(0),
        name="conv",
    )(halo, *[pinned(x) for x in (partial, taps, gain, tail)])


def front_kernel(group, halo, partial, taps, gain_first, gain_second, w_in, w_out, *rest):
    steps, agents, width = halo.shape
    outs = rest[:steps]
    normed, first, second = rest[steps:]
    mixed_rows(halo, partial, taps, gain_first, normed, first)
    result = feed_forward(first[...], gain_second, w_in, w_out)
    for step in range(steps):
        second[step] = result[step * agents : (step + 1) * agents]
    spot = lax.axis_index("agent")
    for k in range(steps):
        outs[k][...] = second[(spot // group) ^ away(k, steps, spot % group, lax.axis_index("tm"))]


def front(group, halo, partial, taps, gains, w_in, w_out):
    steps, agents, width = halo.shape
    rows = steps * agents
    return pl.pallas_call(
        functools.partial(front_kernel, group),
        out_shape=[jax.ShapeDtypeStruct((agents, width), jnp.bfloat16)] * steps,
        in_specs=[VMEM] * 7,
        out_specs=[VMEM] * steps,
        scratch_shapes=[
            pltpu.VMEM((steps, agents, width), jnp.float32),
            pltpu.VMEM((rows, width), jnp.float32),
            pltpu.VMEM((steps, agents, width), jnp.bfloat16),
        ],
        compiler_params=pltpu.CompilerParams(vmem_limit_bytes=12 * MIB),
        cost_estimate=cost(0),
        name="front",
    )(halo, *[pinned(x) for x in (partial, taps, *gains, w_in, w_out)])


def feed_kernel(count, *refs):
    pieces = refs[:count]
    gain_second, gain_third, w_in, w_out, w_key, w_value, w_query = refs[count : count + 7]
    query, keyval, second = refs[count + 7 :]
    width = gain_second.shape[1]
    agents = pieces[0].shape[0]
    for k in range(count):
        keyval[agents * k : agents * (k + 1), 2 * width :] = pieces[k][:, width:]
    first = jnp.concatenate([piece[:, :width].astype(jnp.float32) for piece in pieces], axis=0)
    result = feed_forward(first, gain_second, w_in, w_out)
    second[...] = result
    attn_in = to_keys(result, gain_third, w_key, w_value, keyval)
    query[...] = dot(attn_in, w_query[...]).astype(jnp.bfloat16)


def feed(pieces, gains, weights):
    rows = sum(piece.shape[0] for piece in pieces)
    width = gains[0].shape[1]
    return pl.pallas_call(
        functools.partial(feed_kernel, len(pieces)),
        out_shape=[
            jax.ShapeDtypeStruct((rows, width), jnp.bfloat16),
            jax.ShapeDtypeStruct((rows, width + pieces[0].shape[1]), jnp.bfloat16),
            jax.ShapeDtypeStruct((rows, width), jnp.bfloat16),
        ],
        in_specs=[VMEM] * (len(pieces) + 7),
        out_specs=[VMEM] * 3,
        compiler_params=pltpu.CompilerParams(vmem_limit_bytes=12 * MIB),
        cost_estimate=cost(0),
        name="feed",
    )(*pieces, *[pinned(x) for x in (*gains, *weights)])


def project_kernel(count, *refs):
    pieces = refs[:count][::-1]
    gain, w_key, w_value, attn_in, keyval = refs[count:]
    second = jnp.concatenate([piece[...] for piece in pieces], axis=0)
    attn_in[...] = to_keys(second, gain, w_key, w_value, keyval)


def project(pieces, gain, weights):
    rows = sum(piece.shape[0] for piece in pieces)
    width = gain.shape[1]
    return pl.pallas_call(
        functools.partial(project_kernel, len(pieces)),
        out_shape=[
            jax.ShapeDtypeStruct((rows, width), jnp.bfloat16),
            jax.ShapeDtypeStruct((rows, 2 * width), jnp.bfloat16),
        ],
        in_specs=[VMEM] * (len(pieces) + 3),
        out_specs=[VMEM] * 2,
        compiler_params=pltpu.CompilerParams(vmem_limit_bytes=8 * MIB),
        cost_estimate=cost(25),
        name="project",
    )(*reversed(pieces), *[pinned(x) for x in (gain, *weights)])


def block_order(group, chunks):
    early = [(r, 0) for r in range(group)] + [(0, j) for j in range(1, chunks)]
    return early + [(r, j) for j in range(1, chunks) for r in range(1, group)]


def write_mask(steps, chunks, agents, width, blocks, bias):
    group = len(blocks)
    now = (lax.axis_index("tm") * steps + lax.axis_index("agent") // group).astype(jnp.float32)
    lane = lax.broadcasted_iota(jnp.int32, (agents, 128), 1)
    sublane = lax.broadcasted_iota(jnp.int32, (agents, 128), 0)
    tiles = {}
    for r in range(group):
        for k in range(steps):
            tile = blocks[r][agents * k : agents * (k + 1), 2 * width :].astype(jnp.float32)
            tiles[k, r] = (tile[0:1] * RADIX + tile[1:2], tile[2:3])
    own = jnp.concatenate(
        [
            jnp.sum(jnp.where(lane == sublane + j * agents, tiles[k, 0][0], 0.0), axis=1, keepdims=True)
            for k in range(steps)
            for j in range(chunks)
        ],
        axis=0,
    )
    row_lane = lax.broadcasted_iota(jnp.int32, (1, 128), 1)
    per_tile = 128 // agents
    start = 0
    for r, j in block_order(group, chunks):
        for first in range(0, steps, per_tile):
            both = [None, None]
            for i in range(per_tile):
                for f in (0, 1):
                    moved = pltpu.roll(tiles[first + i, r][f], ((i - j) * agents) % 128, 1)
                    both[f] = moved if i == 0 else jnp.where(row_lane >= i * agents, moved, both[f])
            order, present = both
            alive = jnp.where(now < present, order, 1e9)
            visible = (alive < own) | (order == own)
            bias[:, start : start + 128] = jnp.where(visible, 0.0, -1e30)
            start += 128


def rows_of(parts, ks, agents, columns):
    return jnp.concatenate([part[agents * k : agents * (k + 1), columns] for k in ks for part in parts], axis=0)


def pair_stages(queries_of, blocks, bias, top_of, low):
    width = blocks[0].shape[1] // 2 // 128 * 128

    def products(pair):
        queries = queries_of(pair)
        zeros = jnp.zeros_like(queries)
        stacked = jnp.concatenate([jnp.where(low, queries, zeros), jnp.where(low, zeros, queries)], axis=0)
        key = jnp.concatenate([block[:, 128 * pair : 128 * pair + 128] for block in blocks], axis=0)
        return dot_t(stacked, key)

    def weigh(pair, scores):
        rows, keys = scores.shape[0] // 2, scores.shape[1]
        tops, weights = [], []
        for half in range(2):
            here = scores[half * rows : (half + 1) * rows] * (LOG2E * HEAD ** (-0.5)) + bias
            highest = jnp.broadcast_to(jnp.max(here, axis=1, keepdims=True), (rows, 128))
            if top_of is not None:
                highest = jnp.maximum(highest, top_of(pair, half))
            tops.append(highest)
            wide = jnp.concatenate([highest] * (keys // 128), axis=1)
            weights.append(jnp.exp2(here - wide).astype(jnp.bfloat16))
        return tops, jnp.concatenate(weights, axis=0)

    def sums(pair, made):
        tops, weights = made
        start = width + 128 * pair
        value = jnp.concatenate([block[:, start : start + 128] for block in blocks], axis=0)
        return tops, dot(weights, jnp.concatenate([value, jnp.ones(value.shape, jnp.bfloat16)], axis=1))

    return [products, weigh, sums]


def merged(low, total):
    rows = total.shape[0] // 2
    return jnp.where(low, total[:rows], total[rows:])


def early_kernel(ks, steps, chunks, group, query, attn_in, w_query, *refs):
    count = group + chunks - 1
    blocks, (own_query, bias, number, weight, top_low, top_high) = refs[:count], refs[count:]
    own_query[...] = dot(attn_in[...], w_query[...]).astype(jnp.bfloat16)
    rows, width = number.shape
    write_mask(steps, chunks, query.shape[0] // steps, width, blocks[:group], bias)
    agents = rows // (len(ks) * chunks)
    low = lax.broadcasted_iota(jnp.int32, (rows, 128), 1) < HEAD
    keys = sum(block.shape[0] for block in blocks)
    here = bias[ks[0] * agents * chunks : ks[0] * agents * chunks + rows, :keys]

    def columns(pair):
        return slice(128 * pair, 128 * pair + 128)

    def keep(pair, made):
        tops, total = made
        number[:, columns(pair)] = merged(low, total[:, :128])
        weight[:, columns(pair)] = merged(low, total[:, 128:])
        top_low[:, columns(pair)] = tops[0]
        top_high[:, columns(pair)] = tops[1]

    stages = pair_stages(lambda pair: rows_of((query, own_query), ks, agents, columns(pair)), blocks, here, None, low)
    run_pairs(width // 128, 2, [*stages, keep])


def early(ks, steps, group, query, attn_in, w_query, blocks):
    count, width = query.shape
    rows = count * CHUNKS
    state = pltpu.VMEM((len(ks) * rows // steps, width), jnp.float32)
    return pl.pallas_call(
        functools.partial(early_kernel, ks, steps, CHUNKS, group),
        out_shape=[jax.ShapeDtypeStruct(query.shape, jnp.bfloat16), pltpu.VMEM((rows, rows * group), jnp.float32)]
        + [state] * 4,
        in_specs=[VMEM] * (3 + len(blocks)),
        out_specs=[VMEM] * 6,
        compiler_params=pltpu.CompilerParams(vmem_limit_bytes=16 * MIB),
        cost_estimate=cost(0),
        name="early",
    )(query, attn_in, pinned(w_query), *blocks)


def attend_kernel(ks, chunks, count, begun, skipped, *refs):
    mine = 1 + len(ks) * (chunks - 1)
    queries, seconds, (w_output, bias) = refs[:chunks], refs[chunks : chunks + mine], refs[chunks + mine : chunks + mine + 2]
    rest = refs[chunks + mine + 2 :]
    blocks, state = rest[:count], rest[count : count + begun]
    outs = rest[count + begun :]
    width, agents = w_output.shape[1], queries[0].shape[0] // 4
    rows = len(ks) * chunks * agents
    low = lax.broadcasted_iota(jnp.int32, (rows, 128), 1) < HEAD
    keys = sum(block.shape[0] for block in blocks)
    here = bias[ks[0] * agents * chunks : ks[0] * agents * chunks + rows, bias.shape[1] - keys :]
    begun_rows = slice(skipped, skipped + rows)

    def columns(pair):
        return slice(128 * pair, 128 * pair + 128)

    residual = []
    for i, k in enumerate(ks):
        residual += [seconds[0][agents * k : agents * (k + 1)]]
        residual += [piece[...] for piece in seconds[1 + i * (chunks - 1) : 1 + (i + 1) * (chunks - 1)]]
    result = [jnp.concatenate(residual, axis=0).astype(jnp.float32)]

    def keep(pair, made):
        tops, total = made
        number, weight = merged(low, total[:, :128]), merged(low, total[:, 128:])
        if begun:
            drop = [state[2 + half][begun_rows, columns(pair)] - tops[half] for half in range(2)]
            shrink = jnp.exp2(jnp.where(low, *drop))
            number = number + state[0][begun_rows, columns(pair)] * shrink
            weight = weight + state[1][begun_rows, columns(pair)] * shrink
        return (number / weight).astype(jnp.bfloat16)

    waiting, together = [], 2 if begun else width // 128

    def output(pair, attended):
        waiting.append(attended)
        if len(waiting) == together:
            features = slice(128 * (pair + 1 - together), 128 * (pair + 1))
            result[0] = result[0] + dot(jnp.concatenate(waiting, axis=1), w_output[features, :])
            waiting.clear()

    stages = pair_stages(
        lambda pair: rows_of(queries, ks, agents, columns(pair)),
        blocks,
        here,
        (lambda pair, half: state[2 + half][begun_rows, columns(pair)]) if begun else None,
        low,
    )
    run_pairs(width // 128, 2, [*stages, keep, output])
    for i in range(len(ks)):
        outs[i][...] = result[0][i * agents * chunks : (i + 1) * agents * chunks].astype(jnp.bfloat16)


def attend(ks, queries, seconds, w_output, bias, blocks, state, skipped, agents, microseconds):
    width = queries[0].shape[1]
    piece = jax.ShapeDtypeStruct((agents, width), jnp.bfloat16)
    return pl.pallas_call(
        functools.partial(attend_kernel, ks, len(queries), len(blocks), len(state), skipped),
        out_shape=[piece] * len(ks),
        in_specs=[VMEM] * (len(queries) + len(seconds) + 2 + len(blocks) + len(state)),
        out_specs=[VMEM] * len(ks),
        compiler_params=pltpu.CompilerParams(vmem_limit_bytes=16 * MIB),
        cost_estimate=cost(microseconds),
        name="attend",
    )(*queries, *seconds, pinned(w_output), pinned(bias), *blocks, *[pinned(x) for x in state])


def put_back_kernel(steps, group, *refs):
    pieces, out, sem = refs[:steps][::-1], refs[steps], refs[steps + 1]
    spot = lax.axis_index("agent")
    half = pieces[0].shape[0] // 2
    copies = []
    for k in range(steps):
        target = out.at[(spot // group) ^ away(k, steps, spot % group, lax.axis_index("tm"))]
        for rows in (pl.ds(0, half), pl.ds(half, half)):
            copies.append(pltpu.make_async_copy(pieces[k].at[rows], target.at[rows], sem.at[len(copies)]))
    for copy in copies:
        copy.start()
    for copy in copies:
        copy.wait()


def put_back(group, pieces, shape):
    return pl.pallas_call(
        functools.partial(put_back_kernel, shape[0], group),
        out_shape=jax.ShapeDtypeStruct(shape, jnp.bfloat16),
        in_specs=[VMEM] * len(pieces),
        out_specs=ANY,
        scratch_shapes=[pltpu.SemaphoreType.DMA((2 * len(pieces),))],
        compiler_params=pltpu.CompilerParams(vmem_limit_bytes=4 * MIB),
        cost_estimate=cost(0),
        name="put_back",
    )(*pieces)


def after(x, *others):
    return lax.optimization_barrier((x, *others))[0]


def per_device(
    tokens,
    conv_taps,
    norm_first,
    norm_second,
    norm_third,
    w_in,
    w_out,
    w_query,
    w_key,
    w_value,
    w_output,
    agent_order,
    present_steps,
):
    steps, agents, width = tokens.shape
    tm_count, count = lax.axis_size("tm"), lax.axis_size("agent")
    group = count // steps
    part = agents // CHUNKS
    assert group * steps == count and steps == 4 and 128 % part == 0 and CHUNKS == 2 and group > 1

    def across(x, k):
        if k == steps - 1:
            return x
        pairs = [
            (line * count + i, line * count + ((i // group) ^ away(k, steps, i % group, line)) * group + i % group)
            for line in range(tm_count)
            for i in range(count)
        ]
        return lax.ppermute(x, ("tm", "agent"), pairs)

    def within(x, r):
        return lax.ppermute(x, "agent", [(i, (i // group) * group + ((i % group) ^ r)) for i in range(count)])

    first_part = split(tokens)
    second_part, *partials, tail, taps, gain_first, gain_second, gain_third = stage(
        tokens,
        first_part,
        conv_taps,
        norm_first.reshape(1, width),
        agent_order.reshape(1, agents),
        present_steps.reshape(1, agents),
        [conv_taps] + [x.reshape(1, width) for x in (norm_first, norm_second, norm_third)],
    )
    halos = [lax.ppermute(x, "tm", [(i, (i + 1) % tm_count) for i in range(tm_count)]) for x in (first_part, second_part)]
    halos[0] = after(halos[0], tail)
    made = conv(group, halos[0], partials[0], taps, gain_first, tail)
    last = made[-1]
    pieces = [[across(made[k], k) for k in range(steps)]]
    for j in range(1, CHUNKS):
        halos[j] = after(halos[j], last)
        made = list(front(group, halos[j], partials[j], taps, (gain_first, gain_second), w_in, w_out))
        last = made[-1]
        made[steps - 2] = after(made[steps - 2], pieces[j - 1][0])
        pieces.append([across(made[k], k) for k in range(steps)])
    pieces[0][-1] = after(pieces[0][-1], last)
    query, keyval, second = feed(pieces[0], (gain_second, gain_third), (w_in, w_out, w_key, w_value, w_query))
    blocks = {(0, 0): keyval, **{(r, 0): within(keyval, r) for r in range(1, group)}}
    attn_in, keyval = project(pieces[1], gain_third, (w_key, w_value))
    keyval = after(keyval, *blocks.values())
    blocks.update({(0, 1): keyval, **{(r, 1): within(keyval, r) for r in range(1, group)}})
    blocks = [blocks[spot] for spot in block_order(group, CHUNKS)]
    ready = group + CHUNKS - 1
    far_ks, near_ks = (0, 1), (2, 3)
    own_query, bias, *state = early(far_ks, steps, group, query, attn_in, w_query, blocks[:ready])

    def finish(ks, blocks, state, skipped, microseconds):
        seconds = [second] + [pieces[j][k] for k in ks for j in range(1, CHUNKS)]
        return attend(
            ks, (query, own_query), seconds, w_output, bias, blocks, state, skipped, agents, microseconds
        )

    late = blocks[ready:]
    results = [*finish(far_ks, late, state, 0, 0), *finish(near_ks, blocks, [], 0, 10)]
    return put_back(group, [across(results[k], k) for k in reversed(range(steps))], tokens.shape)


def solution(mesh):
    in_specs = (P("tm", "agent", None),) + (P(),) * 10 + (P("agent"), P("agent"))
    return jax.shard_map(
        per_device, mesh=mesh, in_specs=in_specs, out_specs=P("tm", "agent", None), check_vma=False
    )
```

```python
import functools

import jax
import jax.numpy as jnp
from jax import lax
from jax.experimental import pallas as pl
from jax.experimental.pallas import tpu as pltpu
from jax.sharding import PartitionSpec as P

HEAD = 64
CHUNKS = 2
RADIX = 32
EPS = 1e-05
LOG2E = 1.4426950408889634
MIB = 1024 * 1024
VMEM = pl.BlockSpec(memory_space=pltpu.VMEM)
ANY = pl.BlockSpec(memory_space=pl.ANY)
HBM = pl.BlockSpec(memory_space=pltpu.HBM)


def pinned(x):
    return pltpu.with_memory_space_constraint(x, pltpu.VMEM)


def far(x):
    return pltpu.with_memory_space_constraint(x, pltpu.HBM)


def cost(microseconds):
    return pl.CostEstimate(
        flops=int(1.1e9 * microseconds) + 10**6, bytes_accessed=int(3.5e6 * microseconds) + 10**4, transcendentals=0
    )


def away(k, steps, member, line):
    if k == steps - 1:
        return 0
    odd, first = member % 2, 1 - jnp.minimum(line, 1) if isinstance(line, jax.Array) else int(line == 0)
    first_orders, orders = ((2, 1, 3), (3, 2, 1)), ((2, 3, 1), (2, 1, 3))
    even, odd_away = (a[k] * first + b[k] * (1 - first) for a, b in zip(first_orders, orders))
    return even * (1 - odd) + odd_away * odd


def dot(a, b):
    return jnp.dot(a, b, preferred_element_type=jnp.float32)


def dot_t(a, b):
    return lax.dot_general(a, b, (((1,), (1,)), ((), ())), preferred_element_type=jnp.float32)


def norm_scale(values):
    return lax.rsqrt(jnp.mean(values * values, axis=-1, keepdims=True) + EPS)


def gelu(x):
    return 0.5 * x * (1.0 + lax.erf(x * 0.7071067811865476))


def part_copies(tokens, part, target, sem):
    steps, agents = target.shape[:2]
    return [
        pltpu.make_async_copy(tokens.at[step, pl.ds(part * agents, agents)], target.at[step], sem.at[step])
        for step in range(steps)
    ]


def split_kernel(tokens, out, sem):
    copies = part_copies(tokens, 0, out, sem)
    for copy in copies:
        copy.start()
    for copy in copies:
        copy.wait()


def split(tokens):
    steps, agents, width = tokens.shape
    return pl.pallas_call(
        split_kernel,
        out_shape=pltpu.VMEM((steps, agents // CHUNKS, width), tokens.dtype),
        in_specs=[HBM],
        out_specs=VMEM,
        scratch_shapes=[pltpu.SemaphoreType.DMA((steps,))],
        compiler_params=pltpu.CompilerParams(vmem_limit_bytes=4 * MIB),
        cost_estimate=cost(0),
        name="split",
    )(far(tokens))


def stage_kernel(count, taps, gain, order, present, tokens, first_part, *rest):
    sources, rest = rest[:count], rest[count:]
    second_part, partials, tail, targets = rest[0], rest[1:3], rest[3], rest[4 : 4 + count]
    taps_here, gain_here, order_here, present_here, normed, facts, part_sem, sem = rest[4 + count :]
    pairs = [
        (taps, taps_here),
        (gain, gain_here),
        (order, order_here),
        (present, present_here),
        *zip(sources, targets),
    ]
    copies = [pltpu.make_async_copy(source, target, sem.at[i]) for i, (source, target) in enumerate(pairs)]
    later = part_copies(tokens, 1, second_part, part_sem)
    for copy in copies + later:
        copy.start()
    for copy in copies:
        copy.wait()
    agents = order.shape[1]
    facts[...] = jnp.zeros(facts.shape, jnp.float32)
    facts[0:1, :agents] = (order_here[...] // RADIX).astype(jnp.float32)
    facts[1:2, :agents] = (order_here[...] % RADIX).astype(jnp.float32)
    facts[2:3, :agents] = present_here[...].astype(jnp.float32)
    tail[...] = facts[...].astype(jnp.bfloat16)
    steps, reach = first_part.shape[0], taps.shape[0] - 1
    gains = gain_here[...]
    for j, part in enumerate((first_part, second_part)):
        for step in range(steps):
            if j == 1:
                later[step].wait()
            values = part[step].astype(jnp.float32)
            normed[step] = values * norm_scale(values) * gains
            total = values
            for lag in range(min(step, reach) + 1):
                total = total + taps_here[lag : lag + 1, :] * normed[step - lag]
            partials[j][step] = total


def stage(tokens, first_part, taps, gain, order, present, arrays):
    steps, part, width = first_part.shape
    inputs = (taps, gain, order, present)
    return pl.pallas_call(
        functools.partial(stage_kernel, len(arrays)),
        out_shape=[pltpu.VMEM(first_part.shape, first_part.dtype)]
        + [pltpu.VMEM((steps, part, width), jnp.float32)] * CHUNKS
        + [pltpu.VMEM((part, 128), jnp.bfloat16)]
        + [pltpu.VMEM(x.shape, x.dtype) for x in arrays],
        in_specs=[HBM] * (len(inputs) + 1) + [VMEM] + [HBM] * len(arrays),
        out_specs=[VMEM] * (CHUNKS + 2 + len(arrays)),
        scratch_shapes=[pltpu.VMEM(x.shape, x.dtype) for x in inputs]
        + [
            pltpu.VMEM((steps, part, width), jnp.float32),
            pltpu.VMEM((part, 128), jnp.float32),
            pltpu.SemaphoreType.DMA((steps,)),
            pltpu.SemaphoreType.DMA((len(inputs) + len(arrays),)),
        ],
        compiler_params=pltpu.CompilerParams(vmem_limit_bytes=8 * MIB),
        cost_estimate=cost(30),
        name="stage",
    )(*[far(x) for x in (*inputs, tokens)], pinned(first_part), *[far(x) for x in arrays])


def run_pairs(pairs, lead, stages):
    held = [{} for _ in stages]
    for turn in range(pairs + lead * (len(stages) - 1)):
        for i, stage in enumerate(stages):
            pair = turn - lead * i
            if 0 <= pair < pairs:
                held[i][pair] = stage(pair, held[i - 1].pop(pair)) if i else stage(pair)


def mixed_rows(halo, partial, taps, gain, normed, first):
    steps, agents = halo.shape[:2]
    reach = taps.shape[0] - 1
    gains = gain[...] * (lax.axis_index("tm") > 0).astype(jnp.float32)
    for step in range(steps):
        values = halo[step].astype(jnp.float32)
        normed[step] = values * norm_scale(values) * gains
    for step in range(steps):
        total = partial[step]
        for lag in range(step + 1, reach + 1):
            total = total + taps[lag : lag + 1, :] * normed[steps + step - lag]
        first[step * agents : (step + 1) * agents, :] = total.astype(jnp.bfloat16).astype(first.dtype)


def feed_forward(rows, gain, w_in, w_out):
    inner = (rows * norm_scale(rows) * gain[...]).astype(jnp.bfloat16)
    tile, total = 1024, [rows]

    def enter(i):
        return dot(inner, w_in[:, i * tile : (i + 1) * tile])

    def activate(i, products):
        return gelu(products).astype(jnp.bfloat16)

    def leave(i, hidden):
        total[0] = total[0] + dot(hidden, w_out[i * tile : (i + 1) * tile, :])

    run_pairs(w_in.shape[1] // tile, 1, [enter, activate, leave])
    return total[0].astype(jnp.bfloat16)


def to_keys(second, gain, w_key, w_value, keyval):
    width = second.shape[1]
    values = second.astype(jnp.float32)
    attn_in = (values * norm_scale(values) * gain[...]).astype(jnp.bfloat16)
    keyval[:, :width] = dot(attn_in, w_key[...]).astype(jnp.bfloat16)
    keyval[:, width : 2 * width] = dot(attn_in, w_value[...]).astype(jnp.bfloat16)
    return attn_in


def conv_kernel(group, halo, partial, taps, gain, tail, *rest):
    steps, agents, width = halo.shape
    outs = rest[:steps]
    normed, first = rest[steps:]
    mixed_rows(halo, partial, taps, gain, normed, first)
    spot = lax.axis_index("agent")
    for k in range(steps):
        step = (spot // group) ^ away(k, steps, spot % group, lax.axis_index("tm"))
        outs[k][:, :width] = first[pl.ds(pl.multiple_of(step * agents, agents), agents), :].astype(jnp.bfloat16)
        outs[k][:, width:] = tail[...]


def conv(group, halo, partial, taps, gain, tail):
    steps, agents, width = halo.shape
    return pl.pallas_call(
        functools.partial(conv_kernel, group),
        out_shape=[jax.ShapeDtypeStruct((agents, width + tail.shape[1]), jnp.bfloat16)] * steps,
        in_specs=[VMEM] * 5,
        out_specs=[VMEM] * steps,
        scratch_shapes=[
            pltpu.VMEM((steps, agents, width), jnp.float32),
            pltpu.VMEM((steps * agents, width), jnp.float32),
        ],
        compiler_params=pltpu.CompilerParams(vmem_limit_bytes=8 * MIB),
        cost_estimate=cost(0),
        name="conv",
    )(halo, *[pinned(x) for x in (partial, taps, gain, tail)])


def front_kernel(group, halo, partial, taps, gain_first, gain_second, w_in, w_out, *rest):
    steps, agents, width = halo.shape
    outs = rest[:steps]
    normed, first, second = rest[steps:]
    mixed_rows(halo, partial, taps, gain_first, normed, first)
    result = feed_forward(first[...], gain_second, w_in, w_out)
    for step in range(steps):
        second[step] = result[step * agents : (step + 1) * agents]
    spot = lax.axis_index("agent")
    for k in range(steps):
        outs[k][...] = second[(spot // group) ^ away(k, steps, spot % group, lax.axis_index("tm"))]


def front(group, halo, partial, taps, gains, w_in, w_out):
    steps, agents, width = halo.shape
    rows = steps * agents
    return pl.pallas_call(
        functools.partial(front_kernel, group),
        out_shape=[jax.ShapeDtypeStruct((agents, width), jnp.bfloat16)] * steps,
        in_specs=[VMEM] * 7,
        out_specs=[VMEM] * steps,
        scratch_shapes=[
            pltpu.VMEM((steps, agents, width), jnp.float32),
            pltpu.VMEM((rows, width), jnp.float32),
            pltpu.VMEM((steps, agents, width), jnp.bfloat16),
        ],
        compiler_params=pltpu.CompilerParams(vmem_limit_bytes=12 * MIB),
        cost_estimate=cost(0),
        name="front",
    )(halo, *[pinned(x) for x in (partial, taps, *gains, w_in, w_out)])


def feed_kernel(count, *refs):
    pieces = refs[:count]
    gain_second, gain_third, w_in, w_out, w_key, w_value, w_query = refs[count : count + 7]
    query, keyval, second = refs[count + 7 :]
    width = gain_second.shape[1]
    agents = pieces[0].shape[0]
    for k in range(count):
        keyval[agents * k : agents * (k + 1), 2 * width :] = pieces[k][:, width:]
    first = jnp.concatenate([piece[:, :width].astype(jnp.float32) for piece in pieces], axis=0)
    result = feed_forward(first, gain_second, w_in, w_out)
    second[...] = result
    attn_in = to_keys(result, gain_third, w_key, w_value, keyval)
    query[...] = dot(attn_in, w_query[...]).astype(jnp.bfloat16)


def feed(pieces, gains, weights):
    rows = sum(piece.shape[0] for piece in pieces)
    width = gains[0].shape[1]
    return pl.pallas_call(
        functools.partial(feed_kernel, len(pieces)),
        out_shape=[
            jax.ShapeDtypeStruct((rows, width), jnp.bfloat16),
            jax.ShapeDtypeStruct((rows, width + pieces[0].shape[1]), jnp.bfloat16),
            jax.ShapeDtypeStruct((rows, width), jnp.bfloat16),
        ],
        in_specs=[VMEM] * (len(pieces) + 7),
        out_specs=[VMEM] * 3,
        compiler_params=pltpu.CompilerParams(vmem_limit_bytes=12 * MIB),
        cost_estimate=cost(0),
        name="feed",
    )(*pieces, *[pinned(x) for x in (*gains, *weights)])


def project_kernel(count, *refs):
    pieces = refs[:count][::-1]
    gain, w_key, w_value, attn_in, keyval = refs[count:]
    second = jnp.concatenate([piece[...] for piece in pieces], axis=0)
    attn_in[...] = to_keys(second, gain, w_key, w_value, keyval)


def project(pieces, gain, weights):
    rows = sum(piece.shape[0] for piece in pieces)
    width = gain.shape[1]
    return pl.pallas_call(
        functools.partial(project_kernel, len(pieces)),
        out_shape=[
            jax.ShapeDtypeStruct((rows, width), jnp.bfloat16),
            jax.ShapeDtypeStruct((rows, 2 * width), jnp.bfloat16),
        ],
        in_specs=[VMEM] * (len(pieces) + 3),
        out_specs=[VMEM] * 2,
        compiler_params=pltpu.CompilerParams(vmem_limit_bytes=8 * MIB),
        cost_estimate=cost(25),
        name="project",
    )(*reversed(pieces), *[pinned(x) for x in (gain, *weights)])


def block_order(group, chunks):
    early = [(r, 0) for r in range(group)] + [(0, j) for j in range(1, chunks)]
    return early + [(r, j) for j in range(1, chunks) for r in range(1, group)]


def write_mask(steps, chunks, agents, width, blocks, bias):
    group = len(blocks)
    now = (lax.axis_index("tm") * steps + lax.axis_index("agent") // group).astype(jnp.float32)
    lane = lax.broadcasted_iota(jnp.int32, (agents, 128), 1)
    sublane = lax.broadcasted_iota(jnp.int32, (agents, 128), 0)
    tiles = {}
    for r in range(group):
        for k in range(steps):
            tile = blocks[r][agents * k : agents * (k + 1), 2 * width :].astype(jnp.float32)
            tiles[k, r] = (tile[0:1] * RADIX + tile[1:2], tile[2:3])
    own = jnp.concatenate(
        [
            jnp.sum(jnp.where(lane == sublane + j * agents, tiles[k, 0][0], 0.0), axis=1, keepdims=True)
            for k in range(steps)
            for j in range(chunks)
        ],
        axis=0,
    )
    row_lane = lax.broadcasted_iota(jnp.int32, (1, 128), 1)
    per_tile = 128 // agents
    start = 0
    for r, j in block_order(group, chunks):
        for first in range(0, steps, per_tile):
            both = [None, None]
            for i in range(per_tile):
                for f in (0, 1):
                    moved = pltpu.roll(tiles[first + i, r][f], ((i - j) * agents) % 128, 1)
                    both[f] = moved if i == 0 else jnp.where(row_lane >= i * agents, moved, both[f])
            order, present = both
            alive = jnp.where(now < present, order, 1e9)
            visible = (alive < own) | (order == own)
            bias[:, start : start + 128] = jnp.where(visible, 0.0, -1e30)
            start += 128


def rows_of(parts, ks, agents, columns):
    return jnp.concatenate([part[agents * k : agents * (k + 1), columns] for k in ks for part in parts], axis=0)


def pair_stages(queries_of, blocks, bias, top_of, low):
    width = blocks[0].shape[1] // 2 // 128 * 128

    def products(pair):
        queries = queries_of(pair)
        zeros = jnp.zeros_like(queries)
        stacked = jnp.concatenate([jnp.where(low, queries, zeros), jnp.where(low, zeros, queries)], axis=0)
        key = jnp.concatenate([block[:, 128 * pair : 128 * pair + 128] for block in blocks], axis=0)
        return dot_t(stacked, key)

    def weigh(pair, scores):
        rows, keys = scores.shape[0] // 2, scores.shape[1]
        tops, weights = [], []
        for half in range(2):
            here = scores[half * rows : (half + 1) * rows] * (LOG2E * HEAD ** (-0.5)) + bias
            highest = jnp.broadcast_to(jnp.max(here, axis=1, keepdims=True), (rows, 128))
            if top_of is not None:
                highest = jnp.maximum(highest, top_of(pair, half))
            tops.append(highest)
            wide = jnp.concatenate([highest] * (keys // 128), axis=1)
            weights.append(jnp.exp2(here - wide).astype(jnp.bfloat16))
        return tops, jnp.concatenate(weights, axis=0)

    def sums(pair, made):
        tops, weights = made
        start = width + 128 * pair
        value = jnp.concatenate([block[:, start : start + 128] for block in blocks], axis=0)
        return tops, dot(weights, jnp.concatenate([value, jnp.ones(value.shape, jnp.bfloat16)], axis=1))

    return [products, weigh, sums]


def merged(low, total):
    rows = total.shape[0] // 2
    return jnp.where(low, total[:rows], total[rows:])


def early_kernel(ks, steps, chunks, group, query, attn_in, w_query, *refs):
    count = group + chunks - 1
    blocks, (own_query, bias, number, weight, top_low, top_high) = refs[:count], refs[count:]
    own_query[...] = dot(attn_in[...], w_query[...]).astype(jnp.bfloat16)
    rows, width = number.shape
    write_mask(steps, chunks, query.shape[0] // steps, width, blocks[:group], bias)
    agents = rows // (len(ks) * chunks)
    low = lax.broadcasted_iota(jnp.int32, (rows, 128), 1) < HEAD
    keys = sum(block.shape[0] for block in blocks)
    here = bias[ks[0] * agents * chunks : ks[0] * agents * chunks + rows, :keys]

    def columns(pair):
        return slice(128 * pair, 128 * pair + 128)

    def keep(pair, made):
        tops, total = made
        number[:, columns(pair)] = merged(low, total[:, :128])
        weight[:, columns(pair)] = merged(low, total[:, 128:])
        top_low[:, columns(pair)] = tops[0]
        top_high[:, columns(pair)] = tops[1]

    stages = pair_stages(lambda pair: rows_of((query, own_query), ks, agents, columns(pair)), blocks, here, None, low)
    run_pairs(width // 128, 2, [*stages, keep])


def early(ks, steps, group, query, attn_in, w_query, blocks):
    count, width = query.shape
    rows = count * CHUNKS
    state = pltpu.VMEM((len(ks) * rows // steps, width), jnp.float32)
    return pl.pallas_call(
        functools.partial(early_kernel, ks, steps, CHUNKS, group),
        out_shape=[jax.ShapeDtypeStruct(query.shape, jnp.bfloat16), pltpu.VMEM((rows, rows * group), jnp.float32)]
        + [state] * 4,
        in_specs=[VMEM] * (3 + len(blocks)),
        out_specs=[VMEM] * 6,
        compiler_params=pltpu.CompilerParams(vmem_limit_bytes=16 * MIB),
        cost_estimate=cost(0),
        name="early",
    )(query, attn_in, pinned(w_query), *blocks)


def attend_kernel(ks, chunks, count, begun, skipped, *refs):
    mine = 1 + len(ks) * (chunks - 1)
    queries, seconds, (w_output, bias) = refs[:chunks], refs[chunks : chunks + mine], refs[chunks + mine : chunks + mine + 2]
    rest = refs[chunks + mine + 2 :]
    blocks, state = rest[:count], rest[count : count + begun]
    outs = rest[count + begun :]
    width, agents = w_output.shape[1], queries[0].shape[0] // 4
    rows = len(ks) * chunks * agents
    low = lax.broadcasted_iota(jnp.int32, (rows, 128), 1) < HEAD
    keys = sum(block.shape[0] for block in blocks)
    here = bias[ks[0] * agents * chunks : ks[0] * agents * chunks + rows, bias.shape[1] - keys :]
    begun_rows = slice(skipped, skipped + rows)

    def columns(pair):
        return slice(128 * pair, 128 * pair + 128)

    residual = []
    for i, k in enumerate(ks):
        residual += [seconds[0][agents * k : agents * (k + 1)]]
        residual += [piece[...] for piece in seconds[1 + i * (chunks - 1) : 1 + (i + 1) * (chunks - 1)]]
    result = [jnp.concatenate(residual, axis=0).astype(jnp.float32)]

    def keep(pair, made):
        tops, total = made
        number, weight = merged(low, total[:, :128]), merged(low, total[:, 128:])
        if begun:
            drop = [state[2 + half][begun_rows, columns(pair)] - tops[half] for half in range(2)]
            shrink = jnp.exp2(jnp.where(low, *drop))
            number = number + state[0][begun_rows, columns(pair)] * shrink
            weight = weight + state[1][begun_rows, columns(pair)] * shrink
        return (number / weight).astype(jnp.bfloat16)

    waiting, together = [], 2 if begun else width // 128

    def output(pair, attended):
        waiting.append(attended)
        if len(waiting) == together:
            features = slice(128 * (pair + 1 - together), 128 * (pair + 1))
            result[0] = result[0] + dot(jnp.concatenate(waiting, axis=1), w_output[features, :])
            waiting.clear()

    stages = pair_stages(
        lambda pair: rows_of(queries, ks, agents, columns(pair)),
        blocks,
        here,
        (lambda pair, half: state[2 + half][begun_rows, columns(pair)]) if begun else None,
        low,
    )
    run_pairs(width // 128, 2, [*stages, keep, output])
    for i in range(len(ks)):
        outs[i][...] = result[0][i * agents * chunks : (i + 1) * agents * chunks].astype(jnp.bfloat16)


def attend(ks, queries, seconds, w_output, bias, blocks, state, skipped, agents, microseconds):
    width = queries[0].shape[1]
    piece = jax.ShapeDtypeStruct((agents, width), jnp.bfloat16)
    return pl.pallas_call(
        functools.partial(attend_kernel, ks, len(queries), len(blocks), len(state), skipped),
        out_shape=[piece] * len(ks),
        in_specs=[VMEM] * (len(queries) + len(seconds) + 2 + len(blocks) + len(state)),
        out_specs=[VMEM] * len(ks),
        compiler_params=pltpu.CompilerParams(vmem_limit_bytes=16 * MIB),
        cost_estimate=cost(microseconds),
        name="attend",
    )(*queries, *seconds, pinned(w_output), pinned(bias), *blocks, *[pinned(x) for x in state])


def put_back_kernel(steps, group, *refs):
    pieces, out, sem = refs[:steps][::-1], refs[steps], refs[steps + 1]
    spot = lax.axis_index("agent")
    half = pieces[0].shape[0] // 2
    copies = []
    for k in range(steps):
        target = out.at[(spot // group) ^ away(k, steps, spot % group, lax.axis_index("tm"))]
        for rows in (pl.ds(0, half), pl.ds(half, half)):
            copies.append(pltpu.make_async_copy(pieces[k].at[rows], target.at[rows], sem.at[len(copies)]))
    for copy in copies:
        copy.start()
    for copy in copies:
        copy.wait()


def put_back(group, pieces, shape):
    return pl.pallas_call(
        functools.partial(put_back_kernel, shape[0], group),
        out_shape=jax.ShapeDtypeStruct(shape, jnp.bfloat16),
        in_specs=[VMEM] * len(pieces),
        out_specs=ANY,
        scratch_shapes=[pltpu.SemaphoreType.DMA((2 * len(pieces),))],
        compiler_params=pltpu.CompilerParams(vmem_limit_bytes=4 * MIB),
        cost_estimate=cost(0),
        name="put_back",
    )(*pieces)


def after(x, *others):
    return lax.optimization_barrier((x, *others))[0]


def per_device(
    tokens,
    conv_taps,
    norm_first,
    norm_second,
    norm_third,
    w_in,
    w_out,
    w_query,
    w_key,
    w_value,
    w_output,
    agent_order,
    present_steps,
):
    steps, agents, width = tokens.shape
    tm_count, count = lax.axis_size("tm"), lax.axis_size("agent")
    group = count // steps
    part = agents // CHUNKS
    assert group * steps == count and steps == 4 and 128 % part == 0 and CHUNKS == 2 and group > 1

    def across(x, k):
        if k == steps - 1:
            return x
        pairs = [
            (line * count + i, line * count + ((i // group) ^ away(k, steps, i % group, line)) * group + i % group)
            for line in range(tm_count)
            for i in range(count)
        ]
        return lax.ppermute(x, ("tm", "agent"), pairs)

    def within(x, r):
        return lax.ppermute(x, "agent", [(i, (i // group) * group + ((i % group) ^ r)) for i in range(count)])

    first_part = split(tokens)
    second_part, *partials, tail, taps, gain_first, gain_second, gain_third = stage(
        tokens,
        first_part,
        conv_taps,
        norm_first.reshape(1, width),
        agent_order.reshape(1, agents),
        present_steps.reshape(1, agents),
        [conv_taps] + [x.reshape(1, width) for x in (norm_first, norm_second, norm_third)],
    )
    halos = [lax.ppermute(x, "tm", [(i, (i + 1) % tm_count) for i in range(tm_count)]) for x in (first_part, second_part)]
    halos[0] = after(halos[0], tail)
    made = conv(group, halos[0], partials[0], taps, gain_first, tail)
    last = made[-1]
    pieces = [[across(made[k], k) for k in range(steps)]]
    for j in range(1, CHUNKS):
        halos[j] = after(halos[j], last)
        made = list(front(group, halos[j], partials[j], taps, (gain_first, gain_second), w_in, w_out))
        last = made[-1]
        made[steps - 2] = after(made[steps - 2], pieces[j - 1][0])
        pieces.append([across(made[k], k) for k in range(steps)])
    pieces[0][-1] = after(pieces[0][-1], last)
    query, keyval, second = feed(pieces[0], (gain_second, gain_third), (w_in, w_out, w_key, w_value, w_query))
    blocks = {(0, 0): keyval, **{(r, 0): within(keyval, r) for r in range(1, group)}}
    attn_in, keyval = project(pieces[1], gain_third, (w_key, w_value))
    keyval = after(keyval, *blocks.values())
    blocks.update({(0, 1): keyval, **{(r, 1): within(keyval, r) for r in range(1, group)}})
    blocks = [blocks[spot] for spot in block_order(group, CHUNKS)]
    ready = group + CHUNKS - 1
    far_ks, near_ks = (0, 1), (2, 3)
    own_query, bias, *state = early(far_ks, steps, group, query, attn_in, w_query, blocks[:ready])

    def finish(ks, blocks, state, skipped, microseconds):
        seconds = [second] + [pieces[j][k] for k in ks for j in range(1, CHUNKS)]
        return attend(
            ks, (query, own_query), seconds, w_output, bias, blocks, state, skipped, agents, microseconds
        )

    late = blocks[ready:]
    results = [*finish(far_ks, late, state, 0, 0), *finish(near_ks, blocks, [], 0, 10)]
    return put_back(group, [across(results[k], k) for k in reversed(range(steps))], tokens.shape)


def solution(mesh):
    in_specs = (P("tm", "agent", None),) + (P(),) * 10 + (P("agent"), P("agent"))
    return jax.shard_map(
        per_device, mesh=mesh, in_specs=in_specs, out_specs=P("tm", "agent", None), check_vma=False
    )
```

```python
import functools

import jax
import jax.numpy as jnp
from jax import lax
from jax.experimental import pallas as pl
from jax.experimental.pallas import tpu as pltpu
from jax.sharding import PartitionSpec as P

HEAD = 64
CHUNKS = 2
RADIX = 32
EPS = 1e-05
LOG2E = 1.4426950408889634
MIB = 1024 * 1024
VMEM = pl.BlockSpec(memory_space=pltpu.VMEM)
ANY = pl.BlockSpec(memory_space=pl.ANY)
HBM = pl.BlockSpec(memory_space=pltpu.HBM)


def pinned(x):
    return pltpu.with_memory_space_constraint(x, pltpu.VMEM)


def far(x):
    return pltpu.with_memory_space_constraint(x, pltpu.HBM)


def cost(microseconds):
    return pl.CostEstimate(
        flops=int(1.1e9 * microseconds) + 10**6, bytes_accessed=int(3.5e6 * microseconds) + 10**4, transcendentals=0
    )


def away(k, steps, member, line):
    if k == steps - 1:
        return 0
    odd, first = member % 2, 1 - jnp.minimum(line, 1) if isinstance(line, jax.Array) else int(line == 0)
    first_orders, orders = ((2, 1, 3), (3, 2, 1)), ((2, 3, 1), (2, 1, 3))
    even, odd_away = (a[k] * first + b[k] * (1 - first) for a, b in zip(first_orders, orders))
    return even * (1 - odd) + odd_away * odd


def dot(a, b):
    return jnp.dot(a, b, preferred_element_type=jnp.float32)


def dot_t(a, b):
    return lax.dot_general(a, b, (((1,), (1,)), ((), ())), preferred_element_type=jnp.float32)


def norm_scale(values):
    return lax.rsqrt(jnp.mean(values * values, axis=-1, keepdims=True) + EPS)


def gelu(x):
    return 0.5 * x * (1.0 + lax.erf(x * 0.7071067811865476))


def part_copies(tokens, part, target, sem):
    steps, agents = target.shape[:2]
    return [
        pltpu.make_async_copy(tokens.at[step, pl.ds(part * agents, agents)], target.at[step], sem.at[step])
        for step in range(steps)
    ]


def split_kernel(tokens, out, sem):
    copies = part_copies(tokens, 0, out, sem)
    for copy in copies:
        copy.start()
    for copy in copies:
        copy.wait()


def split(tokens):
    steps, agents, width = tokens.shape
    return pl.pallas_call(
        split_kernel,
        out_shape=pltpu.VMEM((steps, agents // CHUNKS, width), tokens.dtype),
        in_specs=[HBM],
        out_specs=VMEM,
        scratch_shapes=[pltpu.SemaphoreType.DMA((steps,))],
        compiler_params=pltpu.CompilerParams(vmem_limit_bytes=4 * MIB),
        cost_estimate=cost(0),
        name="split",
    )(far(tokens))


def stage_kernel(count, taps, gain, order, present, tokens, first_part, *rest):
    sources, rest = rest[:count], rest[count:]
    second_part, partials, tail, targets = rest[0], rest[1:3], rest[3], rest[4 : 4 + count]
    taps_here, gain_here, order_here, present_here, normed, facts, part_sem, sem = rest[4 + count :]
    pairs = [
        (taps, taps_here),
        (gain, gain_here),
        (order, order_here),
        (present, present_here),
        *zip(sources, targets),
    ]
    copies = [pltpu.make_async_copy(source, target, sem.at[i]) for i, (source, target) in enumerate(pairs)]
    later = part_copies(tokens, 1, second_part, part_sem)
    for copy in copies + later:
        copy.start()
    for copy in copies:
        copy.wait()
    agents = order.shape[1]
    facts[...] = jnp.zeros(facts.shape, jnp.float32)
    facts[0:1, :agents] = (order_here[...] // RADIX).astype(jnp.float32)
    facts[1:2, :agents] = (order_here[...] % RADIX).astype(jnp.float32)
    facts[2:3, :agents] = present_here[...].astype(jnp.float32)
    tail[...] = facts[...].astype(jnp.bfloat16)
    steps, reach = first_part.shape[0], taps.shape[0] - 1
    gains = gain_here[...]
    for j, part in enumerate((first_part, second_part)):
        for step in range(steps):
            if j == 1:
                later[step].wait()
            values = part[step].astype(jnp.float32)
            normed[step] = values * norm_scale(values) * gains
            total = values
            for lag in range(min(step, reach) + 1):
                total = total + taps_here[lag : lag + 1, :] * normed[step - lag]
            partials[j][step] = total


def stage(tokens, first_part, taps, gain, order, present, arrays):
    steps, part, width = first_part.shape
    inputs = (taps, gain, order, present)
    return pl.pallas_call(
        functools.partial(stage_kernel, len(arrays)),
        out_shape=[pltpu.VMEM(first_part.shape, first_part.dtype)]
        + [pltpu.VMEM((steps, part, width), jnp.float32)] * CHUNKS
        + [pltpu.VMEM((part, 128), jnp.bfloat16)]
        + [pltpu.VMEM(x.shape, x.dtype) for x in arrays],
        in_specs=[HBM] * (len(inputs) + 1) + [VMEM] + [HBM] * len(arrays),
        out_specs=[VMEM] * (CHUNKS + 2 + len(arrays)),
        scratch_shapes=[pltpu.VMEM(x.shape, x.dtype) for x in inputs]
        + [
            pltpu.VMEM((steps, part, width), jnp.float32),
            pltpu.VMEM((part, 128), jnp.float32),
            pltpu.SemaphoreType.DMA((steps,)),
            pltpu.SemaphoreType.DMA((len(inputs) + len(arrays),)),
        ],
        compiler_params=pltpu.CompilerParams(vmem_limit_bytes=8 * MIB),
        cost_estimate=cost(30),
        name="stage",
    )(*[far(x) for x in (*inputs, tokens)], pinned(first_part), *[far(x) for x in arrays])


def run_pairs(pairs, lead, stages):
    held = [{} for _ in stages]
    for turn in range(pairs + lead * (len(stages) - 1)):
        for i, stage in enumerate(stages):
            pair = turn - lead * i
            if 0 <= pair < pairs:
                held[i][pair] = stage(pair, held[i - 1].pop(pair)) if i else stage(pair)


def mixed_rows(halo, partial, taps, gain, normed, first):
    steps, agents = halo.shape[:2]
    reach = taps.shape[0] - 1
    gains = gain[...] * (lax.axis_index("tm") > 0).astype(jnp.float32)
    for step in range(steps):
        values = halo[step].astype(jnp.float32)
        normed[step] = values * norm_scale(values) * gains
    for step in range(steps):
        total = partial[step]
        for lag in range(step + 1, reach + 1):
            total = total + taps[lag : lag + 1, :] * normed[steps + step - lag]
        first[step * agents : (step + 1) * agents, :] = total.astype(jnp.bfloat16).astype(first.dtype)


def feed_forward(rows, gain, w_in, w_out):
    inner = (rows * norm_scale(rows) * gain[...]).astype(jnp.bfloat16)
    tile, total = 512, [rows]

    def enter(i):
        return dot(inner, w_in[:, i * tile : (i + 1) * tile])

    def activate(i, products):
        return gelu(products).astype(jnp.bfloat16)

    def leave(i, hidden):
        total[0] = total[0] + dot(hidden, w_out[i * tile : (i + 1) * tile, :])

    run_pairs(w_in.shape[1] // tile, 1, [enter, activate, leave])
    return total[0].astype(jnp.bfloat16)


def to_keys(second, gain, w_key, w_value, keyval):
    width = second.shape[1]
    values = second.astype(jnp.float32)
    attn_in = (values * norm_scale(values) * gain[...]).astype(jnp.bfloat16)
    keyval[:, :width] = dot(attn_in, w_key[...]).astype(jnp.bfloat16)
    keyval[:, width : 2 * width] = dot(attn_in, w_value[...]).astype(jnp.bfloat16)
    return attn_in


def conv_kernel(group, halo, partial, taps, gain, tail, *rest):
    steps, agents, width = halo.shape
    outs = rest[:steps]
    normed, first = rest[steps:]
    mixed_rows(halo, partial, taps, gain, normed, first)
    spot = lax.axis_index("agent")
    for k in range(steps):
        step = (spot // group) ^ away(k, steps, spot % group, lax.axis_index("tm"))
        outs[k][:, :width] = first[pl.ds(pl.multiple_of(step * agents, agents), agents), :].astype(jnp.bfloat16)
        outs[k][:, width:] = tail[...]


def conv(group, halo, partial, taps, gain, tail):
    steps, agents, width = halo.shape
    return pl.pallas_call(
        functools.partial(conv_kernel, group),
        out_shape=[jax.ShapeDtypeStruct((agents, width + tail.shape[1]), jnp.bfloat16)] * steps,
        in_specs=[VMEM] * 5,
        out_specs=[VMEM] * steps,
        scratch_shapes=[
            pltpu.VMEM((steps, agents, width), jnp.float32),
            pltpu.VMEM((steps * agents, width), jnp.float32),
        ],
        compiler_params=pltpu.CompilerParams(vmem_limit_bytes=8 * MIB),
        cost_estimate=cost(0),
        name="conv",
    )(halo, *[pinned(x) for x in (partial, taps, gain, tail)])


def front_kernel(group, halo, partial, taps, gain_first, gain_second, w_in, w_out, *rest):
    steps, agents, width = halo.shape
    outs = rest[:steps]
    normed, first, second = rest[steps:]
    mixed_rows(halo, partial, taps, gain_first, normed, first)
    result = feed_forward(first[...], gain_second, w_in, w_out)
    for step in range(steps):
        second[step] = result[step * agents : (step + 1) * agents]
    spot = lax.axis_index("agent")
    for k in range(steps):
        outs[k][...] = second[(spot // group) ^ away(k, steps, spot % group, lax.axis_index("tm"))]


def front(group, halo, partial, taps, gains, w_in, w_out):
    steps, agents, width = halo.shape
    rows = steps * agents
    return pl.pallas_call(
        functools.partial(front_kernel, group),
        out_shape=[jax.ShapeDtypeStruct((agents, width), jnp.bfloat16)] * steps,
        in_specs=[VMEM] * 7,
        out_specs=[VMEM] * steps,
        scratch_shapes=[
            pltpu.VMEM((steps, agents, width), jnp.float32),
            pltpu.VMEM((rows, width), jnp.float32),
            pltpu.VMEM((steps, agents, width), jnp.bfloat16),
        ],
        compiler_params=pltpu.CompilerParams(vmem_limit_bytes=12 * MIB),
        cost_estimate=cost(0),
        name="front",
    )(halo, *[pinned(x) for x in (partial, taps, *gains, w_in, w_out)])


def feed_kernel(count, *refs):
    pieces = refs[:count]
    gain_second, gain_third, w_in, w_out, w_key, w_value = refs[count : count + 6]
    attn_in, keyval, second = refs[count + 6 :]
    width = gain_second.shape[1]
    agents = pieces[0].shape[0]
    for k in range(count):
        keyval[agents * k : agents * (k + 1), 2 * width :] = pieces[k][:, width:]
    first = jnp.concatenate([piece[:, :width].astype(jnp.float32) for piece in pieces], axis=0)
    result = feed_forward(first, gain_second, w_in, w_out)
    second[...] = result
    attn_in[...] = to_keys(result, gain_third, w_key, w_value, keyval)


def feed(pieces, gains, weights):
    rows = sum(piece.shape[0] for piece in pieces)
    width = gains[0].shape[1]
    return pl.pallas_call(
        functools.partial(feed_kernel, len(pieces)),
        out_shape=[
            jax.ShapeDtypeStruct((rows, width), jnp.bfloat16),
            jax.ShapeDtypeStruct((rows, width + pieces[0].shape[1]), jnp.bfloat16),
            jax.ShapeDtypeStruct((rows, width), jnp.bfloat16),
        ],
        in_specs=[VMEM] * (len(pieces) + 6),
        out_specs=[VMEM] * 3,
        compiler_params=pltpu.CompilerParams(vmem_limit_bytes=12 * MIB),
        cost_estimate=cost(0),
        name="feed",
    )(*pieces, *[pinned(x) for x in (*gains, *weights)])


def project_kernel(count, *refs):
    pieces = refs[:count][::-1]
    gain, w_key, w_value, earlier_in, w_query, attn_in, keyval, query = refs[count:]
    query[...] = dot(earlier_in[...], w_query[...]).astype(jnp.bfloat16)
    second = jnp.concatenate([piece[...] for piece in pieces], axis=0)
    attn_in[...] = to_keys(second, gain, w_key, w_value, keyval)


def project(pieces, gain, weights, earlier_in, w_query):
    rows = sum(piece.shape[0] for piece in pieces)
    width = gain.shape[1]
    return pl.pallas_call(
        functools.partial(project_kernel, len(pieces)),
        out_shape=[
            jax.ShapeDtypeStruct((rows, width), jnp.bfloat16),
            jax.ShapeDtypeStruct((rows, 2 * width), jnp.bfloat16),
            jax.ShapeDtypeStruct(earlier_in.shape, jnp.bfloat16),
        ],
        in_specs=[VMEM] * (len(pieces) + 5),
        out_specs=[VMEM] * 3,
        compiler_params=pltpu.CompilerParams(vmem_limit_bytes=8 * MIB),
        cost_estimate=cost(25),
        name="project",
    )(*reversed(pieces), *[pinned(x) for x in (gain, *weights)], earlier_in, pinned(w_query))


def block_order(group, chunks):
    early = [(r, 0) for r in range(group)] + [(0, j) for j in range(1, chunks)]
    return early + [(r, j) for j in range(1, chunks) for r in range(1, group)]


def write_mask(steps, chunks, agents, width, blocks, bias):
    group = len(blocks)
    now = (lax.axis_index("tm") * steps + lax.axis_index("agent") // group).astype(jnp.float32)
    lane = lax.broadcasted_iota(jnp.int32, (agents, 128), 1)
    sublane = lax.broadcasted_iota(jnp.int32, (agents, 128), 0)
    tiles = {}
    for r in range(group):
        for k in range(steps):
            tile = blocks[r][agents * k : agents * (k + 1), 2 * width :].astype(jnp.float32)
            tiles[k, r] = (tile[0:1] * RADIX + tile[1:2], tile[2:3])
    own = jnp.concatenate(
        [
            jnp.sum(jnp.where(lane == sublane + j * agents, tiles[k, 0][0], 0.0), axis=1, keepdims=True)
            for k in range(steps)
            for j in range(chunks)
        ],
        axis=0,
    )
    row_lane = lax.broadcasted_iota(jnp.int32, (1, 128), 1)
    per_tile = 128 // agents
    start = 0
    for r, j in block_order(group, chunks):
        for first in range(0, steps, per_tile):
            both = [None, None]
            for i in range(per_tile):
                for f in (0, 1):
                    moved = pltpu.roll(tiles[first + i, r][f], ((i - j) * agents) % 128, 1)
                    both[f] = moved if i == 0 else jnp.where(row_lane >= i * agents, moved, both[f])
            order, present = both
            alive = jnp.where(now < present, order, 1e9)
            visible = (alive < own) | (order == own)
            bias[:, start : start + 128] = jnp.where(visible, 0.0, -1e30)
            start += 128


def rows_of(parts, ks, agents, columns):
    return jnp.concatenate([part[agents * k : agents * (k + 1), columns] for k in ks for part in parts], axis=0)


def pair_stages(queries_of, blocks, bias, top_of, low):
    width = blocks[0].shape[1] // 2 // 128 * 128

    def products(pair):
        queries = queries_of(pair)
        zeros = jnp.zeros_like(queries)
        stacked = jnp.concatenate([jnp.where(low, queries, zeros), jnp.where(low, zeros, queries)], axis=0)
        key = jnp.concatenate([block[:, 128 * pair : 128 * pair + 128] for block in blocks], axis=0)
        return dot_t(stacked, key)

    def weigh(pair, scores):
        rows, keys = scores.shape[0] // 2, scores.shape[1]
        tops, weights = [], []
        for half in range(2):
            here = scores[half * rows : (half + 1) * rows] * (LOG2E * HEAD ** (-0.5)) + bias
            highest = jnp.broadcast_to(jnp.max(here, axis=1, keepdims=True), (rows, 128))
            if top_of is not None:
                highest = jnp.maximum(highest, top_of(pair, half))
            tops.append(highest)
            wide = jnp.concatenate([highest] * (keys // 128), axis=1)
            weights.append(jnp.exp2(here - wide).astype(jnp.bfloat16))
        return tops, jnp.concatenate(weights, axis=0)

    def sums(pair, made):
        tops, weights = made
        start = width + 128 * pair
        value = jnp.concatenate([block[:, start : start + 128] for block in blocks], axis=0)
        return tops, dot(weights, jnp.concatenate([value, jnp.ones(value.shape, jnp.bfloat16)], axis=1))

    return [products, weigh, sums]


def merged(low, total):
    rows = total.shape[0] // 2
    return jnp.where(low, total[:rows], total[rows:])


def early_kernel(ks, steps, chunks, group, query, attn_in, w_query, *refs):
    count = group + chunks - 1
    blocks, (own_query, bias, number, weight, top_low, top_high) = refs[:count], refs[count:]
    own_query[...] = dot(attn_in[...], w_query[...]).astype(jnp.bfloat16)
    rows, width = number.shape
    write_mask(steps, chunks, query.shape[0] // steps, width, blocks[:group], bias)
    agents = rows // (len(ks) * chunks)
    low = lax.broadcasted_iota(jnp.int32, (rows, 128), 1) < HEAD
    keys = sum(block.shape[0] for block in blocks)
    here = bias[ks[0] * agents * chunks : ks[0] * agents * chunks + rows, :keys]

    def columns(pair):
        return slice(128 * pair, 128 * pair + 128)

    def keep(pair, made):
        tops, total = made
        number[:, columns(pair)] = merged(low, total[:, :128])
        weight[:, columns(pair)] = merged(low, total[:, 128:])
        top_low[:, columns(pair)] = tops[0]
        top_high[:, columns(pair)] = tops[1]

    stages = pair_stages(lambda pair: rows_of((query, own_query), ks, agents, columns(pair)), blocks, here, None, low)
    run_pairs(width // 128, 2, [*stages, keep])


def early(ks, steps, group, query, attn_in, w_query, blocks):
    count, width = query.shape
    rows = count * CHUNKS
    state = pltpu.VMEM((len(ks) * rows // steps, width), jnp.float32)
    return pl.pallas_call(
        functools.partial(early_kernel, ks, steps, CHUNKS, group),
        out_shape=[jax.ShapeDtypeStruct(query.shape, jnp.bfloat16), pltpu.VMEM((rows, rows * group), jnp.float32)]
        + [state] * 4,
        in_specs=[VMEM] * (3 + len(blocks)),
        out_specs=[VMEM] * 6,
        compiler_params=pltpu.CompilerParams(vmem_limit_bytes=16 * MIB),
        cost_estimate=cost(0),
        name="early",
    )(query, attn_in, pinned(w_query), *blocks)


def attend_kernel(ks, chunks, count, begun, skipped, *refs):
    mine = 1 + len(ks) * (chunks - 1)
    queries, seconds, (w_output, bias) = refs[:chunks], refs[chunks : chunks + mine], refs[chunks + mine : chunks + mine + 2]
    rest = refs[chunks + mine + 2 :]
    blocks, state = rest[:count], rest[count : count + begun]
    outs = rest[count + begun :]
    width, agents = w_output.shape[1], queries[0].shape[0] // 4
    rows = len(ks) * chunks * agents
    low = lax.broadcasted_iota(jnp.int32, (rows, 128), 1) < HEAD
    keys = sum(block.shape[0] for block in blocks)
    here = bias[ks[0] * agents * chunks : ks[0] * agents * chunks + rows, bias.shape[1] - keys :]
    begun_rows = slice(skipped, skipped + rows)

    def columns(pair):
        return slice(128 * pair, 128 * pair + 128)

    residual = []
    for i, k in enumerate(ks):
        residual += [seconds[0][agents * k : agents * (k + 1)]]
        residual += [piece[...] for piece in seconds[1 + i * (chunks - 1) : 1 + (i + 1) * (chunks - 1)]]
    result = [jnp.concatenate(residual, axis=0).astype(jnp.float32)]

    def keep(pair, made):
        tops, total = made
        number, weight = merged(low, total[:, :128]), merged(low, total[:, 128:])
        if begun:
            drop = [state[2 + half][begun_rows, columns(pair)] - tops[half] for half in range(2)]
            shrink = jnp.exp2(jnp.where(low, *drop))
            number = number + state[0][begun_rows, columns(pair)] * shrink
            weight = weight + state[1][begun_rows, columns(pair)] * shrink
        return (number / weight).astype(jnp.bfloat16)

    waiting, together = [], 2 if begun else width // 128

    def output(pair, attended):
        waiting.append(attended)
        if len(waiting) == together:
            features = slice(128 * (pair + 1 - together), 128 * (pair + 1))
            result[0] = result[0] + dot(jnp.concatenate(waiting, axis=1), w_output[features, :])
            waiting.clear()

    stages = pair_stages(
        lambda pair: rows_of(queries, ks, agents, columns(pair)),
        blocks,
        here,
        (lambda pair, half: state[2 + half][begun_rows, columns(pair)]) if begun else None,
        low,
    )
    run_pairs(width // 128, 2, [*stages, keep, output])
    for i in range(len(ks)):
        outs[i][...] = result[0][i * agents * chunks : (i + 1) * agents * chunks].astype(jnp.bfloat16)


def attend(ks, queries, seconds, w_output, bias, blocks, state, skipped, agents, microseconds):
    width = queries[0].shape[1]
    piece = jax.ShapeDtypeStruct((agents, width), jnp.bfloat16)
    return pl.pallas_call(
        functools.partial(attend_kernel, ks, len(queries), len(blocks), len(state), skipped),
        out_shape=[piece] * len(ks),
        in_specs=[VMEM] * (len(queries) + len(seconds) + 2 + len(blocks) + len(state)),
        out_specs=[VMEM] * len(ks),
        compiler_params=pltpu.CompilerParams(vmem_limit_bytes=16 * MIB),
        cost_estimate=cost(microseconds),
        name="attend",
    )(*queries, *seconds, pinned(w_output), pinned(bias), *blocks, *[pinned(x) for x in state])


def put_back_kernel(steps, group, *refs):
    pieces, out, sem = refs[:steps][::-1], refs[steps], refs[steps + 1]
    spot = lax.axis_index("agent")
    copies = []
    for k in reversed(range(steps)):
        target = out.at[(spot // group) ^ away(k, steps, spot % group, lax.axis_index("tm"))]
        copies.append(pltpu.make_async_copy(pieces[k], target, sem.at[k]))
    for copy in copies:
        copy.start()
    for copy in copies:
        copy.wait()


def put_back(group, pieces, shape):
    return pl.pallas_call(
        functools.partial(put_back_kernel, shape[0], group),
        out_shape=jax.ShapeDtypeStruct(shape, jnp.bfloat16),
        in_specs=[VMEM] * len(pieces),
        out_specs=ANY,
        scratch_shapes=[pltpu.SemaphoreType.DMA((len(pieces),))],
        compiler_params=pltpu.CompilerParams(vmem_limit_bytes=4 * MIB),
        cost_estimate=cost(0),
        name="put_back",
    )(*pieces)


def after(x, *others):
    return lax.optimization_barrier((x, *others))[0]


def per_device(
    tokens,
    conv_taps,
    norm_first,
    norm_second,
    norm_third,
    w_in,
    w_out,
    w_query,
    w_key,
    w_value,
    w_output,
    agent_order,
    present_steps,
):
    steps, agents, width = tokens.shape
    tm_count, count = lax.axis_size("tm"), lax.axis_size("agent")
    group = count // steps
    part = agents // CHUNKS
    assert group * steps == count and steps == 4 and 128 % part == 0 and CHUNKS == 2 and group > 1

    def across(x, k):
        if k == steps - 1:
            return x
        pairs = [
            (line * count + i, line * count + ((i // group) ^ away(k, steps, i % group, line)) * group + i % group)
            for line in range(tm_count)
            for i in range(count)
        ]
        return lax.ppermute(x, ("tm", "agent"), pairs)

    def within(x, r):
        return lax.ppermute(x, "agent", [(i, (i // group) * group + ((i % group) ^ r)) for i in range(count)])

    first_part = split(tokens)
    second_part, *partials, tail, taps, gain_first, gain_second, gain_third = stage(
        tokens,
        first_part,
        conv_taps,
        norm_first.reshape(1, width),
        agent_order.reshape(1, agents),
        present_steps.reshape(1, agents),
        [conv_taps] + [x.reshape(1, width) for x in (norm_first, norm_second, norm_third)],
    )
    halos = [lax.ppermute(x, "tm", [(i, (i + 1) % tm_count) for i in range(tm_count)]) for x in (first_part, second_part)]
    halos[0] = after(halos[0], tail)
    made = conv(group, halos[0], partials[0], taps, gain_first, tail)
    last = made[-1]
    pieces = [[across(made[k], k) for k in range(steps)]]
    for j in range(1, CHUNKS):
        halos[j] = after(halos[j], last)
        made = list(front(group, halos[j], partials[j], taps, (gain_first, gain_second), w_in, w_out))
        last = made[-1]
        made[steps - 2] = after(made[steps - 2], pieces[j - 1][0])
        pieces.append([across(made[k], k) for k in range(steps)])
    pieces[0][-1] = after(pieces[0][-1], last)
    first_in, keyval, second = feed(pieces[0], (gain_second, gain_third), (w_in, w_out, w_key, w_value))
    blocks = {(0, 0): keyval, **{(r, 0): within(keyval, r) for r in range(1, group)}}
    attn_in, keyval, query = project(pieces[1], gain_third, (w_key, w_value), first_in, w_query)
    keyval = after(keyval, *blocks.values())
    blocks.update({(0, 1): keyval, **{(r, 1): within(keyval, r) for r in range(1, group)}})
    blocks = [blocks[spot] for spot in block_order(group, CHUNKS)]
    ready = group + CHUNKS - 1
    far_ks, near_ks = (0, 1), (2, 3)
    own_query, bias, *state = early(far_ks, steps, group, query, attn_in, w_query, blocks[:ready])

    def finish(ks, blocks, state, skipped, microseconds):
        seconds = [second] + [pieces[j][k] for k in ks for j in range(1, CHUNKS)]
        return attend(
            ks, (query, own_query), seconds, w_output, bias, blocks, state, skipped, agents, microseconds
        )

    late = blocks[ready:]
    results = [*finish(far_ks, late, state, 0, 0), *finish(near_ks, blocks, [], 0, 10)]
    return put_back(group, [across(results[k], k) for k in reversed(range(steps))], tokens.shape)


def solution(mesh):
    in_specs = (P("tm", "agent", None),) + (P(),) * 10 + (P("agent"), P("agent"))
    return jax.shard_map(
        per_device, mesh=mesh, in_specs=in_specs, out_specs=P("tm", "agent", None), check_vma=False
    )
```
